32 devices in a mesh: dp: 4 (over y, x), seq: 8 (over z, core).
Axes of the slice: x: 2, y: 2, z: 4, core: 2. Of those that a mesh axis runs over, the one named last changes fastest.
Arguments:
- hidden_in: bfloat16 [8, 1024, 768], P('dp', 'seq'), may hold values from -6 to 6
- lengths: int32 [8, 8], P('dp'), may hold values from 0 to 1024, as said below
- gain_one: float32 [768], replicated, may hold values from 0.1 to 1.9
- in_weight: bfloat16 [768, 2304], replicated, may hold values from -0.21875 to 0.21875
- short_kernel: float32 [3, 2304], replicated, may hold values from -3.5 to 3.5
- skip_gain: float32 [768], replicated, may hold values from -1 to 1
- decay_rate: float32 [768], replicated, may hold values from 1e-05 to 0.05
- filt_first: float32 [33, 64], replicated, may hold values from -1 to 1
- filt_second: float32 [64, 64], replicated, may hold values from -0.75 to 0.75
- filt_third: float32 [64, 768], replicated, may hold values from -0.75 to 0.75
- out_weight: bfloat16 [768, 768], replicated, may hold values from -0.21875 to 0.21875
- gain_two: float32 [768], replicated, may hold values from 0.1 to 1.9
- ff_up: bfloat16 [768, 3072], replicated, may hold values from -0.21875 to 0.21875
- ff_down: bfloat16 [3072, 768], replicated, may hold values from -0.109375 to 0.109375
- out_grad: bfloat16 [8, 1024, 768], P('dp', 'seq'), may hold values from -6 to 6
Outputs:
- block_out: bfloat16 [8, 1024, 768], P('dp', 'seq')
- input_grad: float32 [8, 1024, 768], P('dp', 'seq')
- gain_one_grad: float32 [768], replicated
- in_weight_grad: float32 [768, 2304], replicated
- kernel_grad: float32 [3, 2304], replicated
- skip_grad: float32 [768], replicated
- first_grad: float32 [33, 64], replicated
- second_grad: float32 [64, 64], replicated
- third_grad: float32 [64, 768], replicated
- out_weight_grad: float32 [768, 768], replicated
- gain_two_grad: float32 [768], replicated
- up_grad: float32 [768, 3072], replicated
- down_grad: float32 [3072, 768], replicated
The draws below stay inside these ranges and needn't reach their ends.
Inputs may be any that keep to these rules, and one draw needn't show every extreme that they name: Row r lists the lengths of the documents packed in row r, in order from the row's first position, then zeros; every document has 128 positions or more, and the positions after the last document are padding. In each group of 2 rows on one index of dp, one row, drawn from the seed, holds a single document of 1024 positions.
All inputs are finite; a program needn't handle non-finite values.
Results may differ from the reference program's by a relative error of at most 0.012.
Values may be sent and summed in bfloat16 or wider, within the bound.
No kernel may reach another device: no remote copies, remote signals or barrier semaphores. Data moves between devices by JAX's collectives and lax.ppermute only.
A program may use at most 384 MiB of HBM per device.

```python
import math
import jax
import jax.numpy as jnp
from jax import lax

D = 768
FF = 3072
EMB = 33
FILT = 64
KS = 3
ROWS_DP = 2
ROW_LEN = 1024
ROWS = 8
LMIN = 128
MAXDOC = 8
N_DP = 4


def draw_lengths(key, part):
    key = jax.random.fold_in(key, 7)
    level_count = (ROW_LEN // LMIN).bit_length()
    key_level, key_piece, key_pad, key_whole = jax.random.split(key, 4)
    level_pick = jax.random.randint(key_level, (ROWS, 1), 0, level_count)
    longest = jnp.minimum(LMIN * jnp.left_shift(jnp.ones_like(level_pick), level_pick), ROW_LEN)
    pieces = jax.random.randint(key_piece, (ROWS, MAXDOC), LMIN, longest + 1)
    usable_room = ROW_LEN - jax.random.randint(key_pad, (ROWS, 1), 0, LMIN)
    leading = jnp.minimum(pieces[:, :1], usable_room)
    pieces = jnp.concatenate([leading, pieces[:, 1:]], axis=1)
    doc_ends = jnp.cumsum(pieces, axis=1)
    kept_pieces = jnp.where(doc_ends <= usable_room, pieces, 0)
    chosen = jax.random.randint(key_whole, (N_DP, 1), 0, ROWS_DP)
    row_numbers = jnp.arange(ROWS, dtype=jnp.int32).reshape(N_DP, ROWS_DP) % ROWS_DP
    whole_row = (row_numbers == chosen).reshape(ROWS, 1)
    columns = jnp.arange(MAXDOC, dtype=jnp.int32).reshape(1, MAXDOC)
    single_doc = jnp.where(columns == 0, ROW_LEN, 0)
    return jnp.where(whole_row, single_doc, kept_pieces).astype(jnp.int32)


def steps_of(own_key, dims, cuts, least, largest):
    def one(dim, shards_of):
        draws = jax.random.uniform(jax.random.fold_in(jax.random.fold_in(own_key, 6), dim), (shards_of,), jnp.float32, least / len(cuts), largest / len(cuts))
        return jnp.repeat(jnp.exp(draws), dims[dim] // shards_of).reshape((-1,) + (1,) * (len(dims) - dim - 1))

    loudness = one(*cuts[0])
    for cut in cuts[1:]:
        loudness = loudness * one(*cut)
    return loudness


def bell_draw(rng, shape, scale, reach, cuts=(), kind=jnp.bfloat16):
    drawn = scale * jax.random.normal(rng, shape, jnp.float32)
    if cuts:
        drawn = drawn * steps_of(rng, shape, cuts, -0.22, 0.18)
    return jnp.clip(drawn, -reach, reach).astype(kind)


def setup_inputs(seed: int = 0) -> dict:
    keys = jax.random.split(jax.random.key(seed), 16)
    hidden_in = bell_draw(keys[0], (ROWS, ROW_LEN, D), 1.0, 6.0, ((0, 4), (1, 8)))
    lengths = draw_lengths(jax.random.fold_in(keys[15], 71), 0)
    gain_one = jnp.clip(1.0 + 0.18 * jax.random.normal(keys[2], (D,), jnp.float32), 0.1, 1.9)
    in_weight = bell_draw(keys[3], (D, 3 * D), D ** -0.5, 0.21875)
    short_kernel = bell_draw(keys[4], (KS, 3 * D), KS ** -0.5, 3.5, (), jnp.float32)
    skip_gain = jnp.clip(jax.random.uniform(keys[5], (D,), jnp.float32, -1.0, 1.0), -1.0, 1.0)
    decay_rate = jnp.clip(jnp.exp(jax.random.uniform(keys[6], (D,), jnp.float32, math.log(9.999999747378752e-06), math.log(0.05))), 9.999999747378752e-06, 0.05)
    filt_first = bell_draw(keys[7], (EMB, FILT), EMB ** -0.5, 1.0, (), jnp.float32)
    filt_second = bell_draw(keys[8], (FILT, FILT), FILT ** -0.5, 0.75, (), jnp.float32)
    filt_third = bell_draw(keys[9], (FILT, D), FILT ** -0.5, 0.75, (), jnp.float32)
    out_weight = bell_draw(keys[10], (D, D), D ** -0.5, 0.21875)
    gain_two = jnp.clip(1.0 + 0.18 * jax.random.normal(keys[11], (D,), jnp.float32), 0.1, 1.9)
    ff_up = bell_draw(keys[12], (D, FF), D ** -0.5, 0.21875)
    ff_down = bell_draw(keys[13], (FF, D), FF ** -0.5, 0.109375)
    out_grad = bell_draw(keys[14], (ROWS, ROW_LEN, D), 1.0, 6.0, ((0, 4), (1, 8)))
    return {"hidden_in": hidden_in, "lengths": lengths, "gain_one": gain_one, "in_weight": in_weight, "short_kernel": short_kernel, "skip_gain": skip_gain, "decay_rate": decay_rate, "filt_first": filt_first, "filt_second": filt_second, "filt_third": filt_third, "out_weight": out_weight, "gain_two": gain_two, "ff_up": ff_up, "ff_down": ff_down, "out_grad": out_grad}


FULL_PRECISION = lax.Precision.HIGHEST

@jax.custom_vjp
def low(v):
    return lax.optimization_barrier(v.astype(jnp.bfloat16)).astype(jnp.float32)

@jax.custom_vjp
def low_back(v):
    return v

def low_keep(v):
    return (low(v), None)

def low_pass(kept, grad):
    return (grad,)

def back_keep(v):
    return (v, None)

def back_low(kept, grad):
    return (low(grad),)
low.defvjp(low_keep, low_pass)
low_back.defvjp(back_keep, back_low)

def layer_norm(values, gain_vector):
    center = values - lax.optimization_barrier(jnp.mean(values, axis=-1, keepdims=True))
    spread = lax.optimization_barrier(jnp.mean(center * center, axis=-1, keepdims=True))
    return center * lax.rsqrt(spread + 1e-05) * gain_vector

def filter_taps(weight_one, weight_two, weight_three, decay_values, length):
    band_count = (weight_one.shape[0] - 1) // 2
    positions = jnp.arange(length, dtype=jnp.int32)
    orders = jnp.arange(1, band_count + 1, dtype=jnp.int32)
    phase_turns = positions[:, None] * orders[None, :] % length
    angles = phase_turns.astype(jnp.float32) * (2.0 * math.pi / length)
    places = positions.astype(jnp.float32)
    embedding = jnp.concatenate([places[:, None] / length, jnp.cos(angles), jnp.sin(angles)], axis=1)
    hidden_one = jnp.sin(jnp.dot(embedding, weight_one, precision=FULL_PRECISION))
    hidden_two = jnp.sin(jnp.dot(hidden_one, weight_two, precision=FULL_PRECISION))
    raw_taps = jnp.dot(hidden_two, weight_three, precision=FULL_PRECISION)
    return raw_taps * jnp.exp(-places[:, None] * decay_values[None, :]) * length ** (-0.5)

def short_conv_row(projected, kernel_taps, segment):
    zero_row = jnp.zeros((1, projected.shape[1]), jnp.float32)
    prior_one = jnp.concatenate([zero_row, projected[:-1]], axis=0)
    prior_two = jnp.concatenate([zero_row, zero_row, projected[:-2]], axis=0)
    missing = jnp.full((1,), -1, jnp.int32)
    segment_one = jnp.concatenate([missing, segment[:-1].astype(jnp.int32)]).astype(jnp.int32)
    segment_two = jnp.concatenate([missing, missing, segment[:-2].astype(jnp.int32)]).astype(jnp.int32)
    near_one = (segment == segment_one).astype(jnp.float32)[:, None]
    near_two = (segment == segment_two).astype(jnp.float32)[:, None]
    return kernel_taps[0] * projected + kernel_taps[1] * prior_one * near_one + kernel_taps[2] * prior_two * near_two

def long_conv(signal, filter_values, segment):
    padded_len = 2 * ROW_LEN
    filter_spectrum = jnp.fft.rfft(filter_values, n=padded_len, axis=0)

    def add_document(running_sum, document):
        doc_mask = (segment == document).astype(jnp.float32)[:, None]
        spectrum = jnp.fft.rfft(signal * doc_mask, n=padded_len, axis=0) * filter_spectrum
        partial_conv = jnp.fft.irfft(spectrum, n=padded_len, axis=0)[:ROW_LEN]
        return (running_sum + partial_conv * doc_mask, None)
    running_sum, ignored = lax.scan(add_document, jnp.zeros((ROW_LEN, D), jnp.float32), jnp.arange(MAXDOC, dtype=jnp.int32))
    return running_sum

def block_row(row_in, row_lengths, filter_values, weights):
    gain_one, in_weight, short_kernel, skip_gain, out_weight, gain_two, ff_up, ff_down = weights
    doc_ends = jnp.cumsum(row_lengths).astype(jnp.int32)
    positions = jnp.arange(ROW_LEN, dtype=jnp.int32)
    segment = lax.optimization_barrier(jnp.sum((doc_ends[None, :] <= positions[:, None]).astype(jnp.int32), axis=1)).astype(jnp.int32)
    live_rows = (positions < doc_ends[-1]).astype(jnp.float32)[:, None]
    normed_one = low(layer_norm(row_in, gain_one))
    projected = low(low_back(jnp.dot(normed_one, in_weight, precision=FULL_PRECISION)))
    mixed_rows = short_conv_row(projected, short_kernel, segment)
    value_part = mixed_rows[:, :D]
    gate_inner = mixed_rows[:, D:2 * D]
    gate_outer = mixed_rows[:, 2 * D:]
    signal = low(value_part * gate_inner * live_rows)
    conv_out = low_back(long_conv(signal, filter_values, segment) + skip_gain * signal)
    gated_rows = low(gate_outer * conv_out)
    middle = row_in + low_back(jnp.dot(gated_rows, out_weight, precision=FULL_PRECISION))
    normed_two = low(layer_norm(middle, gain_two))
    pre_act = low_back(jnp.dot(normed_two, ff_up, precision=FULL_PRECISION))
    activated = low(jax.nn.gelu(pre_act))
    return middle + jnp.dot(activated, ff_down, precision=FULL_PRECISION)

def reference(hidden_in, lengths, gain_one, in_weight, short_kernel, skip_gain, decay_rate, filt_first, filt_second, filt_third, out_weight, gain_two, ff_up, ff_down, out_grad):
    params = (gain_one, in_weight.astype(jnp.float32), short_kernel, skip_gain, filt_first, filt_second, filt_third, out_weight.astype(jnp.float32), gain_two, ff_up.astype(jnp.float32), ff_down.astype(jnp.float32))

    def forward(inputs, weights):
        filter_values = filter_taps(weights[4], weights[5], weights[6], decay_rate, ROW_LEN)
        row_weights = (weights[0], weights[1], weights[2], weights[3], weights[7], weights[8], weights[9], weights[10])

        def one_row(row_item):
            return block_row(row_item[0], row_item[1], filter_values, row_weights)
        return lax.map(jax.checkpoint(one_row), (inputs, lengths))
    outputs, pullback = jax.vjp(forward, hidden_in.astype(jnp.float32), params)
    grad_inputs, weight_grads = pullback(out_grad.astype(jnp.float32))
    return (outputs.astype(jnp.bfloat16), grad_inputs, weight_grads[0], weight_grads[1], weight_grads[2], weight_grads[3], weight_grads[4], weight_grads[5], weight_grads[6], weight_grads[7], weight_grads[8], weight_grads[9], weight_grads[10])
```

```python
from functools import partial
import math

import jax
import jax.numpy as jnp
import numpy as np
from jax import lax
from jax.experimental import pallas as pl
from jax.experimental.pallas import tpu as pltpu
from jax.sharding import PartitionSpec as P

FULL_PRECISION = lax.Precision.HIGHEST
BF16 = jnp.bfloat16
F32 = jnp.float32
AXES = ("dp", "seq")
VMEM_BYTES = 40 * 1024 * 1024


def swap(value, bit):
    count = lax.axis_size(AXES)
    return lax.ppermute(value, AXES, [(i, i ^ bit) for i in range(count)])


def shifted(value, steps):
    count = lax.axis_size("seq")
    first, last = max(0, -steps), min(count, count - steps)
    return lax.ppermute(value, "seq", [(i, i + steps) for i in range(first, last)])


def my_bit(index, bit):
    return (index // bit) % 2


def halve(value, index, bits):
    for bit in bits:
        pair = value.reshape((2, value.shape[0] // 2) + value.shape[1:])
        mine = my_bit(index, bit)
        keep = lax.dynamic_index_in_dim(pair, mine, 0, keepdims=False)
        send = lax.dynamic_index_in_dim(pair, 1 - mine, 0, keepdims=False)
        value = (keep.astype(F32) + swap(send, bit).astype(F32)).astype(value.dtype)
    return value


def double(value, index, bits):
    for bit in reversed(bits):
        other = swap(value, bit)
        low = my_bit(index, bit) == 0
        value = jnp.concatenate(
            [jnp.where(low, value, other), jnp.where(low, other, value)], axis=0
        )
    return value


def sum_all(value, count):
    bit = 1
    while bit < count:
        value = value + swap(value, bit)
        bit *= 2
    return value


def spectral_tables(block):
    points = 2 * block
    spot = np.arange(block)
    freq = np.arange(block)
    angle = (spot[:, None] * freq[None, :] % points) * (2.0 * math.pi / points)
    real, imag = np.cos(angle), -np.sin(angle)
    imag[:, 0] = 1.0 - 2.0 * (spot % 2)
    forward = np.concatenate([real, imag], axis=1)
    late = spot + block
    angle = (freq[:, None] * late[None, :] % points) * (2.0 * math.pi / points)
    weight = np.where(freq == 0, 1.0, 2.0)[:, None] / points
    real, imag = weight * np.cos(angle), -weight * np.sin(angle)
    imag[0, :] = (1.0 - 2.0 * (late % 2)) / points
    inverse = np.concatenate([real, imag], axis=0)
    return forward.astype(np.float32), inverse.astype(np.float32)


def split_table(table):
    high = table.astype(jnp.bfloat16)
    low = (table - high.astype(np.float32)).astype(jnp.bfloat16)
    return np.asarray(high), np.asarray(low)


def two_pass(table):
    high, low = split_table(table)
    return np.concatenate([high, low], axis=0)


def three_pass(table):
    high, low = split_table(table)
    return np.concatenate([high, high, low], axis=0)


def dot(left, right):
    return jnp.dot(left, right, preferred_element_type=F32)


def spectra(value_ref, head_ref, table_ref, head_out, rest_out, group):
    count, channels, block = value_ref.shape

    def step(i, carry):
        spot = pl.ds(i * group, group)
        whole = value_ref[spot].astype(F32)
        first = whole * head_ref[spot]
        both = jnp.concatenate([first, whole - first], axis=0).astype(BF16)
        both = both.reshape(2 * group * channels, block)
        found = dot(jnp.concatenate([both, both], axis=1), table_ref[...])
        found = found.reshape(2 * group, channels, 2 * block)
        head_out[spot] = found[:group]
        rest_out[spot] = found[group:]
        return carry

    lax.fori_loop(0, count // group, step, 0)


def back_to_time(head_spec, rest_spec, head_ref, table_ref, out_ref, group):
    count, channels, double_block = head_spec.shape

    def step(i, carry):
        spot = pl.ds(i * group, group)
        both = jnp.concatenate([head_spec[spot], rest_spec[spot]], axis=0)
        both = both.reshape(2 * group * channels, double_block)
        high = both.astype(BF16)
        low = (both - high.astype(F32)).astype(BF16)
        found = dot(jnp.concatenate([high, low, high], axis=1), table_ref[...])
        found = found.reshape(2 * group, channels, double_block // 2)
        mask = head_ref[spot]
        rest = found[group:]
        out_ref[spot] = (rest + mask * (found[:group] - rest)).astype(out_ref.dtype)
        return carry

    lax.fori_loop(0, count // group, step, 0)


def conv_kernel(
    rows, group, from_ref, plain_ref, value_ref, head_ref, hr_ref, hi_ref, hm_ref,
    forward_ref, inverse_ref, out_ref, head_spec, rest_spec, head_sum, rest_sum,
):
    count, channels, block = value_ref.shape
    spectra(value_ref, head_ref, forward_ref, head_spec, rest_spec, group)

    def product(real, imag, lag):
        hr, hi, hm = hr_ref[lag], hi_ref[lag], hm_ref[lag]
        return real * hr - imag * hi, real * hi + imag * hm

    def own(j, carry):
        head_real, head_imag = product(head_spec[j, :, :block], head_spec[j, :, block:], 0)
        head_sum[j, :, :block] = head_real
        head_sum[j, :, block:] = head_imag
        rest_real, rest_imag = product(rest_spec[j, :, :block], rest_spec[j, :, block:], 0)
        rest_sum[j, :, :block] = rest_real
        rest_sum[j, :, block:] = rest_imag
        rest_spec[j] = rest_spec[j] + plain_ref[j].astype(F32) * head_spec[j]
        return carry

    lax.fori_loop(0, count, own, 0)

    def reach(j, carry):
        spot, row = j // rows, j % rows

        def include(source, sums):
            k = source * rows + row
            real, imag = product(
                rest_spec[k, :, :block], rest_spec[k, :, block:], spot - source
            )
            return sums[0] + real, sums[1] + imag

        start = (head_sum[j, :, :block], head_sum[j, :, block:])
        real, imag = lax.fori_loop(from_ref[j], spot, include, start)
        head_sum[j, :, :block] = real
        head_sum[j, :, block:] = imag
        return carry

    lax.fori_loop(rows, count, reach, 0)
    back_to_time(head_sum, rest_sum, head_ref, inverse_ref, out_ref, group)


def conv_back_kernel(
    rows, group, until_ref, plain_ref, value_ref, head_ref, hr_ref, hi_ref, hm_ref,
    forward_ref, inverse_ref, out_ref, head_spec, rest_spec, head_sum, rest_sum,
):
    count, channels, block = value_ref.shape
    spectra(value_ref, head_ref, inverse_ref, head_spec, rest_spec, group)

    def product(real, imag, lag):
        hr, hi, hm = hr_ref[lag], hi_ref[lag], hm_ref[lag]
        return real * hr + imag * hi, imag * hm - real * hi

    def reach(j, carry):
        spot, row = j // rows, j % rows

        def include(source, sums):
            k = source * rows + row
            real, imag = product(
                head_spec[k, :, :block], head_spec[k, :, block:], source - spot
            )
            return sums[0] + real, sums[1] + imag

        empty = jnp.zeros((channels, block), F32)
        real, imag = lax.fori_loop(spot + 1, until_ref[j] + 1, include, (empty, empty))
        plain = plain_ref[j].astype(F32)
        head_real, head_imag = product(head_spec[j, :, :block], head_spec[j, :, block:], 0)
        head_sum[j, :, :block] = head_real + plain * real
        head_sum[j, :, block:] = head_imag + plain * imag
        rest_real, rest_imag = product(rest_spec[j, :, :block], rest_spec[j, :, block:], 0)
        rest_sum[j, :, :block] = rest_real + (1.0 - plain) * real
        rest_sum[j, :, block:] = rest_imag + (1.0 - plain) * imag
        return carry

    lax.fori_loop(0, count, reach, 0)
    back_to_time(head_sum, rest_sum, head_ref, forward_ref, out_ref, group)


def filter_grad_kernel(
    rows, group, from_ref, plain_ref, value_ref, grad_ref, head_ref, forward_ref,
    inverse_ref, back_ref, out_ref, head_spec, rest_spec, grad_head, grad_rest, total,
):
    count, channels, block = value_ref.shape
    lags = count // rows
    spectra(value_ref, head_ref, forward_ref, head_spec, rest_spec, group)
    spectra(grad_ref, head_ref, inverse_ref, grad_head, grad_rest, group)
    lane = lax.broadcasted_iota(jnp.int32, (channels, block), 1)
    base = lane == 0

    def product(grad, spec, k, j):
        gr, gi = grad[k, :, :block], grad[k, :, block:]
        sr, si = spec[j, :, :block], spec[j, :, block:]
        masked = jnp.where(base, 0.0, si)
        swapped = jnp.where(base, si, sr)
        return gr * sr + gi * masked, gi * swapped - gr * masked

    def own(j, sums):
        head = product(grad_head, head_spec, j, j)
        rest = product(grad_rest, rest_spec, j, j)
        rest_spec[j] = rest_spec[j] + plain_ref[j].astype(F32) * head_spec[j]
        return sums[0] + head[0] + rest[0], sums[1] + head[1] + rest[1]

    empty = jnp.zeros((channels, block), F32)
    real, imag = lax.fori_loop(0, count, own, (empty, empty))
    total[0, :, :block] = real
    total[0, :, block:] = imag

    def one_lag(lag, carry):
        def include(j, sums):
            source = j - lag * rows
            near = (from_ref[j] <= j // rows - lag).astype(F32)
            real, imag = product(grad_head, rest_spec, j, source)
            return sums[0] + near * real, sums[1] + near * imag

        real, imag = lax.fori_loop(lag * rows, count, include, (empty, empty))
        total[lag, :, :block] = real
        total[lag, :, block:] = imag
        return carry

    lax.fori_loop(1, lags, one_lag, 0)
    wide = lax.broadcasted_iota(jnp.int32, (channels, 2 * block), 1)
    sign = (1 - 2 * (wide % 2)).astype(F32)
    total[lags] = jnp.zeros((channels, 2 * block), F32)

    def one_piece(lag, carry):
        piece = total[lag + 1] + sign * total[lag]
        high = piece.astype(BF16)
        low = (piece - high.astype(F32)).astype(BF16)
        out_ref[lag] = dot(jnp.concatenate([high, low, high], axis=1), back_ref[...])
        return carry

    lax.fori_loop(0, lags, one_piece, 0)


def whole_vmem(count):
    return [pl.BlockSpec(memory_space=pltpu.VMEM)] * count


def scalars(count):
    return [pl.BlockSpec(memory_space=pltpu.SMEM)] * count


def run_conv(kernel, rows, ends, plain, value, head, spectrum, forward, inverse):
    count, channels, block = value.shape
    group = 4 if count % 4 == 0 else 1
    spec = pltpu.VMEM((count, channels, 2 * block), F32)
    return pl.pallas_call(
        partial(kernel, rows, group),
        out_shape=jax.ShapeDtypeStruct(value.shape, BF16),
        in_specs=scalars(2) + whole_vmem(7),
        out_specs=pl.BlockSpec(memory_space=pltpu.VMEM),
        scratch_shapes=[spec] * 4,
        compiler_params=pltpu.CompilerParams(vmem_limit_bytes=VMEM_BYTES),
    )(ends, plain, value, head, *spectrum, forward, inverse)


def run_filter_grad(rows, begins, plain, value, grad, head, forward, inverse, back):
    count, channels, block = value.shape
    group = 4 if count % 4 == 0 else 1
    lags = count // rows
    spec = pltpu.VMEM((count, channels, 2 * block), F32)
    return pl.pallas_call(
        partial(filter_grad_kernel, rows, group),
        out_shape=jax.ShapeDtypeStruct((lags, channels, block), F32),
        in_specs=scalars(2) + whole_vmem(6),
        out_specs=pl.BlockSpec(memory_space=pltpu.VMEM),
        scratch_shapes=[spec] * 4 + [pltpu.VMEM((lags + 1, channels, 2 * block), F32)],
        compiler_params=pltpu.CompilerParams(vmem_limit_bytes=VMEM_BYTES),
    )(begins, plain, value, grad, head, forward, inverse, back)


def to_channels(value, padded):
    rows, block, width = value.shape
    count = lax.axis_size("seq")
    mine = width // count
    sent = value.transpose(0, 2, 1).reshape(rows, count, mine, block).transpose(1, 0, 2, 3)
    got = lax.all_to_all(sent, "seq", 0, 0, tiled=True).reshape(count * rows, mine, block)
    if padded != mine:
        got = jnp.pad(got, ((0, 0), (0, padded - mine), (0, 0)))
    return got


def to_tokens(value, rows, mine):
    count = lax.axis_size("seq")
    block = value.shape[2]
    value = value[:, :mine].reshape(count, rows, mine, block)
    got = lax.all_to_all(value, "seq", 0, 0, tiled=True)
    return got.transpose(1, 3, 0, 2).reshape(rows, block, count * mine)


def layer_norm(values, gain_vector):
    center = values - jnp.mean(values, axis=-1, keepdims=True)
    spread = jnp.mean(center * center, axis=-1, keepdims=True)
    return center * lax.rsqrt(spread + 1e-05) * gain_vector


def segment_at(doc_ends, spots):
    flat_spots = jnp.reshape(spots, (1, -1, 1))
    return jnp.sum((doc_ends[:, None, :] <= flat_spots).astype(jnp.int32), axis=2)


def per_device(
    hidden_in, lengths, gain_one, in_weight, short_kernel, skip_gain, decay_rate, filt_first,
    filt_second, filt_third, out_weight, gain_two, ff_up, ff_down, out_grad,
):
    rows, block, width = hidden_in.shape
    hidden_units = ff_up.shape[1]
    seq_count, seq_pos = lax.axis_size("seq"), lax.axis_index("seq")
    dp_count = lax.axis_size("dp")
    world = seq_count * dp_count
    index = lax.axis_index(AXES)
    core = my_bit(index, 1)
    row_len = block * seq_count
    tokens = rows * block
    seq_bits = [1 << i for i in range(1, seq_count.bit_length() - 1)]
    dp_bits = [seq_count << i for i in range(dp_count.bit_length() - 1)]
    order_a = dp_bits + seq_bits
    order_b = dp_bits[::-1] + seq_bits
    mine = width // seq_count
    padded = -(-mine // 16) * 16

    forward, inverse = spectral_tables(block)
    forward_two, inverse_three = jnp.asarray(two_pass(forward)), jnp.asarray(three_pass(inverse))
    forward_three, inverse_two = jnp.asarray(three_pass(forward.T)), jnp.asarray(two_pass(inverse.T))

    before = shifted(hidden_in[:, block - 2 :], 1)
    after = shifted(hidden_in[:, :2], -1)

    doc_ends = jnp.cumsum(lengths, axis=1)
    all_spots = jnp.arange(row_len, dtype=jnp.int32)
    segment_all = segment_at(doc_ends, all_spots).reshape(rows, seq_count, block)
    seg_first, seg_last = segment_all[:, :, 0], segment_all[:, :, -1]
    block_ids = jnp.arange(seq_count, dtype=jnp.int32)
    match = (seg_first[:, :, None] == seg_last[:, None, :]) & (
        block_ids[None, :, None] > block_ids[None, None, :]
    )
    begins = (block_ids[None, :] - jnp.sum(match, axis=2, dtype=jnp.int32)).T.reshape(-1)
    untils = (block_ids[None, :] + jnp.sum(match, axis=1, dtype=jnp.int32)).T.reshape(-1)
    plain = (seg_first == seg_last).astype(jnp.int32).T.reshape(-1)
    head_all = (segment_all == seg_first[:, :, None]).astype(F32)
    head_all = head_all.transpose(1, 0, 2).reshape(seq_count * rows, 1, block)

    wide_spots = seq_pos * block - 2 + jnp.arange(block + 4, dtype=jnp.int32)
    wide_seg = segment_at(doc_ends, wide_spots)
    inside = (wide_spots[None, :] >= 0) & (wide_spots[None, :] < row_len)
    near_one = (wide_seg[:, 2:] == wide_seg[:, 1:-1]) & inside[:, 2:] & inside[:, 1:-1]
    near_two = (wide_seg[:, 2:] == wide_seg[:, :-2]) & inside[:, 2:] & inside[:, :-2]
    near_one = near_one.astype(F32)[:, :, None]
    near_two = near_two.astype(F32)[:, :, None]
    live = (wide_spots[None, 2:] < doc_ends[:, -1:]).astype(F32)[:, :, None]

    bands = (filt_first.shape[0] - 1) // 2
    spots = np.arange(row_len)
    turns = (np.arange(1, bands + 1)[:, None] * spots[None, :] % row_len) * (2.0 * math.pi / row_len)
    embedding = jnp.asarray(
        np.concatenate([spots[None, :] / row_len, np.cos(turns), np.sin(turns)], axis=0).astype(
            np.float32
        )
    )
    pre_one = jnp.einsum("ef,el->fl", filt_first, embedding, precision=FULL_PRECISION)
    act_one = jnp.sin(pre_one)
    pre_two = jnp.einsum("fg,fl->gl", filt_second, act_one, precision=FULL_PRECISION)
    act_two = jnp.sin(pre_two)
    my_third = lax.dynamic_slice_in_dim(filt_third, seq_pos * mine, mine, 1)
    my_decay = lax.dynamic_slice_in_dim(decay_rate, seq_pos * mine, mine, 0)
    envelope = jnp.exp(-my_decay[:, None] * all_spots.astype(F32)[None, :]) * row_len ** (-0.5)
    taps = jnp.einsum("gc,gl->cl", my_third, act_two, precision=FULL_PRECISION) * envelope
    taps = taps.reshape(mine, seq_count, block).transpose(1, 0, 2)
    if padded != mine:
        taps = jnp.pad(taps, ((0, 0), (0, padded - mine), (0, 0)))
    pieces = jnp.einsum("kct,tf->kcf", taps, jnp.asarray(forward), precision=FULL_PRECISION)
    sign = jnp.asarray(np.tile(1.0 - 2.0 * (np.arange(block) % 2), 2).astype(np.float32))
    earlier = jnp.concatenate([jnp.zeros_like(pieces[:1]), pieces[:-1]], axis=0)
    spectrum = earlier + sign * pieces
    spec_real, spec_imag = spectrum[..., :block], spectrum[..., block:]
    base = jnp.arange(block) == 0
    spectrum = (
        spec_real,
        jnp.where(base, 0.0, spec_imag),
        jnp.where(base, spec_imag, spec_real),
    )

    inputs = hidden_in.astype(F32)
    normed, norm_one_pull = jax.vjp(layer_norm, inputs, gain_one)
    normed_one = normed.astype(BF16).reshape(tokens, width)
    halo = jnp.concatenate([before, after], axis=1).astype(F32)
    halo_normed = layer_norm(halo, gain_one).astype(BF16).reshape(4 * rows, width)
    projected = jnp.dot(
        jnp.concatenate([normed_one, halo_normed], axis=0),
        in_weight,
        preferred_element_type=F32,
    ).astype(BF16)
    halo_proj = projected[tokens:].reshape(rows, 4, 3 * width)
    extended = jnp.concatenate(
        [halo_proj[:, :2], projected[:tokens].reshape(rows, block, 3 * width), halo_proj[:, 2:]],
        axis=1,
    ).astype(F32)
    mixed = (
        short_kernel[0] * extended[:, 2:]
        + short_kernel[1] * extended[:, 1:-1] * near_one
        + short_kernel[2] * extended[:, :-2] * near_two
    )
    value = mixed[..., :width]
    inner = mixed[..., width : 2 * width]
    outer = mixed[:, :block, 2 * width :]
    signal = (value * inner * live)[:, :block].astype(BF16)

    signal_ch = to_channels(signal, padded)
    conv_ch = run_conv(
        conv_kernel, rows, begins, plain, signal_ch, head_all, spectrum, forward_two, inverse_three
    )
    signal32 = signal.astype(F32)
    conv = to_tokens(conv_ch, rows, mine).astype(F32) + skip_gain * signal32

    gated = (outer * conv).astype(BF16).reshape(tokens, width)
    middle = inputs.reshape(tokens, width) + jnp.dot(gated, out_weight, preferred_element_type=F32)
    normed, norm_two_pull = jax.vjp(layer_norm, middle, gain_two)
    normed_two = normed.astype(BF16)
    pre_act = jnp.dot(normed_two, ff_up, preferred_element_type=F32)
    activated, gelu_pull = jax.vjp(jax.nn.gelu, pre_act)
    activated = activated.astype(BF16)
    block_out = (middle + jnp.dot(activated, ff_down, preferred_element_type=F32)).astype(BF16)

    upstream = out_grad.reshape(tokens, width)
    grad_act = jnp.einsum("td,fd->tf", upstream, ff_down, preferred_element_type=F32)
    grad_pre = gelu_pull(grad_act)[0].astype(BF16)

    def my_half(array):
        half = array.shape[1] // 2
        return lax.dynamic_slice_in_dim(array, core * half, half, 1)

    def their_half(array):
        half = array.shape[1] // 2
        return lax.dynamic_slice_in_dim(array, (1 - core) * half, half, 1)

    def both(array):
        return jnp.concatenate([array, swap(array, 1)], axis=0)

    def both_halves(array):
        return jnp.concatenate([my_half(array), swap(their_half(array), 1)], axis=0)

    def outer_sum(left, right):
        return jnp.einsum("ta,tb->ab", left, right, preferred_element_type=F32).astype(BF16)

    grad_up = outer_sum(both(normed_two), both_halves(grad_pre))
    grad_down = outer_sum(both_halves(activated), both(upstream))
    up_piece = halve(grad_up, index, order_a)
    down_piece = halve(grad_down, index, order_b)

    grad_normed_two = jnp.einsum("tf,df->td", grad_pre, ff_up, preferred_element_type=F32)
    grad_middle_norm, grad_gain_two = norm_two_pull(grad_normed_two)
    grad_middle = upstream.astype(F32) + grad_middle_norm
    grad_branch = grad_middle.astype(BF16)
    grad_gated = jnp.einsum("te,de->td", grad_branch, out_weight, preferred_element_type=F32)
    grad_gated = grad_gated.reshape(rows, block, width)
    grad_conv = (grad_gated * outer).astype(BF16)
    grad_outer = grad_gated * conv
    grad_out = outer_sum(both(gated), both_halves(grad_branch))

    grad_ch = to_channels(grad_conv, padded)
    grad_signal_ch = run_conv(
        conv_back_kernel, rows, untils, plain, grad_ch, head_all, spectrum, forward_three, inverse_two
    )
    grad_conv32 = grad_conv.astype(F32)
    grad_signal = to_tokens(grad_signal_ch, rows, mine).astype(F32) + skip_gain * grad_conv32
    skip_grad = jnp.sum(grad_conv32 * signal32, axis=(0, 1))
    grad_taps = run_filter_grad(
        rows, begins, plain, signal_ch, grad_ch, head_all, forward_two, inverse_two, forward_three
    )
    grad_taps = grad_taps[:, :mine].transpose(1, 0, 2).reshape(mine, row_len) * envelope
    my_third_grad = jnp.einsum("gl,cl->gc", act_two, grad_taps, precision=FULL_PRECISION)
    third_grad = lax.dynamic_update_slice_in_dim(
        jnp.zeros_like(filt_third), my_third_grad, seq_pos * mine, 1
    )
    grad_two = jnp.cos(pre_two) * jnp.einsum(
        "gc,cl->gl", my_third, grad_taps, precision=FULL_PRECISION
    )
    second_grad = jnp.einsum("fl,gl->fg", act_one, grad_two, precision=FULL_PRECISION)
    grad_one = jnp.cos(pre_one) * jnp.einsum(
        "fg,gl->fl", filt_second, grad_two, precision=FULL_PRECISION
    )
    first_grad = jnp.einsum("el,fl->ef", embedding, grad_one, precision=FULL_PRECISION)

    grad_mixed = jnp.concatenate(
        [
            grad_signal * inner[:, :block] * live[:, :block],
            grad_signal * value[:, :block] * live[:, :block],
            grad_outer,
        ],
        axis=-1,
    )
    grad_mixed = jnp.concatenate([grad_mixed, shifted(grad_mixed[:, :2], -1)], axis=1)
    grad_proj = (
        short_kernel[0] * grad_mixed[:, :block]
        + short_kernel[1] * grad_mixed[:, 1 : block + 1] * near_one[:, 1 : block + 1]
        + short_kernel[2] * grad_mixed[:, 2 : block + 2] * near_two[:, 2 : block + 2]
    )
    grad_proj = grad_proj.astype(BF16).reshape(tokens, 3 * width)
    own = grad_mixed[:, :block]
    kernel_grad = jnp.stack(
        [
            jnp.sum(own * extended[:, 2 : block + 2], axis=(0, 1)),
            jnp.sum(own * extended[:, 1 : block + 1] * near_one[:, :block], axis=(0, 1)),
            jnp.sum(own * extended[:, :block] * near_two[:, :block], axis=(0, 1)),
        ]
    )
    grad_in = outer_sum(both(normed_one), both_halves(grad_proj))
    grad_normed_one = jnp.einsum("te,de->td", grad_proj, in_weight, preferred_element_type=F32)
    grad_inputs, grad_gain_one = norm_one_pull(grad_normed_one.reshape(rows, block, width))
    input_grad = grad_inputs + grad_middle.reshape(rows, block, width)

    last_a = jnp.concatenate([grad_in[: width // 2], grad_out[: width // 2]], axis=1)
    last_b = jnp.concatenate([grad_in[width // 2 :], grad_out[width // 2 :]], axis=1)
    a_piece = halve(last_a, index, order_a)
    b_piece = halve(last_b, index, order_b)

    def assemble(half, axis):
        other = swap(half, 1)
        low = core == 0
        return jnp.concatenate(
            [jnp.where(low, half, other), jnp.where(low, other, half)], axis=axis
        ).astype(F32)

    up_total = assemble(double(up_piece, index, order_a), 1)
    down_total = assemble(double(down_piece, index, order_b), 0)
    last = jnp.concatenate(
        [double(a_piece, index, order_a), double(b_piece, index, order_b)], axis=0
    )
    cut = 3 * width // 2
    in_total = assemble(last[:, :cut], 1)
    out_total = assemble(last[:, cut:], 1)

    small = [grad_gain_one, kernel_grad, skip_grad, first_grad, second_grad, third_grad, grad_gain_two]
    flat = jnp.concatenate([part.reshape(-1) for part in small])
    length = flat.shape[0]
    flat = jnp.pad(flat, (0, -length % 1024)).reshape(-1, 128)
    flat = sum_all(flat, world).reshape(-1)
    summed, offset = [], 0
    for part in small:
        summed.append(flat[offset : offset + part.size].reshape(part.shape))
        offset += part.size
    return (
        block_out.reshape(rows, block, width),
        input_grad,
        summed[0],
        in_total,
        summed[1],
        summed[2],
        summed[3],
        summed[4],
        summed[5],
        out_total,
        summed[6],
        up_total,
        down_total,
    )


def solution(mesh):
    tokens = P("dp", "seq", None)
    return jax.shard_map(
        per_device,
        mesh=mesh,
        in_specs=(tokens, P("dp", None)) + (P(),) * 12 + (tokens,),
        out_specs=(tokens, tokens) + (P(),) * 11,
        check_vma=False,
    )
```

```python
from functools import partial
import math

import jax
import jax.numpy as jnp
import numpy as np
from jax import lax
from jax.experimental import pallas as pl
from jax.experimental.pallas import tpu as pltpu
from jax.sharding import PartitionSpec as P

FULL_PRECISION = lax.Precision.HIGHEST
BF16 = jnp.bfloat16
F32 = jnp.float32
AXES = ("dp", "seq")
VMEM_BYTES = 40 * 1024 * 1024


def swap(value, bit):
    count = lax.axis_size(AXES)
    return lax.ppermute(value, AXES, [(i, i ^ bit) for i in range(count)])


def shifted(value, steps):
    count = lax.axis_size("seq")
    first, last = max(0, -steps), min(count, count - steps)
    return lax.ppermute(value, "seq", [(i, i + steps) for i in range(first, last)])


def my_bit(index, bit):
    return (index // bit) % 2


def halve(value, index, bits):
    for bit in bits:
        pair = value.reshape((2, value.shape[0] // 2) + value.shape[1:])
        mine = my_bit(index, bit)
        keep = lax.dynamic_index_in_dim(pair, mine, 0, keepdims=False)
        send = lax.dynamic_index_in_dim(pair, 1 - mine, 0, keepdims=False)
        value = (keep.astype(F32) + swap(send, bit).astype(F32)).astype(value.dtype)
    return value


def double(value, index, bits):
    for bit in reversed(bits):
        other = swap(value, bit)
        low = my_bit(index, bit) == 0
        value = jnp.concatenate(
            [jnp.where(low, value, other), jnp.where(low, other, value)], axis=0
        )
    return value


def sum_all(value, count):
    bit = 1
    while bit < count:
        value = value + swap(value, bit)
        bit *= 2
    return value


def spectral_tables(block):
    points = 2 * block
    spot = np.arange(block)
    freq = np.arange(block)
    angle = (spot[:, None] * freq[None, :] % points) * (2.0 * math.pi / points)
    real, imag = np.cos(angle), -np.sin(angle)
    imag[:, 0] = 1.0 - 2.0 * (spot % 2)
    forward = np.concatenate([real, imag], axis=1)
    late = spot + block
    angle = (freq[:, None] * late[None, :] % points) * (2.0 * math.pi / points)
    weight = np.where(freq == 0, 1.0, 2.0)[:, None] / points
    real, imag = weight * np.cos(angle), -weight * np.sin(angle)
    imag[0, :] = (1.0 - 2.0 * (late % 2)) / points
    inverse = np.concatenate([real, imag], axis=0)
    return forward.astype(np.float32), inverse.astype(np.float32)


def split_table(table):
    high = table.astype(jnp.bfloat16)
    low = (table - high.astype(np.float32)).astype(jnp.bfloat16)
    return np.asarray(high), np.asarray(low)


def two_pass(table):
    high, low = split_table(table)
    return np.concatenate([high, low], axis=0)


def three_pass(table):
    high, low = split_table(table)
    return np.concatenate([high, high, low], axis=0)


def ends_of(lengths_ref, row):
    total, ends = 0, []
    for k in range(lengths_ref.shape[1]):
        total = total + lengths_ref[row, k]
        ends.append(total)
    return ends


def next_end(ends, spot, row_len):
    found = row_len
    for end in reversed(ends):
        found = jnp.where(end > spot, end, found)
    return found


def last_end(ends, spot):
    found = 0
    for end in ends:
        found = jnp.where(end <= spot, end, found)
    return found


def near_mask(ends, spots, step):
    apart = spots < step
    for end in ends:
        apart = apart | ((end <= spots) & (end > spots - step))
    return jnp.where(apart, 0.0, 1.0)


def dot(left, right):
    return jnp.dot(left, right, preferred_element_type=F32)


def dot_nt(left, right):
    return lax.dot_general(left, right, (((1,), (1,)), ((), ())), preferred_element_type=F32)


def head_masks(ends, spot, group, rows, block, row_len):
    lane = lax.broadcasted_iota(jnp.int32, (1, 1, block), 2)
    masks = []
    for g in range(group):
        start = (spot + g) // rows * block
        stop = jnp.where((spot + g) % rows == 0, next_end(ends[0], start, row_len), 0)
        for row in range(1, rows):
            stop = jnp.where(
                (spot + g) % rows == row, next_end(ends[row], start, row_len), stop
            )
        masks.append(jnp.where(lane < stop - start, 1.0, 0.0))
    return jnp.concatenate(masks, axis=0)


def spectra(value_ref, masks, table_ref, head_out, rest_out, group):
    count, channels, block = value_ref.shape

    def step(i, carry):
        spot = pl.ds(i * group, group)
        whole = value_ref[spot].astype(F32)
        first = whole * masks(i * group)
        both = jnp.concatenate([first, whole - first], axis=0).astype(BF16)
        both = both.reshape(2 * group * channels, block)
        found = dot(jnp.concatenate([both, both], axis=1), table_ref[...])
        found = found.reshape(2 * group, channels, 2 * block)
        head_out[spot] = found[:group]
        rest_out[spot] = found[group:]
        return carry

    lax.fori_loop(0, count // group, step, 0)


def back_to_time(head_spec, rest_spec, masks, table_ref, value_ref, skip_ref, group, store):
    count, channels, double_block = head_spec.shape

    def step(i, carry):
        spot = pl.ds(i * group, group)
        both = jnp.concatenate([head_spec[spot], rest_spec[spot]], axis=0)
        both = both.reshape(2 * group * channels, double_block)
        high = both.astype(BF16)
        low = (both - high.astype(F32)).astype(BF16)
        found = dot(jnp.concatenate([high, low, high], axis=1), table_ref[...])
        found = found.reshape(2 * group, channels, double_block // 2)
        rest = found[group:]
        found = rest + masks(i * group) * (found[:group] - rest)
        store(i * group, found + skip_ref[...][None] * value_ref[spot].astype(F32))
        return carry

    lax.fori_loop(0, count // group, step, 0)


def of_row(per_row, row):
    found = per_row[0]
    for k in range(1, len(per_row)):
        found = jnp.where(row == k, per_row[k], found)
    return found


def conv_kernel(
    rows, group, row_len, lengths_ref, value_ref, skip_ref, hr_ref, hi_ref, hm_ref,
    forward_ref, inverse_ref, out_ref, head_spec, rest_spec, head_sum, rest_sum,
):
    count, channels, block = value_ref.shape
    ends = [ends_of(lengths_ref, row) for row in range(rows)]

    def masks(spot):
        return head_masks(ends, spot, group, rows, block, row_len)

    spectra(value_ref, masks, forward_ref, head_spec, rest_spec, group)

    def product(real, imag, lag):
        hr, hi, hm = hr_ref[lag], hi_ref[lag], hm_ref[lag]
        return real * hr - imag * hi, real * hi + imag * hm

    def own(j, carry):
        start = j // rows * block
        stop = of_row([next_end(e, start, row_len) for e in ends], j % rows)
        plain = (stop >= start + block).astype(F32)
        head_real, head_imag = product(head_spec[j, :, :block], head_spec[j, :, block:], 0)
        head_sum[j, :, :block] = head_real
        head_sum[j, :, block:] = head_imag
        rest_real, rest_imag = product(rest_spec[j, :, :block], rest_spec[j, :, block:], 0)
        rest_sum[j, :, :block] = rest_real
        rest_sum[j, :, block:] = rest_imag
        rest_spec[j] = rest_spec[j] + plain * head_spec[j]
        return carry

    lax.fori_loop(0, count, own, 0)

    def reach(j, carry):
        spot, row = j // rows, j % rows
        begin = of_row([last_end(e, spot * block) for e in ends], row) // block

        def include(source, sums):
            k = source * rows + row
            real, imag = product(
                rest_spec[k, :, :block], rest_spec[k, :, block:], spot - source
            )
            return sums[0] + real, sums[1] + imag

        start = (head_sum[j, :, :block], head_sum[j, :, block:])
        real, imag = lax.fori_loop(begin, spot, include, start)
        head_sum[j, :, :block] = real
        head_sum[j, :, block:] = imag
        return carry

    lax.fori_loop(rows, count, reach, 0)

    def store(spot, found):
        out_ref[pl.ds(spot, group)] = found.astype(BF16)

    back_to_time(head_sum, rest_sum, masks, inverse_ref, value_ref, skip_ref, group, store)


def conv_back_kernel(
    rows, group, row_len, lengths_ref, value_ref, skip_ref, hr_ref, hi_ref, hm_ref,
    forward_ref, inverse_ref, out_ref, head_spec, rest_spec, head_sum, rest_sum, found_ref,
):
    count, channels, block = value_ref.shape
    ends = [ends_of(lengths_ref, row) for row in range(rows)]

    def masks(spot):
        return head_masks(ends, spot, group, rows, block, row_len)

    spectra(value_ref, masks, inverse_ref, head_spec, rest_spec, group)

    def product(real, imag, lag):
        hr, hi, hm = hr_ref[lag], hi_ref[lag], hm_ref[lag]
        return real * hr + imag * hi, imag * hm - real * hi

    def reach(j, carry):
        spot, row = j // rows, j % rows
        start = spot * block
        plain = of_row([next_end(e, start, row_len) for e in ends], row) >= start + block
        plain = plain.astype(F32)
        until = of_row([next_end(e, start + block - 1, row_len) for e in ends], row)
        until = (until - 1) // block + 1

        def include(source, sums):
            k = source * rows + row
            real, imag = product(
                head_spec[k, :, :block], head_spec[k, :, block:], source - spot
            )
            return sums[0] + real, sums[1] + imag

        empty = jnp.zeros((channels, block), F32)
        real, imag = lax.fori_loop(spot + 1, until, include, (empty, empty))
        head_real, head_imag = product(head_spec[j, :, :block], head_spec[j, :, block:], 0)
        head_sum[j, :, :block] = head_real + plain * real
        head_sum[j, :, block:] = head_imag + plain * imag
        rest_real, rest_imag = product(rest_spec[j, :, :block], rest_spec[j, :, block:], 0)
        rest_sum[j, :, :block] = rest_real + (1.0 - plain) * real
        rest_sum[j, :, block:] = rest_imag + (1.0 - plain) * imag
        return carry

    lax.fori_loop(0, count, reach, 0)

    def store(spot, found):
        found_ref[pl.ds(spot, group)] = found
        out_ref[pl.ds(spot, group), :channels] = found.astype(BF16)

    back_to_time(head_sum, rest_sum, masks, forward_ref, value_ref, skip_ref, group, store)

    lane = lax.broadcasted_iota(jnp.int32, (channels, block), 1)
    per_turn = block // 2
    blocks = count // rows
    for turn in range(-(-count // per_turn)):
        first = turn * per_turn
        last = min(count, first + per_turn)

        def gather(j, picked):
            at = 2 * (j - first)
            moved = pltpu.roll(found_ref[j], at, 1)
            return jnp.where((lane >= at) & (lane < at + 2), moved, picked)

        picked = lax.fori_loop(first, last, gather, jnp.zeros((channels, block), F32))
        if channels < block:
            picked = jnp.concatenate(
                [picked, jnp.zeros((block - channels, block), F32)], axis=0
            )
        flipped = picked.T
        for spot in range(first // rows, last // rows):
            at = 2 * (spot * rows - first)
            tile = jnp.concatenate(
                [flipped[at : at + 2 * rows], jnp.zeros((16 - 2 * rows, block), F32)], axis=0
            )
            if spot > 0:
                out_ref[(spot - 1) * rows, channels:] = tile.astype(BF16)
    out_ref[(blocks - 1) * rows, channels:] = jnp.zeros((16, block), BF16)
    for spot in range(blocks):
        for row in range(1, rows):
            out_ref[spot * rows + row, channels:] = jnp.zeros((16, block), BF16)


def filter_grad_kernel(
    rows, group, row_len, lengths_ref, value_ref, grad_ref, forward_ref,
    inverse_ref, back_ref, out_ref, head_spec, rest_spec, grad_head, grad_rest, total,
):
    count, channels, block = value_ref.shape
    lags = count // rows
    ends = [ends_of(lengths_ref, row) for row in range(rows)]

    def masks(spot):
        return head_masks(ends, spot, group, rows, block, row_len)

    spectra(value_ref, masks, forward_ref, head_spec, rest_spec, group)
    spectra(grad_ref, masks, inverse_ref, grad_head, grad_rest, group)
    lane = lax.broadcasted_iota(jnp.int32, (channels, block), 1)
    base = lane == 0

    def product(grad, spec, k, j):
        gr, gi = grad[k, :, :block], grad[k, :, block:]
        sr, si = spec[j, :, :block], spec[j, :, block:]
        masked = jnp.where(base, 0.0, si)
        swapped = jnp.where(base, si, sr)
        return gr * sr + gi * masked, gi * swapped - gr * masked

    def own(j, sums):
        start = j // rows * block
        stop = of_row([next_end(e, start, row_len) for e in ends], j % rows)
        plain = (stop >= start + block).astype(F32)
        head = product(grad_head, head_spec, j, j)
        rest = product(grad_rest, rest_spec, j, j)
        rest_spec[j] = rest_spec[j] + plain * head_spec[j]
        return sums[0] + head[0] + rest[0], sums[1] + head[1] + rest[1]

    empty = jnp.zeros((channels, block), F32)
    real, imag = lax.fori_loop(0, count, own, (empty, empty))
    total[0, :, :block] = real
    total[0, :, block:] = imag

    def one_lag(lag, carry):
        def include(j, sums):
            spot = j // rows
            begin = of_row([last_end(e, spot * block) for e in ends], j % rows) // block
            near = (begin <= spot - lag).astype(F32)
            real, imag = product(grad_head, rest_spec, j, j - lag * rows)
            return sums[0] + near * real, sums[1] + near * imag

        real, imag = lax.fori_loop(lag * rows, count, include, (empty, empty))
        total[lag, :, :block] = real
        total[lag, :, block:] = imag
        return carry

    lax.fori_loop(1, lags, one_lag, 0)
    wide = lax.broadcasted_iota(jnp.int32, (channels, 2 * block), 1)
    sign = (1 - 2 * (wide % 2)).astype(F32)
    total[lags] = jnp.zeros((channels, 2 * block), F32)

    def one_piece(lag, carry):
        piece = total[lag + 1] + sign * total[lag]
        high = piece.astype(BF16)
        low = (piece - high.astype(F32)).astype(BF16)
        out_ref[lag] = dot(jnp.concatenate([high, low, high], axis=1), back_ref[...])
        return carry

    lax.fori_loop(0, lags, one_piece, 0)


def vmem(count):
    return [pl.BlockSpec(memory_space=pltpu.VMEM)] * count


def smem(count):
    return [pl.BlockSpec(memory_space=pltpu.SMEM)] * count


def hbm(count):
    return [pl.BlockSpec(memory_space=pl.ANY)] * count


def params():
    return pltpu.CompilerParams(vmem_limit_bytes=VMEM_BYTES)


def cost(flops, bytes_accessed):
    return pl.CostEstimate(
        flops=int(flops), bytes_accessed=int(bytes_accessed), transcendentals=0
    )


def run_conv(lengths, row_len, value, skip, spectrum, forward, inverse, backward=False):
    count, channels, block = value.shape
    rows = lengths.shape[0]
    group = 4 if count % 4 == 0 else 1
    spec = pltpu.VMEM((count, channels, 2 * block), F32)
    extra = [pltpu.VMEM((count, channels, block), F32)] if backward else []
    sent = channels + 16 if backward else channels
    return pl.pallas_call(
        partial(conv_back_kernel if backward else conv_kernel, rows, group, row_len),
        out_shape=jax.ShapeDtypeStruct((count, sent, block), BF16),
        in_specs=smem(1) + vmem(7),
        out_specs=pl.BlockSpec(memory_space=pltpu.VMEM),
        scratch_shapes=[spec] * 4 + extra,
        compiler_params=params(),
        cost_estimate=cost(1e9, 10e6),
    )(lengths, value, skip, *spectrum, forward, inverse)


def run_filter_grad(lengths, row_len, value, grad, forward, inverse, back):
    count, channels, block = value.shape
    rows = lengths.shape[0]
    group = 4 if count % 4 == 0 else 1
    lags = count // rows
    spec = pltpu.VMEM((count, channels, 2 * block), F32)
    return pl.pallas_call(
        partial(filter_grad_kernel, rows, group, row_len),
        out_shape=jax.ShapeDtypeStruct((lags, channels, block), F32),
        in_specs=smem(1) + vmem(5),
        out_specs=pl.BlockSpec(memory_space=pltpu.VMEM),
        scratch_shapes=[spec] * 4 + [pltpu.VMEM((lags + 1, channels, 2 * block), F32)],
        compiler_params=params(),
        cost_estimate=cost(1e9, 10e6),
    )(lengths, value, grad, forward, inverse, back)


def put_channels(ref, row, chunk, value):
    groups, _, size, _ = ref.shape
    wide = value.shape[0]
    if groups == 1:
        ref[0, row, chunk * wide : (chunk + 1) * wide] = value
    else:
        per = wide // size
        for k in range(per):
            ref[chunk * per + k, row] = value[k * size : (k + 1) * size]


def get_channels(ref, row, chunk, wide, size):
    groups = ref.shape[0]
    if groups == 1:
        return ref[0, row, chunk * wide : (chunk + 1) * wide]
    per = wide // size
    return jnp.concatenate([ref[chunk * per + k, row, :size] for k in range(per)], axis=0)


def moments(value):
    center = value - jnp.mean(value, axis=-1, keepdims=True)
    spread = jnp.mean(center * center, axis=-1, keepdims=True)
    return center, lax.rsqrt(spread + 1e-05)


def norm_back(center, scale, gain, grad):
    unit = center * scale
    inner = grad * gain
    mean_one = jnp.mean(inner, axis=-1, keepdims=True)
    mean_two = jnp.mean(inner * unit, axis=-1, keepdims=True)
    return scale * (inner - mean_one - unit * mean_two), grad * unit


PIECE = 64


def front_kernel(
    lengths_ref, hidden_ref, before_ref, after_ref, gain_ref, taps_ref, weight_hbm,
    normed_ref, extended_ref, outer_ref, sent_ref,
    weight_ref, halo_ref, wide_ref, mixed_ref, sem,
):
    rows, block, width = hidden_ref.shape
    copy = pltpu.make_async_copy(weight_hbm, weight_ref, sem)
    copy.start()
    gain = gain_ref[...]
    for row in range(rows):
        for start in range(0, block, PIECE):
            center, scale = moments(hidden_ref[row, start : start + PIECE].astype(F32))
            at = row * block + start
            normed_ref[at : at + PIECE] = (center * scale * gain).astype(BF16)
    halo = jnp.concatenate(
        [part for row in range(rows) for part in (before_ref[row], after_ref[row])], axis=0
    ).astype(F32)
    center, scale = moments(halo)
    halo = center * scale * gain
    halo_ref[...] = jnp.concatenate(
        [halo, jnp.zeros((halo_ref.shape[0] - 4 * rows, width), F32)], axis=0
    ).astype(BF16)
    first = lax.axis_index("seq") * block
    ends = [ends_of(lengths_ref, row) for row in range(rows)]
    spots = first + lax.broadcasted_iota(jnp.int32, (block, 1), 0)
    near_one = [near_mask(e, spots, 1) for e in ends]
    near_two = [near_mask(e, spots, 2) for e in ends]
    live = [jnp.where(spots < e[-1], 1.0, 0.0) for e in ends]
    chunk = width // 2
    copy.wait()
    for half in range(2):
        for part in range(3):
            cols = slice(part * width + half * chunk, part * width + (half + 1) * chunk)
            main = dot(normed_ref[...], weight_ref[:, cols])
            edge = dot(halo_ref[...], weight_ref[:, cols])
            taps = taps_ref[:, cols]
            for row in range(rows):
                wide_ref[row, 0:8] = jnp.zeros((8, chunk), F32)
                wide_ref[row, block + 8 :] = jnp.zeros((8, chunk), F32)
                wide_ref[row, 6:8] = edge[4 * row : 4 * row + 2]
                wide_ref[row, 8 : block + 8] = main[row * block : (row + 1) * block]
                wide_ref[row, block + 8 : block + 10] = edge[4 * row + 2 : 4 * row + 4]
                rounded = wide_ref[row].astype(BF16)
                extended_ref[row, :, cols] = rounded
                wide_ref[row] = rounded.astype(F32)
                mixed = (
                    taps[0:1] * wide_ref[row, 8 : block + 8]
                    + taps[1:2] * wide_ref[row, 7 : block + 7] * near_one[row]
                    + taps[2:3] * wide_ref[row, 6 : block + 6] * near_two[row]
                )
                if part == 0:
                    mixed_ref[row] = mixed
                elif part == 1:
                    signal = mixed_ref[row] * mixed * live[row]
                    put_channels(sent_ref, row, half, signal.T.astype(BF16))
                else:
                    outer_ref[row, :, half * chunk : (half + 1) * chunk] = mixed


def run_front(lengths, hidden, before, after, gain, taps, weight, groups):
    rows, block, width = hidden.shape
    chunk = width // 2
    return pl.pallas_call(
        front_kernel,
        out_shape=(
            jax.ShapeDtypeStruct((rows * block, width), BF16),
            jax.ShapeDtypeStruct((rows, block + 16, 3 * width), BF16),
            jax.ShapeDtypeStruct((rows, block, width), F32),
            jax.ShapeDtypeStruct((groups, rows, width // groups, block), BF16),
        ),
        in_specs=smem(1) + vmem(5) + hbm(1),
        out_specs=tuple(vmem(4)),
        scratch_shapes=[
            pltpu.VMEM(weight.shape, BF16),
            pltpu.VMEM((16, width), BF16),
            pltpu.VMEM((rows, block + 16, chunk), F32),
            pltpu.VMEM((rows, block, chunk), F32),
            pltpu.SemaphoreType.DMA,
        ],
        compiler_params=params(),
        cost_estimate=cost(2e9, 8e6),
    )(lengths, hidden, before, after, gain, taps, weight)


def middle_kernel(
    size, conv_ref, outer_ref, hidden_ref, gain_ref, upstream_ref, out_hbm, up_hbm, down_hbm,
    result_ref, gated_ref, normed_ref, act_mine, act_theirs, pre_mine, pre_theirs,
    grad_middle_ref, branch_mine, branch_theirs, grad_outer_ref, sent_ref, gain_grad_ref,
    out_ref, up_ref, down_ref, conv_scr, middle_ref, grad_ref, sems,
):
    rows, block, width = hidden_ref.shape
    parts = down_ref.shape[0] // width
    chunk = width // 2
    core = lax.axis_index("seq") % 2
    copies = [pltpu.make_async_copy(out_hbm, out_ref, sems.at[0])]
    for part in range(parts):
        cols = slice(part * width, (part + 1) * width)
        copies.append(
            pltpu.make_async_copy(up_hbm.at[:, cols], up_ref.at[:, cols], sems.at[2 * part + 1])
        )
        copies.append(
            pltpu.make_async_copy(down_hbm.at[cols], down_ref.at[cols], sems.at[2 * part + 2])
        )
    for copy in copies:
        copy.start()
    for row in range(rows):
        here = slice(row * block, (row + 1) * block)
        for half in range(2):
            cols = slice(half * chunk, (half + 1) * chunk)
            conv = get_channels(conv_ref, row, half, chunk, size).astype(F32).T
            conv_scr[here, cols] = conv
            gated_ref[here, cols] = (outer_ref[row, :, cols] * conv).astype(BF16)
    copies[0].wait()
    middle_ref[...] = dot(gated_ref[...], out_ref[...])
    gain = gain_ref[...]
    for row in range(rows):
        for start in range(0, block, PIECE):
            here = slice(row * block + start, row * block + start + PIECE)
            middle = middle_ref[here] + hidden_ref[row, start : start + PIECE].astype(F32)
            middle_ref[here] = middle
            center, scale = moments(middle)
            normed_ref[here] = (center * scale * gain).astype(BF16)
    slope = math.sqrt(2.0 / math.pi)
    for part in range(parts):
        cols = slice(part * width, (part + 1) * width)
        copies[2 * part + 1].wait()
        pre = dot(normed_ref[...], up_ref[:, cols])
        copies[2 * part + 2].wait()
        grad_act = dot_nt(upstream_ref[...], down_ref[cols])
        square = pre * pre
        bend = jnp.tanh(slope * pre * (1.0 + 0.044715 * square))
        half_up = 0.5 * (1.0 + bend)
        act = (pre * half_up).astype(BF16)
        turn = half_up + 0.5 * pre * (1.0 - bend * bend) * (
            slope * (1.0 + 3.0 * 0.044715 * square)
        )
        grad_pre = (grad_act * turn).astype(BF16)
        owner = part // (parts // 2)
        inside = slice((part % (parts // 2)) * width, (part % (parts // 2) + 1) * width)

        @pl.when(core == owner)
        def _():
            act_mine[:, inside] = act
            pre_mine[:, inside] = grad_pre

        @pl.when(core != owner)
        def _():
            act_theirs[:, inside] = act
            pre_theirs[:, inside] = grad_pre

        if part == 0:
            grad_ref[...] = dot_nt(grad_pre, up_ref[:, cols])
        else:
            grad_ref[...] += dot_nt(grad_pre, up_ref[:, cols])
        found = dot(act, down_ref[cols])
        for row in range(rows):
            here = slice(row * block, (row + 1) * block)
            if part == 0:
                grad_middle_ref[here] = middle_ref[here] + found[here]
            elif part < parts - 1:
                grad_middle_ref[here] += found[here]
            else:
                result_ref[row] = (grad_middle_ref[here] + found[here]).astype(BF16)
    gain_grad = jnp.zeros((1, width), F32)
    for at in range(0, rows * block, PIECE):
        here = slice(at, at + PIECE)
        center, scale = moments(middle_ref[here])
        grad, terms = norm_back(center, scale, gain, grad_ref[here])
        gain_grad = gain_grad + jnp.sum(terms, axis=0, keepdims=True)
        grad = upstream_ref[here].astype(F32) + grad
        grad_middle_ref[here] = grad
        branch = grad.astype(BF16)

        @pl.when(core == 0)
        def _():
            branch_mine[here] = branch[:, :chunk]
            branch_theirs[here] = branch[:, chunk:]

        @pl.when(core != 0)
        def _():
            branch_mine[here] = branch[:, chunk:]
            branch_theirs[here] = branch[:, :chunk]

    gain_grad_ref[...] = gain_grad
    grad_ref[...] = dot_nt(grad_middle_ref[...].astype(BF16), out_ref[...])
    for row in range(rows):
        here = slice(row * block, (row + 1) * block)
        for half in range(2):
            cols = slice(half * chunk, (half + 1) * chunk)
            grad_gated = grad_ref[here, cols]
            grad_outer_ref[row, :, cols] = grad_gated * conv_scr[here, cols]
            grad_conv = grad_gated * outer_ref[row, :, cols]
            put_channels(sent_ref, row, half, grad_conv.T.astype(BF16))


def run_middle(conv, size, outer, hidden, gain, upstream, out_weight, up, down, groups):
    rows, block, width = hidden.shape
    tokens = rows * block
    units = up.shape[1]
    parts = units // width

    def shape(*dims, kind=BF16):
        return jax.ShapeDtypeStruct(dims, kind)

    outs = (
        shape(rows, block, width),
        shape(tokens, width),
        shape(tokens, width),
        shape(tokens, units // 2),
        shape(tokens, units // 2),
        shape(tokens, units // 2),
        shape(tokens, units // 2),
        shape(tokens, width, kind=F32),
        shape(tokens, width // 2),
        shape(tokens, width // 2),
        shape(rows, block, width, kind=F32),
        shape(groups, rows, width // groups, block),
        shape(1, width, kind=F32),
    )
    return pl.pallas_call(
        partial(middle_kernel, size),
        out_shape=outs,
        in_specs=vmem(5) + hbm(3),
        out_specs=tuple(vmem(len(outs))),
        scratch_shapes=[
            pltpu.VMEM(out_weight.shape, BF16),
            pltpu.VMEM(up.shape, BF16),
            pltpu.VMEM(down.shape, BF16),
            pltpu.VMEM((tokens, width), F32),
            pltpu.VMEM((tokens, width), F32),
            pltpu.VMEM((tokens, width), F32),
            pltpu.SemaphoreType.DMA((2 * parts + 1,)),
        ],
        compiler_params=params(),
        cost_estimate=cost(8e9, 30e6),
    )(conv, outer, hidden, gain, upstream, out_weight, up, down)


def last_kernel(
    size, lengths_ref, signal_ref, halo_ref, extended_ref, outer_ref, outer_halo_ref, hidden_ref,
    gain_ref, taps_ref, grad_middle_ref, weight_hbm,
    proj_mine, proj_theirs, result_ref, taps_grad_ref, gain_grad_ref,
    weight_ref, wide_ref, mixed_ref, grad_ref, proj_ref, normed_grad, sem,
):
    rows, block, width = hidden_ref.shape
    chunk = width // 2
    copy = pltpu.make_async_copy(weight_hbm, weight_ref, sem)
    copy.start()
    core = lax.axis_index("seq") % 2
    first = lax.axis_index("seq") * block
    longer = block + 8
    spots = first + lax.broadcasted_iota(jnp.int32, (longer, 1), 0)
    taps_grad_ref[...] = jnp.zeros(taps_grad_ref.shape, F32)
    for row in range(rows):
        ends = ends_of(lengths_ref, row)
        near_one, near_two = near_mask(ends, spots, 1), near_mask(ends, spots, 2)
        live = jnp.where(spots < ends[-1], 1.0, 0.0)
        for half in range(2):
            cols = slice(half * chunk, (half + 1) * chunk)
            grad_ref[0, :block] = get_channels(signal_ref, row, half, chunk, size).astype(F32).T
            grad_ref[0, block:] = jnp.concatenate(
                [halo_ref[row, :, cols], jnp.zeros((6, chunk), F32)], axis=0
            )
            for part in range(2):
                at = slice(part * width + half * chunk, part * width + (half + 1) * chunk)
                taps = taps_ref[:, at]
                wide_ref[part] = extended_ref[row, :, at].astype(F32)
                mixed_ref[part] = (
                    taps[0:1] * wide_ref[part, 8 : longer + 8]
                    + taps[1:2] * wide_ref[part, 7 : longer + 7] * near_one
                    + taps[2:3] * wide_ref[part, 6 : longer + 6] * near_two
                )
            at = slice(2 * width + half * chunk, 2 * width + (half + 1) * chunk)
            wide_ref[2] = extended_ref[row, :, at].astype(F32)
            signal_grad = grad_ref[0] * live
            grad_ref[0] = signal_grad * mixed_ref[1]
            grad_ref[1] = signal_grad * mixed_ref[0]
            grad_ref[2, :block] = outer_ref[row, :, cols]
            grad_ref[2, block:] = jnp.concatenate(
                [outer_halo_ref[row, :, cols], jnp.zeros((6, chunk), F32)], axis=0
            )
            for part in range(3):
                at = slice(part * width + half * chunk, part * width + (half + 1) * chunk)
                taps = taps_ref[:, at]
                own = grad_ref[part, :block]
                proj = (
                    taps[0:1] * own
                    + taps[1:2] * (grad_ref[part, 1 : block + 1] * near_one[1 : block + 1])
                    + taps[2:3] * (grad_ref[part, 2 : block + 2] * near_two[2 : block + 2])
                )
                proj_ref[row * block : (row + 1) * block, at] = proj.astype(BF16)
                taps_grad_ref[0:1, at] += jnp.sum(
                    own * wide_ref[part, 8 : block + 8], axis=0, keepdims=True
                )
                taps_grad_ref[1:2, at] += jnp.sum(
                    own * wide_ref[part, 7 : block + 7] * near_one[:block], axis=0, keepdims=True
                )
                taps_grad_ref[2:3, at] += jnp.sum(
                    own * wide_ref[part, 6 : block + 6] * near_two[:block], axis=0, keepdims=True
                )
    middle = 3 * width // 2

    @pl.when(core == 0)
    def _():
        proj_mine[...] = proj_ref[:, :middle]
        proj_theirs[...] = proj_ref[:, middle:]

    @pl.when(core != 0)
    def _():
        proj_mine[...] = proj_ref[:, middle:]
        proj_theirs[...] = proj_ref[:, :middle]

    copy.wait()
    normed_grad[...] = dot_nt(proj_ref[...], weight_ref[...])
    gain = gain_ref[...]
    gain_grad = jnp.zeros((1, width), F32)
    for row in range(rows):
        for start in range(0, block, PIECE):
            here = slice(row * block + start, row * block + start + PIECE)
            center, scale = moments(hidden_ref[row, start : start + PIECE].astype(F32))
            grad, terms = norm_back(center, scale, gain, normed_grad[here])
            gain_grad = gain_grad + jnp.sum(terms, axis=0, keepdims=True)
            result_ref[row, start : start + PIECE] = grad_middle_ref[here] + grad
    gain_grad_ref[...] = gain_grad


def run_last(
    lengths, signal, size, halo, extended, outer, outer_halo, hidden, gain, taps, grad_middle,
    weight,
):
    rows, block, width = hidden.shape
    tokens = rows * block
    chunk = width // 2
    middle = 3 * width // 2
    return pl.pallas_call(
        partial(last_kernel, size),
        out_shape=(
            jax.ShapeDtypeStruct((tokens, middle), BF16),
            jax.ShapeDtypeStruct((tokens, middle), BF16),
            jax.ShapeDtypeStruct(hidden.shape, F32),
            jax.ShapeDtypeStruct((8, 3 * width), F32),
            jax.ShapeDtypeStruct((1, width), F32),
        ),
        in_specs=smem(1) + vmem(9) + hbm(1),
        out_specs=tuple(vmem(5)),
        scratch_shapes=[
            pltpu.VMEM(weight.shape, BF16),
            pltpu.VMEM((3, block + 16, chunk), F32),
            pltpu.VMEM((2, block + 8, chunk), F32),
            pltpu.VMEM((3, block + 8, chunk), F32),
            pltpu.VMEM((tokens, 3 * width), BF16),
            pltpu.VMEM((tokens, width), F32),
            pltpu.SemaphoreType.DMA,
        ],
        compiler_params=params(),
        cost_estimate=cost(3e9, 12e6),
    )(lengths, signal, halo, extended, outer, outer_halo, hidden, gain, taps, grad_middle, weight)


def to_owner(sent, mine, padded):
    count = lax.axis_size("seq")
    groups, rows, size, block = sent.shape
    if groups != count:
        sent = sent.reshape(rows, count, mine, block).transpose(1, 0, 2, 3)
    got = lax.all_to_all(sent, "seq", 0, 0, tiled=True).reshape(count * rows, mine, block)
    if padded != mine:
        got = jnp.pad(got, ((0, 0), (0, padded - mine), (0, 0)))
    return got


def to_block(value, rows, mine, groups):
    count = lax.axis_size("seq")
    size, block = value.shape[1:]
    got = lax.all_to_all(
        value.reshape(count, rows, size, block), "seq", 0, 0, tiled=True
    )
    if groups == count:
        return got
    return got[:, :, :mine].transpose(1, 0, 2, 3).reshape(1, rows, count * mine, block), got


def per_device(
    hidden_in, lengths, gain_one, in_weight, short_kernel, skip_gain, decay_rate, filt_first,
    filt_second, filt_third, out_weight, gain_two, ff_up, ff_down, out_grad,
):
    rows, block, width = hidden_in.shape
    seq_count, seq_pos = lax.axis_size("seq"), lax.axis_index("seq")
    dp_count = lax.axis_size("dp")
    world = seq_count * dp_count
    index = lax.axis_index(AXES)
    core = my_bit(index, 1)
    row_len = block * seq_count
    tokens = rows * block
    seq_bits = [1 << i for i in range(1, seq_count.bit_length() - 1)]
    dp_bits = [seq_count << i for i in range(dp_count.bit_length() - 1)]
    order_a = dp_bits + seq_bits
    order_b = dp_bits[::-1] + seq_bits
    mine = width // seq_count
    padded = -(-mine // 16) * 16
    groups = seq_count if mine == padded and (width // 2) % mine == 0 else 1

    forward, inverse = spectral_tables(block)
    forward_two, inverse_three = jnp.asarray(two_pass(forward)), jnp.asarray(three_pass(inverse))
    forward_three, inverse_two = jnp.asarray(three_pass(forward.T)), jnp.asarray(two_pass(inverse.T))

    before = shifted(hidden_in[:, block - 2 :], 1)
    after = shifted(hidden_in[:, :2], -1)
    normed_one, extended, outer, signal_sent = run_front(
        lengths, hidden_in, before, after, gain_one[None], short_kernel, in_weight, groups
    )
    signal_ch = to_owner(signal_sent, mine, padded)

    signal_sent, filt_first, decay_rate, skip_gain = lax.optimization_barrier(
        (signal_sent, filt_first, decay_rate, skip_gain)
    )
    bands = (filt_first.shape[0] - 1) // 2
    spots = np.arange(row_len)
    turns = (np.arange(1, bands + 1)[:, None] * spots[None, :] % row_len) * (2.0 * math.pi / row_len)
    embedding = jnp.asarray(
        np.concatenate([spots[None, :] / row_len, np.cos(turns), np.sin(turns)], axis=0).astype(
            np.float32
        )
    )
    pre_one = jnp.einsum("ef,el->fl", filt_first, embedding, precision=FULL_PRECISION)
    act_one = jnp.sin(pre_one)
    pre_two = jnp.einsum("fg,fl->gl", filt_second, act_one, precision=FULL_PRECISION)
    act_two = jnp.sin(pre_two)
    my_third = lax.dynamic_slice_in_dim(filt_third, seq_pos * mine, mine, 1)
    my_decay = lax.dynamic_slice_in_dim(decay_rate, seq_pos * mine, mine, 0)
    my_skip = lax.dynamic_slice_in_dim(skip_gain, seq_pos * mine, mine, 0)
    my_skip = jnp.pad(my_skip, (0, padded - mine))[:, None]
    places = jnp.asarray(spots.astype(np.float32))
    envelope = jnp.exp(-my_decay[:, None] * places[None, :]) * row_len ** (-0.5)
    taps = jnp.einsum("gc,gl->cl", my_third, act_two, precision=FULL_PRECISION) * envelope
    taps = taps.reshape(mine, seq_count, block).transpose(1, 0, 2)
    if padded != mine:
        taps = jnp.pad(taps, ((0, 0), (0, padded - mine), (0, 0)))
    pieces = jnp.einsum("kct,tf->kcf", taps, jnp.asarray(forward), precision=FULL_PRECISION)
    sign = jnp.asarray(np.tile(1.0 - 2.0 * (np.arange(block) % 2), 2).astype(np.float32))
    earlier = jnp.concatenate([jnp.zeros_like(pieces[:1]), pieces[:-1]], axis=0)
    spectrum = earlier + sign * pieces
    spec_real, spec_imag = spectrum[..., :block], spectrum[..., block:]
    base = jnp.arange(block) == 0
    spectrum = (
        spec_real,
        jnp.where(base, 0.0, spec_imag),
        jnp.where(base, spec_imag, spec_real),
    )

    conv_ch = run_conv(
        lengths, row_len, signal_ch, my_skip, spectrum, forward_two, inverse_three
    )
    conv = to_block(conv_ch, rows, mine, groups)
    if groups == 1:
        conv = conv[0]

    upstream = out_grad.reshape(tokens, width)
    (
        block_out, gated, normed_two, act_mine, act_theirs, pre_mine, pre_theirs, grad_middle,
        branch_mine, branch_theirs, grad_outer, grad_sent, gain_two_grad,
    ) = run_middle(
        conv, mine, outer, hidden_in, gain_two[None], upstream, out_weight, ff_up, ff_down, groups
    )
    grad_ch = to_owner(grad_sent, mine, padded)
    outer_halo = shifted(grad_outer[:, :2], -1)

    def both(array):
        return jnp.concatenate([array, swap(array, 1)], axis=0)

    def both_halves(kept, sent):
        return jnp.concatenate([kept, swap(sent, 1)], axis=0)

    def outer_sum(left, right):
        return jnp.einsum("ta,tb->ab", left, right, preferred_element_type=F32).astype(BF16)

    grad_up = outer_sum(both(normed_two), both_halves(pre_mine, pre_theirs))
    grad_down = outer_sum(both_halves(act_mine, act_theirs), both(upstream))
    grad_out = outer_sum(both(gated), both_halves(branch_mine, branch_theirs))
    up_piece = halve(grad_up, index, order_a)
    down_piece = halve(grad_down, index, order_b)

    back_ch = run_conv(
        lengths, row_len, grad_ch, my_skip, spectrum, forward_three, inverse_two, backward=True
    )
    got = to_block(back_ch, rows, mine, groups)
    grad_signal, got = (got, got) if groups > 1 else got
    halo = got[:, 0, padded : padded + 2 * rows, :mine].astype(F32)
    halo = halo.transpose(1, 0, 2).reshape(rows, 2, width)
    back_ch, signal_late = lax.optimization_barrier((back_ch, signal_ch))
    grad_taps = run_filter_grad(
        lengths, row_len, signal_late, grad_ch, forward_two, inverse_two, forward_three
    )
    grad_taps = grad_taps[:, :mine].transpose(1, 0, 2).reshape(mine, row_len)
    skip_grad = lax.dynamic_update_slice_in_dim(
        jnp.zeros_like(skip_gain), grad_taps[:, 0], seq_pos * mine, 0
    )
    grad_taps = grad_taps * envelope
    my_third_grad = jnp.einsum("gl,cl->gc", act_two, grad_taps, precision=FULL_PRECISION)
    third_grad = lax.dynamic_update_slice_in_dim(
        jnp.zeros_like(filt_third), my_third_grad, seq_pos * mine, 1
    )
    grad_two = jnp.cos(pre_two) * jnp.einsum(
        "gc,cl->gl", my_third, grad_taps, precision=FULL_PRECISION
    )
    second_grad = jnp.einsum("fl,gl->fg", act_one, grad_two, precision=FULL_PRECISION)
    grad_one = jnp.cos(pre_one) * jnp.einsum(
        "fg,gl->fl", filt_second, grad_two, precision=FULL_PRECISION
    )
    first_grad = jnp.einsum("el,fl->ef", embedding, grad_one, precision=FULL_PRECISION)

    proj_mine, proj_theirs, input_grad, kernel_grad, gain_one_grad = run_last(
        lengths, grad_signal, mine, halo, extended, grad_outer, outer_halo, hidden_in,
        gain_one[None], short_kernel, grad_middle, in_weight,
    )
    grad_in = outer_sum(both(normed_one), both_halves(proj_mine, proj_theirs))

    last_a = jnp.concatenate([grad_in[: width // 2], grad_out[: width // 2]], axis=1)
    last_b = jnp.concatenate([grad_in[width // 2 :], grad_out[width // 2 :]], axis=1)
    a_piece = halve(last_a, index, order_a)
    b_piece = halve(last_b, index, order_b)

    def assemble(half, axis):
        other = swap(half, 1)
        low = core == 0
        return jnp.concatenate(
            [jnp.where(low, half, other), jnp.where(low, other, half)], axis=axis
        ).astype(F32)

    up_total = assemble(double(up_piece, index, order_a), 1)
    down_total = assemble(double(down_piece, index, order_b), 0)
    last = jnp.concatenate(
        [double(a_piece, index, order_a), double(b_piece, index, order_b)], axis=0
    )
    cut = 3 * width // 2
    in_total = assemble(last[:, :cut], 1)
    out_total = assemble(last[:, cut:], 1)

    small = [
        gain_one_grad[0], kernel_grad[:3], skip_grad, first_grad, second_grad, third_grad,
        gain_two_grad[0],
    ]
    flat = jnp.concatenate([part.reshape(-1) for part in small])
    flat = jnp.pad(flat, (0, -flat.shape[0] % 1024)).reshape(-1, 128)
    flat = sum_all(flat, world).reshape(-1)
    summed, offset = [], 0
    for part in small:
        summed.append(flat[offset : offset + part.size].reshape(part.shape))
        offset += part.size
    return (
        block_out, input_grad, summed[0], in_total, summed[1], summed[2], summed[3], summed[4],
        summed[5], out_total, summed[6], up_total, down_total,
    )


def solution(mesh):
    tokens = P("dp", "seq", None)
    return jax.shard_map(
        per_device,
        mesh=mesh,
        in_specs=(tokens, P("dp", None)) + (P(),) * 12 + (tokens,),
        out_specs=(tokens, tokens) + (P(),) * 11,
        check_vma=False,
    )
```

```python
from functools import partial
import math

import jax
import jax.numpy as jnp
import numpy as np
from jax import lax
from jax.experimental import pallas as pl
from jax.experimental.pallas import tpu as pltpu
from jax.sharding import PartitionSpec as P

FULL_PRECISION = lax.Precision.HIGHEST
BF16 = jnp.bfloat16
F32 = jnp.float32
AXES = ("dp", "seq")
VMEM_BYTES = 32 * 1024 * 1024
FULL_BYTES = 54 * 1024 * 1024
PLACE_BYTES = 57 * 1024 * 1024
KS = 3


def swap(value, bit):
    count = lax.axis_size(AXES)
    return lax.ppermute(value, AXES, [(i, i ^ bit) for i in range(count)])


def shifted(value, steps):
    count = lax.axis_size("seq")
    first, last = max(0, -steps), min(count, count - steps)
    return lax.ppermute(value, "seq", [(i, i + steps) for i in range(first, last)])


def my_bit(index, bit):
    return (index // bit) % 2


def add(kept, got):
    return (kept.astype(F32) + got.astype(F32)).astype(kept.dtype)


def halve(value, index, bits, axis):
    for bit in bits:
        size = value.shape[axis] // 2
        mine = my_bit(index, bit)
        keep = lax.dynamic_slice_in_dim(value, mine * size, size, axis)
        send = lax.dynamic_slice_in_dim(value, (1 - mine) * size, size, axis)
        value = add(keep, swap(send, bit))
    return value


def double(value, index, bits, axis):
    for bit in reversed(bits):
        other = swap(value, bit)
        low = my_bit(index, bit) == 0
        value = jnp.concatenate(
            [jnp.where(low, value, other), jnp.where(low, other, value)], axis=axis
        )
    return value


def sum_over(value, bits):
    for bit in bits:
        value = value + swap(value, bit)
    return value


def spectral_tables(block):
    points = 2 * block
    spot = np.arange(block)
    freq = np.arange(block)
    angle = (spot[:, None] * freq[None, :] % points) * (2.0 * math.pi / points)
    real, imag = np.cos(angle), -np.sin(angle)
    imag[:, 0] = 1.0 - 2.0 * (spot % 2)
    forward = np.concatenate([real, imag], axis=1)
    late = spot + block
    angle = (freq[:, None] * late[None, :] % points) * (2.0 * math.pi / points)
    weight = np.where(freq == 0, 1.0, 2.0)[:, None] / points
    real, imag = weight * np.cos(angle), -weight * np.sin(angle)
    imag[0, :] = (1.0 - 2.0 * (late % 2)) / points
    inverse = np.concatenate([real, imag], axis=0)
    return forward.astype(np.float32), inverse.astype(np.float32)


def split_table(table):
    high = table.astype(jnp.bfloat16)
    low = (table - high.astype(np.float32)).astype(jnp.bfloat16)
    return np.asarray(high), np.asarray(low)


def two_pass(table):
    high, low = split_table(table)
    return np.concatenate([high, low], axis=0)


def three_pass(table):
    high, low = split_table(table)
    return np.concatenate([high, high, low], axis=0)


def ends_of(lengths_ref, row):
    total, ends = 0, []
    for k in range(lengths_ref.shape[1]):
        total = total + lengths_ref[row, k]
        ends.append(total)
    return ends


def next_end(ends, spot, row_len):
    found = row_len
    for end in reversed(ends):
        found = jnp.where(end > spot, end, found)
    return found


def last_end(ends, spot):
    found = 0
    for end in ends:
        found = jnp.where(end <= spot, end, found)
    return found


def near_mask(ends, spots, step):
    apart = spots < step
    for end in ends:
        apart = apart | ((end <= spots) & (end > spots - step))
    return jnp.where(apart, 0.0, 1.0)


def dot(left, right):
    return jnp.dot(left, right, preferred_element_type=F32)


def dot_nt(left, right):
    return lax.dot_general(left, right, (((1,), (1,)), ((), ())), preferred_element_type=F32)


def head_masks(ends, spot, group, rows, block, row_len):
    lane = lax.broadcasted_iota(jnp.int32, (1, 1, block), 2)
    masks = []
    for g in range(group):
        start = (spot + g) // rows * block
        stop = jnp.where((spot + g) % rows == 0, next_end(ends[0], start, row_len), 0)
        for row in range(1, rows):
            stop = jnp.where(
                (spot + g) % rows == row, next_end(ends[row], start, row_len), stop
            )
        masks.append(jnp.where(lane < stop - start, 1.0, 0.0))
    return jnp.concatenate(masks, axis=0)


def spectra(value_ref, masks, table_ref, head_out, rest_out, group):
    count, channels, block = value_ref.shape

    def step(i, carry):
        spot = pl.ds(i * group, group)
        whole = value_ref[spot].astype(F32)
        first = whole * masks(i * group)
        both = jnp.concatenate([first, whole - first], axis=0).astype(BF16)
        both = both.reshape(2 * group * channels, block)
        found = dot(jnp.concatenate([both, both], axis=1), table_ref[...])
        found = found.reshape(2 * group, channels, 2 * block)
        head_out[spot] = found[:group]
        rest_out[spot] = found[group:]
        return carry

    lax.fori_loop(0, count // group, step, 0)


def back_to_time(head_spec, rest_spec, masks, table_ref, value_ref, skip_ref, group, store):
    count, channels, double_block = head_spec.shape

    def step(i, carry):
        spot = pl.ds(i * group, group)
        both = jnp.concatenate([head_spec[spot], rest_spec[spot]], axis=0)
        both = both.reshape(2 * group * channels, double_block)
        high = both.astype(BF16)
        low = (both - high.astype(F32)).astype(BF16)
        found = dot(jnp.concatenate([high, low, high], axis=1), table_ref[...])
        found = found.reshape(2 * group, channels, double_block // 2)
        rest = found[group:]
        found = rest + masks(i * group) * (found[:group] - rest)
        store(i * group, found + skip_ref[...][None] * value_ref[spot].astype(F32))
        return carry

    lax.fori_loop(0, count // group, step, 0)


def of_row(per_row, row):
    found = per_row[0]
    for k in range(1, len(per_row)):
        found = jnp.where(row == k, per_row[k], found)
    return found


def start_loads(moves, sems):
    loads = [
        pltpu.make_async_copy(source, target, sems.at[i])
        for i, (source, target) in enumerate(moves)
    ]
    for load in loads:
        load.start()
    return loads


def conv_kernel(
    rows, group, row_len, lengths_ref, value_ref, skip_hbm, hr_hbm, hi_hbm, hm_hbm,
    forward_hbm, inverse_hbm, out_ref, skip_ref, hr_ref, hi_ref, hm_ref, forward_ref, inverse_ref,
    sems, head_spec, rest_spec, head_sum, rest_sum,
):
    count, channels, block = value_ref.shape
    loads = start_loads(
        [
            (forward_hbm, forward_ref), (hr_hbm, hr_ref), (hi_hbm, hi_ref), (hm_hbm, hm_ref),
            (inverse_hbm, inverse_ref), (skip_hbm, skip_ref),
        ],
        sems,
    )
    ends = [ends_of(lengths_ref, row) for row in range(rows)]

    def masks(spot):
        return head_masks(ends, spot, group, rows, block, row_len)

    loads[0].wait()
    spectra(value_ref, masks, forward_ref, head_spec, rest_spec, group)
    for load in loads[1:]:
        load.wait()

    def product(real, imag, lag):
        hr, hi, hm = hr_ref[lag], hi_ref[lag], hm_ref[lag]
        return real * hr - imag * hi, real * hi + imag * hm

    def own(j, carry):
        start = j // rows * block
        stop = of_row([next_end(e, start, row_len) for e in ends], j % rows)
        plain = (stop >= start + block).astype(F32)
        head_real, head_imag = product(head_spec[j, :, :block], head_spec[j, :, block:], 0)
        head_sum[j, :, :block] = head_real
        head_sum[j, :, block:] = head_imag
        rest_real, rest_imag = product(rest_spec[j, :, :block], rest_spec[j, :, block:], 0)
        rest_sum[j, :, :block] = rest_real
        rest_sum[j, :, block:] = rest_imag
        rest_spec[j] = rest_spec[j] + plain * head_spec[j]
        return carry

    lax.fori_loop(0, count, own, 0)

    def reach(j, carry):
        spot, row = j // rows, j % rows
        begin = of_row([last_end(e, spot * block) for e in ends], row) // block

        def include(source, sums):
            k = source * rows + row
            real, imag = product(
                rest_spec[k, :, :block], rest_spec[k, :, block:], spot - source
            )
            return sums[0] + real, sums[1] + imag

        start = (head_sum[j, :, :block], head_sum[j, :, block:])
        real, imag = lax.fori_loop(begin, spot, include, start)
        head_sum[j, :, :block] = real
        head_sum[j, :, block:] = imag
        return carry

    lax.fori_loop(rows, count, reach, 0)

    def store(spot, found):
        out_ref[pl.ds(spot, group)] = found.astype(BF16)

    back_to_time(head_sum, rest_sum, masks, inverse_ref, value_ref, skip_ref, group, store)


def conv_back_kernel(
    rows, group, row_len, lengths_ref, value_ref, skip_hbm, hr_hbm, hi_hbm, hm_hbm,
    forward_hbm, inverse_hbm, out_ref, skip_ref, hr_ref, hi_ref, hm_ref, forward_ref, inverse_ref,
    sems, head_spec, rest_spec, head_sum, rest_sum, found_ref,
):
    count, channels, block = value_ref.shape
    loads = start_loads(
        [
            (inverse_hbm, inverse_ref), (hr_hbm, hr_ref), (hi_hbm, hi_ref), (hm_hbm, hm_ref),
            (forward_hbm, forward_ref), (skip_hbm, skip_ref),
        ],
        sems,
    )
    ends = [ends_of(lengths_ref, row) for row in range(rows)]

    def masks(spot):
        return head_masks(ends, spot, group, rows, block, row_len)

    loads[0].wait()
    spectra(value_ref, masks, inverse_ref, head_spec, rest_spec, group)
    for load in loads[1:]:
        load.wait()

    def product(real, imag, lag):
        hr, hi, hm = hr_ref[lag], hi_ref[lag], hm_ref[lag]
        return real * hr + imag * hi, imag * hm - real * hi

    def reach(j, carry):
        spot, row = j // rows, j % rows
        start = spot * block
        plain = of_row([next_end(e, start, row_len) for e in ends], row) >= start + block
        plain = plain.astype(F32)
        until = of_row([next_end(e, start + block - 1, row_len) for e in ends], row)
        until = (until - 1) // block + 1

        def include(source, sums):
            k = source * rows + row
            real, imag = product(
                head_spec[k, :, :block], head_spec[k, :, block:], source - spot
            )
            return sums[0] + real, sums[1] + imag

        empty = jnp.zeros((channels, block), F32)
        real, imag = lax.fori_loop(spot + 1, until, include, (empty, empty))
        head_real, head_imag = product(head_spec[j, :, :block], head_spec[j, :, block:], 0)
        head_sum[j, :, :block] = head_real + plain * real
        head_sum[j, :, block:] = head_imag + plain * imag
        rest_real, rest_imag = product(rest_spec[j, :, :block], rest_spec[j, :, block:], 0)
        rest_sum[j, :, :block] = rest_real + (1.0 - plain) * real
        rest_sum[j, :, block:] = rest_imag + (1.0 - plain) * imag
        return carry

    lax.fori_loop(0, count, reach, 0)

    def store(spot, found):
        found_ref[pl.ds(spot, group)] = found
        out_ref[pl.ds(spot, group), :channels] = found.astype(BF16)

    back_to_time(head_sum, rest_sum, masks, forward_ref, value_ref, skip_ref, group, store)

    lane = lax.broadcasted_iota(jnp.int32, (channels, block), 1)
    per_turn = block // 2
    blocks = count // rows
    for turn in range(-(-count // per_turn)):
        first = turn * per_turn
        last = min(count, first + per_turn)

        def gather(j, picked):
            at = 2 * (j - first)
            moved = pltpu.roll(found_ref[j], at, 1)
            return jnp.where((lane >= at) & (lane < at + 2), moved, picked)

        picked = lax.fori_loop(first, last, gather, jnp.zeros((channels, block), F32))
        if channels < block:
            picked = jnp.concatenate(
                [picked, jnp.zeros((block - channels, block), F32)], axis=0
            )
        flipped = picked.T
        for spot in range(first // rows, last // rows):
            at = 2 * (spot * rows - first)
            tile = jnp.concatenate(
                [flipped[at : at + 2 * rows], jnp.zeros((16 - 2 * rows, block), F32)], axis=0
            )
            if spot > 0:
                out_ref[(spot - 1) * rows, channels:] = tile.astype(BF16)
    out_ref[(blocks - 1) * rows, channels:] = jnp.zeros((16, block), BF16)
    for spot in range(blocks):
        for row in range(1, rows):
            out_ref[spot * rows + row, channels:] = jnp.zeros((16, block), BF16)


def filter_grad_kernel(
    rows, group, row_len, lengths_ref, value_ref, grad_ref, forward_ref,
    inverse_ref, back_ref, out_ref, head_spec, rest_spec, grad_head, grad_rest, total,
):
    count, channels, block = value_ref.shape
    lags = count // rows
    ends = [ends_of(lengths_ref, row) for row in range(rows)]

    def masks(spot):
        return head_masks(ends, spot, group, rows, block, row_len)

    spectra(value_ref, masks, forward_ref, head_spec, rest_spec, group)
    spectra(grad_ref, masks, inverse_ref, grad_head, grad_rest, group)
    lane = lax.broadcasted_iota(jnp.int32, (channels, block), 1)
    base = lane == 0

    def product(grad, spec, k, j):
        gr, gi = grad[k, :, :block], grad[k, :, block:]
        sr, si = spec[j, :, :block], spec[j, :, block:]
        masked = jnp.where(base, 0.0, si)
        swapped = jnp.where(base, si, sr)
        return gr * sr + gi * masked, gi * swapped - gr * masked

    def own(j, sums):
        start = j // rows * block
        stop = of_row([next_end(e, start, row_len) for e in ends], j % rows)
        plain = (stop >= start + block).astype(F32)
        head = product(grad_head, head_spec, j, j)
        rest = product(grad_rest, rest_spec, j, j)
        rest_spec[j] = rest_spec[j] + plain * head_spec[j]
        return sums[0] + head[0] + rest[0], sums[1] + head[1] + rest[1]

    empty = jnp.zeros((channels, block), F32)
    real, imag = lax.fori_loop(0, count, own, (empty, empty))
    total[0, :, :block] = real
    total[0, :, block:] = imag

    def one_lag(lag, carry):
        def include(j, sums):
            spot = j // rows
            begin = of_row([last_end(e, spot * block) for e in ends], j % rows) // block
            near = (begin <= spot - lag).astype(F32)
            real, imag = product(grad_head, rest_spec, j, j - lag * rows)
            return sums[0] + near * real, sums[1] + near * imag

        real, imag = lax.fori_loop(lag * rows, count, include, (empty, empty))
        total[lag, :, :block] = real
        total[lag, :, block:] = imag
        return carry

    lax.fori_loop(1, lags, one_lag, 0)
    wide = lax.broadcasted_iota(jnp.int32, (channels, 2 * block), 1)
    sign = (1 - 2 * (wide % 2)).astype(F32)
    total[lags] = jnp.zeros((channels, 2 * block), F32)

    def one_piece(lag, carry):
        piece = total[lag + 1] + sign * total[lag]
        high = piece.astype(BF16)
        low = (piece - high.astype(F32)).astype(BF16)
        out_ref[lag] = dot(jnp.concatenate([high, low, high], axis=1), back_ref[...])
        return carry

    lax.fori_loop(0, lags, one_piece, 0)


def vmem(count):
    return [pl.BlockSpec(memory_space=pltpu.VMEM)] * count


def smem(count):
    return [pl.BlockSpec(memory_space=pltpu.SMEM)] * count


def hbm(count):
    return [pl.BlockSpec(memory_space=pltpu.HBM)] * count


def anywhere(count):
    return [pl.BlockSpec(memory_space=pl.ANY)] * count


def params(limit=VMEM_BYTES):
    return pltpu.CompilerParams(vmem_limit_bytes=limit)


SHORT = pl.CostEstimate(flops=1, bytes_accessed=1, transcendentals=0)


def ordered(kernel, used, extra):
    def call(*refs):
        kernel(*refs[:used], *refs[used + extra :])

    return call


def run_conv(
    lengths, row_len, value, skip, spectrum, forward, inverse, backward=False, after=()
):
    count, channels, block = value.shape
    rows = lengths.shape[0]
    group = 4 if count % 4 == 0 else 1
    spec = pltpu.VMEM((count, channels, 2 * block), F32)
    extra = [pltpu.VMEM((count, channels, block), F32)] if backward else []
    sent = channels + 16 if backward else channels
    return pl.pallas_call(
        ordered(
            partial(conv_back_kernel if backward else conv_kernel, rows, group, row_len),
            8,
            len(after),
        ),
        out_shape=jax.ShapeDtypeStruct((count, sent, block), BF16),
        in_specs=smem(1) + vmem(1) + anywhere(6 + len(after)),
        out_specs=pl.BlockSpec(memory_space=pltpu.VMEM),
        scratch_shapes=[
            *[pltpu.VMEM(part.shape, part.dtype) for part in (skip, *spectrum, forward, inverse)],
            pltpu.SemaphoreType.DMA((6,)),
            *[spec] * 4,
            *extra,
        ],
        compiler_params=params(),
        cost_estimate=SHORT,
    )(lengths, value, skip, *spectrum, forward, inverse, *after)


def run_filter_grad(lengths, row_len, value, grad, forward, inverse, back, after=()):
    count, channels, block = value.shape
    rows = lengths.shape[0]
    group = 4 if count % 4 == 0 else 1
    lags = count // rows
    spec = pltpu.VMEM((count, channels, 2 * block), F32)
    return pl.pallas_call(
        ordered(partial(filter_grad_kernel, rows, group, row_len), 6, len(after)),
        out_shape=jax.ShapeDtypeStruct((lags, channels, block), F32),
        in_specs=smem(1) + vmem(5) + anywhere(len(after)),
        out_specs=pl.BlockSpec(memory_space=pltpu.VMEM),
        scratch_shapes=[spec] * 4 + [pltpu.VMEM((lags + 1, channels, 2 * block), F32)],
        compiler_params=params(),
        cost_estimate=SHORT,
    )(lengths, value, grad, forward, inverse, back, *after)


def put_channels(ref, row, chunk, value):
    groups, _, size, _ = ref.shape
    wide = value.shape[0]
    if groups == 1:
        ref[0, row, chunk * wide : (chunk + 1) * wide] = value
    else:
        per = wide // size
        for k in range(per):
            ref[chunk * per + k, row] = value[k * size : (k + 1) * size]


def get_channels(ref, row, chunk, wide, size):
    groups = ref.shape[0]
    if groups == 1:
        return ref[0, row, chunk * wide : (chunk + 1) * wide]
    per = wide // size
    return jnp.concatenate([ref[chunk * per + k, row, :size] for k in range(per)], axis=0)


def moments(value):
    center = value - jnp.mean(value, axis=-1, keepdims=True)
    spread = jnp.mean(center * center, axis=-1, keepdims=True)
    return center, lax.rsqrt(spread + 1e-05)


def norm_back(center, scale, gain, grad):
    unit = center * scale
    inner = grad * gain
    mean_one = jnp.mean(inner, axis=-1, keepdims=True)
    mean_two = jnp.mean(inner * unit, axis=-1, keepdims=True)
    return scale * (inner - mean_one - unit * mean_two), grad * unit


PIECE = 64


def front_kernel(
    lengths_ref, before_ref, after_ref, gain_ref, hidden_hbm, taps_hbm, weight_hbm,
    normed_hbm, extended_hbm, outer_hbm, sent_hbm,
    hidden_ref, taps_ref, weight_ref, normed_ref, extended_ref, outer_ref, sent_ref,
    halo_ref, wide_ref, mixed_ref, sems,
):
    rows, block, width = hidden_ref.shape
    loads = [
        pltpu.make_async_copy(source, target, sems.at[i])
        for i, (source, target) in enumerate(
            [(hidden_hbm, hidden_ref), (weight_hbm, weight_ref), (taps_hbm, taps_ref)]
        )
    ]
    for load in loads:
        load.start()
    gain = gain_ref[...]
    halo = jnp.concatenate(
        [part for row in range(rows) for part in (before_ref[row], after_ref[row])], axis=0
    ).astype(F32)
    center, scale = moments(halo)
    halo = center * scale * gain
    halo_ref[...] = jnp.concatenate(
        [halo, jnp.zeros((halo_ref.shape[0] - 4 * rows, width), F32)], axis=0
    ).astype(BF16)
    first = lax.axis_index("seq") * block
    ends = [ends_of(lengths_ref, row) for row in range(rows)]
    spots = first + lax.broadcasted_iota(jnp.int32, (block, 1), 0)
    near_one = [near_mask(e, spots, 1) for e in ends]
    near_two = [near_mask(e, spots, 2) for e in ends]
    live = [jnp.where(spots < e[-1], 1.0, 0.0) for e in ends]
    loads[0].wait()
    for row in range(rows):
        for start in range(0, block, PIECE):
            center, scale = moments(hidden_ref[row, start : start + PIECE].astype(F32))
            at = row * block + start
            normed_ref[at : at + PIECE] = (center * scale * gain).astype(BF16)
    saves = [
        pltpu.make_async_copy(source, target, sems.at[3 + i])
        for i, (source, target) in enumerate(
            [
                (normed_ref, normed_hbm),
                (sent_ref, sent_hbm),
                (extended_ref, extended_hbm),
                (outer_ref, outer_hbm),
            ]
        )
    ]
    saves[0].start()
    chunk = width // 2
    loads[1].wait()
    loads[2].wait()
    for part in range(3):
        for half in range(2):
            cols = slice(part * width + half * chunk, part * width + (half + 1) * chunk)
            main = dot(normed_ref[...], weight_ref[:, cols])
            edge = dot(halo_ref[...], weight_ref[:, cols])
            taps = taps_ref[:, cols]
            for row in range(rows):
                wide_ref[row, 0:8] = jnp.zeros((8, chunk), F32)
                wide_ref[row, block + 8 :] = jnp.zeros((8, chunk), F32)
                wide_ref[row, 6:8] = edge[4 * row : 4 * row + 2]
                wide_ref[row, 8 : block + 8] = main[row * block : (row + 1) * block]
                wide_ref[row, block + 8 : block + 10] = edge[4 * row + 2 : 4 * row + 4]
                rounded = wide_ref[row].astype(BF16)
                extended_ref[row, :, cols] = rounded
                wide_ref[row] = rounded.astype(F32)
                mixed = (
                    taps[0:1] * wide_ref[row, 8 : block + 8]
                    + taps[1:2] * wide_ref[row, 7 : block + 7] * near_one[row]
                    + taps[2:3] * wide_ref[row, 6 : block + 6] * near_two[row]
                )
                here = slice(half * chunk, (half + 1) * chunk)
                if part == 0:
                    mixed_ref[row, :, here] = mixed
                elif part == 1:
                    signal = mixed_ref[row, :, here] * mixed * live[row]
                    put_channels(sent_ref, row, half, signal.T.astype(BF16))
                else:
                    outer_ref[row, :, here] = mixed
        if part == 1:
            saves[1].start()
    saves[2].start()
    saves[3].start()
    for save in saves:
        save.wait()


def run_front(lengths, hidden, before, after, gain, taps, weight, groups):
    rows, block, width = hidden.shape
    chunk = width // 2
    outs = (
        ((rows * block, width), BF16),
        ((rows, block + 16, 3 * width), BF16),
        ((rows, block, width), F32),
        ((groups, rows, width // groups, block), BF16),
    )
    return pl.pallas_call(
        front_kernel,
        out_shape=tuple(jax.ShapeDtypeStruct(*out) for out in outs),
        in_specs=smem(1) + vmem(3) + hbm(3),
        out_specs=tuple(hbm(4)),
        scratch_shapes=[
            pltpu.VMEM(hidden.shape, BF16),
            pltpu.VMEM(taps.shape, F32),
            pltpu.VMEM(weight.shape, BF16),
            *[pltpu.VMEM(*out) for out in outs],
            pltpu.VMEM((16, width), BF16),
            pltpu.VMEM((rows, block + 16, chunk), F32),
            pltpu.VMEM((rows, block, width), F32),
            pltpu.SemaphoreType.DMA((7,)),
        ],
        compiler_params=params(FULL_BYTES),
        cost_estimate=SHORT,
    )(lengths, before, after, gain, hidden, taps, weight)


def middle_kernel(
    size, conv_ref, gain_ref, outer_hbm, hidden_hbm, upstream_hbm, out_hbm, up_hbm, down_hbm,
    gain_grad_ref, factors_mine_hbm, factors_theirs_hbm, result_hbm, last_mine_hbm, last_theirs_hbm,
    grad_middle_hbm, grad_outer_hbm, sent_hbm,
    outer_ref, hidden_ref, upstream_ref, out_ref, up_ref, down_ref,
    factors_mine, factors_theirs, result_ref, last_mine, last_theirs, grad_middle_ref,
    grad_outer_ref, sent_ref,
    conv_scr, middle_ref, grad_ref, sems,
):
    rows, block, width = hidden_ref.shape
    parts = down_ref.shape[0] // width
    per_core = parts // 2
    units = per_core * width
    chunk = width // 2
    core = lax.axis_index("seq") % 2
    copies = [
        pltpu.make_async_copy(outer_hbm, outer_ref, sems.at[0]),
        pltpu.make_async_copy(out_hbm, out_ref, sems.at[1]),
        pltpu.make_async_copy(hidden_hbm, hidden_ref, sems.at[2]),
        pltpu.make_async_copy(upstream_hbm, upstream_ref, sems.at[3]),
    ]
    for part in range(parts):
        cols = slice(part * width, (part + 1) * width)
        copies.append(
            pltpu.make_async_copy(up_hbm.at[:, cols], up_ref.at[:, cols], sems.at[2 * part + 4])
        )
        copies.append(
            pltpu.make_async_copy(down_hbm.at[cols], down_ref.at[cols], sems.at[2 * part + 5])
        )
    for copy in copies:
        copy.start()
    saves = [
        pltpu.make_async_copy(source, target, sems.at[2 * parts + 4 + i])
        for i, (source, target) in enumerate(
            [
                (result_ref, result_hbm),
                (grad_middle_ref, grad_middle_hbm),
                (last_mine, last_mine_hbm),
                (last_theirs, last_theirs_hbm),
                (sent_ref, sent_hbm),
                (grad_outer_ref, grad_outer_hbm),
                (factors_theirs, factors_theirs_hbm),
                (factors_mine, factors_mine_hbm),
            ]
        )
    ]
    for row in range(rows):
        here = slice(row * block, (row + 1) * block)
        for half in range(2):
            cols = slice(half * chunk, (half + 1) * chunk)
            conv_scr[here, cols] = get_channels(conv_ref, row, half, chunk, size).astype(F32).T
    copies[0].wait()
    for row in range(rows):
        here = slice(row * block, (row + 1) * block)
        gated = (outer_ref[row] * conv_scr[here]).astype(BF16)
        last_mine[here, :width] = gated
        last_theirs[here, :width] = gated
    copies[1].wait()
    middle_ref[...] = dot(last_mine[:, :width], out_ref[...])
    copies[2].wait()
    gain = gain_ref[...]
    normed = slice(2 * units, 2 * units + width)
    for row in range(rows):
        for start in range(0, block, PIECE):
            here = slice(row * block + start, row * block + start + PIECE)
            middle = middle_ref[here] + hidden_ref[row, start : start + PIECE].astype(F32)
            middle_ref[here] = middle
            center, scale = moments(middle)
            rounded = (center * scale * gain).astype(BF16)
            factors_mine[here, normed] = rounded
            factors_theirs[here, normed] = rounded
    slope = math.sqrt(2.0 / math.pi)
    copies[3].wait()
    for part in range(parts):
        cols = slice(part * width, (part + 1) * width)
        copies[2 * part + 4].wait()
        pre = dot(factors_mine[:, normed], up_ref[:, cols])
        copies[2 * part + 5].wait()
        grad_act = dot_nt(upstream_ref[...], down_ref[cols])
        square = pre * pre
        bend = jnp.tanh(slope * pre * (1.0 + 0.044715 * square))
        half_up = 0.5 * (1.0 + bend)
        act = (pre * half_up).astype(BF16)
        turn = half_up + 0.5 * pre * (1.0 - bend * bend) * (
            slope * (1.0 + 3.0 * 0.044715 * square)
        )
        grad_pre = (grad_act * turn).astype(BF16)
        owner = part // per_core
        at = part % per_core * width

        @pl.when(core == owner)
        def _():
            factors_mine[:, at : at + width] = act
            factors_mine[:, units + at : units + at + width] = grad_pre

        @pl.when(core != owner)
        def _():
            factors_theirs[:, at : at + width] = act
            factors_theirs[:, units + at : units + at + width] = grad_pre

        if part == 0:
            grad_ref[...] = dot_nt(grad_pre, up_ref[:, cols])
        else:
            grad_ref[...] += dot_nt(grad_pre, up_ref[:, cols])
        found = dot(act, down_ref[cols])
        for row in range(rows):
            here = slice(row * block, (row + 1) * block)
            if part == 0:
                grad_middle_ref[here] = middle_ref[here] + found[here]
            elif part < parts - 1:
                grad_middle_ref[here] += found[here]
            else:
                result_ref[row] = (grad_middle_ref[here] + found[here]).astype(BF16)
    saves[6].start()
    saves[7].start()
    saves[0].start()
    gain_grad = jnp.zeros((1, width), F32)
    branch_cols = slice(width, width + chunk)
    for at in range(0, rows * block, PIECE):
        here = slice(at, at + PIECE)
        center, scale = moments(middle_ref[here])
        grad, terms = norm_back(center, scale, gain, grad_ref[here])
        gain_grad = gain_grad + jnp.sum(terms, axis=0, keepdims=True)
        grad = upstream_ref[here].astype(F32) + grad
        grad_middle_ref[here] = grad
        branch = grad.astype(BF16)

        @pl.when(core == 0)
        def _():
            last_mine[here, branch_cols] = branch[:, :chunk]
            last_theirs[here, branch_cols] = branch[:, chunk:]

        @pl.when(core != 0)
        def _():
            last_mine[here, branch_cols] = branch[:, chunk:]
            last_theirs[here, branch_cols] = branch[:, :chunk]

    for save in saves[1:4]:
        save.start()
    gain_grad_ref[...] = gain_grad
    grad_ref[...] = dot_nt(grad_middle_ref[...].astype(BF16), out_ref[...])
    for row in range(rows):
        here = slice(row * block, (row + 1) * block)
        for half in range(2):
            cols = slice(half * chunk, (half + 1) * chunk)
            grad_conv = grad_ref[here, cols] * outer_ref[row, :, cols]
            put_channels(sent_ref, row, half, grad_conv.T.astype(BF16))
    saves[4].start()
    for row in range(rows):
        here = slice(row * block, (row + 1) * block)
        grad_outer_ref[row] = grad_ref[here] * conv_scr[here]
    saves[5].start()
    for save in saves:
        save.wait()


def run_middle(conv, size, outer, hidden, gain, upstream, out_weight, up, down, groups):
    rows, block, width = hidden.shape
    tokens = rows * block
    units = up.shape[1]
    parts = units // width
    near = (((1, width), F32),)
    far = (
        ((tokens, units + width), BF16),
        ((tokens, units + width), BF16),
        ((rows, block, width), BF16),
        ((tokens, 3 * width // 2), BF16),
        ((tokens, 3 * width // 2), BF16),
        ((tokens, width), F32),
        ((rows, block, width), F32),
        ((groups, rows, width // groups, block), BF16),
    )
    return pl.pallas_call(
        partial(middle_kernel, size),
        out_shape=tuple(jax.ShapeDtypeStruct(*out) for out in near + far),
        in_specs=vmem(2) + hbm(6),
        out_specs=tuple(vmem(1) + hbm(8)),
        scratch_shapes=[
            pltpu.VMEM(outer.shape, F32),
            pltpu.VMEM(hidden.shape, BF16),
            pltpu.VMEM(upstream.shape, BF16),
            pltpu.VMEM(out_weight.shape, BF16),
            pltpu.VMEM(up.shape, BF16),
            pltpu.VMEM(down.shape, BF16),
            *[pltpu.VMEM(*out) for out in far],
            pltpu.VMEM((tokens, width), F32),
            pltpu.VMEM((tokens, width), F32),
            pltpu.VMEM((tokens, width), F32),
            pltpu.SemaphoreType.DMA((2 * parts + 12,)),
        ],
        compiler_params=params(FULL_BYTES),
        cost_estimate=SHORT,
    )(conv, gain, outer, hidden, upstream, out_weight, up, down)


def last_kernel(
    size, lengths_ref, signal_ref, halo_ref, outer_halo_ref, gain_ref, taps_ref,
    extended_hbm, outer_hbm, hidden_hbm, grad_middle_hbm, weight_hbm,
    proj_mine, proj_theirs, taps_grad_ref, gain_grad_ref, result_hbm,
    extended_ref, outer_ref, hidden_ref, grad_middle_ref, weight_ref, result_ref,
    wide_ref, mixed_ref, grad_ref, proj_ref, normed_grad, sems,
):
    rows, block, width = hidden_ref.shape
    chunk = width // 2
    loads = [
        pltpu.make_async_copy(source, target, sems.at[i])
        for i, (source, target) in enumerate(
            [
                (extended_hbm, extended_ref),
                (outer_hbm, outer_ref),
                (weight_hbm, weight_ref),
                (hidden_hbm, hidden_ref),
                (grad_middle_hbm, grad_middle_ref),
            ]
        )
    ]
    for load in loads:
        load.start()
    core = lax.axis_index("seq") % 2
    first = lax.axis_index("seq") * block
    longer = block + 8
    spots = first + lax.broadcasted_iota(jnp.int32, (longer, 1), 0)
    taps_grad_ref[...] = jnp.zeros(taps_grad_ref.shape, F32)
    loads[0].wait()
    loads[1].wait()
    for row in range(rows):
        ends = ends_of(lengths_ref, row)
        near_one, near_two = near_mask(ends, spots, 1), near_mask(ends, spots, 2)
        live = jnp.where(spots < ends[-1], 1.0, 0.0)
        for half in range(2):
            cols = slice(half * chunk, (half + 1) * chunk)
            grad_ref[0, :block] = get_channels(signal_ref, row, half, chunk, size).astype(F32).T
            grad_ref[0, block:] = jnp.concatenate(
                [halo_ref[row, :, cols], jnp.zeros((6, chunk), F32)], axis=0
            )
            for part in range(2):
                at = slice(part * width + half * chunk, part * width + (half + 1) * chunk)
                taps = taps_ref[:, at]
                wide_ref[part] = extended_ref[row, :, at].astype(F32)
                mixed_ref[part] = (
                    taps[0:1] * wide_ref[part, 8 : longer + 8]
                    + taps[1:2] * wide_ref[part, 7 : longer + 7] * near_one
                    + taps[2:3] * wide_ref[part, 6 : longer + 6] * near_two
                )
            at = slice(2 * width + half * chunk, 2 * width + (half + 1) * chunk)
            wide_ref[2] = extended_ref[row, :, at].astype(F32)
            signal_grad = grad_ref[0] * live
            grad_ref[0] = signal_grad * mixed_ref[1]
            grad_ref[1] = signal_grad * mixed_ref[0]
            grad_ref[2, :block] = outer_ref[row, :, cols]
            grad_ref[2, block:] = jnp.concatenate(
                [outer_halo_ref[row, :, cols], jnp.zeros((6, chunk), F32)], axis=0
            )
            for part in range(3):
                at = slice(part * width + half * chunk, part * width + (half + 1) * chunk)
                taps = taps_ref[:, at]
                own = grad_ref[part, :block]
                proj = (
                    taps[0:1] * own
                    + taps[1:2] * (grad_ref[part, 1 : block + 1] * near_one[1 : block + 1])
                    + taps[2:3] * (grad_ref[part, 2 : block + 2] * near_two[2 : block + 2])
                )
                proj_ref[row * block : (row + 1) * block, at] = proj.astype(BF16)
                taps_grad_ref[0:1, at] += jnp.sum(
                    own * wide_ref[part, 8 : block + 8], axis=0, keepdims=True
                )
                taps_grad_ref[1:2, at] += jnp.sum(
                    own * wide_ref[part, 7 : block + 7] * near_one[:block], axis=0, keepdims=True
                )
                taps_grad_ref[2:3, at] += jnp.sum(
                    own * wide_ref[part, 6 : block + 6] * near_two[:block], axis=0, keepdims=True
                )
    middle = 3 * width // 2

    @pl.when(core == 0)
    def _():
        proj_mine[...] = proj_ref[:, :middle]
        proj_theirs[...] = proj_ref[:, middle:]

    @pl.when(core != 0)
    def _():
        proj_mine[...] = proj_ref[:, middle:]
        proj_theirs[...] = proj_ref[:, :middle]

    loads[2].wait()
    normed_grad[...] = dot_nt(proj_ref[...], weight_ref[...])
    loads[3].wait()
    loads[4].wait()
    gain = gain_ref[...]
    gain_grad = jnp.zeros((1, width), F32)
    for row in range(rows):
        for start in range(0, block, PIECE):
            here = slice(row * block + start, row * block + start + PIECE)
            center, scale = moments(hidden_ref[row, start : start + PIECE].astype(F32))
            grad, terms = norm_back(center, scale, gain, normed_grad[here])
            gain_grad = gain_grad + jnp.sum(terms, axis=0, keepdims=True)
            result_ref[row, start : start + PIECE] = grad_middle_ref[here] + grad
    gain_grad_ref[...] = gain_grad
    save = pltpu.make_async_copy(result_ref, result_hbm, sems.at[5])
    save.start()
    save.wait()


def run_last(
    lengths, signal, size, halo, extended, outer, outer_halo, hidden, gain, taps, grad_middle,
    weight, after,
):
    rows, block, width = hidden.shape
    tokens = rows * block
    chunk = width // 2
    middle = 3 * width // 2
    return pl.pallas_call(
        ordered(partial(last_kernel, size), 11, len(after)),
        out_shape=(
            jax.ShapeDtypeStruct((tokens, middle), BF16),
            jax.ShapeDtypeStruct((tokens, middle), BF16),
            jax.ShapeDtypeStruct((8, 3 * width), F32),
            jax.ShapeDtypeStruct((1, width), F32),
            jax.ShapeDtypeStruct(hidden.shape, F32),
        ),
        in_specs=smem(1) + vmem(5) + hbm(5) + anywhere(len(after)),
        out_specs=tuple(vmem(4) + hbm(1)),
        scratch_shapes=[
            pltpu.VMEM(extended.shape, BF16),
            pltpu.VMEM(outer.shape, F32),
            pltpu.VMEM(hidden.shape, BF16),
            pltpu.VMEM(grad_middle.shape, F32),
            pltpu.VMEM(weight.shape, BF16),
            pltpu.VMEM(hidden.shape, F32),
            pltpu.VMEM((3, block + 16, chunk), F32),
            pltpu.VMEM((2, block + 8, chunk), F32),
            pltpu.VMEM((3, block + 8, chunk), F32),
            pltpu.VMEM((tokens, 3 * width), BF16),
            pltpu.VMEM((tokens, width), F32),
            pltpu.SemaphoreType.DMA((6,)),
        ],
        compiler_params=params(FULL_BYTES),
        cost_estimate=SHORT,
    )(
        lengths, signal, halo, outer_halo, gain, taps, extended, outer, hidden, grad_middle, weight,
        *after,
    )


def dot_tn(left, right):
    return lax.dot_general(left, right, (((0,), (0,)), ((), ())), preferred_element_type=F32)


def bit_inside(bit):
    count = lax.axis_size("seq")
    if bit < count:
        return lax.axis_index("seq") // bit % 2
    return lax.axis_index("dp") // (bit // count) % 2


def side(bit, sent):
    mine = bit_inside(bit)
    return 1 - mine if sent else mine


def ff_products_kernel(
    bits, sent, mine_hbm, got_hbm, upstream_hbm, upstream_got_hbm, a_ref, b_ref,
    left_ref, right_ref, act_ref, upstream_ref, sems,
):
    blocks, rows, width = a_ref.shape
    units = blocks * width
    rows_b = b_ref.shape[1]
    at = pl.multiple_of(side(bits[0], sent) * rows, 128)
    at_b = pl.multiple_of(side(bits[1], sent) * rows_b, 128)
    loads = []
    for i, (factors, upstream) in enumerate(
        ((mine_hbm, upstream_hbm), (got_hbm, upstream_got_hbm))
    ):
        for source, target in (
            (factors.at[:, pl.ds(2 * units + at, rows)], left_ref.at[i]),
            (factors.at[:, units : 2 * units], right_ref.at[i]),
            (factors.at[:, pl.ds(at_b, rows_b)], act_ref.at[i]),
            (upstream, upstream_ref.at[i]),
        ):
            loads.append(pltpu.make_async_copy(source, target, sems.at[len(loads)]))
    for i in (0, 4, 1, 5, 2, 6, 3, 7):
        loads[i].start()
    for i in (0, 4, 1, 5):
        loads[i].wait()
    for block in range(blocks):
        cols = slice(block * width, (block + 1) * width)
        found = dot_tn(left_ref[0], right_ref[0, :, cols]) + dot_tn(
            left_ref[1], right_ref[1, :, cols]
        )
        a_ref[block] = found.astype(BF16)
    for i in (2, 6, 3, 7):
        loads[i].wait()
    half = rows_b // 2
    for part in range(2):
        here = slice(part * half, (part + 1) * half)
        found = dot_tn(act_ref[0, :, here], upstream_ref[0]) + dot_tn(
            act_ref[1, :, here], upstream_ref[1]
        )
        b_ref[0, here] = found.astype(BF16)


def last_products_kernel(
    bits, sent, normed_ref, normed_got_ref, proj_ref, proj_got_ref, last_ref, last_got_ref,
    a_ref, b_ref,
):
    rows, width = a_ref.shape[1:]
    half = width // 2
    at = pl.multiple_of(side(bits[0], sent) * rows, 128)
    found = dot_tn(normed_ref[:, pl.ds(at, rows)], proj_ref[:, :width]) + dot_tn(
        normed_got_ref[:, pl.ds(at, rows)], proj_got_ref[:, :width]
    )
    a_ref[0] = found.astype(BF16)
    at = pl.multiple_of(side(bits[1], sent) * rows, 128)
    found = dot_tn(normed_ref[:, pl.ds(at, rows)], proj_ref[:, width:]) + dot_tn(
        normed_got_ref[:, pl.ds(at, rows)], proj_got_ref[:, width:]
    )
    b_ref[0, :, :half] = found.astype(BF16)
    found = dot_tn(last_ref[:, pl.ds(at, rows)], last_ref[:, width:]) + dot_tn(
        last_got_ref[:, pl.ds(at, rows)], last_got_ref[:, width:]
    )
    b_ref[0, :, half:] = found.astype(BF16)


def run_ff_products(bits, sent, operands, shapes, after=()):
    tokens, width = operands[2].shape
    units = shapes[0][0] * width
    return pl.pallas_call(
        ordered(partial(ff_products_kernel, bits, sent), 4, len(after)),
        out_shape=tuple(jax.ShapeDtypeStruct(shape, BF16) for shape in shapes),
        in_specs=anywhere(4 + len(after)),
        out_specs=tuple(vmem(2)),
        scratch_shapes=[
            pltpu.VMEM((2, tokens, shapes[0][1]), BF16),
            pltpu.VMEM((2, tokens, units), BF16),
            pltpu.VMEM((2, tokens, shapes[1][1]), BF16),
            pltpu.VMEM((2, tokens, width), BF16),
            pltpu.SemaphoreType.DMA((8,)),
        ],
        compiler_params=params(FULL_BYTES),
        cost_estimate=SHORT,
    )(*operands, *after)


def run_last_products(bits, sent, operands, shapes, after=()):
    return pl.pallas_call(
        ordered(partial(last_products_kernel, bits, sent), len(operands), len(after)),
        out_shape=tuple(jax.ShapeDtypeStruct(shape, BF16) for shape in shapes),
        in_specs=vmem(len(operands)) + anywhere(len(after)),
        out_specs=tuple(vmem(2)),
        compiler_params=params(),
        cost_estimate=SHORT,
    )(*operands, *after)


STEP = 96


def steps(rows):
    step = STEP if rows % STEP == 0 else rows
    return [(start, step) for start in range(0, rows, step)]


def halve_kernel(
    bits, kept_a, got_a, kept_b, got_b, sent_a, next_a, sent_b, next_b,
    kept_a_ref, got_a_ref, kept_b_ref, got_b_ref, sems,
):
    moves, work = [], []
    for sent, outs in ((True, (sent_a, sent_b)), (False, (next_a, next_b))):
        for bit, out, kept, got, kept_ref, got_ref in (
            (bits[0], outs[0], kept_a, got_a, kept_a_ref, got_a_ref),
            (bits[1], outs[1], kept_b, got_b, kept_b_ref, got_b_ref),
        ):
            rows = out.shape[1]
            at = pl.ds(pl.multiple_of(side(bit, sent) * rows, 16), rows)
            slot = slice(0, rows) if sent else slice(rows, 2 * rows)
            moves.append((kept.at[:, at], kept_ref.at[:, slot]))
            moves.append((got.at[:, at], got_ref.at[:, slot]))
            work.append((out, kept_ref, got_ref, 0 if sent else rows))
    loads = start_loads(moves, sems)
    for i, (out, kept_ref, got_ref, first) in enumerate(work):
        loads[2 * i].wait()
        loads[2 * i + 1].wait()
        for block in range(out.shape[0]):
            for start, step in steps(out.shape[1]):
                at = slice(first + start, first + start + step)
                total = kept_ref[block, at].astype(F32) + got_ref[block, at].astype(F32)
                out[block, start : start + step] = total.astype(BF16)


def run_halve(bits, kept_a, got_a, kept_b, got_b, after=()):
    def half(array):
        return jax.ShapeDtypeStruct((array.shape[0], array.shape[1] // 2, array.shape[2]), BF16)

    return pl.pallas_call(
        ordered(partial(halve_kernel, bits), 4, len(after)),
        out_shape=(half(kept_a), half(kept_a), half(kept_b), half(kept_b)),
        in_specs=anywhere(4 + len(after)),
        out_specs=tuple(vmem(4)),
        scratch_shapes=[
            *[pltpu.VMEM(part.shape, BF16) for part in (kept_a, got_a, kept_b, got_b)],
            pltpu.SemaphoreType.DMA((8,)),
        ],
        compiler_params=params(),
        cost_estimate=SHORT,
    )(kept_a, got_a, kept_b, got_b, *after)


def line_spot():
    return lax.axis_index("seq") // 2


def pieces_of(a_ref, b_ref, count):
    at = 0
    for ref in (a_ref, b_ref):
        blocks, rows, _ = ref.shape
        size = rows // count
        for block in range(blocks):
            yield ref, block, size, at
            at += size


def scatter_kernel(kept_a, got_a, kept_b, got_b, *outs):
    spot = line_spot()
    for away, out in enumerate(outs):
        for (kept, block, size, at), (got, _, _, _) in zip(
            pieces_of(kept_a, kept_b, len(outs)), pieces_of(got_a, got_b, len(outs))
        ):
            rows = pl.ds(pl.multiple_of((spot ^ away) * size, 16), size)
            total = kept[block, rows].astype(F32) + got[block, rows].astype(F32)
            out[at : at + size] = total.astype(BF16)


def run_scatter(kept_a, got_a, kept_b, got_b, count, after=()):
    share = (kept_a.shape[0] * kept_a.shape[1] + kept_b.shape[0] * kept_b.shape[1]) // count
    out = jax.ShapeDtypeStruct((share, kept_a.shape[2]), BF16)
    return pl.pallas_call(
        ordered(scatter_kernel, 4, len(after)),
        out_shape=(out,) * count,
        in_specs=vmem(4) + anywhere(len(after)),
        out_specs=tuple(vmem(count)),
        compiler_params=params(),
        cost_estimate=SHORT,
    )(kept_a, got_a, kept_b, got_b, *after)


def total_kernel(*refs):
    *parts, out = refs
    for start, step in steps(out.shape[0]):
        rows = slice(start, start + step)
        total = parts[0][rows].astype(F32)
        for part in parts[1:]:
            total = total + part[rows].astype(F32)
        out[rows] = total.astype(out.dtype)


def run_total(parts, after=()):
    return pl.pallas_call(
        ordered(total_kernel, len(parts), len(after)),
        out_shape=jax.ShapeDtypeStruct(parts[0].shape, parts[0].dtype),
        in_specs=vmem(len(parts)) + anywhere(len(after)),
        out_specs=pl.BlockSpec(memory_space=pltpu.VMEM),
        compiler_params=params(),
        cost_estimate=SHORT,
    )(*parts, *after)


def gather_kernel(count, *refs):
    shares, outs = refs[:count], refs[count:]
    spot = line_spot()
    for away, share in enumerate(shares):
        for out, block, size, at in pieces_of(*outs, count):
            rows = pl.ds(pl.multiple_of((spot ^ away) * size, 16), size)
            out[block, rows] = share[at : at + size]


def run_gather(shares, shapes, after=()):
    return pl.pallas_call(
        ordered(partial(gather_kernel, len(shares)), len(shares), len(after)),
        out_shape=tuple(jax.ShapeDtypeStruct(shape, BF16) for shape in shapes),
        in_specs=vmem(len(shares)) + anywhere(len(after)),
        out_specs=tuple(vmem(2)),
        compiler_params=params(),
        cost_estimate=SHORT,
    )(*shares, *after)


def join_kernel(bits, mine_a, got_a, mine_b, got_b, out_a, out_b):
    for bit, mine, got, out in (
        (bits[0], mine_a, got_a, out_a),
        (bits[1], mine_b, got_b, out_b),
    ):
        blocks, rows, _ = mine.shape
        for source, which in ((mine, side(bit, False)), (got, side(bit, True))):
            at = pl.ds(pl.multiple_of(which * rows, 16), rows)
            for block in range(blocks):
                out[block, at] = source[block]


def run_join(bits, mine_a, got_a, mine_b, got_b, after=()):
    def twice(array):
        return jax.ShapeDtypeStruct((array.shape[0], array.shape[1] * 2, array.shape[2]), BF16)

    return pl.pallas_call(
        ordered(partial(join_kernel, bits), 4, len(after)),
        out_shape=(twice(mine_a), twice(mine_b)),
        in_specs=vmem(4) + anywhere(len(after)),
        out_specs=tuple(vmem(2)),
        compiler_params=params(),
        cost_estimate=SHORT,
    )(mine_a, got_a, mine_b, got_b, *after)


PLACE = 192
SLOTS = 4


def place_all(moves, slots, sems):
    copies = []
    for i, (source, target) in enumerate(moves):
        value = source()
        rows, cols = value.shape
        slot = i % SLOTS
        if i >= SLOTS:
            copies[i - SLOTS].wait()
        slots[slot, :rows, :cols] = value.astype(F32)
        copy = pltpu.make_async_copy(slots.at[slot, :rows, :cols], target, sems.at[slot])
        copy.start()
        copies.append(copy)
    for copy in copies[-SLOTS:]:
        copy.wait()


def ff_place_kernel(bits, sent, own_a, other_a, own_b, other_b, *refs):
    up_hbm, down_hbm, slots, sems = refs[-4:]
    blocks, rows_a, width = own_a.shape
    rows_b = own_b.shape[1]
    core = lax.axis_index("seq") % 2
    moves = []
    for source_a, source_b, owner in ((own_a, own_b, core), (other_a, other_b, 1 - core)):
        for block in range(blocks):
            for start in range(0, rows_a, PLACE):
                row = pl.multiple_of(side(bits[0], sent) * rows_a + start, 16)
                col = pl.multiple_of((owner * blocks + block) * width, 128)
                moves.append(
                    (
                        lambda r=source_a, b=block, s=start: r[b, s : s + PLACE],
                        up_hbm.at[pl.ds(row, PLACE), pl.ds(col, width)],
                    )
                )
        for start in range(0, rows_b, PLACE):
            row = pl.multiple_of((owner * 2 + side(bits[1], sent)) * rows_b + start, 16)
            moves.append(
                (
                    lambda r=source_b, s=start: r[0, s : s + PLACE],
                    down_hbm.at[pl.ds(row, PLACE)],
                )
            )
    place_all(moves, slots, sems)


def last_place_kernel(bits, sent, own_a, other_a, own_b, other_b, *refs):
    in_hbm, out_hbm, slots, sems = refs[-4:]
    _, rows, width = own_a.shape
    half = width // 2
    core = lax.axis_index("seq") % 2
    moves = []
    for source_a, source_b, owner in ((own_a, own_b, core), (other_a, other_b, 1 - core)):
        for start in range(0, rows, PLACE):
            row = pl.multiple_of(side(bits[0], sent) * rows + start, 16)
            col = pl.multiple_of(owner * 3 * half, 128)
            moves.append(
                (
                    lambda r=source_a, s=start: r[0, s : s + PLACE],
                    in_hbm.at[pl.ds(row, PLACE), pl.ds(col, width)],
                )
            )
            row = pl.multiple_of(side(bits[1], sent) * rows + start, 16)
            col = pl.multiple_of(owner * 3 * half + width, 128)
            moves.append(
                (
                    lambda r=source_b, s=start: r[0, s : s + PLACE, :half],
                    in_hbm.at[pl.ds(row, PLACE), pl.ds(col, half)],
                )
            )
            col = pl.multiple_of(owner * half, 128)
            moves.append(
                (
                    lambda r=source_b, s=start: r[0, s : s + PLACE, half:],
                    out_hbm.at[pl.ds(row, PLACE), pl.ds(col, half)],
                )
            )
    place_all(moves, slots, sems)


def run_place(kernel, bits, sent, sources, outs, shapes, after=()):
    width = sources[0].shape[2]
    given = () if outs is None else outs
    return pl.pallas_call(
        ordered(partial(kernel, bits, sent), 4, len(after)),
        out_shape=tuple(jax.ShapeDtypeStruct(shape, F32) for shape in shapes),
        in_specs=vmem(4) + anywhere(len(after)) + hbm(len(given)),
        out_specs=tuple(hbm(2)),
        scratch_shapes=[
            pltpu.VMEM((SLOTS, PLACE, width), F32),
            pltpu.SemaphoreType.DMA((SLOTS,)),
        ],
        input_output_aliases={4 + len(after) + i: i for i in range(len(given))},
        compiler_params=params(PLACE_BYTES),
        cost_estimate=SHORT,
    )(*sources, *after, *given)


def small_places(hidden):
    second = hidden + 8
    first = second + hidden
    taps = first + 40
    return second, first, taps, taps + 56, taps + 72


def pack_kernel(third_ref, skip_ref, taps_ref, gains_one, gains_two, second_ref, first_ref, out_ref):
    hidden, mine = third_ref.shape
    second, first, taps, gains, _ = small_places(hidden)
    out_ref[...] = jnp.zeros(out_ref.shape, F32)
    out_ref[:hidden, :mine] = third_ref[...]
    out_ref[hidden : hidden + 1, :mine] = skip_ref[...]
    out_ref[second : second + hidden, :hidden] = second_ref[...]
    out_ref[first : first + first_ref.shape[0], :hidden] = first_ref[...]
    per = taps_ref.shape[1] // 128
    for tap in range(KS):
        for part in range(per):
            row = taps + tap * per + part
            out_ref[row : row + 1] = taps_ref[tap : tap + 1, part * 128 : (part + 1) * 128]
    per = gains_one.shape[1] // 128
    for i, ref in enumerate((gains_one, gains_two)):
        for part in range(per):
            row = gains + i * per + part
            out_ref[row : row + 1] = ref[:, part * 128 : (part + 1) * 128]


def run_pack(third, skip, taps, gain_one, gain_two, second, first):
    return pl.pallas_call(
        pack_kernel,
        out_shape=jax.ShapeDtypeStruct((small_places(third.shape[0])[-1], 128), F32),
        in_specs=vmem(7),
        out_specs=pl.BlockSpec(memory_space=pltpu.VMEM),
        compiler_params=params(),
        cost_estimate=SHORT,
    )(third, skip, taps, gain_one, gain_two, second, first)


def line_kernel(shared, *refs):
    *parts, out = refs
    spot = line_spot()
    total = parts[0][shared:]
    for part in parts[1:]:
        total = total + part[shared:]
    out[len(parts) * shared :] = total
    for away, part in enumerate(parts):
        out[pl.ds(pl.multiple_of((spot ^ away) * shared, 8), shared)] = part[:shared]


def run_line(parts, shared, after):
    rows = len(parts) * shared + parts[0].shape[0] - shared
    return pl.pallas_call(
        ordered(partial(line_kernel, shared), len(parts), len(after)),
        out_shape=jax.ShapeDtypeStruct((rows, 128), F32),
        in_specs=vmem(len(parts)) + anywhere(len(after)),
        out_specs=pl.BlockSpec(memory_space=pltpu.VMEM),
        compiler_params=params(),
        cost_estimate=SHORT,
    )(*parts, *after)


def unpack_kernel(
    count, mine, mine_ref, got_ref, third_ref, skip_ref, taps_ref, gain_one, gain_two, second_ref,
    first_ref, owner_ref, sum_ref,
):
    hidden, width = third_ref.shape
    second, first, taps, gains, end = small_places(hidden)
    core = lax.axis_index("seq") % 2
    for spot in range(count):
        here = slice(spot * second, (spot + 1) * second)
        owner_ref[2 * spot + core] = mine_ref[here]
        owner_ref[2 * spot + 1 - core] = got_ref[here]
    sum_ref[...] = mine_ref[count * second :] + got_ref[count * second :]
    lane = lax.broadcasted_iota(jnp.int32, (second, 128), 1)
    wide = [jnp.zeros((second, 128), F32) for _ in range(width // 128)]
    for owner in range(2 * count):
        at, shift = divmod(owner * mine, 128)
        moved = owner_ref[owner]
        if shift:
            moved = pltpu.roll(moved, shift, 1)
        wide[at] = wide[at] + jnp.where(lane >= shift, moved, 0.0)
        if shift + mine > 128:
            wide[at + 1] = wide[at + 1] + jnp.where(lane < shift, moved, 0.0)
    for at, value in enumerate(wide):
        cols = slice(at * 128, (at + 1) * 128)
        third_ref[:, cols] = value[:hidden]
        skip_ref[:, cols] = value[hidden : hidden + 1]
    second_ref[...] = sum_ref[:hidden, :hidden]
    first_ref[...] = sum_ref[first - second : first - second + first_ref.shape[0], :hidden]
    per = taps_ref.shape[1] // 128
    for tap in range(KS):
        for part in range(per):
            row = taps - second + tap * per + part
            taps_ref[tap : tap + 1, part * 128 : (part + 1) * 128] = sum_ref[row : row + 1]
    per = width // 128
    for i, ref in enumerate((gain_one, gain_two)):
        for part in range(per):
            row = gains - second + i * per + part
            ref[:, part * 128 : (part + 1) * 128] = sum_ref[row : row + 1]


def run_unpack(count, mine, packed, got, hidden, width, embedded, after):
    shapes = (
        (hidden, width), (1, width), (KS, 3 * width), (1, width), (1, width), (hidden, hidden),
        (embedded, hidden),
    )
    shared = hidden + 8
    return pl.pallas_call(
        ordered(partial(unpack_kernel, count, mine), 2, len(after)),
        out_shape=tuple(jax.ShapeDtypeStruct(shape, F32) for shape in shapes),
        in_specs=vmem(2) + anywhere(len(after)),
        out_specs=tuple(vmem(7)),
        scratch_shapes=[
            pltpu.VMEM((2 * count, shared, 128), F32),
            pltpu.VMEM((packed.shape[0] - count * shared, 128), F32),
        ],
        compiler_params=params(),
        cost_estimate=SHORT,
    )(packed, got, *after)


def hold(value, after):
    return pl.pallas_call(
        lambda *refs: None,
        out_shape=jax.ShapeDtypeStruct(value.shape, value.dtype),
        in_specs=anywhere(1 + len(after)),
        out_specs=pl.BlockSpec(memory_space=pl.ANY),
        input_output_aliases={0: 0},
        cost_estimate=SHORT,
    )(value, *after)


class Group:
    def __init__(self, orders, line_bits, sent):
        self.orders, self.line_bits = orders, line_bits
        self.sent = sent
        self.got = self.swap(sent, 0)
        self.aways = [0]
        for bit in line_bits:
            self.aways += [away | bit for away in self.aways]

    def bits(self, level):
        return self.orders[0][level], self.orders[1][level]

    def swap(self, pair, level):
        return tuple(swap(value, bit) for value, bit in zip(pair, self.bits(level)))

    def halve(self, kept, after=()):
        sent_a, next_a, sent_b, next_b = run_halve(
            self.bits(1), kept[0], self.got[0], kept[1], self.got[1], after
        )
        self.kept, self.sent = (next_a, next_b), (sent_a, sent_b)
        self.got = self.swap(self.sent, 1)

    def scatter(self, after=()):
        self.shapes = [part.shape for part in self.kept]
        if len(self.aways) == 4:
            self.shares = run_scatter(
                self.kept[0], self.got[0], self.kept[1], self.got[1], len(self.aways), after
            )
            self.arrived = [
                swap(share, away) for share, away in zip(self.shares[1:], self.aways[1:])
            ]
        else:
            self.shares = tuple(
                halve(add(kept, got), lax.axis_index(AXES), self.line_bits[::-1], 1)
                for kept, got in zip(self.kept, self.got)
            )

    def total(self, after=()):
        if len(self.aways) == 4:
            self.share = run_total([self.shares[0], *self.arrived], after)
            self.arrived = [swap(self.share, away) for away in self.aways[1:]]
        else:
            self.share = self.shares[0]

    def gather(self, after=()):
        if len(self.aways) == 4:
            self.mine = run_gather([self.share, *self.arrived], self.shapes, after)
        else:
            self.mine = tuple(
                double(share, lax.axis_index(AXES), self.line_bits[::-1], 1)
                for share in self.shares
            )
        self.got = self.swap(self.mine, 1)

    def join(self, after=()):
        self.mine = run_join(
            self.bits(1), self.mine[0], self.got[0], self.mine[1], self.got[1], after
        )
        self.got = self.swap(self.mine, 0)
        self.mine_core = tuple(swap(value, 1) for value in self.mine)

    def place(self, kernel, shapes, after=()):
        self.outs = run_place(
            kernel, self.bits(0), False,
            (self.mine[0], self.mine_core[0], self.mine[1], self.mine_core[1]), None, shapes, after,
        )

    def finish(self, kernel, shapes, after=()):
        got_core = tuple(swap(value, 1) for value in self.got)
        return run_place(
            kernel, self.bits(0), True, (self.got[0], got_core[0], self.got[1], got_core[1]),
            self.outs, shapes, after,
        )


def to_owner(sent, mine, padded):
    count = lax.axis_size("seq")
    groups, rows, size, block = sent.shape
    if groups != count:
        sent = sent.reshape(rows, count, mine, block).transpose(1, 0, 2, 3)
    got = lax.all_to_all(sent, "seq", 0, 0, tiled=True).reshape(count * rows, mine, block)
    if padded != mine:
        got = jnp.pad(got, ((0, 0), (0, padded - mine), (0, 0)))
    return got


def to_block(value, rows, mine, groups):
    count = lax.axis_size("seq")
    size, block = value.shape[1:]
    got = lax.all_to_all(
        value.reshape(count, rows, size, block), "seq", 0, 0, tiled=True
    )
    if groups == count:
        return got
    return got[:, :, :mine].transpose(1, 0, 2, 3).reshape(1, rows, count * mine, block), got


def per_device(
    hidden_in, lengths, gain_one, in_weight, short_kernel, skip_gain, decay_rate, filt_first,
    filt_second, filt_third, out_weight, gain_two, ff_up, ff_down, out_grad,
):
    rows, block, width = hidden_in.shape
    seq_count, seq_pos = lax.axis_size("seq"), lax.axis_index("seq")
    dp_count = lax.axis_size("dp")
    index = lax.axis_index(AXES)
    units = ff_up.shape[1]
    row_len = block * seq_count
    tokens = rows * block
    seq_bits = [1 << i for i in range(1, seq_count.bit_length() - 1)]
    dp_bits = [seq_count << i for i in range(dp_count.bit_length() - 1)]
    mine = width // seq_count
    padded = -(-mine // 16) * 16
    groups = seq_count if mine == padded and (width // 2) % mine == 0 else 1

    forward, inverse = spectral_tables(block)
    forward_two, inverse_three = jnp.asarray(two_pass(forward)), jnp.asarray(three_pass(inverse))
    forward_three, inverse_two = jnp.asarray(three_pass(forward.T)), jnp.asarray(two_pass(inverse.T))

    before = shifted(hidden_in[:, block - 2 :], 1)
    after = shifted(hidden_in[:, :2], -1)
    normed_one, extended, outer, signal_sent = run_front(
        lengths, hidden_in, before, after, gain_one[None], short_kernel, in_weight, groups
    )
    signal_ch = to_owner(signal_sent, mine, padded)

    signal_sent, filt_first, decay_rate, skip_gain = lax.optimization_barrier(
        (signal_sent, filt_first, decay_rate, skip_gain)
    )
    bands = (filt_first.shape[0] - 1) // 2
    spots = np.arange(row_len)
    turns = (np.arange(1, bands + 1)[:, None] * spots[None, :] % row_len) * (2.0 * math.pi / row_len)
    embedding = jnp.asarray(
        np.concatenate([spots[None, :] / row_len, np.cos(turns), np.sin(turns)], axis=0).astype(
            np.float32
        )
    )
    pre_one = jnp.einsum("ef,el->fl", filt_first, embedding, precision=FULL_PRECISION)
    act_one = jnp.sin(pre_one)
    pre_two = jnp.einsum("fg,fl->gl", filt_second, act_one, precision=FULL_PRECISION)
    act_two = jnp.sin(pre_two)
    my_third = lax.dynamic_slice_in_dim(filt_third, seq_pos * mine, mine, 1)
    my_decay = lax.dynamic_slice_in_dim(decay_rate, seq_pos * mine, mine, 0)
    my_skip = lax.dynamic_slice_in_dim(skip_gain, seq_pos * mine, mine, 0)
    my_skip = jnp.pad(my_skip, (0, padded - mine))[:, None]
    places = jnp.asarray(spots.astype(np.float32))
    envelope = jnp.exp(-my_decay[:, None] * places[None, :]) * row_len ** (-0.5)
    taps = jnp.einsum("gc,gl->cl", my_third, act_two, precision=FULL_PRECISION) * envelope
    taps = taps.reshape(mine, seq_count, block).transpose(1, 0, 2)
    if padded != mine:
        taps = jnp.pad(taps, ((0, 0), (0, padded - mine), (0, 0)))
    pieces = jnp.einsum("kct,tf->kcf", taps, jnp.asarray(forward), precision=FULL_PRECISION)
    sign = jnp.asarray(np.tile(1.0 - 2.0 * (np.arange(block) % 2), 2).astype(np.float32))
    earlier = jnp.concatenate([jnp.zeros_like(pieces[:1]), pieces[:-1]], axis=0)
    spectrum = earlier + sign * pieces
    spec_real, spec_imag = spectrum[..., :block], spectrum[..., block:]
    base = jnp.arange(block) == 0
    spectrum = (
        spec_real,
        jnp.where(base, 0.0, spec_imag),
        jnp.where(base, spec_imag, spec_real),
    )

    conv_ch = run_conv(
        lengths, row_len, signal_ch, my_skip, spectrum, forward_two, inverse_three
    )
    conv = to_block(conv_ch, rows, mine, groups)
    if groups == 1:
        conv = conv[0]

    upstream = out_grad.reshape(tokens, width)
    upstream_got = swap(upstream, 1)
    (
        gain_two_grad, factors_mine, factors_theirs, block_out, last_mine, last_theirs, grad_middle,
        grad_outer, grad_sent,
    ) = run_middle(
        conv, mine, outer, hidden_in, gain_two[None], upstream, out_weight, ff_up, ff_down, groups
    )
    factors_got = swap(factors_theirs, 1)
    grad_ch = to_owner(grad_sent, mine, padded)
    orders = (dp_bits, dp_bits[::-1])
    firsts = (orders[0][0], orders[1][0])
    ff_operands = (factors_mine, factors_got, upstream, upstream_got)
    ff_halves = ((units // (2 * width), width // 2, width), (1, units // 4, width))
    ff = Group(
        orders, seq_bits, run_ff_products(firsts, True, ff_operands, ff_halves)
    )
    outer_halo = shifted(grad_outer[:, :2], -1)

    back_ch = run_conv(
        lengths, row_len, grad_ch, my_skip, spectrum, forward_three, inverse_two, backward=True,
        after=ff.sent,
    )
    got = to_block(back_ch, rows, mine, groups)
    grad_signal, got = (got, got) if groups > 1 else got
    halo = got[:, 0, padded : padded + 2 * rows, :mine].astype(F32)
    halo = halo.transpose(1, 0, 2).reshape(rows, 2, width)
    ff_kept = run_ff_products(firsts, False, ff_operands, ff_halves, (back_ch,))
    last_got, normed_got = swap(last_theirs, 1), swap(normed_one, 1)

    ff.halve(ff_kept)

    proj_mine, proj_theirs, kernel_grad, gain_one_grad, input_grad = run_last(
        lengths, grad_signal, mine, halo, extended, grad_outer, outer_halo, hidden_in,
        gain_one[None], short_kernel, grad_middle, in_weight, ff.sent,
    )
    last_operands = (normed_one, normed_got, proj_mine, swap(proj_theirs, 1), last_mine, last_got)
    last_halves = ((1, width // 2, width),) * 2
    ff.scatter()
    last = Group(
        orders,
        seq_bits,
        run_last_products(firsts, True, last_operands, last_halves, ff.shares[:1]),
    )
    last_kept = run_last_products(firsts, False, last_operands, last_halves, last.sent)
    last.halve(last_kept)

    grad_taps = run_filter_grad(
        lengths, row_len, signal_ch, grad_ch, forward_two, inverse_two, forward_three,
        after=last.sent,
    )
    grad_taps = grad_taps[:, :mine].transpose(1, 0, 2).reshape(mine, row_len)
    skip_grad = grad_taps[:, 0]
    grad_taps = grad_taps * envelope
    my_third_grad = jnp.einsum("gl,cl->gc", act_two, grad_taps, precision=FULL_PRECISION)
    grad_two = jnp.cos(pre_two) * jnp.einsum(
        "gc,cl->gl", my_third, grad_taps, precision=FULL_PRECISION
    )
    second_grad = jnp.einsum("fl,gl->fg", act_one, grad_two, precision=FULL_PRECISION)
    grad_one = jnp.cos(pre_one) * jnp.einsum(
        "fg,gl->fl", filt_second, grad_two, precision=FULL_PRECISION
    )
    first_grad = jnp.einsum("el,fl->ef", embedding, grad_one, precision=FULL_PRECISION)

    small = (
        my_third_grad, skip_grad[None], kernel_grad, gain_one_grad, gain_two_grad, second_grad,
        first_grad,
    )

    ff_shapes = (ff_up.shape, ff_down.shape)
    last_shapes = (in_weight.shape, out_weight.shape)
    direct = len(ff.aways) == 4
    if direct:
        packed = run_pack(*small)
        ff.total((packed, *last.got))
        packed = run_total([packed, swap(packed, orders[0][0])], (ff.share,))
        packed = run_total([packed, swap(packed, orders[0][1])])
        ff.gather((packed,))
        last.scatter(ff.mine)
        packed = hold(packed, last.shares[:1])
        arrived = [swap(packed, away) for away in ff.aways[1:]]
        ff.join()
        last.total(ff.mine)
        ff.place(ff_place_kernel, ff_shapes, (last.share,))
        packed = run_line([packed, *arrived], small[0].shape[0] + 8, (last.share,))
        last.gather((packed, *ff.outs[:1]))
        small = run_unpack(
            len(ff.aways), mine, packed, swap(packed, 1), small[0].shape[0], width,
            filt_first.shape[0], last.mine,
        )
    else:
        ff.total()
        ff.gather()
        last.scatter()
        last.total()
        spread = [
            lax.dynamic_update_slice_in_dim(
                jnp.zeros((part.shape[0], width), F32), part, seq_pos * mine, 1
            )
            for part in small[:2]
        ]
        small = lax.psum((*spread, small[2][:KS], *small[3:]), AXES)
        ff.join()
        ff.place(ff_place_kernel, ff_shapes)
        last.gather()
    last.join()
    last.place(last_place_kernel, last_shapes, small[:1])
    up_total, down_total = ff.finish(ff_place_kernel, ff_shapes, last.outs[:1])
    in_total, out_total = last.finish(last_place_kernel, last_shapes)
    return (
        block_out, input_grad, small[3][0], in_total, small[2], small[1][0], small[6], small[5],
        small[0], out_total, small[4][0], up_total, down_total,
    )


def solution(mesh):
    tokens = P("dp", "seq", None)
    return jax.shard_map(
        per_device,
        mesh=mesh,
        in_specs=(tokens, P("dp", None)) + (P(),) * 12 + (tokens,),
        out_specs=(tokens, tokens) + (P(),) * 11,
        check_vma=False,
    )
```

```python
from functools import partial
import math

import jax
import jax.numpy as jnp
import numpy as np
from jax import lax
from jax.experimental import pallas as pl
from jax.experimental.pallas import tpu as pltpu
from jax.sharding import PartitionSpec as P

FULL_PRECISION = lax.Precision.HIGHEST
BF16 = jnp.bfloat16
F32 = jnp.float32
AXES = ("dp", "seq")
VMEM_BYTES = 32 * 1024 * 1024
FULL_BYTES = 54 * 1024 * 1024
PLACE_BYTES = 57 * 1024 * 1024
KS = 3


def swap(value, bit):
    count = lax.axis_size(AXES)
    return lax.ppermute(value, AXES, [(i, i ^ bit) for i in range(count)])


def shifted(value, steps):
    count = lax.axis_size("seq")
    first, last = max(0, -steps), min(count, count - steps)
    return lax.ppermute(value, "seq", [(i, i + steps) for i in range(first, last)])


def my_bit(index, bit):
    return (index // bit) % 2


def add(kept, got):
    return (kept.astype(F32) + got.astype(F32)).astype(kept.dtype)


def halve(value, index, bits, axis):
    for bit in bits:
        size = value.shape[axis] // 2
        mine = my_bit(index, bit)
        keep = lax.dynamic_slice_in_dim(value, mine * size, size, axis)
        send = lax.dynamic_slice_in_dim(value, (1 - mine) * size, size, axis)
        value = add(keep, swap(send, bit))
    return value


def double(value, index, bits, axis):
    for bit in reversed(bits):
        other = swap(value, bit)
        low = my_bit(index, bit) == 0
        value = jnp.concatenate(
            [jnp.where(low, value, other), jnp.where(low, other, value)], axis=axis
        )
    return value


def sum_over(value, bits):
    for bit in bits:
        value = value + swap(value, bit)
    return value


def spectral_tables(block):
    points = 2 * block
    spot = np.arange(block)
    freq = np.arange(block)
    angle = (spot[:, None] * freq[None, :] % points) * (2.0 * math.pi / points)
    real, imag = np.cos(angle), -np.sin(angle)
    imag[:, 0] = 1.0 - 2.0 * (spot % 2)
    forward = np.concatenate([real, imag], axis=1)
    late = spot + block
    angle = (freq[:, None] * late[None, :] % points) * (2.0 * math.pi / points)
    weight = np.where(freq == 0, 1.0, 2.0)[:, None] / points
    real, imag = weight * np.cos(angle), -weight * np.sin(angle)
    imag[0, :] = (1.0 - 2.0 * (late % 2)) / points
    inverse = np.concatenate([real, imag], axis=0)
    return forward.astype(np.float32), inverse.astype(np.float32)


def split_table(table):
    high = table.astype(jnp.bfloat16)
    low = (table - high.astype(np.float32)).astype(jnp.bfloat16)
    return np.asarray(high), np.asarray(low)


def two_pass(table):
    high, low = split_table(table)
    return np.concatenate([high, low], axis=0)


def three_pass(table):
    high, low = split_table(table)
    return np.concatenate([high, high, low], axis=0)


def ends_of(lengths_ref, row):
    total, ends = 0, []
    for k in range(lengths_ref.shape[1]):
        total = total + lengths_ref[row, k]
        ends.append(total)
    return ends


def next_end(ends, spot, row_len):
    found = row_len
    for end in reversed(ends):
        found = jnp.where(end > spot, end, found)
    return found


def last_end(ends, spot):
    found = 0
    for end in ends:
        found = jnp.where(end <= spot, end, found)
    return found


def near_mask(ends, spots, step):
    apart = spots < step
    for end in ends:
        apart = apart | ((end <= spots) & (end > spots - step))
    return jnp.where(apart, 0.0, 1.0)


def dot(left, right):
    return jnp.dot(left, right, preferred_element_type=F32)


def dot_nt(left, right):
    return lax.dot_general(left, right, (((1,), (1,)), ((), ())), preferred_element_type=F32)


def head_masks(ends, spot, group, rows, block, row_len):
    lane = lax.broadcasted_iota(jnp.int32, (1, 1, block), 2)
    masks = []
    for g in range(group):
        start = (spot + g) // rows * block
        stop = jnp.where((spot + g) % rows == 0, next_end(ends[0], start, row_len), 0)
        for row in range(1, rows):
            stop = jnp.where(
                (spot + g) % rows == row, next_end(ends[row], start, row_len), stop
            )
        masks.append(jnp.where(lane < stop - start, 1.0, 0.0))
    return jnp.concatenate(masks, axis=0)


def spectra(value_ref, masks, table_ref, head_out, rest_out, group):
    count, channels, block = value_ref.shape

    def step(i, carry):
        spot = pl.ds(i * group, group)
        whole = value_ref[spot].astype(F32)
        first = whole * masks(i * group)
        both = jnp.concatenate([first, whole - first], axis=0).astype(BF16)
        both = both.reshape(2 * group * channels, block)
        found = dot(jnp.concatenate([both, both], axis=1), table_ref[...])
        found = found.reshape(2 * group, channels, 2 * block)
        head_out[spot] = found[:group]
        rest_out[spot] = found[group:]
        return carry

    lax.fori_loop(0, count // group, step, 0)


def back_to_time(head_spec, rest_spec, masks, table_ref, value_ref, skip_ref, group, store):
    count, channels, double_block = head_spec.shape

    def step(i, carry):
        spot = pl.ds(i * group, group)
        both = jnp.concatenate([head_spec[spot], rest_spec[spot]], axis=0)
        both = both.reshape(2 * group * channels, double_block)
        high = both.astype(BF16)
        low = (both - high.astype(F32)).astype(BF16)
        found = dot(jnp.concatenate([high, low, high], axis=1), table_ref[...])
        found = found.reshape(2 * group, channels, double_block // 2)
        rest = found[group:]
        found = rest + masks(i * group) * (found[:group] - rest)
        store(i * group, found + skip_ref[...][None] * value_ref[spot].astype(F32))
        return carry

    lax.fori_loop(0, count // group, step, 0)


def of_row(per_row, row):
    found = per_row[0]
    for k in range(1, len(per_row)):
        found = jnp.where(row == k, per_row[k], found)
    return found


def start_loads(moves, sems):
    loads = [
        pltpu.make_async_copy(source, target, sems.at[i])
        for i, (source, target) in enumerate(moves)
    ]
    for load in loads:
        load.start()
    return loads


def conv_kernel(
    rows, group, row_len, lengths_ref, value_ref, skip_hbm, hr_hbm, hi_hbm, hm_hbm,
    forward_hbm, inverse_hbm, out_ref, skip_ref, hr_ref, hi_ref, hm_ref, forward_ref, inverse_ref,
    sems, head_spec, rest_spec, head_sum, rest_sum,
):
    count, channels, block = value_ref.shape
    loads = start_loads(
        [
            (forward_hbm, forward_ref), (hr_hbm, hr_ref), (hi_hbm, hi_ref), (hm_hbm, hm_ref),
            (inverse_hbm, inverse_ref), (skip_hbm, skip_ref),
        ],
        sems,
    )
    ends = [ends_of(lengths_ref, row) for row in range(rows)]

    def masks(spot):
        return head_masks(ends, spot, group, rows, block, row_len)

    loads[0].wait()
    spectra(value_ref, masks, forward_ref, head_spec, rest_spec, group)
    for load in loads[1:]:
        load.wait()

    def product(real, imag, lag):
        hr, hi, hm = hr_ref[lag], hi_ref[lag], hm_ref[lag]
        return real * hr - imag * hi, real * hi + imag * hm

    def own(j, carry):
        start = j // rows * block
        stop = of_row([next_end(e, start, row_len) for e in ends], j % rows)
        plain = (stop >= start + block).astype(F32)
        head_real, head_imag = product(head_spec[j, :, :block], head_spec[j, :, block:], 0)
        head_sum[j, :, :block] = head_real
        head_sum[j, :, block:] = head_imag
        rest_real, rest_imag = product(rest_spec[j, :, :block], rest_spec[j, :, block:], 0)
        rest_sum[j, :, :block] = rest_real
        rest_sum[j, :, block:] = rest_imag
        rest_spec[j] = rest_spec[j] + plain * head_spec[j]
        return carry

    lax.fori_loop(0, count, own, 0)

    def reach(j, carry):
        spot, row = j // rows, j % rows
        begin = of_row([last_end(e, spot * block) for e in ends], row) // block

        def include(source, sums):
            k = source * rows + row
            real, imag = product(
                rest_spec[k, :, :block], rest_spec[k, :, block:], spot - source
            )
            return sums[0] + real, sums[1] + imag

        start = (head_sum[j, :, :block], head_sum[j, :, block:])
        real, imag = lax.fori_loop(begin, spot, include, start)
        head_sum[j, :, :block] = real
        head_sum[j, :, block:] = imag
        return carry

    lax.fori_loop(rows, count, reach, 0)

    def store(spot, found):
        out_ref[pl.ds(spot, group)] = found.astype(BF16)

    back_to_time(head_sum, rest_sum, masks, inverse_ref, value_ref, skip_ref, group, store)


def conv_back_kernel(
    rows, group, row_len, lengths_ref, value_ref, skip_hbm, hr_hbm, hi_hbm, hm_hbm,
    forward_hbm, inverse_hbm, out_ref, skip_ref, hr_ref, hi_ref, hm_ref, forward_ref, inverse_ref,
    sems, head_spec, rest_spec, head_sum, rest_sum, found_ref,
):
    count, channels, block = value_ref.shape
    loads = start_loads(
        [
            (inverse_hbm, inverse_ref), (hr_hbm, hr_ref), (hi_hbm, hi_ref), (hm_hbm, hm_ref),
            (forward_hbm, forward_ref), (skip_hbm, skip_ref),
        ],
        sems,
    )
    ends = [ends_of(lengths_ref, row) for row in range(rows)]

    def masks(spot):
        return head_masks(ends, spot, group, rows, block, row_len)

    loads[0].wait()
    spectra(value_ref, masks, inverse_ref, head_spec, rest_spec, group)
    for load in loads[1:]:
        load.wait()

    def product(real, imag, lag):
        hr, hi, hm = hr_ref[lag], hi_ref[lag], hm_ref[lag]
        return real * hr + imag * hi, imag * hm - real * hi

    def reach(j, carry):
        spot, row = j // rows, j % rows
        start = spot * block
        plain = of_row([next_end(e, start, row_len) for e in ends], row) >= start + block
        plain = plain.astype(F32)
        until = of_row([next_end(e, start + block - 1, row_len) for e in ends], row)
        until = (until - 1) // block + 1

        def include(source, sums):
            k = source * rows + row
            real, imag = product(
                head_spec[k, :, :block], head_spec[k, :, block:], source - spot
            )
            return sums[0] + real, sums[1] + imag

        empty = jnp.zeros((channels, block), F32)
        real, imag = lax.fori_loop(spot + 1, until, include, (empty, empty))
        head_real, head_imag = product(head_spec[j, :, :block], head_spec[j, :, block:], 0)
        head_sum[j, :, :block] = head_real + plain * real
        head_sum[j, :, block:] = head_imag + plain * imag
        rest_real, rest_imag = product(rest_spec[j, :, :block], rest_spec[j, :, block:], 0)
        rest_sum[j, :, :block] = rest_real + (1.0 - plain) * real
        rest_sum[j, :, block:] = rest_imag + (1.0 - plain) * imag
        return carry

    lax.fori_loop(0, count, reach, 0)

    def store(spot, found):
        found_ref[pl.ds(spot, group)] = found
        out_ref[pl.ds(spot, group), :channels] = found.astype(BF16)

    back_to_time(head_sum, rest_sum, masks, forward_ref, value_ref, skip_ref, group, store)

    lane = lax.broadcasted_iota(jnp.int32, (channels, block), 1)
    per_turn = block // 2
    blocks = count // rows
    for turn in range(-(-count // per_turn)):
        first = turn * per_turn
        last = min(count, first + per_turn)

        def gather(j, picked):
            at = 2 * (j - first)
            moved = pltpu.roll(found_ref[j], at, 1)
            return jnp.where((lane >= at) & (lane < at + 2), moved, picked)

        picked = lax.fori_loop(first, last, gather, jnp.zeros((channels, block), F32))
        if channels < block:
            picked = jnp.concatenate(
                [picked, jnp.zeros((block - channels, block), F32)], axis=0
            )
        flipped = picked.T
        for spot in range(first // rows, last // rows):
            at = 2 * (spot * rows - first)
            tile = jnp.concatenate(
                [flipped[at : at + 2 * rows], jnp.zeros((16 - 2 * rows, block), F32)], axis=0
            )
            if spot > 0:
                out_ref[(spot - 1) * rows, channels:] = tile.astype(BF16)
    out_ref[(blocks - 1) * rows, channels:] = jnp.zeros((16, block), BF16)
    for spot in range(blocks):
        for row in range(1, rows):
            out_ref[spot * rows + row, channels:] = jnp.zeros((16, block), BF16)


def filter_grad_kernel(
    rows, group, row_len, lengths_ref, value_ref, grad_ref, forward_ref,
    inverse_ref, back_ref, out_ref, head_spec, rest_spec, grad_head, grad_rest, total,
):
    count, channels, block = value_ref.shape
    lags = count // rows
    ends = [ends_of(lengths_ref, row) for row in range(rows)]

    def masks(spot):
        return head_masks(ends, spot, group, rows, block, row_len)

    spectra(value_ref, masks, forward_ref, head_spec, rest_spec, group)
    spectra(grad_ref, masks, inverse_ref, grad_head, grad_rest, group)
    lane = lax.broadcasted_iota(jnp.int32, (channels, block), 1)
    base = lane == 0

    def product(grad, spec, k, j):
        gr, gi = grad[k, :, :block], grad[k, :, block:]
        sr, si = spec[j, :, :block], spec[j, :, block:]
        masked = jnp.where(base, 0.0, si)
        swapped = jnp.where(base, si, sr)
        return gr * sr + gi * masked, gi * swapped - gr * masked

    def own(j, sums):
        start = j // rows * block
        stop = of_row([next_end(e, start, row_len) for e in ends], j % rows)
        plain = (stop >= start + block).astype(F32)
        head = product(grad_head, head_spec, j, j)
        rest = product(grad_rest, rest_spec, j, j)
        rest_spec[j] = rest_spec[j] + plain * head_spec[j]
        return sums[0] + head[0] + rest[0], sums[1] + head[1] + rest[1]

    empty = jnp.zeros((channels, block), F32)
    real, imag = lax.fori_loop(0, count, own, (empty, empty))
    total[0, :, :block] = real
    total[0, :, block:] = imag

    def one_lag(lag, carry):
        def include(j, sums):
            spot = j // rows
            begin = of_row([last_end(e, spot * block) for e in ends], j % rows) // block
            near = (begin <= spot - lag).astype(F32)
            real, imag = product(grad_head, rest_spec, j, j - lag * rows)
            return sums[0] + near * real, sums[1] + near * imag

        real, imag = lax.fori_loop(lag * rows, count, include, (empty, empty))
        total[lag, :, :block] = real
        total[lag, :, block:] = imag
        return carry

    lax.fori_loop(1, lags, one_lag, 0)
    wide = lax.broadcasted_iota(jnp.int32, (channels, 2 * block), 1)
    sign = (1 - 2 * (wide % 2)).astype(F32)
    total[lags] = jnp.zeros((channels, 2 * block), F32)

    def one_piece(lag, carry):
        piece = total[lag + 1] + sign * total[lag]
        high = piece.astype(BF16)
        low = (piece - high.astype(F32)).astype(BF16)
        out_ref[lag] = dot(jnp.concatenate([high, low, high], axis=1), back_ref[...])
        return carry

    lax.fori_loop(0, lags, one_piece, 0)


def vmem(count):
    return [pl.BlockSpec(memory_space=pltpu.VMEM)] * count


def smem(count):
    return [pl.BlockSpec(memory_space=pltpu.SMEM)] * count


def hbm(count):
    return [pl.BlockSpec(memory_space=pltpu.HBM)] * count


def anywhere(count):
    return [pl.BlockSpec(memory_space=pl.ANY)] * count


def params(limit=VMEM_BYTES):
    return pltpu.CompilerParams(vmem_limit_bytes=limit)


SHORT = pl.CostEstimate(flops=1, bytes_accessed=1, transcendentals=0)


def takes(micro):
    return pl.CostEstimate(flops=int(micro * 1e9), bytes_accessed=1, transcendentals=0)


BRIDGE_A, BRIDGE_B = takes(5), takes(12)
LINE = takes(8)

TOKEN = (16384, 1024), F32


def launch(
    kernel, operands, outs, in_specs=None, out_specs=None, scratch=(), limit=VMEM_BYTES, after=(),
    aliases=None, estimate=SHORT,
):
    used, made = len(operands), len(outs)

    def call(*refs):
        rest = refs[used + len(after) :]
        kernel(*refs[:used], *rest[:made], *rest[made + 1 :])

    results = pl.pallas_call(
        call,
        name=getattr(kernel, "func", kernel).__name__.replace("<lambda>", "hold"),
        out_shape=tuple(jax.ShapeDtypeStruct(*out) for out in (*outs, TOKEN)),
        in_specs=(vmem(used) if in_specs is None else in_specs) + anywhere(len(after)),
        out_specs=tuple((vmem(made) if out_specs is None else out_specs) + hbm(1)),
        scratch_shapes=list(scratch),
        input_output_aliases=aliases or {},
        compiler_params=params(limit),
        cost_estimate=estimate,
    )(*operands, *after)
    return tuple(results[:-1]), results[-1]


def run_conv(
    lengths, row_len, value, skip, spectrum, forward, inverse, backward=False, after=()
):
    count, channels, block = value.shape
    rows = lengths.shape[0]
    group = 4 if count % 4 == 0 else 1
    spec = pltpu.VMEM((count, channels, 2 * block), F32)
    extra = [pltpu.VMEM((count, channels, block), F32)] if backward else []
    sent = channels + 16 if backward else channels
    (found,), token = launch(
        partial(conv_back_kernel if backward else conv_kernel, rows, group, row_len),
        (lengths, value, skip, *spectrum, forward, inverse),
        [((count, sent, block), BF16)],
        in_specs=smem(1) + vmem(1) + anywhere(6),
        scratch=[
            *[pltpu.VMEM(part.shape, part.dtype) for part in (skip, *spectrum, forward, inverse)],
            pltpu.SemaphoreType.DMA((6,)),
            *[spec] * 4,
            *extra,
        ],
        after=after,
    )
    return found, token


def run_filter_grad(lengths, row_len, value, grad, forward, inverse, back, after=()):
    count, channels, block = value.shape
    rows = lengths.shape[0]
    group = 4 if count % 4 == 0 else 1
    lags = count // rows
    spec = pltpu.VMEM((count, channels, 2 * block), F32)
    (found,), token = launch(
        partial(filter_grad_kernel, rows, group, row_len),
        (lengths, value, grad, forward, inverse, back),
        [((lags, channels, block), F32)],
        in_specs=smem(1) + vmem(5),
        scratch=[spec] * 4 + [pltpu.VMEM((lags + 1, channels, 2 * block), F32)],
        after=after,
    )
    return found, token


def put_channels(ref, row, chunk, value):
    groups, _, size, _ = ref.shape
    wide = value.shape[0]
    if groups == 1:
        ref[0, row, chunk * wide : (chunk + 1) * wide] = value
    else:
        per = wide // size
        for k in range(per):
            ref[chunk * per + k, row] = value[k * size : (k + 1) * size]


def get_channels(ref, row, chunk, wide, size):
    groups = ref.shape[0]
    if groups == 1:
        return ref[0, row, chunk * wide : (chunk + 1) * wide]
    per = wide // size
    return jnp.concatenate([ref[chunk * per + k, row, :size] for k in range(per)], axis=0)


def moments(value):
    center = value - jnp.mean(value, axis=-1, keepdims=True)
    spread = jnp.mean(center * center, axis=-1, keepdims=True)
    return center, lax.rsqrt(spread + 1e-05)


def norm_back(center, scale, gain, grad):
    unit = center * scale
    inner = grad * gain
    mean_one = jnp.mean(inner, axis=-1, keepdims=True)
    mean_two = jnp.mean(inner * unit, axis=-1, keepdims=True)
    return scale * (inner - mean_one - unit * mean_two), grad * unit


PIECE = 64


def front_kernel(
    lengths_ref, before_ref, after_ref, gain_ref, hidden_hbm, taps_hbm, weight_hbm,
    normed_hbm, extended_hbm, outer_hbm, sent_hbm,
    hidden_ref, taps_ref, weight_ref, normed_ref, extended_ref, outer_ref, sent_ref,
    halo_ref, wide_ref, mixed_ref, sems,
):
    rows, block, width = hidden_ref.shape
    loads = [
        pltpu.make_async_copy(source, target, sems.at[i])
        for i, (source, target) in enumerate(
            [(hidden_hbm, hidden_ref), (weight_hbm, weight_ref), (taps_hbm, taps_ref)]
        )
    ]
    for load in loads:
        load.start()
    gain = gain_ref[...]
    halo = jnp.concatenate(
        [part for row in range(rows) for part in (before_ref[row], after_ref[row])], axis=0
    ).astype(F32)
    center, scale = moments(halo)
    halo = center * scale * gain
    halo_ref[...] = jnp.concatenate(
        [halo, jnp.zeros((halo_ref.shape[0] - 4 * rows, width), F32)], axis=0
    ).astype(BF16)
    first = lax.axis_index("seq") * block
    ends = [ends_of(lengths_ref, row) for row in range(rows)]
    spots = first + lax.broadcasted_iota(jnp.int32, (block, 1), 0)
    near_one = [near_mask(e, spots, 1) for e in ends]
    near_two = [near_mask(e, spots, 2) for e in ends]
    live = [jnp.where(spots < e[-1], 1.0, 0.0) for e in ends]
    loads[0].wait()
    for row in range(rows):
        for start in range(0, block, PIECE):
            center, scale = moments(hidden_ref[row, start : start + PIECE].astype(F32))
            at = row * block + start
            normed_ref[at : at + PIECE] = (center * scale * gain).astype(BF16)
    saves = [
        pltpu.make_async_copy(source, target, sems.at[3 + i])
        for i, (source, target) in enumerate(
            [
                (normed_ref, normed_hbm),
                (sent_ref, sent_hbm),
                (extended_ref, extended_hbm),
                (outer_ref, outer_hbm),
            ]
        )
    ]
    saves[0].start()
    chunk = width // 2
    loads[1].wait()
    loads[2].wait()
    for part in range(3):
        for half in range(2):
            cols = slice(part * width + half * chunk, part * width + (half + 1) * chunk)
            main = dot(normed_ref[...], weight_ref[:, cols])
            edge = dot(halo_ref[...], weight_ref[:, cols])
            taps = taps_ref[:, cols]
            for row in range(rows):
                wide_ref[row, 0:8] = jnp.zeros((8, chunk), F32)
                wide_ref[row, block + 8 :] = jnp.zeros((8, chunk), F32)
                wide_ref[row, 6:8] = edge[4 * row : 4 * row + 2]
                wide_ref[row, 8 : block + 8] = main[row * block : (row + 1) * block]
                wide_ref[row, block + 8 : block + 10] = edge[4 * row + 2 : 4 * row + 4]
                rounded = wide_ref[row].astype(BF16)
                extended_ref[row, :, cols] = rounded
                wide_ref[row] = rounded.astype(F32)
                mixed = (
                    taps[0:1] * wide_ref[row, 8 : block + 8]
                    + taps[1:2] * wide_ref[row, 7 : block + 7] * near_one[row]
                    + taps[2:3] * wide_ref[row, 6 : block + 6] * near_two[row]
                )
                here = slice(half * chunk, (half + 1) * chunk)
                if part == 0:
                    mixed_ref[row, :, here] = mixed
                elif part == 1:
                    signal = mixed_ref[row, :, here] * mixed * live[row]
                    put_channels(sent_ref, row, half, signal.T.astype(BF16))
                else:
                    outer_ref[row, :, here] = mixed
        if part == 1:
            saves[1].start()
    saves[2].start()
    saves[3].start()
    for save in saves:
        save.wait()


def run_front(lengths, hidden, before, after, gain, taps, weight, groups):
    rows, block, width = hidden.shape
    chunk = width // 2
    outs = (
        ((rows * block, width), BF16),
        ((rows, block + 16, 3 * width), BF16),
        ((rows, block, width), F32),
        ((groups, rows, width // groups, block), BF16),
    )
    return pl.pallas_call(
        front_kernel,
        out_shape=tuple(jax.ShapeDtypeStruct(*out) for out in outs),
        in_specs=smem(1) + vmem(3) + hbm(3),
        out_specs=tuple(hbm(4)),
        scratch_shapes=[
            pltpu.VMEM(hidden.shape, BF16),
            pltpu.VMEM(taps.shape, F32),
            pltpu.VMEM(weight.shape, BF16),
            *[pltpu.VMEM(*out) for out in outs],
            pltpu.VMEM((16, width), BF16),
            pltpu.VMEM((rows, block + 16, chunk), F32),
            pltpu.VMEM((rows, block, width), F32),
            pltpu.SemaphoreType.DMA((7,)),
        ],
        compiler_params=params(FULL_BYTES),
        cost_estimate=SHORT,
    )(lengths, before, after, gain, hidden, taps, weight)


def middle_kernel(
    size, conv_ref, gain_ref, outer_hbm, hidden_hbm, upstream_hbm, out_hbm, up_hbm, down_hbm,
    gain_grad_ref, factors_mine_hbm, factors_theirs_hbm, result_hbm, last_mine_hbm, last_theirs_hbm,
    grad_middle_hbm, grad_outer_hbm, sent_hbm,
    outer_ref, hidden_ref, upstream_ref, out_ref, up_ref, down_ref,
    factors_mine, factors_theirs, result_ref, last_mine, last_theirs, grad_middle_ref,
    grad_outer_ref, sent_ref,
    conv_scr, middle_ref, grad_ref, sems,
):
    rows, block, width = hidden_ref.shape
    parts = down_ref.shape[0] // width
    per_core = parts // 2
    units = per_core * width
    chunk = width // 2
    core = lax.axis_index("seq") % 2
    copies = [
        pltpu.make_async_copy(outer_hbm, outer_ref, sems.at[0]),
        pltpu.make_async_copy(out_hbm, out_ref, sems.at[1]),
        pltpu.make_async_copy(hidden_hbm, hidden_ref, sems.at[2]),
        pltpu.make_async_copy(upstream_hbm, upstream_ref, sems.at[3]),
    ]
    for part in range(parts):
        cols = slice(part * width, (part + 1) * width)
        copies.append(
            pltpu.make_async_copy(up_hbm.at[:, cols], up_ref.at[:, cols], sems.at[2 * part + 4])
        )
        copies.append(
            pltpu.make_async_copy(down_hbm.at[cols], down_ref.at[cols], sems.at[2 * part + 5])
        )
    for copy in copies:
        copy.start()
    saves = [
        pltpu.make_async_copy(source, target, sems.at[2 * parts + 4 + i])
        for i, (source, target) in enumerate(
            [
                (result_ref, result_hbm),
                (grad_middle_ref, grad_middle_hbm),
                (last_mine, last_mine_hbm),
                (last_theirs, last_theirs_hbm),
                (sent_ref, sent_hbm),
                (grad_outer_ref, grad_outer_hbm),
                (factors_theirs, factors_theirs_hbm),
                (factors_mine, factors_mine_hbm),
            ]
        )
    ]
    for row in range(rows):
        here = slice(row * block, (row + 1) * block)
        for half in range(2):
            cols = slice(half * chunk, (half + 1) * chunk)
            conv_scr[here, cols] = get_channels(conv_ref, row, half, chunk, size).astype(F32).T
    copies[0].wait()
    for row in range(rows):
        here = slice(row * block, (row + 1) * block)
        gated = (outer_ref[row] * conv_scr[here]).astype(BF16)
        last_mine[here, :width] = gated
        last_theirs[here, :width] = gated
    copies[1].wait()
    middle_ref[...] = dot(last_mine[:, :width], out_ref[...])
    copies[2].wait()
    gain = gain_ref[...]
    normed = slice(2 * units, 2 * units + width)
    for row in range(rows):
        for start in range(0, block, PIECE):
            here = slice(row * block + start, row * block + start + PIECE)
            middle = middle_ref[here] + hidden_ref[row, start : start + PIECE].astype(F32)
            middle_ref[here] = middle
            center, scale = moments(middle)
            rounded = (center * scale * gain).astype(BF16)
            factors_mine[here, normed] = rounded
            factors_theirs[here, normed] = rounded
    slope = math.sqrt(2.0 / math.pi)
    copies[3].wait()
    for part in range(parts):
        cols = slice(part * width, (part + 1) * width)
        copies[2 * part + 4].wait()
        pre = dot(factors_mine[:, normed], up_ref[:, cols])
        copies[2 * part + 5].wait()
        grad_act = dot_nt(upstream_ref[...], down_ref[cols])
        square = pre * pre
        bend = jnp.tanh(slope * pre * (1.0 + 0.044715 * square))
        half_up = 0.5 * (1.0 + bend)
        act = (pre * half_up).astype(BF16)
        turn = half_up + 0.5 * pre * (1.0 - bend * bend) * (
            slope * (1.0 + 3.0 * 0.044715 * square)
        )
        grad_pre = (grad_act * turn).astype(BF16)
        owner = part // per_core
        at = part % per_core * width

        @pl.when(core == owner)
        def _():
            factors_mine[:, at : at + width] = act
            factors_mine[:, units + at : units + at + width] = grad_pre

        @pl.when(core != owner)
        def _():
            factors_theirs[:, at : at + width] = act
            factors_theirs[:, units + at : units + at + width] = grad_pre

        if part == 0:
            grad_ref[...] = dot_nt(grad_pre, up_ref[:, cols])
        else:
            grad_ref[...] += dot_nt(grad_pre, up_ref[:, cols])
        found = dot(act, down_ref[cols])
        for row in range(rows):
            here = slice(row * block, (row + 1) * block)
            if part == 0:
                grad_middle_ref[here] = middle_ref[here] + found[here]
            elif part < parts - 1:
                grad_middle_ref[here] += found[here]
            else:
                result_ref[row] = (grad_middle_ref[here] + found[here]).astype(BF16)
    saves[6].start()
    saves[7].start()
    saves[0].start()
    gain_grad = jnp.zeros((1, width), F32)
    branch_cols = slice(width, width + chunk)
    for at in range(0, rows * block, PIECE):
        here = slice(at, at + PIECE)
        center, scale = moments(middle_ref[here])
        grad, terms = norm_back(center, scale, gain, grad_ref[here])
        gain_grad = gain_grad + jnp.sum(terms, axis=0, keepdims=True)
        grad = upstream_ref[here].astype(F32) + grad
        grad_middle_ref[here] = grad
        branch = grad.astype(BF16)

        @pl.when(core == 0)
        def _():
            last_mine[here, branch_cols] = branch[:, :chunk]
            last_theirs[here, branch_cols] = branch[:, chunk:]

        @pl.when(core != 0)
        def _():
            last_mine[here, branch_cols] = branch[:, chunk:]
            last_theirs[here, branch_cols] = branch[:, :chunk]

    for save in saves[1:4]:
        save.start()
    gain_grad_ref[...] = gain_grad
    grad_ref[...] = dot_nt(grad_middle_ref[...].astype(BF16), out_ref[...])
    for row in range(rows):
        here = slice(row * block, (row + 1) * block)
        for half in range(2):
            cols = slice(half * chunk, (half + 1) * chunk)
            grad_conv = grad_ref[here, cols] * outer_ref[row, :, cols]
            put_channels(sent_ref, row, half, grad_conv.T.astype(BF16))
    saves[4].start()
    for row in range(rows):
        here = slice(row * block, (row + 1) * block)
        grad_outer_ref[row] = grad_ref[here] * conv_scr[here]
    saves[5].start()
    for save in saves:
        save.wait()


def run_middle(conv, size, outer, hidden, gain, upstream, out_weight, up, down, groups):
    rows, block, width = hidden.shape
    tokens = rows * block
    units = up.shape[1]
    parts = units // width
    near = (((1, width), F32),)
    far = (
        ((tokens, units + width), BF16),
        ((tokens, units + width), BF16),
        ((rows, block, width), BF16),
        ((tokens, 3 * width // 2), BF16),
        ((tokens, 3 * width // 2), BF16),
        ((tokens, width), F32),
        ((rows, block, width), F32),
        ((groups, rows, width // groups, block), BF16),
    )
    return pl.pallas_call(
        partial(middle_kernel, size),
        out_shape=tuple(jax.ShapeDtypeStruct(*out) for out in near + far),
        in_specs=vmem(2) + hbm(6),
        out_specs=tuple(vmem(1) + hbm(8)),
        scratch_shapes=[
            pltpu.VMEM(outer.shape, F32),
            pltpu.VMEM(hidden.shape, BF16),
            pltpu.VMEM(upstream.shape, BF16),
            pltpu.VMEM(out_weight.shape, BF16),
            pltpu.VMEM(up.shape, BF16),
            pltpu.VMEM(down.shape, BF16),
            *[pltpu.VMEM(*out) for out in far],
            pltpu.VMEM((tokens, width), F32),
            pltpu.VMEM((tokens, width), F32),
            pltpu.VMEM((tokens, width), F32),
            pltpu.SemaphoreType.DMA((2 * parts + 12,)),
        ],
        compiler_params=params(FULL_BYTES),
        cost_estimate=SHORT,
    )(conv, gain, outer, hidden, upstream, out_weight, up, down)


def last_kernel(
    size, lengths_ref, signal_ref, halo_ref, outer_halo_ref, gain_ref, taps_ref,
    extended_hbm, outer_hbm, hidden_hbm, grad_middle_hbm, weight_hbm,
    proj_mine, proj_theirs, taps_grad_ref, gain_grad_ref, result_hbm,
    extended_ref, outer_ref, hidden_ref, grad_middle_ref, weight_ref, result_ref,
    wide_ref, mixed_ref, grad_ref, proj_ref, normed_grad, sems,
):
    rows, block, width = hidden_ref.shape
    chunk = width // 2
    loads = [
        pltpu.make_async_copy(source, target, sems.at[i])
        for i, (source, target) in enumerate(
            [
                (extended_hbm, extended_ref),
                (outer_hbm, outer_ref),
                (weight_hbm, weight_ref),
                (hidden_hbm, hidden_ref),
                (grad_middle_hbm, grad_middle_ref),
            ]
        )
    ]
    for load in loads:
        load.start()
    core = lax.axis_index("seq") % 2
    first = lax.axis_index("seq") * block
    longer = block + 8
    spots = first + lax.broadcasted_iota(jnp.int32, (longer, 1), 0)
    taps_grad_ref[...] = jnp.zeros(taps_grad_ref.shape, F32)
    loads[0].wait()
    loads[1].wait()
    for row in range(rows):
        ends = ends_of(lengths_ref, row)
        near_one, near_two = near_mask(ends, spots, 1), near_mask(ends, spots, 2)
        live = jnp.where(spots < ends[-1], 1.0, 0.0)
        for half in range(2):
            cols = slice(half * chunk, (half + 1) * chunk)
            grad_ref[0, :block] = get_channels(signal_ref, row, half, chunk, size).astype(F32).T
            grad_ref[0, block:] = jnp.concatenate(
                [halo_ref[row, :, cols], jnp.zeros((6, chunk), F32)], axis=0
            )
            for part in range(2):
                at = slice(part * width + half * chunk, part * width + (half + 1) * chunk)
                taps = taps_ref[:, at]
                wide_ref[part] = extended_ref[row, :, at].astype(F32)
                mixed_ref[part] = (
                    taps[0:1] * wide_ref[part, 8 : longer + 8]
                    + taps[1:2] * wide_ref[part, 7 : longer + 7] * near_one
                    + taps[2:3] * wide_ref[part, 6 : longer + 6] * near_two
                )
            at = slice(2 * width + half * chunk, 2 * width + (half + 1) * chunk)
            wide_ref[2] = extended_ref[row, :, at].astype(F32)
            signal_grad = grad_ref[0] * live
            grad_ref[0] = signal_grad * mixed_ref[1]
            grad_ref[1] = signal_grad * mixed_ref[0]
            grad_ref[2, :block] = outer_ref[row, :, cols]
            grad_ref[2, block:] = jnp.concatenate(
                [outer_halo_ref[row, :, cols], jnp.zeros((6, chunk), F32)], axis=0
            )
            for part in range(3):
                at = slice(part * width + half * chunk, part * width + (half + 1) * chunk)
                taps = taps_ref[:, at]
                own = grad_ref[part, :block]
                proj = (
                    taps[0:1] * own
                    + taps[1:2] * (grad_ref[part, 1 : block + 1] * near_one[1 : block + 1])
                    + taps[2:3] * (grad_ref[part, 2 : block + 2] * near_two[2 : block + 2])
                )
                proj_ref[row * block : (row + 1) * block, at] = proj.astype(BF16)
                taps_grad_ref[0:1, at] += jnp.sum(
                    own * wide_ref[part, 8 : block + 8], axis=0, keepdims=True
                )
                taps_grad_ref[1:2, at] += jnp.sum(
                    own * wide_ref[part, 7 : block + 7] * near_one[:block], axis=0, keepdims=True
                )
                taps_grad_ref[2:3, at] += jnp.sum(
                    own * wide_ref[part, 6 : block + 6] * near_two[:block], axis=0, keepdims=True
                )
    middle = 3 * width // 2

    @pl.when(core == 0)
    def _():
        proj_mine[...] = proj_ref[:, :middle]
        proj_theirs[...] = proj_ref[:, middle:]

    @pl.when(core != 0)
    def _():
        proj_mine[...] = proj_ref[:, middle:]
        proj_theirs[...] = proj_ref[:, :middle]

    loads[2].wait()
    normed_grad[...] = dot_nt(proj_ref[...], weight_ref[...])
    loads[3].wait()
    loads[4].wait()
    gain = gain_ref[...]
    gain_grad = jnp.zeros((1, width), F32)
    for row in range(rows):
        for start in range(0, block, PIECE):
            here = slice(row * block + start, row * block + start + PIECE)
            center, scale = moments(hidden_ref[row, start : start + PIECE].astype(F32))
            grad, terms = norm_back(center, scale, gain, normed_grad[here])
            gain_grad = gain_grad + jnp.sum(terms, axis=0, keepdims=True)
            result_ref[row, start : start + PIECE] = grad_middle_ref[here] + grad
    gain_grad_ref[...] = gain_grad
    save = pltpu.make_async_copy(result_ref, result_hbm, sems.at[5])
    save.start()
    save.wait()


def run_last(
    lengths, signal, size, halo, extended, outer, outer_halo, hidden, gain, taps, grad_middle,
    weight, after,
):
    rows, block, width = hidden.shape
    tokens = rows * block
    chunk = width // 2
    middle = 3 * width // 2
    return launch(
        partial(last_kernel, size),
        (
            lengths, signal, halo, outer_halo, gain, taps, extended, outer, hidden, grad_middle,
            weight,
        ),
        [
            ((tokens, middle), BF16),
            ((tokens, middle), BF16),
            ((8, 3 * width), F32),
            ((1, width), F32),
            (hidden.shape, F32),
        ],
        in_specs=smem(1) + vmem(5) + hbm(5),
        out_specs=vmem(4) + hbm(1),
        scratch=[
            pltpu.VMEM(extended.shape, BF16),
            pltpu.VMEM(outer.shape, F32),
            pltpu.VMEM(hidden.shape, BF16),
            pltpu.VMEM(grad_middle.shape, F32),
            pltpu.VMEM(weight.shape, BF16),
            pltpu.VMEM(hidden.shape, F32),
            pltpu.VMEM((3, block + 16, chunk), F32),
            pltpu.VMEM((2, block + 8, chunk), F32),
            pltpu.VMEM((3, block + 8, chunk), F32),
            pltpu.VMEM((tokens, 3 * width), BF16),
            pltpu.VMEM((tokens, width), F32),
            pltpu.SemaphoreType.DMA((6,)),
        ],
        limit=FULL_BYTES,
        after=after,
    )


def to_owner(sent, mine, padded):
    count = lax.axis_size("seq")
    groups, rows, size, block = sent.shape
    if groups != count:
        sent = sent.reshape(rows, count, mine, block).transpose(1, 0, 2, 3)
    got = lax.all_to_all(sent, "seq", 0, 0, tiled=True).reshape(count * rows, mine, block)
    if padded != mine:
        got = jnp.pad(got, ((0, 0), (0, padded - mine), (0, 0)))
    return got


def to_block(value, rows, mine, groups):
    count = lax.axis_size("seq")
    size, block = value.shape[1:]
    got = lax.all_to_all(
        value.reshape(count, rows, size, block), "seq", 0, 0, tiled=True
    )
    if groups == count:
        return got
    return got[:, :, :mine].transpose(1, 0, 2, 3).reshape(1, rows, count * mine, block), got


def dot_tn(left, right):
    return lax.dot_general(left, right, (((0,), (0,)), ((), ())), preferred_element_type=F32)


def bit_inside(bit):
    count = lax.axis_size("seq")
    if bit < count:
        return lax.axis_index("seq") // bit % 2
    return lax.axis_index("dp") // (bit // count) % 2


def side(bit, sent):
    mine = bit_inside(bit)
    return 1 - mine if sent else mine


def up_products_kernel(
    bits, sent, mine_hbm, got_hbm, a_ref, b_ref, left_ref, right_ref, sems
):
    _, rows, width = a_ref.shape
    units = 2 * width
    moves = []
    for part in range(2):
        at = pl.multiple_of(2 * units + side(bits[part], sent) * rows, 128)
        cols = slice(units + part * width, units + (part + 1) * width)
        for i, factors in enumerate((mine_hbm, got_hbm)):
            moves.append((factors.at[:, pl.ds(at, rows)], left_ref.at[part, i]))
            moves.append((factors.at[:, cols], right_ref.at[part, i]))
    loads = start_loads(moves, sems)
    for part, out in enumerate((a_ref, b_ref)):
        for load in loads[4 * part : 4 * part + 4]:
            load.wait()
        found = dot_tn(left_ref[part, 0], right_ref[part, 0]) + dot_tn(
            left_ref[part, 1], right_ref[part, 1]
        )
        out[0] = found.astype(BF16)


def down_products_kernel(
    bits, sent, mine_hbm, got_hbm, upstream_hbm, upstream_got_hbm, a_ref, b_ref,
    left_ref, right_ref, sems,
):
    _, rows, width = a_ref.shape
    moves = [(upstream_hbm, right_ref.at[0]), (upstream_got_hbm, right_ref.at[1])]
    for part in range(2):
        at = pl.multiple_of(part * width + side(bits[part], sent) * rows, 128)
        for i, factors in enumerate((mine_hbm, got_hbm)):
            moves.append((factors.at[:, pl.ds(at, rows)], left_ref.at[part, i]))
    loads = start_loads(moves, sems)
    loads[0].wait()
    loads[1].wait()
    for part, out in enumerate((a_ref, b_ref)):
        loads[2 * part + 2].wait()
        loads[2 * part + 3].wait()
        found = dot_tn(left_ref[part, 0], right_ref[0]) + dot_tn(left_ref[part, 1], right_ref[1])
        out[0] = found.astype(BF16)


def last_products_kernel(
    bits, sent, normed_ref, normed_got_ref, proj_ref, proj_got_ref, last_ref, last_got_ref,
    a_ref, b_ref,
):
    rows, width = a_ref.shape[1:]
    half = width // 2
    at = pl.multiple_of(side(bits[0], sent) * rows, 128)
    found = dot_tn(normed_ref[:, pl.ds(at, rows)], proj_ref[:, :width]) + dot_tn(
        normed_got_ref[:, pl.ds(at, rows)], proj_got_ref[:, :width]
    )
    a_ref[0] = found.astype(BF16)
    at = pl.multiple_of(side(bits[1], sent) * rows, 128)
    found = dot_tn(normed_ref[:, pl.ds(at, rows)], proj_ref[:, width:]) + dot_tn(
        normed_got_ref[:, pl.ds(at, rows)], proj_got_ref[:, width:]
    )
    b_ref[0, :, :half] = found.astype(BF16)
    found = dot_tn(last_ref[:, pl.ds(at, rows)], last_ref[:, width:]) + dot_tn(
        last_got_ref[:, pl.ds(at, rows)], last_got_ref[:, width:]
    )
    b_ref[0, :, half:] = found.astype(BF16)


def run_up_products(bits, sent, operands, shape, after=()):
    tokens, (_, rows, width) = operands[0].shape[0], shape
    return launch(
        partial(up_products_kernel, bits, sent),
        operands,
        [(shape, BF16)] * 2,
        in_specs=anywhere(2),
        scratch=[
            pltpu.VMEM((2, 2, tokens, rows), BF16),
            pltpu.VMEM((2, 2, tokens, width), BF16),
            pltpu.SemaphoreType.DMA((8,)),
        ],
        limit=FULL_BYTES,
        after=after,
    )


def run_down_products(bits, sent, operands, shape, after=()):
    tokens, (_, rows, width) = operands[0].shape[0], shape
    return launch(
        partial(down_products_kernel, bits, sent),
        operands,
        [(shape, BF16)] * 2,
        in_specs=anywhere(4),
        scratch=[
            pltpu.VMEM((2, 2, tokens, rows), BF16),
            pltpu.VMEM((2, tokens, width), BF16),
            pltpu.SemaphoreType.DMA((6,)),
        ],
        limit=FULL_BYTES,
        after=after,
    )


def run_last_products(bits, sent, operands, shape, after=()):
    return launch(
        partial(last_products_kernel, bits, sent),
        operands,
        [(shape, BF16)] * 2,
        after=after,
    )


STEP = 96


def steps(rows):
    step = STEP if rows % STEP == 0 else rows
    return [(start, step) for start in range(0, rows, step)]


def halve_kernel(
    bits, kept_a, got_a, kept_b, got_b, sent_a, next_a, sent_b, next_b,
    kept_a_ref, got_a_ref, kept_b_ref, got_b_ref, sems,
):
    moves, work = [], []
    for sent, outs in ((True, (sent_a, sent_b)), (False, (next_a, next_b))):
        for bit, out, kept, got, kept_ref, got_ref in (
            (bits[0], outs[0], kept_a, got_a, kept_a_ref, got_a_ref),
            (bits[1], outs[1], kept_b, got_b, kept_b_ref, got_b_ref),
        ):
            rows = out.shape[1]
            at = pl.ds(pl.multiple_of(side(bit, sent) * rows, 16), rows)
            slot = slice(0, rows) if sent else slice(rows, 2 * rows)
            moves.append((kept.at[:, at], kept_ref.at[:, slot]))
            moves.append((got.at[:, at], got_ref.at[:, slot]))
            work.append((out, kept_ref, got_ref, 0 if sent else rows))
    loads = start_loads(moves, sems)
    for i, (out, kept_ref, got_ref, first) in enumerate(work):
        loads[2 * i].wait()
        loads[2 * i + 1].wait()
        for block in range(out.shape[0]):
            for start, step in steps(out.shape[1]):
                at = slice(first + start, first + start + step)
                total = kept_ref[block, at].astype(F32) + got_ref[block, at].astype(F32)
                out[block, start : start + step] = total.astype(BF16)


def run_halve(bits, parts, after=()):
    def half(array):
        return (array.shape[0], array.shape[1] // 2, array.shape[2]), BF16

    return launch(
        partial(halve_kernel, bits),
        parts,
        [half(parts[0]), half(parts[0]), half(parts[2]), half(parts[2])],
        in_specs=anywhere(4),
        scratch=[
            *[pltpu.VMEM(part.shape, BF16) for part in parts],
            pltpu.SemaphoreType.DMA((8,)),
        ],
        limit=FULL_BYTES,
        after=after,
    )


SHARED, OWNED = 32, 16
GROUPS = 6
EXTRA = 16


def line_spot():
    return lax.axis_index("seq") // 2


def pieces_of(a_ref, b_ref, count):
    at = 0
    for ref in (a_ref, b_ref):
        blocks, rows, _ = ref.shape
        size = rows // count
        for block in range(blocks):
            yield ref, block, size, at
            at += size


def scatter_kernel(with_small, *refs):
    kept_a, got_a, kept_b, got_b = refs[:4]
    outs = refs[5:] if with_small else refs[4:]
    spot = line_spot()
    for away, out in enumerate(outs):
        for (kept, block, size, at), (got, _, _, _) in zip(
            pieces_of(kept_a, kept_b, len(outs)), pieces_of(got_a, got_b, len(outs))
        ):
            rows = pl.ds(pl.multiple_of((spot ^ away) * size, 16), size)
            total = kept[block, rows].astype(F32) + got[block, rows].astype(F32)
            out[at : at + size] = total.astype(BF16)
        if with_small:
            at = out.shape[0] - EXTRA
            size = SHARED // len(outs)
            part = refs[4][pl.ds(pl.multiple_of((spot ^ away) * size, 8), size)]
            part = jnp.concatenate([part, jnp.zeros((EXTRA - size, part.shape[1]), F32)], axis=0)
            out[at:] = part.astype(BF16)


def run_scatter(parts, count, small=None, after=(), estimate=SHORT):
    share = sum(part.shape[0] * part.shape[1] for part in (parts[0], parts[2])) // count
    share += 0 if small is None else EXTRA
    return launch(
        partial(scatter_kernel, small is not None),
        parts if small is None else (*parts, small),
        [((share, parts[0].shape[2]), BF16)] * count,
        after=after,
        estimate=estimate,
    )


def total_kernel(with_small, *refs):
    *parts, out = refs
    if with_small:
        *parts, small = parts
    rows_in = parts[0].shape[0]
    for start, step in steps(rows_in):
        rows = slice(start, start + step)
        total = parts[0][rows].astype(F32)
        for part in parts[1:]:
            total = total + part[rows].astype(F32)
        out[rows] = total.astype(out.dtype)
    if with_small:
        out[rows_in:] = small[SHARED:].astype(out.dtype)


def run_total(parts, small=None, after=(), estimate=SHORT):
    rows, width = parts[0].shape
    return launch(
        partial(total_kernel, small is not None),
        parts if small is None else (*parts, small),
        [((rows if small is None else rows + OWNED, width), parts[0].dtype)],
        after=after,
        estimate=estimate,
    )


def gather_kernel(count, with_small, *refs):
    shares, outs = refs[:count], refs[count:]
    spot = line_spot()
    for away, share in enumerate(shares):
        for out, block, size, at in pieces_of(outs[0], outs[1], count):
            rows = pl.ds(pl.multiple_of((spot ^ away) * size, 16), size)
            out[block, rows] = share[at : at + size]
        if with_small:
            at = share.shape[0] - EXTRA - OWNED
            size = SHARED // count
            shared = share[at : at + EXTRA].astype(F32)[:size]
            outs[2][pl.ds(pl.multiple_of((spot ^ away) * size, 8), size)] = shared
            rows = pl.ds(pl.multiple_of(SHARED + (spot ^ away) * OWNED, 8), OWNED)
            outs[2][rows] = share[at + EXTRA :].astype(F32)


def run_gather(shares, shapes, with_small, after=(), estimate=SHORT):
    count = len(shares)
    outs = [(shape, BF16) for shape in shapes]
    if with_small:
        outs.append(((SHARED + count * OWNED, shares[0].shape[1]), F32))
    return launch(
        partial(gather_kernel, count, with_small), shares, outs, after=after, estimate=estimate
    )


def join_kernel(bits, mine_a, got_a, mine_b, got_b, out_a, out_b):
    for bit, mine, got, out in (
        (bits[0], mine_a, got_a, out_a),
        (bits[1], mine_b, got_b, out_b),
    ):
        blocks, rows, _ = mine.shape
        for source, which in ((mine, side(bit, False)), (got, side(bit, True))):
            at = pl.ds(pl.multiple_of(which * rows, 16), rows)
            for block in range(blocks):
                out[block, at] = source[block]


def run_join(bits, parts, after=()):
    def twice(array):
        return (array.shape[0], array.shape[1] * 2, array.shape[2]), BF16

    return launch(
        partial(join_kernel, bits), parts, [twice(parts[0]), twice(parts[2])], after=after
    )


PLACE = 192
SLOTS = 4


def place_all(moves, narrow, wide, sems):
    loads, stores = [], []

    def load(i):
        source, _ = moves[i]
        rows, cols = source.shape
        copy = pltpu.make_async_copy(
            source, narrow.at[i % SLOTS, :rows, :cols], sems.at[i % SLOTS]
        )
        copy.start()
        loads.append(copy)

    for i in range(min(SLOTS, len(moves))):
        load(i)
    for i, (source, target) in enumerate(moves):
        rows, cols = source.shape
        slot = i % SLOTS
        loads[i].wait()
        if i >= SLOTS:
            stores[i - SLOTS].wait()
        wide[slot, :rows, :cols] = narrow[slot, :rows, :cols].astype(F32)
        copy = pltpu.make_async_copy(wide.at[slot, :rows, :cols], target, sems.at[SLOTS + slot])
        copy.start()
        stores.append(copy)
        if i + SLOTS < len(moves):
            load(i + SLOTS)
    for copy in stores[-SLOTS:]:
        copy.wait()


def up_place_kernel(bits, sides, *refs):
    out_hbm, narrow, wide, sems = refs[-4:]
    core = lax.axis_index("seq") % 2
    moves = []
    for i, (sent, owner) in enumerate((s, o) for s in sides for o in (core, 1 - core)):
        for part, source in enumerate(refs[2 * i : 2 * i + 2]):
            _, rows, width = source.shape
            for start in range(0, rows, PLACE):
                row = pl.multiple_of(side(bits[part], sent) * rows + start, 16)
                col = pl.multiple_of((2 * owner + part) * width, 128)
                moves.append(
                    (
                        source.at[0, start : start + PLACE],
                        out_hbm.at[pl.ds(row, PLACE), pl.ds(col, width)],
                    )
                )
    place_all(moves, narrow, wide, sems)


def down_place_kernel(bits, sides, *refs):
    out_hbm, narrow, wide, sems = refs[-4:]
    core = lax.axis_index("seq") % 2
    moves = []
    for i, (sent, owner) in enumerate((s, o) for s in sides for o in (core, 1 - core)):
        for part, source in enumerate(refs[2 * i : 2 * i + 2]):
            rows = source.shape[1]
            for start in range(0, rows, PLACE):
                half = 2 * (2 * owner + part) + side(bits[part], sent)
                row = pl.multiple_of(half * rows + start, 16)
                moves.append(
                    (source.at[0, start : start + PLACE], out_hbm.at[pl.ds(row, PLACE)])
                )
    place_all(moves, narrow, wide, sems)


def last_place_kernel(bits, sides, *refs):
    in_hbm, out_hbm, narrow, wide, sems = refs[-5:]
    core = lax.axis_index("seq") % 2
    moves = []
    for i, (sent, owner) in enumerate((s, o) for s in sides for o in (core, 1 - core)):
        source_a, source_b = refs[2 * i : 2 * i + 2]
        _, rows, width = source_a.shape
        half = width // 2
        for start in range(0, rows, PLACE):
            row = pl.multiple_of(side(bits[0], sent) * rows + start, 16)
            col = pl.multiple_of(owner * 3 * half, 128)
            moves.append(
                (
                    source_a.at[0, start : start + PLACE],
                    in_hbm.at[pl.ds(row, PLACE), pl.ds(col, width)],
                )
            )
            row = pl.multiple_of(side(bits[1], sent) * rows + start, 16)
            col = pl.multiple_of(owner * 3 * half + width, 128)
            moves.append(
                (
                    source_b.at[0, start : start + PLACE, :half],
                    in_hbm.at[pl.ds(row, PLACE), pl.ds(col, half)],
                )
            )
            col = pl.multiple_of(owner * half, 128)
            moves.append(
                (
                    source_b.at[0, start : start + PLACE, half:],
                    out_hbm.at[pl.ds(row, PLACE), pl.ds(col, half)],
                )
            )
    place_all(moves, narrow, wide, sems)


def run_place(kernel, bits, sides, sources, outs, shapes, after=()):
    width = sources[0].shape[2]
    return launch(
        partial(kernel, bits, sides),
        (*sources, *outs),
        [(shape, F32) for shape in shapes],
        in_specs=anywhere(len(sources)) + hbm(len(outs)),
        out_specs=hbm(len(shapes)),
        scratch=[
            pltpu.VMEM((SLOTS, PLACE, width), BF16),
            pltpu.VMEM((SLOTS, PLACE, width), F32),
            pltpu.SemaphoreType.DMA((2 * SLOTS,)),
        ],
        limit=PLACE_BYTES,
        after=after,
        aliases={len(sources) + i: i for i in range(len(outs))},
    )


def pack_kernel(
    third_ref, skip_ref, taps_ref, gain_one, gain_two, second_ref, first_ref, out_ref,
    owned_ref, hidden_ref,
):
    hidden, mine = third_ref.shape
    out_ref[...] = jnp.zeros(out_ref.shape, F32)
    width = out_ref.shape[1]
    for tap in range(KS):
        for part in range(3):
            row = 3 * tap + part
            out_ref[row : row + 1] = taps_ref[tap : tap + 1, part * width : (part + 1) * width]
    row = 3 * KS
    out_ref[row : row + 1] = gain_one[...]
    out_ref[row + 1 : row + 2] = gain_two[...]
    row += 2
    owned_ref[...] = jnp.zeros(owned_ref.shape, F32)
    owned_ref[:hidden, :mine] = third_ref[...]
    owned_ref[hidden : hidden + 1, :mine] = skip_ref[...]
    hidden_ref[...] = jnp.zeros(hidden_ref.shape, F32)
    hidden_ref[:hidden, :hidden] = second_ref[...]
    hidden_ref[hidden : hidden + first_ref.shape[0], :hidden] = first_ref[...]
    each, size = hidden_ref.shape[0] // GROUPS, owned_ref.shape[0] // GROUPS
    for group in range(GROUPS):
        lanes = slice(128 * group, 128 * (group + 1))
        out_ref[row : row + each, lanes] = hidden_ref[group * each : (group + 1) * each]
        out_ref[SHARED : SHARED + size, lanes] = owned_ref[group * size : (group + 1) * size]


def small_rows(hidden, embedded):
    return -(-(hidden + 1) // GROUPS) * GROUPS, -(-(hidden + embedded) // GROUPS) * GROUPS


def run_pack(third, skip, taps, gain_one, gain_two, second, first):
    owned, hidden = small_rows(second.shape[0], first.shape[0])
    return launch(
        pack_kernel,
        (third, skip, taps, gain_one, gain_two, second, first),
        [((SHARED + OWNED, gain_one.shape[1]), F32)],
        scratch=[pltpu.VMEM((owned, 128), F32), pltpu.VMEM((hidden, 128), F32)],
    )


def unpack_kernel(
    count, mine, mine_ref, got_ref, third_ref, skip_ref, taps_ref, gain_one, gain_two, second_ref,
    first_ref, owner_ref, sum_ref, owned_ref, hidden_ref,
):
    hidden, width = third_ref.shape
    core = lax.axis_index("seq") % 2
    for spot in range(count):
        here = slice(SHARED + spot * OWNED, SHARED + (spot + 1) * OWNED)
        owner_ref[2 * spot + core] = mine_ref[here]
        owner_ref[2 * spot + 1 - core] = got_ref[here]
    sum_ref[...] = mine_ref[:SHARED] + got_ref[:SHARED]
    each, size = hidden_ref.shape[0] // GROUPS, owned_ref.shape[0] // GROUPS
    rows = owned_ref.shape[0]
    lane = lax.broadcasted_iota(jnp.int32, (rows, 128), 1)
    wide = [jnp.zeros((rows, 128), F32) for _ in range(width // 128)]
    for owner in range(2 * count):
        for group in range(GROUPS):
            lanes = slice(128 * group, 128 * (group + 1))
            owned_ref[group * size : (group + 1) * size] = owner_ref[owner, :size, lanes]
        at, shift = divmod(owner * mine, 128)
        moved = owned_ref[...]
        if shift:
            moved = pltpu.roll(moved, shift, 1)
        wide[at] = wide[at] + jnp.where(lane >= shift, moved, 0.0)
        if shift + mine > 128:
            wide[at + 1] = wide[at + 1] + jnp.where(lane < shift, moved, 0.0)
    for at, value in enumerate(wide):
        cols = slice(at * 128, (at + 1) * 128)
        third_ref[:, cols] = value[:hidden]
        skip_ref[:, cols] = value[hidden : hidden + 1]
    for tap in range(KS):
        for part in range(3):
            row = 3 * tap + part
            taps_ref[tap : tap + 1, part * width : (part + 1) * width] = sum_ref[row : row + 1]
    row = 3 * KS
    gain_one[...] = sum_ref[row : row + 1]
    gain_two[...] = sum_ref[row + 1 : row + 2]
    row += 2
    for group in range(GROUPS):
        lanes = slice(128 * group, 128 * (group + 1))
        hidden_ref[group * each : (group + 1) * each] = sum_ref[row : row + each, lanes]
    second_ref[...] = hidden_ref[:hidden, :hidden]
    first_ref[...] = hidden_ref[hidden : hidden + first_ref.shape[0], :hidden]


def run_unpack(count, mine, packed, got, hidden, embedded, after):
    width = packed.shape[1]
    owned, both = small_rows(hidden, embedded)
    shapes = (
        (hidden, width), (1, width), (KS, 3 * width), (1, width), (1, width), (hidden, hidden),
        (embedded, hidden),
    )
    return launch(
        partial(unpack_kernel, count, mine),
        (packed, got),
        [(shape, F32) for shape in shapes],
        scratch=[
            pltpu.VMEM((2 * count, OWNED, width), F32),
            pltpu.VMEM((SHARED, width), F32),
            pltpu.VMEM((owned, 128), F32),
            pltpu.VMEM((both, 128), F32),
        ],
        after=after,
    )


def hold(values, after):
    return launch(
        lambda *refs: None,
        values,
        [(value.shape, value.dtype) for value in values],
        in_specs=anywhere(len(values)),
        out_specs=anywhere(len(values)),
        limit=FULL_BYTES,
        after=after,
        aliases={i: i for i in range(len(values))},
    )[0]


class Group:
    def __init__(self, orders, line_bits, sent):
        self.orders, self.line_bits = orders, line_bits
        self.sent = sent
        self.got = self.swap(sent, 0)
        self.aways = [0]
        for bit in line_bits:
            self.aways += [away | bit for away in self.aways]
        self.direct = len(self.aways) == 4

    def bits(self, level):
        return self.orders[0][level], self.orders[1][level]

    def swap(self, pair, level):
        return tuple(swap(value, bit) for value, bit in zip(pair, self.bits(level)))

    def woven(self):
        return self.kept[0], self.got[0], self.kept[1], self.got[1]

    def halve(self, kept, after=()):
        self.kept = kept
        (sent_a, next_a, sent_b, next_b), self.token = run_halve(
            self.bits(1), self.woven(), after
        )
        self.kept, self.sent = (next_a, next_b), (sent_a, sent_b)
        self.got = self.swap(self.sent, 1)

    def scatter(self, small=None, after=(), estimate=SHORT):
        self.shapes = [part.shape for part in self.kept]
        self.small = small
        if self.direct:
            self.shares, self.token = run_scatter(
                self.woven(), len(self.aways), small, after, estimate
            )
            self.arrived = [
                swap(share, away) for share, away in zip(self.shares[1:], self.aways[1:])
            ]
        else:
            self.shares = tuple(
                halve(add(kept, got), lax.axis_index(AXES), self.line_bits[::-1], 1)
                for kept, got in zip(self.kept, self.got)
            )

    def total(self, after=(), estimate=LINE):
        if self.direct:
            (self.share,), self.token = run_total(
                (self.shares[0], *self.arrived), self.small, after, estimate
            )
            self.arrived = [swap(self.share, away) for away in self.aways[1:]]

    def gather(self, after=()):
        if self.direct:
            made, self.token = run_gather(
                (self.share, *self.arrived), self.shapes, self.small is not None, after, LINE
            )
            self.mine = made[:2]
            if self.small is not None:
                self.small = made[2]
        else:
            self.mine = tuple(
                double(share, lax.axis_index(AXES), self.line_bits[::-1], 1)
                for share in self.shares
            )
        self.got = self.swap(self.mine, 1)

    def join(self, after=()):
        self.mine, self.token = run_join(
            self.bits(1), (self.mine[0], self.got[0], self.mine[1], self.got[1]), after
        )
        self.got = self.swap(self.mine, 0)
        self.mine_core = tuple(swap(value, 1) for value in self.mine)
        self.outs = ()

    def place(self, kernel, shapes, after=()):
        self.outs, self.token = run_place(
            kernel, self.bits(0), (False,), (*self.mine, *self.mine_core), (), shapes, after
        )

    def finish(self, kernel, shapes, after=(), held=()):
        if held:
            self.got = hold(self.got, held)
        got_core = tuple(swap(value, 1) for value in self.got)
        sides, sources = (True,), (*self.got, *got_core)
        if not self.outs:
            sides, sources = (False, True), (*self.mine, *self.mine_core, *sources)
        outs, self.token = run_place(
            kernel, self.bits(0), sides, sources, self.outs, shapes, after
        )
        return outs


def per_device(
    hidden_in, lengths, gain_one, in_weight, short_kernel, skip_gain, decay_rate, filt_first,
    filt_second, filt_third, out_weight, gain_two, ff_up, ff_down, out_grad,
):
    rows, block, width = hidden_in.shape
    seq_count, seq_pos = lax.axis_size("seq"), lax.axis_index("seq")
    dp_count = lax.axis_size("dp")
    index = lax.axis_index(AXES)
    units = ff_up.shape[1]
    row_len = block * seq_count
    tokens = rows * block
    seq_bits = [1 << i for i in range(1, seq_count.bit_length() - 1)]
    dp_bits = [seq_count << i for i in range(dp_count.bit_length() - 1)]
    mine = width // seq_count
    padded = -(-mine // 16) * 16
    groups = seq_count if mine == padded and (width // 2) % mine == 0 else 1

    forward, inverse = spectral_tables(block)
    forward_two, inverse_three = jnp.asarray(two_pass(forward)), jnp.asarray(three_pass(inverse))
    forward_three, inverse_two = jnp.asarray(three_pass(forward.T)), jnp.asarray(two_pass(inverse.T))

    before = shifted(hidden_in[:, block - 2 :], 1)
    after = shifted(hidden_in[:, :2], -1)
    normed_one, extended, outer, signal_sent = run_front(
        lengths, hidden_in, before, after, gain_one[None], short_kernel, in_weight, groups
    )
    signal_ch = to_owner(signal_sent, mine, padded)

    signal_sent, filt_first, decay_rate, skip_gain = lax.optimization_barrier(
        (signal_sent, filt_first, decay_rate, skip_gain)
    )
    bands = (filt_first.shape[0] - 1) // 2
    spots = np.arange(row_len)
    turns = (np.arange(1, bands + 1)[:, None] * spots[None, :] % row_len) * (2.0 * math.pi / row_len)
    embedding = jnp.asarray(
        np.concatenate([spots[None, :] / row_len, np.cos(turns), np.sin(turns)], axis=0).astype(
            np.float32
        )
    )
    pre_one = jnp.einsum("ef,el->fl", filt_first, embedding, precision=FULL_PRECISION)
    act_one = jnp.sin(pre_one)
    pre_two = jnp.einsum("fg,fl->gl", filt_second, act_one, precision=FULL_PRECISION)
    act_two = jnp.sin(pre_two)
    my_third = lax.dynamic_slice_in_dim(filt_third, seq_pos * mine, mine, 1)
    my_decay = lax.dynamic_slice_in_dim(decay_rate, seq_pos * mine, mine, 0)
    my_skip = lax.dynamic_slice_in_dim(skip_gain, seq_pos * mine, mine, 0)
    my_skip = jnp.pad(my_skip, (0, padded - mine))[:, None]
    places = jnp.asarray(spots.astype(np.float32))
    envelope = jnp.exp(-my_decay[:, None] * places[None, :]) * row_len ** (-0.5)
    taps = jnp.einsum("gc,gl->cl", my_third, act_two, precision=FULL_PRECISION) * envelope
    taps = taps.reshape(mine, seq_count, block).transpose(1, 0, 2)
    if padded != mine:
        taps = jnp.pad(taps, ((0, 0), (0, padded - mine), (0, 0)))
    pieces = jnp.einsum("kct,tf->kcf", taps, jnp.asarray(forward), precision=FULL_PRECISION)
    sign = jnp.asarray(np.tile(1.0 - 2.0 * (np.arange(block) % 2), 2).astype(np.float32))
    earlier = jnp.concatenate([jnp.zeros_like(pieces[:1]), pieces[:-1]], axis=0)
    spectrum = earlier + sign * pieces
    spec_real, spec_imag = spectrum[..., :block], spectrum[..., block:]
    base = jnp.arange(block) == 0
    spectrum = (
        spec_real,
        jnp.where(base, 0.0, spec_imag),
        jnp.where(base, spec_imag, spec_real),
    )

    conv_ch, _ = run_conv(
        lengths, row_len, signal_ch, my_skip, spectrum, forward_two, inverse_three
    )
    conv = to_block(conv_ch, rows, mine, groups)
    if groups == 1:
        conv = conv[0]

    upstream = out_grad.reshape(tokens, width)
    upstream_got = swap(upstream, 1)
    (
        gain_two_grad, factors_mine, factors_theirs, block_out, last_mine, last_theirs, grad_middle,
        grad_outer, grad_sent,
    ) = run_middle(
        conv, mine, outer, hidden_in, gain_two[None], upstream, out_weight, ff_up, ff_down, groups
    )
    factors_got = swap(factors_theirs, 1)
    grad_ch = to_owner(grad_sent, mine, padded)
    orders = (dp_bits, dp_bits[::-1])
    firsts = (orders[0][0], orders[1][0])
    shape = (1, width // 2, width)
    up_operands = (factors_mine, factors_got)
    down_operands = (factors_mine, factors_got, upstream, upstream_got)
    up_sent, token = run_up_products(firsts, True, up_operands, shape)
    up = Group(orders, seq_bits, up_sent)
    down_sent, token = run_down_products(firsts, True, down_operands, shape, (token,))
    down = Group(orders, seq_bits, down_sent)
    outer_halo = shifted(grad_outer[:, :2], -1)

    back_ch, token = run_conv(
        lengths, row_len, grad_ch, my_skip, spectrum, forward_three, inverse_two, backward=True,
        after=(token,),
    )
    got = to_block(back_ch, rows, mine, groups)
    grad_signal, got = (got, got) if groups > 1 else got
    halo = got[:, 0, padded : padded + 2 * rows, :mine].astype(F32)
    halo = halo.transpose(1, 0, 2).reshape(rows, 2, width)
    last_got, normed_got = swap(last_theirs, 1), swap(normed_one, 1)
    up_kept, token = run_up_products(firsts, False, up_operands, shape, (token,))
    up.halve(up_kept)
    down_kept, token = run_down_products(firsts, False, down_operands, shape, (up.token,))
    down.halve(down_kept)
    up.scatter(None, (down.token,), BRIDGE_A)

    (proj_mine, proj_theirs, kernel_grad, gain_one_grad, input_grad), token = run_last(
        lengths, grad_signal, mine, halo, extended, grad_outer, outer_halo, hidden_in,
        gain_one[None], short_kernel, grad_middle, in_weight, (up.token,) if up.direct else (),
    )
    last_operands = (normed_one, normed_got, proj_mine, swap(proj_theirs, 1), last_mine, last_got)
    down.scatter(None, (token,))
    up.total((down.token,) if up.direct else (), BRIDGE_B)
    last_sent, token = run_last_products(firsts, True, last_operands, shape, (up.token,))
    last = Group(orders, seq_bits, last_sent)
    last_kept, token = run_last_products(firsts, False, last_operands, shape, (token,))

    grad_taps, token = run_filter_grad(
        lengths, row_len, signal_ch, grad_ch, forward_two, inverse_two, forward_three,
        after=(token,),
    )
    last.halve(last_kept, (token,))
    (grad_taps,) = hold((grad_taps,), (last.token,))
    grad_taps = grad_taps[:, :mine].transpose(1, 0, 2).reshape(mine, row_len)
    skip_grad = grad_taps[:, 0]
    grad_taps = grad_taps * envelope
    my_third_grad = jnp.einsum("gl,cl->gc", act_two, grad_taps, precision=FULL_PRECISION)
    grad_two = jnp.cos(pre_two) * jnp.einsum(
        "gc,cl->gl", my_third, grad_taps, precision=FULL_PRECISION
    )
    second_grad = jnp.einsum("fl,gl->fg", act_one, grad_two, precision=FULL_PRECISION)
    grad_one = jnp.cos(pre_one) * jnp.einsum(
        "fg,gl->fl", filt_second, grad_two, precision=FULL_PRECISION
    )
    first_grad = jnp.einsum("el,fl->ef", embedding, grad_one, precision=FULL_PRECISION)

    small = (
        my_third_grad, skip_grad[None], kernel_grad, gain_one_grad, gain_two_grad, second_grad,
        first_grad,
    )

    in_shapes = (in_weight.shape, out_weight.shape)
    if up.direct:
        (packed,), token = run_pack(*small)
        bits = orders[0]
        arrived = [swap(packed, bit) for bit in (bits[0], bits[1], bits[0] | bits[1])]
        down.total((token,))
        (packed,), token = run_total((packed, *arrived), None, (down.token,))
        last.scatter(packed, (token,))
        up.gather((last.token,))
        down.gather((up.token,))
        up.join((down.token,))
        last.total((up.token,))
        down.join((last.token,))
        up.place(up_place_kernel, (ff_up.shape,), (down.token,))
        down.place(down_place_kernel, (ff_down.shape,), (up.token,))
        last.gather((down.token,))
        (up_total,) = up.finish(up_place_kernel, (ff_up.shape,), (last.token,))
        last.join((up.token,))
        last.place(last_place_kernel, in_shapes, (last.token,))
        (down_total,) = down.finish(down_place_kernel, (ff_down.shape,), (last.token,))
        small, token = run_unpack(
            len(up.aways), mine, last.small, swap(last.small, 1), filt_third.shape[0],
            filt_first.shape[0], (down.token,),
        )
        in_total, out_total = last.finish(last_place_kernel, in_shapes, (), (token,))
    else:
        last.scatter()
        for group in (up, down, last):
            group.gather()
            group.join()
        (up_total,) = up.finish(up_place_kernel, (ff_up.shape,))
        (down_total,) = down.finish(down_place_kernel, (ff_down.shape,))
        in_total, out_total = last.finish(last_place_kernel, in_shapes)
        spread = [
            lax.dynamic_update_slice_in_dim(
                jnp.zeros((part.shape[0], width), F32), part, seq_pos * mine, 1
            )
            for part in small[:2]
        ]
        small = lax.psum((*spread, small[2][:KS], *small[3:]), AXES)
    return (
        block_out, input_grad, small[3][0], in_total, small[2], small[1][0], small[6], small[5],
        small[0], out_total, small[4][0], up_total, down_total,
    )


def solution(mesh):
    tokens = P("dp", "seq", None)
    return jax.shard_map(
        per_device,
        mesh=mesh,
        in_specs=(tokens, P("dp", None)) + (P(),) * 12 + (tokens,),
        out_specs=(tokens, tokens) + (P(),) * 11,
        check_vma=False,
    )
```

```python
from functools import partial
import math

import jax
import jax.numpy as jnp
import numpy as np
from jax import lax
from jax.experimental import pallas as pl
from jax.experimental.pallas import tpu as pltpu
from jax.sharding import PartitionSpec as P

FULL_PRECISION = lax.Precision.HIGHEST
BF16 = jnp.bfloat16
F32 = jnp.float32
AXES = ("dp", "seq")
VMEM_BYTES = 32 * 1024 * 1024
FULL_BYTES = 54 * 1024 * 1024
PLACE_BYTES = 57 * 1024 * 1024
WHOLE_BYTES = 55 * 1024 * 1024
KS = 3


def swap(value, bit):
    count = lax.axis_size(AXES)
    return lax.ppermute(value, AXES, [(i, i ^ bit) for i in range(count)])


def shifted(value, steps):
    count = lax.axis_size("seq")
    first, last = max(0, -steps), min(count, count - steps)
    return lax.ppermute(value, "seq", [(i, i + steps) for i in range(first, last)])


def my_bit(index, bit):
    return (index // bit) % 2


def add(kept, got):
    return (kept.astype(F32) + got.astype(F32)).astype(kept.dtype)


def halve(value, index, bits, axis):
    for bit in bits:
        size = value.shape[axis] // 2
        mine = my_bit(index, bit)
        keep = lax.dynamic_slice_in_dim(value, mine * size, size, axis)
        send = lax.dynamic_slice_in_dim(value, (1 - mine) * size, size, axis)
        value = add(keep, swap(send, bit))
    return value


def double(value, index, bits, axis):
    for bit in reversed(bits):
        other = swap(value, bit)
        low = my_bit(index, bit) == 0
        value = jnp.concatenate(
            [jnp.where(low, value, other), jnp.where(low, other, value)], axis=axis
        )
    return value


def sum_over(value, bits):
    for bit in bits:
        value = value + swap(value, bit)
    return value


def spectral_tables(block):
    points = 2 * block
    spot = np.arange(block)
    freq = np.arange(block)
    angle = (spot[:, None] * freq[None, :] % points) * (2.0 * math.pi / points)
    real, imag = np.cos(angle), -np.sin(angle)
    imag[:, 0] = 1.0 - 2.0 * (spot % 2)
    forward = np.concatenate([real, imag], axis=1)
    late = spot + block
    angle = (freq[:, None] * late[None, :] % points) * (2.0 * math.pi / points)
    weight = np.where(freq == 0, 1.0, 2.0)[:, None] / points
    real, imag = weight * np.cos(angle), -weight * np.sin(angle)
    imag[0, :] = (1.0 - 2.0 * (late % 2)) / points
    inverse = np.concatenate([real, imag], axis=0)
    return forward.astype(np.float32), inverse.astype(np.float32)


def split_table(table):
    high = table.astype(jnp.bfloat16)
    low = (table - high.astype(np.float32)).astype(jnp.bfloat16)
    return np.asarray(high), np.asarray(low)


def two_pass(table):
    high, low = split_table(table)
    return np.concatenate([high, low], axis=0)


def three_pass(table):
    high, low = split_table(table)
    return np.concatenate([high, high, low], axis=0)


def ends_of(lengths_ref, row):
    total, ends = 0, []
    for k in range(lengths_ref.shape[1]):
        total = total + lengths_ref[row, k]
        ends.append(total)
    return ends


def next_end(ends, spot, row_len):
    found = row_len
    for end in reversed(ends):
        found = jnp.where(end > spot, end, found)
    return found


def last_end(ends, spot):
    found = 0
    for end in ends:
        found = jnp.where(end <= spot, end, found)
    return found


def near_mask(ends, spots, step):
    apart = spots < step
    for end in ends:
        apart = apart | ((end <= spots) & (end > spots - step))
    return jnp.where(apart, 0.0, 1.0)


def dot(left, right):
    return jnp.dot(left, right, preferred_element_type=F32)


def dot_nt(left, right):
    return lax.dot_general(left, right, (((1,), (1,)), ((), ())), preferred_element_type=F32)


def head_masks(ends, spot, group, rows, block, row_len):
    lane = lax.broadcasted_iota(jnp.int32, (1, 1, block), 2)
    masks = []
    for g in range(group):
        start = (spot + g) // rows * block
        stop = jnp.where((spot + g) % rows == 0, next_end(ends[0], start, row_len), 0)
        for row in range(1, rows):
            stop = jnp.where(
                (spot + g) % rows == row, next_end(ends[row], start, row_len), stop
            )
        masks.append(jnp.where(lane < stop - start, 1.0, 0.0))
    return jnp.concatenate(masks, axis=0)


def spectra(value_ref, masks, table_ref, head_out, rest_out, group):
    count, channels, block = value_ref.shape

    def step(i, carry):
        spot = pl.ds(i * group, group)
        whole = value_ref[spot].astype(F32)
        first = whole * masks(i * group)
        both = jnp.concatenate([first, whole - first], axis=0).astype(BF16)
        both = both.reshape(2 * group * channels, block)
        found = dot(jnp.concatenate([both, both], axis=1), table_ref[...])
        found = found.reshape(2 * group, channels, 2 * block)
        head_out[spot] = found[:group]
        rest_out[spot] = found[group:]
        return carry

    lax.fori_loop(0, count // group, step, 0)


def back_to_time(head_spec, rest_spec, masks, table_ref, value_ref, skip_ref, group, store):
    count, channels, double_block = head_spec.shape

    def step(i, carry):
        spot = pl.ds(i * group, group)
        both = jnp.concatenate([head_spec[spot], rest_spec[spot]], axis=0)
        both = both.reshape(2 * group * channels, double_block)
        high = both.astype(BF16)
        low = (both - high.astype(F32)).astype(BF16)
        found = dot(jnp.concatenate([high, low, high], axis=1), table_ref[...])
        found = found.reshape(2 * group, channels, double_block // 2)
        rest = found[group:]
        found = rest + masks(i * group) * (found[:group] - rest)
        store(i * group, found + skip_ref[...][None] * value_ref[spot].astype(F32))
        return carry

    lax.fori_loop(0, count // group, step, 0)


def of_row(per_row, row):
    found = per_row[0]
    for k in range(1, len(per_row)):
        found = jnp.where(row == k, per_row[k], found)
    return found


def start_loads(moves, sems):
    loads = [
        pltpu.make_async_copy(source, target, sems.at[i])
        for i, (source, target) in enumerate(moves)
    ]
    for load in loads:
        load.start()
    return loads


def conv_kernel(
    rows, group, row_len, lengths_ref, value_ref, skip_hbm, hr_hbm, hi_hbm, hm_hbm,
    forward_hbm, inverse_hbm, out_ref, skip_ref, hr_ref, hi_ref, hm_ref, forward_ref, inverse_ref,
    sems, head_spec, rest_spec, head_sum, rest_sum,
):
    count, channels, block = value_ref.shape
    loads = start_loads(
        [
            (forward_hbm, forward_ref), (hr_hbm, hr_ref), (hi_hbm, hi_ref), (hm_hbm, hm_ref),
            (inverse_hbm, inverse_ref), (skip_hbm, skip_ref),
        ],
        sems,
    )
    ends = [ends_of(lengths_ref, row) for row in range(rows)]

    def masks(spot):
        return head_masks(ends, spot, group, rows, block, row_len)

    loads[0].wait()
    spectra(value_ref, masks, forward_ref, head_spec, rest_spec, group)
    for load in loads[1:]:
        load.wait()

    def product(real, imag, lag):
        hr, hi, hm = hr_ref[lag], hi_ref[lag], hm_ref[lag]
        return real * hr - imag * hi, real * hi + imag * hm

    def own(j, carry):
        start = j // rows * block
        stop = of_row([next_end(e, start, row_len) for e in ends], j % rows)
        plain = (stop >= start + block).astype(F32)
        head_real, head_imag = product(head_spec[j, :, :block], head_spec[j, :, block:], 0)
        head_sum[j, :, :block] = head_real
        head_sum[j, :, block:] = head_imag
        rest_real, rest_imag = product(rest_spec[j, :, :block], rest_spec[j, :, block:], 0)
        rest_sum[j, :, :block] = rest_real
        rest_sum[j, :, block:] = rest_imag
        rest_spec[j] = rest_spec[j] + plain * head_spec[j]
        return carry

    lax.fori_loop(0, count, own, 0)

    def reach(j, carry):
        spot, row = j // rows, j % rows
        begin = of_row([last_end(e, spot * block) for e in ends], row) // block

        def include(source, sums):
            k = source * rows + row
            real, imag = product(
                rest_spec[k, :, :block], rest_spec[k, :, block:], spot - source
            )
            return sums[0] + real, sums[1] + imag

        start = (head_sum[j, :, :block], head_sum[j, :, block:])
        real, imag = lax.fori_loop(begin, spot, include, start)
        head_sum[j, :, :block] = real
        head_sum[j, :, block:] = imag
        return carry

    lax.fori_loop(rows, count, reach, 0)

    def store(spot, found):
        out_ref[pl.ds(spot, group)] = found.astype(BF16)

    back_to_time(head_sum, rest_sum, masks, inverse_ref, value_ref, skip_ref, group, store)


def conv_back_kernel(
    rows, group, row_len, lengths_ref, value_ref, skip_hbm, hr_hbm, hi_hbm, hm_hbm,
    forward_hbm, inverse_hbm, out_ref, skip_ref, hr_ref, hi_ref, hm_ref, forward_ref, inverse_ref,
    sems, head_spec, rest_spec, head_sum, rest_sum, found_ref,
):
    count, channels, block = value_ref.shape
    loads = start_loads(
        [
            (inverse_hbm, inverse_ref), (hr_hbm, hr_ref), (hi_hbm, hi_ref), (hm_hbm, hm_ref),
            (forward_hbm, forward_ref), (skip_hbm, skip_ref),
        ],
        sems,
    )
    ends = [ends_of(lengths_ref, row) for row in range(rows)]

    def masks(spot):
        return head_masks(ends, spot, group, rows, block, row_len)

    loads[0].wait()
    spectra(value_ref, masks, inverse_ref, head_spec, rest_spec, group)
    for load in loads[1:]:
        load.wait()

    def product(real, imag, lag):
        hr, hi, hm = hr_ref[lag], hi_ref[lag], hm_ref[lag]
        return real * hr + imag * hi, imag * hm - real * hi

    def reach(j, carry):
        spot, row = j // rows, j % rows
        start = spot * block
        plain = of_row([next_end(e, start, row_len) for e in ends], row) >= start + block
        plain = plain.astype(F32)
        until = of_row([next_end(e, start + block - 1, row_len) for e in ends], row)
        until = (until - 1) // block + 1

        def include(source, sums):
            k = source * rows + row
            real, imag = product(
                head_spec[k, :, :block], head_spec[k, :, block:], source - spot
            )
            return sums[0] + real, sums[1] + imag

        empty = jnp.zeros((channels, block), F32)
        real, imag = lax.fori_loop(spot + 1, until, include, (empty, empty))
        head_real, head_imag = product(head_spec[j, :, :block], head_spec[j, :, block:], 0)
        head_sum[j, :, :block] = head_real + plain * real
        head_sum[j, :, block:] = head_imag + plain * imag
        rest_real, rest_imag = product(rest_spec[j, :, :block], rest_spec[j, :, block:], 0)
        rest_sum[j, :, :block] = rest_real + (1.0 - plain) * real
        rest_sum[j, :, block:] = rest_imag + (1.0 - plain) * imag
        return carry

    lax.fori_loop(0, count, reach, 0)

    def store(spot, found):
        found_ref[pl.ds(spot, group)] = found
        out_ref[pl.ds(spot, group), :channels] = found.astype(BF16)

    back_to_time(head_sum, rest_sum, masks, forward_ref, value_ref, skip_ref, group, store)

    lane = lax.broadcasted_iota(jnp.int32, (channels, block), 1)
    per_turn = block // 2
    blocks = count // rows
    for turn in range(-(-count // per_turn)):
        first = turn * per_turn
        last = min(count, first + per_turn)

        def gather(j, picked):
            at = 2 * (j - first)
            moved = pltpu.roll(found_ref[j], at, 1)
            return jnp.where((lane >= at) & (lane < at + 2), moved, picked)

        picked = lax.fori_loop(first, last, gather, jnp.zeros((channels, block), F32))
        if channels < block:
            picked = jnp.concatenate(
                [picked, jnp.zeros((block - channels, block), F32)], axis=0
            )
        flipped = picked.T
        for spot in range(first // rows, last // rows):
            at = 2 * (spot * rows - first)
            tile = jnp.concatenate(
                [flipped[at : at + 2 * rows], jnp.zeros((16 - 2 * rows, block), F32)], axis=0
            )
            if spot > 0:
                out_ref[(spot - 1) * rows, channels:] = tile.astype(BF16)
    out_ref[(blocks - 1) * rows, channels:] = jnp.zeros((16, block), BF16)
    for spot in range(blocks):
        for row in range(1, rows):
            out_ref[spot * rows + row, channels:] = jnp.zeros((16, block), BF16)


def filter_grad_kernel(
    rows, group, row_len, lengths_ref, value_ref, grad_ref, forward_ref,
    inverse_ref, back_ref, out_ref, head_spec, rest_spec, grad_head, grad_rest, total,
):
    count, channels, block = value_ref.shape
    lags = count // rows
    ends = [ends_of(lengths_ref, row) for row in range(rows)]

    def masks(spot):
        return head_masks(ends, spot, group, rows, block, row_len)

    spectra(value_ref, masks, forward_ref, head_spec, rest_spec, group)
    spectra(grad_ref, masks, inverse_ref, grad_head, grad_rest, group)
    lane = lax.broadcasted_iota(jnp.int32, (channels, block), 1)
    base = lane == 0

    def product(grad, spec, k, j):
        gr, gi = grad[k, :, :block], grad[k, :, block:]
        sr, si = spec[j, :, :block], spec[j, :, block:]
        masked = jnp.where(base, 0.0, si)
        swapped = jnp.where(base, si, sr)
        return gr * sr + gi * masked, gi * swapped - gr * masked

    def own(j, sums):
        start = j // rows * block
        stop = of_row([next_end(e, start, row_len) for e in ends], j % rows)
        plain = (stop >= start + block).astype(F32)
        head = product(grad_head, head_spec, j, j)
        rest = product(grad_rest, rest_spec, j, j)
        rest_spec[j] = rest_spec[j] + plain * head_spec[j]
        return sums[0] + head[0] + rest[0], sums[1] + head[1] + rest[1]

    empty = jnp.zeros((channels, block), F32)
    real, imag = lax.fori_loop(0, count, own, (empty, empty))
    total[0, :, :block] = real
    total[0, :, block:] = imag

    def one_lag(lag, carry):
        def include(j, sums):
            spot = j // rows
            begin = of_row([last_end(e, spot * block) for e in ends], j % rows) // block
            near = (begin <= spot - lag).astype(F32)
            real, imag = product(grad_head, rest_spec, j, j - lag * rows)
            return sums[0] + near * real, sums[1] + near * imag

        real, imag = lax.fori_loop(lag * rows, count, include, (empty, empty))
        total[lag, :, :block] = real
        total[lag, :, block:] = imag
        return carry

    lax.fori_loop(1, lags, one_lag, 0)
    wide = lax.broadcasted_iota(jnp.int32, (channels, 2 * block), 1)
    sign = (1 - 2 * (wide % 2)).astype(F32)
    total[lags] = jnp.zeros((channels, 2 * block), F32)

    def one_piece(lag, carry):
        piece = total[lag + 1] + sign * total[lag]
        high = piece.astype(BF16)
        low = (piece - high.astype(F32)).astype(BF16)
        out_ref[lag] = dot(jnp.concatenate([high, low, high], axis=1), back_ref[...])
        return carry

    lax.fori_loop(0, lags, one_piece, 0)


def vmem(count):
    return [pl.BlockSpec(memory_space=pltpu.VMEM)] * count


def smem(count):
    return [pl.BlockSpec(memory_space=pltpu.SMEM)] * count


def hbm(count):
    return [pl.BlockSpec(memory_space=pltpu.HBM)] * count


def anywhere(count):
    return [pl.BlockSpec(memory_space=pl.ANY)] * count


def params(limit=VMEM_BYTES):
    return pltpu.CompilerParams(vmem_limit_bytes=limit)


SHORT = pl.CostEstimate(flops=1, bytes_accessed=1, transcendentals=0)


def takes(micro):
    return pl.CostEstimate(flops=int(micro * 1e9), bytes_accessed=1, transcendentals=0)


BRIDGE_A, BRIDGE_B = takes(2), takes(12)
LINE = takes(8)

TOKEN = (16384, 1024), F32


def launch(
    kernel, operands, outs, in_specs=None, out_specs=None, scratch=(), limit=VMEM_BYTES, after=(),
    aliases=None, estimate=SHORT,
):
    used, made = len(operands), len(outs)

    def call(*refs):
        rest = refs[used + len(after) :]
        kernel(*refs[:used], *rest[:made], *rest[made + 1 :])

    results = pl.pallas_call(
        call,
        name=getattr(kernel, "func", kernel).__name__.replace("<lambda>", "hold"),
        out_shape=tuple(jax.ShapeDtypeStruct(*out) for out in (*outs, TOKEN)),
        in_specs=(vmem(used) if in_specs is None else in_specs) + anywhere(len(after)),
        out_specs=tuple((vmem(made) if out_specs is None else out_specs) + hbm(1)),
        scratch_shapes=list(scratch),
        input_output_aliases=aliases or {},
        compiler_params=params(limit),
        cost_estimate=estimate,
    )(*operands, *after)
    return tuple(results[:-1]), results[-1]


def run_conv(
    lengths, row_len, value, skip, spectrum, forward, inverse, backward=False, after=()
):
    count, channels, block = value.shape
    rows = lengths.shape[0]
    group = 4 if count % 4 == 0 else 1
    spec = pltpu.VMEM((count, channels, 2 * block), F32)
    extra = [pltpu.VMEM((count, channels, block), F32)] if backward else []
    sent = channels + 16 if backward else channels
    (found,), token = launch(
        partial(conv_back_kernel if backward else conv_kernel, rows, group, row_len),
        (lengths, value, skip, *spectrum, forward, inverse),
        [((count, sent, block), BF16)],
        in_specs=smem(1) + vmem(1) + anywhere(6),
        scratch=[
            *[pltpu.VMEM(part.shape, part.dtype) for part in (skip, *spectrum, forward, inverse)],
            pltpu.SemaphoreType.DMA((6,)),
            *[spec] * 4,
            *extra,
        ],
        after=after,
    )
    return found, token


def run_filter_grad(lengths, row_len, value, grad, forward, inverse, back, after=()):
    count, channels, block = value.shape
    rows = lengths.shape[0]
    group = 4 if count % 4 == 0 else 1
    lags = count // rows
    spec = pltpu.VMEM((count, channels, 2 * block), F32)
    (found,), token = launch(
        partial(filter_grad_kernel, rows, group, row_len),
        (lengths, value, grad, forward, inverse, back),
        [((lags, channels, block), F32)],
        in_specs=smem(1) + vmem(5),
        scratch=[spec] * 4 + [pltpu.VMEM((lags + 1, channels, 2 * block), F32)],
        after=after,
    )
    return found, token


def exact(left, right, contract):
    return lax.dot_general(
        left, right, (contract, ((), ())), precision=FULL_PRECISION, preferred_element_type=F32
    )


def filter_back_kernel(
    taps_ref, envelope_ref, act_one_ref, pre_one_ref, act_two_ref, pre_two_ref, third_ref,
    second_ref, embedding_ref, third_grad, skip_grad, second_grad, first_grad,
):
    lags, channels, block = taps_ref.shape
    pick = lax.broadcasted_iota(jnp.int32, (8, block), 1) == 0
    skip_grad[...] = exact(jnp.where(pick, 1.0, 0.0), taps_ref[0], ((1,), (1,)))
    third_grad[...] = jnp.zeros(third_grad.shape, F32)
    second_grad[...] = jnp.zeros(second_grad.shape, F32)
    first_grad[...] = jnp.zeros(first_grad.shape, F32)

    def one_lag(lag, carry):
        here = pl.ds(pl.multiple_of(lag * block, 128), block)
        grad = taps_ref[lag] * envelope_ref[:, here]
        third_grad[...] += exact(act_two_ref[:, here], grad, ((1,), (1,)))
        grad = jnp.cos(pre_two_ref[:, here]) * exact(third_ref[...], grad, ((1,), (0,)))
        second_grad[...] += exact(act_one_ref[:, here], grad, ((1,), (1,)))
        grad = jnp.cos(pre_one_ref[:, here]) * exact(second_ref[...], grad, ((1,), (0,)))
        first_grad[...] += exact(embedding_ref[:, here], grad, ((1,), (1,)))
        return carry

    lax.fori_loop(0, lags, one_lag, 0)


def run_filter_back(taps, envelope, net, third, second, embedding, after):
    hidden, channels = third.shape
    return launch(
        filter_back_kernel,
        (taps, envelope, *net, third, second, embedding),
        [
            ((hidden, channels), F32),
            ((8, channels), F32),
            ((hidden, hidden), F32),
            ((embedding.shape[0], hidden), F32),
        ],
        after=after,
    )


def put_channels(ref, row, chunk, value):
    groups, _, size, _ = ref.shape
    wide = value.shape[0]
    if groups == 1:
        ref[0, row, chunk * wide : (chunk + 1) * wide] = value
    else:
        per = wide // size
        for k in range(per):
            ref[chunk * per + k, row] = value[k * size : (k + 1) * size]


def get_channels(ref, row, chunk, wide, size):
    groups = ref.shape[0]
    if groups == 1:
        return ref[0, row, chunk * wide : (chunk + 1) * wide]
    per = wide // size
    return jnp.concatenate([ref[chunk * per + k, row, :size] for k in range(per)], axis=0)


def moments(value):
    center = value - jnp.mean(value, axis=-1, keepdims=True)
    spread = jnp.mean(center * center, axis=-1, keepdims=True)
    return center, lax.rsqrt(spread + 1e-05)


def norm_back(center, scale, gain, grad):
    unit = center * scale
    inner = grad * gain
    mean_one = jnp.mean(inner, axis=-1, keepdims=True)
    mean_two = jnp.mean(inner * unit, axis=-1, keepdims=True)
    return scale * (inner - mean_one - unit * mean_two), grad * unit


PIECE = 64


def front_kernel(
    lengths_ref, before_ref, after_ref, gain_ref, hidden_hbm, taps_hbm, weight_hbm,
    normed_hbm, extended_hbm, outer_hbm, sent_hbm,
    hidden_ref, taps_ref, weight_ref, normed_ref, extended_ref, outer_ref, sent_ref,
    halo_ref, wide_ref, mixed_ref, sems,
):
    rows, block, width = hidden_ref.shape
    loads = [
        pltpu.make_async_copy(source, target, sems.at[i])
        for i, (source, target) in enumerate(
            [(hidden_hbm, hidden_ref), (weight_hbm, weight_ref), (taps_hbm, taps_ref)]
        )
    ]
    for load in loads:
        load.start()
    gain = gain_ref[...]
    halo = jnp.concatenate(
        [part for row in range(rows) for part in (before_ref[row], after_ref[row])], axis=0
    ).astype(F32)
    center, scale = moments(halo)
    halo = center * scale * gain
    halo_ref[...] = jnp.concatenate(
        [halo, jnp.zeros((halo_ref.shape[0] - 4 * rows, width), F32)], axis=0
    ).astype(BF16)
    first = lax.axis_index("seq") * block
    ends = [ends_of(lengths_ref, row) for row in range(rows)]
    spots = first + lax.broadcasted_iota(jnp.int32, (block, 1), 0)
    near_one = [near_mask(e, spots, 1) for e in ends]
    near_two = [near_mask(e, spots, 2) for e in ends]
    live = [jnp.where(spots < e[-1], 1.0, 0.0) for e in ends]
    loads[0].wait()
    for row in range(rows):
        for start in range(0, block, PIECE):
            center, scale = moments(hidden_ref[row, start : start + PIECE].astype(F32))
            at = row * block + start
            normed_ref[at : at + PIECE] = (center * scale * gain).astype(BF16)
    saves = [
        pltpu.make_async_copy(source, target, sems.at[3 + i])
        for i, (source, target) in enumerate(
            [
                (normed_ref, normed_hbm),
                (sent_ref, sent_hbm),
                (extended_ref, extended_hbm),
                (outer_ref, outer_hbm),
            ]
        )
    ]
    saves[0].start()
    chunk = width // 2
    loads[1].wait()
    loads[2].wait()
    for part in range(3):
        for half in range(2):
            cols = slice(part * width + half * chunk, part * width + (half + 1) * chunk)
            main = dot(normed_ref[...], weight_ref[:, cols])
            edge = dot(halo_ref[...], weight_ref[:, cols])
            taps = taps_ref[:, cols]
            for row in range(rows):
                wide_ref[row, 0:8] = jnp.zeros((8, chunk), F32)
                wide_ref[row, block + 8 :] = jnp.zeros((8, chunk), F32)
                wide_ref[row, 6:8] = edge[4 * row : 4 * row + 2]
                wide_ref[row, 8 : block + 8] = main[row * block : (row + 1) * block]
                wide_ref[row, block + 8 : block + 10] = edge[4 * row + 2 : 4 * row + 4]
                rounded = wide_ref[row].astype(BF16)
                extended_ref[row, :, cols] = rounded
                wide_ref[row] = rounded.astype(F32)
                mixed = (
                    taps[0:1] * wide_ref[row, 8 : block + 8]
                    + taps[1:2] * wide_ref[row, 7 : block + 7] * near_one[row]
                    + taps[2:3] * wide_ref[row, 6 : block + 6] * near_two[row]
                )
                here = slice(half * chunk, (half + 1) * chunk)
                if part == 0:
                    mixed_ref[row, :, here] = mixed
                elif part == 1:
                    signal = mixed_ref[row, :, here] * mixed * live[row]
                    put_channels(sent_ref, row, half, signal.T.astype(BF16))
                else:
                    outer_ref[row, :, here] = mixed
        if part == 1:
            saves[1].start()
    saves[2].start()
    saves[3].start()
    for save in saves:
        save.wait()


def run_front(lengths, hidden, before, after, gain, taps, weight, groups):
    rows, block, width = hidden.shape
    chunk = width // 2
    outs = (
        ((rows * block, width), BF16),
        ((rows, block + 16, 3 * width), BF16),
        ((rows, block, width), F32),
        ((groups, rows, width // groups, block), BF16),
    )
    return pl.pallas_call(
        front_kernel,
        out_shape=tuple(jax.ShapeDtypeStruct(*out) for out in outs),
        in_specs=smem(1) + vmem(3) + hbm(3),
        out_specs=tuple(hbm(4)),
        scratch_shapes=[
            pltpu.VMEM(hidden.shape, BF16),
            pltpu.VMEM(taps.shape, F32),
            pltpu.VMEM(weight.shape, BF16),
            *[pltpu.VMEM(*out) for out in outs],
            pltpu.VMEM((16, width), BF16),
            pltpu.VMEM((rows, block + 16, chunk), F32),
            pltpu.VMEM((rows, block, width), F32),
            pltpu.SemaphoreType.DMA((7,)),
        ],
        compiler_params=params(FULL_BYTES),
        cost_estimate=SHORT,
    )(lengths, before, after, gain, hidden, taps, weight)


def middle_kernel(
    size, conv_ref, gain_ref, outer_hbm, hidden_hbm, upstream_hbm, out_hbm, up_hbm, down_hbm,
    gain_grad_ref, factors_mine_hbm, factors_theirs_hbm, result_hbm, last_mine_hbm, last_theirs_hbm,
    grad_middle_hbm, grad_outer_hbm, sent_hbm,
    outer_ref, hidden_ref, upstream_ref, out_ref, up_ref, down_ref,
    factors_ref, result_ref, last_ref, grad_middle_ref, grad_outer_ref, sent_ref,
    conv_scr, middle_ref, grad_ref, sems,
):
    rows, block, width = hidden_ref.shape
    parts = down_ref.shape[0] // width
    per_core = parts // 2
    units = per_core * width
    chunk = width // 2
    core = lax.axis_index("seq") % 2
    copies = [
        pltpu.make_async_copy(outer_hbm, outer_ref, sems.at[0]),
        pltpu.make_async_copy(out_hbm, out_ref, sems.at[1]),
        pltpu.make_async_copy(hidden_hbm, hidden_ref, sems.at[2]),
        pltpu.make_async_copy(upstream_hbm, upstream_ref, sems.at[3]),
    ]
    for part in range(parts):
        cols = slice(part * width, (part + 1) * width)
        copies.append(
            pltpu.make_async_copy(up_hbm.at[:, cols], up_ref.at[:, cols], sems.at[2 * part + 4])
        )
        copies.append(
            pltpu.make_async_copy(down_hbm.at[cols], down_ref.at[cols], sems.at[2 * part + 5])
        )
    for copy in copies:
        copy.start()
    saves = [
        pltpu.make_async_copy(source, target, sems.at[2 * parts + 4 + i])
        for i, (source, target) in enumerate(
            [
                (result_ref, result_hbm),
                (grad_middle_ref, grad_middle_hbm),
                (last_ref.at[0], last_mine_hbm),
                (last_ref.at[1], last_theirs_hbm),
                (sent_ref, sent_hbm),
                (grad_outer_ref, grad_outer_hbm),
                (factors_ref.at[1], factors_theirs_hbm),
                (factors_ref.at[0], factors_mine_hbm),
            ]
        )
    ]
    for row in range(rows):
        here = slice(row * block, (row + 1) * block)
        for half in range(2):
            cols = slice(half * chunk, (half + 1) * chunk)
            conv_scr[here, cols] = get_channels(conv_ref, row, half, chunk, size).astype(F32).T
    copies[0].wait()
    for row in range(rows):
        here = slice(row * block, (row + 1) * block)
        gated = (outer_ref[row] * conv_scr[here]).astype(BF16)
        last_ref[0, here, :width] = gated
        last_ref[1, here, :width] = gated
    copies[1].wait()
    middle_ref[...] = dot(last_ref[0, :, :width], out_ref[...])
    copies[2].wait()
    gain = gain_ref[...]
    normed = slice(2 * units, 2 * units + width)
    for row in range(rows):
        for start in range(0, block, PIECE):
            here = slice(row * block + start, row * block + start + PIECE)
            middle = middle_ref[here] + hidden_ref[row, start : start + PIECE].astype(F32)
            middle_ref[here] = middle
            center, scale = moments(middle)
            rounded = (center * scale * gain).astype(BF16)
            factors_ref[0, here, normed] = rounded
            factors_ref[1, here, normed] = rounded
    slope = math.sqrt(2.0 / math.pi)
    copies[3].wait()
    for part in range(parts):
        cols = slice(part * width, (part + 1) * width)
        copies[2 * part + 4].wait()
        pre = dot(factors_ref[0, :, normed], up_ref[:, cols])
        copies[2 * part + 5].wait()
        grad_act = dot_nt(upstream_ref[...], down_ref[cols])
        square = pre * pre
        bend = jnp.tanh(slope * pre * (1.0 + 0.044715 * square))
        half_up = 0.5 * (1.0 + bend)
        act = (pre * half_up).astype(BF16)
        turn = half_up + 0.5 * pre * (1.0 - bend * bend) * (
            slope * (1.0 + 3.0 * 0.044715 * square)
        )
        grad_pre = (grad_act * turn).astype(BF16)
        slot = (part // per_core + core) % 2
        at = part % per_core * width
        factors_ref[slot, :, at : at + width] = act
        factors_ref[slot, :, units + at : units + at + width] = grad_pre
        if part == 0:
            grad_ref[...] = dot_nt(grad_pre, up_ref[:, cols])
        else:
            grad_ref[...] += dot_nt(grad_pre, up_ref[:, cols])
        found = dot(act, down_ref[cols])
        for row in range(rows):
            here = slice(row * block, (row + 1) * block)
            if part == 0:
                grad_middle_ref[here] = middle_ref[here] + found[here]
            elif part < parts - 1:
                grad_middle_ref[here] += found[here]
            else:
                result_ref[row] = (grad_middle_ref[here] + found[here]).astype(BF16)
    saves[6].start()
    saves[7].start()
    saves[0].start()
    gain_grad = jnp.zeros((1, width), F32)
    branch_cols = slice(width, width + chunk)
    for at in range(0, rows * block, PIECE):
        here = slice(at, at + PIECE)
        center, scale = moments(middle_ref[here])
        grad, terms = norm_back(center, scale, gain, grad_ref[here])
        gain_grad = gain_grad + jnp.sum(terms, axis=0, keepdims=True)
        grad = upstream_ref[here].astype(F32) + grad
        grad_middle_ref[here] = grad
        branch = grad.astype(BF16)

        last_ref[core, here, branch_cols] = branch[:, :chunk]
        last_ref[1 - core, here, branch_cols] = branch[:, chunk:]

    for save in saves[1:4]:
        save.start()
    gain_grad_ref[...] = gain_grad
    grad_ref[...] = dot_nt(grad_middle_ref[...].astype(BF16), out_ref[...])
    for row in range(rows):
        here = slice(row * block, (row + 1) * block)
        for half in range(2):
            cols = slice(half * chunk, (half + 1) * chunk)
            grad_conv = grad_ref[here, cols] * outer_ref[row, :, cols]
            put_channels(sent_ref, row, half, grad_conv.T.astype(BF16))
    saves[4].start()
    for row in range(rows):
        here = slice(row * block, (row + 1) * block)
        grad_outer_ref[row] = grad_ref[here] * conv_scr[here]
    saves[5].start()
    for save in saves:
        save.wait()


def run_middle(conv, size, outer, hidden, gain, upstream, out_weight, up, down, groups):
    rows, block, width = hidden.shape
    tokens = rows * block
    units = up.shape[1]
    parts = units // width
    near = (((1, width), F32),)
    far = (
        ((tokens, units + width), BF16),
        ((tokens, units + width), BF16),
        ((rows, block, width), BF16),
        ((tokens, 3 * width // 2), BF16),
        ((tokens, 3 * width // 2), BF16),
        ((tokens, width), F32),
        ((rows, block, width), F32),
        ((groups, rows, width // groups, block), BF16),
    )
    return pl.pallas_call(
        partial(middle_kernel, size),
        out_shape=tuple(jax.ShapeDtypeStruct(*out) for out in near + far),
        in_specs=vmem(2) + hbm(6),
        out_specs=tuple(vmem(1) + hbm(8)),
        scratch_shapes=[
            pltpu.VMEM(outer.shape, F32),
            pltpu.VMEM(hidden.shape, BF16),
            pltpu.VMEM(upstream.shape, BF16),
            pltpu.VMEM(out_weight.shape, BF16),
            pltpu.VMEM(up.shape, BF16),
            pltpu.VMEM(down.shape, BF16),
            pltpu.VMEM((2, *far[0][0]), BF16),
            pltpu.VMEM(*far[2]),
            pltpu.VMEM((2, *far[3][0]), BF16),
            *[pltpu.VMEM(*out) for out in far[5:]],
            pltpu.VMEM((tokens, width), F32),
            pltpu.VMEM((tokens, width), F32),
            pltpu.VMEM((tokens, width), F32),
            pltpu.SemaphoreType.DMA((2 * parts + 12,)),
        ],
        compiler_params=params(FULL_BYTES),
        cost_estimate=SHORT,
    )(conv, gain, outer, hidden, upstream, out_weight, up, down)


def last_kernel(
    size, lengths_ref, signal_ref, halo_ref, outer_halo_ref, gain_ref, taps_ref,
    extended_hbm, outer_hbm, hidden_hbm, grad_middle_hbm, weight_hbm,
    proj_mine, proj_theirs, taps_grad_ref, gain_grad_ref, result_hbm,
    extended_ref, outer_ref, hidden_ref, grad_middle_ref, weight_ref, result_ref,
    wide_ref, mixed_ref, grad_ref, proj_ref, normed_grad, sems,
):
    rows, block, width = hidden_ref.shape
    chunk = width // 2
    loads = [
        pltpu.make_async_copy(source, target, sems.at[i])
        for i, (source, target) in enumerate(
            [
                (extended_hbm, extended_ref),
                (outer_hbm, outer_ref),
                (weight_hbm, weight_ref),
                (hidden_hbm, hidden_ref),
                (grad_middle_hbm, grad_middle_ref),
            ]
        )
    ]
    for load in loads:
        load.start()
    core = lax.axis_index("seq") % 2
    first = lax.axis_index("seq") * block
    longer = block + 8
    spots = first + lax.broadcasted_iota(jnp.int32, (longer, 1), 0)
    taps_grad_ref[...] = jnp.zeros(taps_grad_ref.shape, F32)
    loads[0].wait()
    loads[1].wait()
    for row in range(rows):
        ends = ends_of(lengths_ref, row)
        near_one, near_two = near_mask(ends, spots, 1), near_mask(ends, spots, 2)
        live = jnp.where(spots < ends[-1], 1.0, 0.0)
        for half in range(2):
            cols = slice(half * chunk, (half + 1) * chunk)
            grad_ref[0, :block] = get_channels(signal_ref, row, half, chunk, size).astype(F32).T
            grad_ref[0, block:] = jnp.concatenate(
                [halo_ref[row, :, cols], jnp.zeros((6, chunk), F32)], axis=0
            )
            for part in range(2):
                at = slice(part * width + half * chunk, part * width + (half + 1) * chunk)
                taps = taps_ref[:, at]
                wide_ref[part] = extended_ref[row, :, at].astype(F32)
                mixed_ref[part] = (
                    taps[0:1] * wide_ref[part, 8 : longer + 8]
                    + taps[1:2] * wide_ref[part, 7 : longer + 7] * near_one
                    + taps[2:3] * wide_ref[part, 6 : longer + 6] * near_two
                )
            at = slice(2 * width + half * chunk, 2 * width + (half + 1) * chunk)
            wide_ref[2] = extended_ref[row, :, at].astype(F32)
            signal_grad = grad_ref[0] * live
            grad_ref[0] = signal_grad * mixed_ref[1]
            grad_ref[1] = signal_grad * mixed_ref[0]
            grad_ref[2, :block] = outer_ref[row, :, cols]
            grad_ref[2, block:] = jnp.concatenate(
                [outer_halo_ref[row, :, cols], jnp.zeros((6, chunk), F32)], axis=0
            )
            for part in range(3):
                at = slice(part * width + half * chunk, part * width + (half + 1) * chunk)
                taps = taps_ref[:, at]
                own = grad_ref[part, :block]
                proj = (
                    taps[0:1] * own
                    + taps[1:2] * (grad_ref[part, 1 : block + 1] * near_one[1 : block + 1])
                    + taps[2:3] * (grad_ref[part, 2 : block + 2] * near_two[2 : block + 2])
                )
                proj_ref[row * block : (row + 1) * block, at] = proj.astype(BF16)
                taps_grad_ref[0:1, at] += jnp.sum(
                    own * wide_ref[part, 8 : block + 8], axis=0, keepdims=True
                )
                taps_grad_ref[1:2, at] += jnp.sum(
                    own * wide_ref[part, 7 : block + 7] * near_one[:block], axis=0, keepdims=True
                )
                taps_grad_ref[2:3, at] += jnp.sum(
                    own * wide_ref[part, 6 : block + 6] * near_two[:block], axis=0, keepdims=True
                )
    middle = 3 * width // 2

    @pl.when(core == 0)
    def _():
        proj_mine[...] = proj_ref[:, :middle]
        proj_theirs[...] = proj_ref[:, middle:]

    @pl.when(core != 0)
    def _():
        proj_mine[...] = proj_ref[:, middle:]
        proj_theirs[...] = proj_ref[:, :middle]

    loads[2].wait()
    normed_grad[...] = dot_nt(proj_ref[...], weight_ref[...])
    loads[3].wait()
    loads[4].wait()
    gain = gain_ref[...]
    gain_grad = jnp.zeros((1, width), F32)
    for row in range(rows):
        for start in range(0, block, PIECE):
            here = slice(row * block + start, row * block + start + PIECE)
            center, scale = moments(hidden_ref[row, start : start + PIECE].astype(F32))
            grad, terms = norm_back(center, scale, gain, normed_grad[here])
            gain_grad = gain_grad + jnp.sum(terms, axis=0, keepdims=True)
            result_ref[row, start : start + PIECE] = grad_middle_ref[here] + grad
    gain_grad_ref[...] = gain_grad
    save = pltpu.make_async_copy(result_ref, result_hbm, sems.at[5])
    save.start()
    save.wait()


def run_last(
    lengths, signal, size, halo, extended, outer, outer_halo, hidden, gain, taps, grad_middle,
    weight, after,
):
    rows, block, width = hidden.shape
    tokens = rows * block
    chunk = width // 2
    middle = 3 * width // 2
    return launch(
        partial(last_kernel, size),
        (
            lengths, signal, halo, outer_halo, gain, taps, extended, outer, hidden, grad_middle,
            weight,
        ),
        [
            ((tokens, middle), BF16),
            ((tokens, middle), BF16),
            ((8, 3 * width), F32),
            ((1, width), F32),
            (hidden.shape, F32),
        ],
        in_specs=smem(1) + vmem(5) + hbm(5),
        out_specs=vmem(4) + hbm(1),
        scratch=[
            pltpu.VMEM(extended.shape, BF16),
            pltpu.VMEM(outer.shape, F32),
            pltpu.VMEM(hidden.shape, BF16),
            pltpu.VMEM(grad_middle.shape, F32),
            pltpu.VMEM(weight.shape, BF16),
            pltpu.VMEM(hidden.shape, F32),
            pltpu.VMEM((3, block + 16, chunk), F32),
            pltpu.VMEM((2, block + 8, chunk), F32),
            pltpu.VMEM((3, block + 8, chunk), F32),
            pltpu.VMEM((tokens, 3 * width), BF16),
            pltpu.VMEM((tokens, width), F32),
            pltpu.SemaphoreType.DMA((6,)),
        ],
        limit=FULL_BYTES,
        after=after,
    )


def to_owner(sent, mine, padded):
    count = lax.axis_size("seq")
    groups, rows, size, block = sent.shape
    if groups != count:
        sent = sent.reshape(rows, count, mine, block).transpose(1, 0, 2, 3)
    got = lax.all_to_all(sent, "seq", 0, 0, tiled=True).reshape(count * rows, mine, block)
    if padded != mine:
        got = jnp.pad(got, ((0, 0), (0, padded - mine), (0, 0)))
    return got


def to_block(value, rows, mine, groups):
    count = lax.axis_size("seq")
    size, block = value.shape[1:]
    got = lax.all_to_all(
        value.reshape(count, rows, size, block), "seq", 0, 0, tiled=True
    )
    if groups == count:
        return got
    return got[:, :, :mine].transpose(1, 0, 2, 3).reshape(1, rows, count * mine, block), got


def dot_tn(left, right):
    return lax.dot_general(left, right, (((0,), (0,)), ((), ())), preferred_element_type=F32)


def bit_inside(bit):
    count = lax.axis_size("seq")
    if bit < count:
        return lax.axis_index("seq") // bit % 2
    return lax.axis_index("dp") // (bit // count) % 2


def side(bit, sent):
    mine = bit_inside(bit)
    return 1 - mine if sent else mine


def up_products_kernel(
    bits, sent, mine_hbm, got_hbm, a_ref, b_ref, left_ref, right_ref, sems
):
    _, rows, width = a_ref.shape
    units = 2 * width
    moves = []
    for part in range(2):
        at = pl.multiple_of(2 * units + side(bits[part], sent) * rows, 128)
        cols = slice(units + part * width, units + (part + 1) * width)
        for i, factors in enumerate((mine_hbm, got_hbm)):
            moves.append((factors.at[:, pl.ds(at, rows)], left_ref.at[part, i]))
            moves.append((factors.at[:, cols], right_ref.at[part, i]))
    loads = start_loads(moves, sems)
    for part, out in enumerate((a_ref, b_ref)):
        for load in loads[4 * part : 4 * part + 4]:
            load.wait()
        found = dot_tn(left_ref[part, 0], right_ref[part, 0]) + dot_tn(
            left_ref[part, 1], right_ref[part, 1]
        )
        out[0] = found.astype(BF16)


def down_products_kernel(
    bits, sent, mine_hbm, got_hbm, upstream_hbm, upstream_got_hbm, a_ref, b_ref,
    left_ref, right_ref, sems,
):
    _, rows, width = a_ref.shape
    moves = [(upstream_hbm, right_ref.at[0]), (upstream_got_hbm, right_ref.at[1])]
    for part in range(2):
        at = pl.multiple_of(part * width + side(bits[part], sent) * rows, 128)
        for i, factors in enumerate((mine_hbm, got_hbm)):
            moves.append((factors.at[:, pl.ds(at, rows)], left_ref.at[part, i]))
    loads = start_loads(moves, sems)
    loads[0].wait()
    loads[1].wait()
    for part, out in enumerate((a_ref, b_ref)):
        loads[2 * part + 2].wait()
        loads[2 * part + 3].wait()
        found = dot_tn(left_ref[part, 0], right_ref[0]) + dot_tn(left_ref[part, 1], right_ref[1])
        out[0] = found.astype(BF16)


def last_products_kernel(
    bits, sent, normed_ref, normed_got_ref, proj_ref, proj_got_ref, last_ref, last_got_ref,
    a_ref, b_ref,
):
    rows, width = a_ref.shape[1:]
    half = width // 2
    at = pl.multiple_of(side(bits[0], sent) * rows, 128)
    found = dot_tn(normed_ref[:, pl.ds(at, rows)], proj_ref[:, :width]) + dot_tn(
        normed_got_ref[:, pl.ds(at, rows)], proj_got_ref[:, :width]
    )
    a_ref[0] = found.astype(BF16)
    at = pl.multiple_of(side(bits[1], sent) * rows, 128)
    found = dot_tn(normed_ref[:, pl.ds(at, rows)], proj_ref[:, width:]) + dot_tn(
        normed_got_ref[:, pl.ds(at, rows)], proj_got_ref[:, width:]
    )
    b_ref[0, :, :half] = found.astype(BF16)
    found = dot_tn(last_ref[:, pl.ds(at, rows)], last_ref[:, width:]) + dot_tn(
        last_got_ref[:, pl.ds(at, rows)], last_got_ref[:, width:]
    )
    b_ref[0, :, half:] = found.astype(BF16)


def run_up_products(bits, sent, operands, shape, after=()):
    tokens, (_, rows, width) = operands[0].shape[0], shape
    return launch(
        partial(up_products_kernel, bits, sent),
        operands,
        [(shape, BF16)] * 2,
        in_specs=anywhere(2),
        scratch=[
            pltpu.VMEM((2, 2, tokens, rows), BF16),
            pltpu.VMEM((2, 2, tokens, width), BF16),
            pltpu.SemaphoreType.DMA((8,)),
        ],
        limit=FULL_BYTES,
        after=after,
    )


def run_down_products(bits, sent, operands, shape, after=()):
    tokens, (_, rows, width) = operands[0].shape[0], shape
    return launch(
        partial(down_products_kernel, bits, sent),
        operands,
        [(shape, BF16)] * 2,
        in_specs=anywhere(4),
        scratch=[
            pltpu.VMEM((2, 2, tokens, rows), BF16),
            pltpu.VMEM((2, tokens, width), BF16),
            pltpu.SemaphoreType.DMA((6,)),
        ],
        limit=FULL_BYTES,
        after=after,
    )


def run_last_products(bits, sent, operands, shape, after=()):
    return launch(
        partial(last_products_kernel, bits, sent),
        operands,
        [(shape, BF16)] * 2,
        after=after,
    )


STEP = 96


def steps(rows):
    step = STEP if rows % STEP == 0 else rows
    return [(start, step) for start in range(0, rows, step)]


def halve_kernel(
    bits, kept_a, got_a, kept_b, got_b, sent_a, next_a, sent_b, next_b,
    kept_a_ref, got_a_ref, kept_b_ref, got_b_ref, sems,
):
    moves, work = [], []
    for sent, outs in ((True, (sent_a, sent_b)), (False, (next_a, next_b))):
        for bit, out, kept, got, kept_ref, got_ref in (
            (bits[0], outs[0], kept_a, got_a, kept_a_ref, got_a_ref),
            (bits[1], outs[1], kept_b, got_b, kept_b_ref, got_b_ref),
        ):
            rows = out.shape[1]
            at = pl.ds(pl.multiple_of(side(bit, sent) * rows, 16), rows)
            slot = slice(0, rows) if sent else slice(rows, 2 * rows)
            moves.append((kept.at[:, at], kept_ref.at[:, slot]))
            moves.append((got.at[:, at], got_ref.at[:, slot]))
            work.append((out, kept_ref, got_ref, 0 if sent else rows))
    loads = start_loads(moves, sems)
    for i, (out, kept_ref, got_ref, first) in enumerate(work):
        loads[2 * i].wait()
        loads[2 * i + 1].wait()
        for block in range(out.shape[0]):
            for start, step in steps(out.shape[1]):
                at = slice(first + start, first + start + step)
                total = kept_ref[block, at].astype(F32) + got_ref[block, at].astype(F32)
                out[block, start : start + step] = total.astype(BF16)


def run_halve(bits, parts, after=(), estimate=SHORT):
    def half(array):
        return (array.shape[0], array.shape[1] // 2, array.shape[2]), BF16

    return launch(
        partial(halve_kernel, bits),
        parts,
        [half(parts[0]), half(parts[0]), half(parts[2]), half(parts[2])],
        in_specs=anywhere(4),
        scratch=[
            *[pltpu.VMEM(part.shape, BF16) for part in parts],
            pltpu.SemaphoreType.DMA((8,)),
        ],
        limit=FULL_BYTES,
        after=after,
        estimate=estimate,
    )


SHARED, OWNED = 32, 16
GROUPS = 6
EXTRA = 16


def line_spot():
    return lax.axis_index("seq") // 2


def pieces_of(a_ref, b_ref, count):
    at = 0
    for ref in (a_ref, b_ref):
        blocks, rows, _ = ref.shape
        size = rows // count
        for block in range(blocks):
            yield ref, block, size, at
            at += size


def scatter_kernel(with_small, bit, *refs):
    kept_a, got_a, kept_b, got_b = refs[:4]
    for out, sent in zip(refs[-2:], (True, False)):
        half = out.shape[0] // 2
        for high in range(2):
            place = 2 * high + side(bit, sent)
            for (kept, block, size, at), (got, _, _, _) in zip(
                pieces_of(kept_a, kept_b, 4), pieces_of(got_a, got_b, 4)
            ):
                rows = pl.ds(pl.multiple_of(place * size, 16), size)
                total = kept[block, rows].astype(F32) + got[block, rows].astype(F32)
                out[high * half + at : high * half + at + size] = total.astype(BF16)
            if with_small:
                at = (high + 1) * half - EXTRA
                size = SHARED // 4
                part = refs[4][pl.ds(pl.multiple_of(place * size, 8), size)]
                part = jnp.concatenate(
                    [part, jnp.zeros((EXTRA - size, part.shape[1]), F32)], axis=0
                )
                out[at : at + EXTRA] = part.astype(BF16)


def run_scatter(parts, bit, small=None, after=(), estimate=SHORT):
    share = sum(part.shape[0] * part.shape[1] for part in (parts[0], parts[2])) // 4
    share += 0 if small is None else EXTRA
    return launch(
        partial(scatter_kernel, small is not None, bit),
        parts if small is None else (*parts, small),
        [((2 * share, parts[0].shape[2]), BF16)] * 2,
        after=after,
        estimate=estimate,
    )


def split_kernel(bit, kept, got, sent, following):
    rows = sent.shape[0]
    for out, which in ((sent, side(bit, True)), (following, side(bit, False))):
        at = pl.ds(pl.multiple_of(which * rows, 16), rows)
        out[...] = (kept[at].astype(F32) + got[at].astype(F32)).astype(BF16)


def run_split(bit, kept, got, after=(), estimate=SHORT):
    rows, width = kept.shape
    return launch(
        partial(split_kernel, bit),
        (kept, got),
        [((rows // 2, width), BF16)] * 2,
        after=after,
        estimate=estimate,
    )


def pair_kernel(bit, mine, got, out):
    rows = mine.shape[0]
    out[pl.ds(pl.multiple_of(side(bit, False) * rows, 16), rows)] = mine[...]
    out[pl.ds(pl.multiple_of(side(bit, True) * rows, 16), rows)] = got[...]


def run_pair(bit, mine, got, after=(), estimate=SHORT):
    rows, width = mine.shape
    return launch(
        partial(pair_kernel, bit),
        (mine, got),
        [((2 * rows, width), BF16)],
        after=after,
        estimate=estimate,
    )


def total_kernel(with_small, *refs):
    *parts, out = refs
    if with_small:
        *parts, small = parts
    rows_in = parts[0].shape[0]
    for start, step in steps(rows_in):
        rows = slice(start, start + step)
        total = parts[0][rows].astype(F32)
        for part in parts[1:]:
            total = total + part[rows].astype(F32)
        out[rows] = total.astype(out.dtype)
    if with_small:
        out[rows_in:] = small[SHARED:].astype(out.dtype)


def run_total(parts, small=None, after=(), estimate=SHORT):
    rows, width = parts[0].shape
    return launch(
        partial(total_kernel, small is not None),
        parts if small is None else (*parts, small),
        [((rows if small is None else rows + OWNED, width), parts[0].dtype)],
        after=after,
        estimate=estimate,
    )


def total_all_kernel(parts, out):
    count, rows_in, _ = parts.shape
    for start, step in steps(rows_in):
        rows = slice(start, start + step)
        total = parts[0, rows].astype(F32)
        for place in range(1, count):
            total = total + parts[place, rows].astype(F32)
        out[rows] = total.astype(out.dtype)


def run_total_all(parts, after, kind=F32):
    return launch(total_all_kernel, (parts,), [(parts.shape[1:], kind)], after=after)


def gather_kernel(with_small, bit, mine, got, *outs):
    half = mine.shape[0] // 2
    for pair, sent in ((mine, False), (got, True)):
        for high in range(2):
            place = 2 * high + side(bit, sent)
            for out, block, size, at in pieces_of(outs[0], outs[1], 4):
                rows = pl.ds(pl.multiple_of(place * size, 16), size)
                out[block, rows] = pair[high * half + at : high * half + at + size]
            if with_small:
                at = (high + 1) * half - EXTRA - OWNED
                size = SHARED // 4
                shared = pair[at : at + EXTRA].astype(F32)[:size]
                outs[2][pl.ds(pl.multiple_of(place * size, 8), size)] = shared
                rows = pl.ds(pl.multiple_of(SHARED + place * OWNED, 8), OWNED)
                outs[2][rows] = pair[at + EXTRA : at + EXTRA + OWNED].astype(F32)


def run_gather(bit, mine, got, shapes, with_small, after=(), estimate=SHORT):
    outs = [(shape, BF16) for shape in shapes]
    if with_small:
        outs.append(((SHARED + 4 * OWNED, mine.shape[1]), F32))
    return launch(
        partial(gather_kernel, with_small, bit), (mine, got), outs, after=after, estimate=estimate
    )


def join_kernel(bits, mine_a, got_a, mine_b, got_b, out_a, out_b):
    for bit, mine, got, out in (
        (bits[0], mine_a, got_a, out_a),
        (bits[1], mine_b, got_b, out_b),
    ):
        blocks, rows, _ = mine.shape
        for source, which in ((mine, side(bit, False)), (got, side(bit, True))):
            at = pl.ds(pl.multiple_of(which * rows, 16), rows)
            for block in range(blocks):
                out[block, at] = source[block]


def run_join(bits, parts, after=()):
    def twice(array):
        return (array.shape[0], array.shape[1] * 2, array.shape[2]), BF16

    return launch(
        partial(join_kernel, bits), parts, [twice(parts[0]), twice(parts[2])], after=after
    )


PLACE = 192
SLOTS = 4


def place_all(moves, narrow, wide, sems):
    loads, stores = [], []

    def load(i):
        source, _ = moves[i]
        rows, cols = source.shape
        copy = pltpu.make_async_copy(
            source, narrow.at[i % SLOTS, :rows, :cols], sems.at[i % SLOTS]
        )
        copy.start()
        loads.append(copy)

    for i in range(min(SLOTS, len(moves))):
        load(i)
    for i, (source, target) in enumerate(moves):
        rows, cols = source.shape
        slot = i % SLOTS
        loads[i].wait()
        if i >= SLOTS:
            stores[i - SLOTS].wait()
        wide[slot, :rows, :cols] = narrow[slot, :rows, :cols].astype(F32)
        copy = pltpu.make_async_copy(wide.at[slot, :rows, :cols], target, sems.at[SLOTS + slot])
        copy.start()
        stores.append(copy)
        if i + SLOTS < len(moves):
            load(i + SLOTS)
    for copy in stores[-SLOTS:]:
        copy.wait()


def stack_kernel(bits, mine_a, mine_b, got_a, got_b, out):
    for part, (mine, got) in enumerate(((mine_a, got_a), (mine_b, got_b))):
        rows = mine.shape[1]
        for source, sent in ((mine, False), (got, True)):
            at = pl.ds(pl.multiple_of(side(bits[part], sent) * rows, 16), rows)
            out[part, at] = source[0]


def up_place_kernel(mine, other, out_hbm, narrow, wide, sems):
    core = lax.axis_index("seq") % 2
    moves = []
    for source, owner in ((mine, core), (other, 1 - core)):
        parts, rows, width = source.shape
        for part in range(parts):
            col = pl.multiple_of((2 * owner + part) * width, 128)
            for row in range(0, rows, PLACE):
                target = out_hbm.at[row : row + PLACE, pl.ds(col, width)]
                moves.append((source.at[part, row : row + PLACE], target))
    place_all(moves, narrow, wide, sems)


def down_place_kernel(mine, other, out_hbm, narrow, wide, sems):
    core = lax.axis_index("seq") % 2
    moves = []
    for source, owner in ((mine, core), (other, 1 - core)):
        parts, rows, _ = source.shape
        for part in range(parts):
            for start in range(0, rows, PLACE):
                row = pl.multiple_of((2 * owner + part) * rows + start, 16)
                target = out_hbm.at[pl.ds(row, PLACE)]
                moves.append((source.at[part, start : start + PLACE], target))
    place_all(moves, narrow, wide, sems)


def last_place_kernel(bits, sides, *refs):
    in_hbm, out_hbm, narrow, wide, sems = refs[-5:]
    core = lax.axis_index("seq") % 2
    moves = []
    for i, (sent, owner) in enumerate((s, o) for s in sides for o in (core, 1 - core)):
        source_a, source_b = refs[2 * i : 2 * i + 2]
        _, rows, width = source_a.shape
        half = width // 2
        for start in range(0, rows, PLACE):
            row = pl.multiple_of(side(bits[0], sent) * rows + start, 16)
            col = pl.multiple_of(owner * 3 * half, 128)
            moves.append(
                (
                    source_a.at[0, start : start + PLACE],
                    in_hbm.at[pl.ds(row, PLACE), pl.ds(col, width)],
                )
            )
            row = pl.multiple_of(side(bits[1], sent) * rows + start, 16)
            col = pl.multiple_of(owner * 3 * half + width, 128)
            moves.append(
                (
                    source_b.at[0, start : start + PLACE, :half],
                    in_hbm.at[pl.ds(row, PLACE), pl.ds(col, half)],
                )
            )
            col = pl.multiple_of(owner * half, 128)
            moves.append(
                (
                    source_b.at[0, start : start + PLACE, half:],
                    out_hbm.at[pl.ds(row, PLACE), pl.ds(col, half)],
                )
            )
    place_all(moves, narrow, wide, sems)


def run_place(kernel, bits, sides, sources, outs, shapes, after=()):
    width = sources[0].shape[2]
    return launch(
        partial(kernel, bits, sides),
        (*sources, *outs),
        [(shape, F32) for shape in shapes],
        in_specs=anywhere(len(sources)) + hbm(len(outs)),
        out_specs=hbm(len(shapes)),
        scratch=[
            pltpu.VMEM((SLOTS, PLACE, width), BF16),
            pltpu.VMEM((SLOTS, PLACE, width), F32),
            pltpu.SemaphoreType.DMA((2 * SLOTS,)),
        ],
        limit=PLACE_BYTES,
        after=after,
        aliases={len(sources) + i: i for i in range(len(outs))},
    )


def pack_kernel(
    third_ref, skip_ref, taps_ref, gain_one, gain_two, second_ref, first_ref, copies_ref,
    out_ref, owned_ref, hidden_ref,
):
    hidden, mine = third_ref.shape
    out_ref[...] = jnp.zeros(out_ref.shape, F32)
    width = out_ref.shape[1]
    for tap in range(KS):
        for part in range(3):
            row = 3 * tap + part
            out_ref[row : row + 1] = taps_ref[tap : tap + 1, part * width : (part + 1) * width]
    row = 3 * KS
    out_ref[row : row + 1] = gain_one[...]
    out_ref[row + 1 : row + 2] = gain_two[...]
    row += 2
    owned_ref[...] = jnp.zeros(owned_ref.shape, F32)
    owned_ref[:hidden, :mine] = third_ref[...]
    owned_ref[hidden : hidden + 1, :mine] = skip_ref[...]
    hidden_ref[...] = jnp.zeros(hidden_ref.shape, F32)
    hidden_ref[:hidden, :hidden] = second_ref[...]
    hidden_ref[hidden : hidden + first_ref.shape[0], :hidden] = first_ref[...]
    each, size = hidden_ref.shape[0] // GROUPS, owned_ref.shape[0] // GROUPS
    for group in range(GROUPS):
        lanes = slice(128 * group, 128 * (group + 1))
        out_ref[row : row + each, lanes] = hidden_ref[group * each : (group + 1) * each]
        out_ref[SHARED : SHARED + size, lanes] = owned_ref[group * size : (group + 1) * size]
    for copy in range(copies_ref.shape[0]):
        copies_ref[copy] = out_ref[...]


def small_rows(hidden, embedded):
    return -(-(hidden + 1) // GROUPS) * GROUPS, -(-(hidden + embedded) // GROUPS) * GROUPS


def run_pack(copies, third, skip, taps, gain_one, gain_two, second, first):
    owned, hidden = small_rows(second.shape[0], first.shape[0])
    return launch(
        pack_kernel,
        (third, skip, taps, gain_one, gain_two, second, first),
        [((copies, SHARED + OWNED, gain_one.shape[1]), F32)],
        scratch=[pltpu.VMEM((SHARED + OWNED, gain_one.shape[1]), F32), pltpu.VMEM((owned, 128), F32), pltpu.VMEM((hidden, 128), F32)],
    )


def unpack_kernel(
    count, mine, mine_ref, got_ref, third_ref, skip_ref, taps_ref, gain_one, gain_two, second_ref,
    first_ref, owner_ref, sum_ref, owned_ref, hidden_ref,
):
    hidden, width = third_ref.shape
    core = lax.axis_index("seq") % 2
    for spot in range(count):
        here = slice(SHARED + spot * OWNED, SHARED + (spot + 1) * OWNED)
        owner_ref[2 * spot + core] = mine_ref[here]
        owner_ref[2 * spot + 1 - core] = got_ref[here]
    sum_ref[...] = mine_ref[:SHARED] + got_ref[:SHARED]
    each, size = hidden_ref.shape[0] // GROUPS, owned_ref.shape[0] // GROUPS
    rows = owned_ref.shape[0]
    lane = lax.broadcasted_iota(jnp.int32, (rows, 128), 1)
    wide = [jnp.zeros((rows, 128), F32) for _ in range(width // 128)]
    for owner in range(2 * count):
        for group in range(GROUPS):
            lanes = slice(128 * group, 128 * (group + 1))
            owned_ref[group * size : (group + 1) * size] = owner_ref[owner, :size, lanes]
        at, shift = divmod(owner * mine, 128)
        moved = owned_ref[...]
        if shift:
            moved = pltpu.roll(moved, shift, 1)
        wide[at] = wide[at] + jnp.where(lane >= shift, moved, 0.0)
        if shift + mine > 128:
            wide[at + 1] = wide[at + 1] + jnp.where(lane < shift, moved, 0.0)
    for at, value in enumerate(wide):
        cols = slice(at * 128, (at + 1) * 128)
        third_ref[:, cols] = value[:hidden]
        skip_ref[:, cols] = value[hidden : hidden + 1]
    for tap in range(KS):
        for part in range(3):
            row = 3 * tap + part
            taps_ref[tap : tap + 1, part * width : (part + 1) * width] = sum_ref[row : row + 1]
    row = 3 * KS
    gain_one[...] = sum_ref[row : row + 1]
    gain_two[...] = sum_ref[row + 1 : row + 2]
    row += 2
    for group in range(GROUPS):
        lanes = slice(128 * group, 128 * (group + 1))
        hidden_ref[group * each : (group + 1) * each] = sum_ref[row : row + each, lanes]
    second_ref[...] = hidden_ref[:hidden, :hidden]
    first_ref[...] = hidden_ref[hidden : hidden + first_ref.shape[0], :hidden]


def run_unpack(count, mine, packed, got, hidden, embedded, after):
    width = packed.shape[1]
    owned, both = small_rows(hidden, embedded)
    shapes = (
        (hidden, width), (1, width), (KS, 3 * width), (1, width), (1, width), (hidden, hidden),
        (embedded, hidden),
    )
    return launch(
        partial(unpack_kernel, count, mine),
        (packed, got),
        [(shape, F32) for shape in shapes],
        scratch=[
            pltpu.VMEM((2 * count, OWNED, width), F32),
            pltpu.VMEM((SHARED, width), F32),
            pltpu.VMEM((owned, 128), F32),
            pltpu.VMEM((both, 128), F32),
        ],
        after=after,
    )


def mark(values):
    return launch(
        lambda *refs: None, values, (), in_specs=anywhere(len(values)), limit=FULL_BYTES
    )[1]


def hold(values, after):
    return launch(
        lambda *refs: None,
        values,
        [(value.shape, value.dtype) for value in values],
        in_specs=anywhere(len(values)),
        out_specs=anywhere(len(values)),
        limit=FULL_BYTES,
        after=after,
        aliases={i: i for i in range(len(values))},
    )[0]


class Group:
    def __init__(self, orders, line_bits, sent):
        self.orders, self.line_bits = orders, line_bits
        self.sent = sent
        self.got = self.swap(sent, 0)
        self.aways = [0]
        for bit in line_bits:
            self.aways += [away | bit for away in self.aways]
        self.direct = len(self.aways) == 4

    def bits(self, level):
        return self.orders[0][level], self.orders[1][level]

    def swap(self, pair, level):
        return tuple(swap(value, bit) for value, bit in zip(pair, self.bits(level)))

    def woven(self):
        return self.kept[0], self.got[0], self.kept[1], self.got[1]

    def halve(self, kept, after=(), estimate=SHORT):
        self.kept = kept
        (sent_a, next_a, sent_b, next_b), self.token = run_halve(
            self.bits(1), self.woven(), after, estimate
        )
        self.kept, self.sent = (next_a, next_b), (sent_a, sent_b)
        self.got = self.swap(self.sent, 1)

    def scatter(self, small=None, after=(), estimate=SHORT):
        self.shapes = [part.shape for part in self.kept]
        self.small = small
        if self.direct:
            (sent, self.line_kept), self.token = run_scatter(
                self.woven(), self.line_bits[0], small, after, estimate
            )
            self.line_got = swap(sent, self.line_bits[0])
        else:
            self.shares = tuple(
                halve(add(kept, got), lax.axis_index(AXES), self.line_bits[::-1], 1)
                for kept, got in zip(self.kept, self.got)
            )

    def split(self, after=(), estimate=SHORT):
        (sent, self.line_kept), self.token = run_split(
            self.line_bits[1], self.line_kept, self.line_got, after, estimate
        )
        self.line_got = swap(sent, self.line_bits[1])

    def total(self, after=(), estimate=SHORT):
        (self.share,), self.token = run_total(
            (self.line_kept, self.line_got), self.small, after, estimate
        )
        self.line_got = swap(self.share, self.line_bits[1])

    def pair(self, after=(), estimate=SHORT):
        (self.share,), self.token = run_pair(
            self.line_bits[1], self.share, self.line_got, after, estimate
        )
        self.line_got = swap(self.share, self.line_bits[0])

    def gather(self, after=()):
        if self.direct:
            made, self.token = run_gather(
                self.line_bits[0], self.share, self.line_got, self.shapes,
                self.small is not None, after,
            )
            self.mine = made[:2]
            if self.small is not None:
                self.small = made[2]
        else:
            self.mine = tuple(
                double(share, lax.axis_index(AXES), self.line_bits[::-1], 1)
                for share in self.shares
            )
        self.got = self.swap(self.mine, 1)

    def join(self, after=()):
        self.mine, self.token = run_join(
            self.bits(1), (self.mine[0], self.got[0], self.mine[1], self.got[1]), after
        )
        self.got = self.swap(self.mine, 0)
        self.mine_core = tuple(swap(value, 1) for value in self.mine)
        self.outs = ()

    def join_last(self, after=()):
        self.mine, self.token = run_join(
            self.bits(1), (self.mine[0], self.got[0], self.mine[1], self.got[1]), after
        )
        self.got = self.swap(self.mine, 0)

    def stack(self, after=()):
        _, rows, width = self.mine[0].shape
        (self.whole,), self.token = launch(
            partial(stack_kernel, self.bits(0)),
            (*self.mine, *self.got),
            [((2, 2 * rows, width), BF16)],
            after=after,
        )
        self.other = swap(self.whole, 1)

    def place_whole(self, kernel, shape, after=()):
        width = self.whole.shape[2]
        (out,), self.token = launch(
            kernel,
            (self.whole, self.other),
            [(shape, F32)],
            in_specs=anywhere(2),
            out_specs=hbm(1),
            scratch=[
                pltpu.VMEM((SLOTS, PLACE, width), BF16),
                pltpu.VMEM((SLOTS, PLACE, width), F32),
                pltpu.SemaphoreType.DMA((2 * SLOTS,)),
            ],
            limit=WHOLE_BYTES,
            after=after,
        )
        return out

    def place(self, kernel, shapes, after=()):
        self.outs, self.token = run_place(
            kernel, self.bits(0), (False,), (*self.mine, *self.mine_core), (), shapes, after
        )

    def finish(self, kernel, shapes, after=(), held=()):
        if held:
            self.got = hold(self.got, held)
        got_core = tuple(swap(value, 1) for value in self.got)
        sides, sources = (True,), (*self.got, *got_core)
        if not self.outs:
            sides, sources = (False, True), (*self.mine, *self.mine_core, *sources)
        outs, self.token = run_place(
            kernel, self.bits(0), sides, sources, self.outs, shapes, after
        )
        return outs


def per_device(
    hidden_in, lengths, gain_one, in_weight, short_kernel, skip_gain, decay_rate, filt_first,
    filt_second, filt_third, out_weight, gain_two, ff_up, ff_down, out_grad,
):
    rows, block, width = hidden_in.shape
    seq_count, seq_pos = lax.axis_size("seq"), lax.axis_index("seq")
    dp_count = lax.axis_size("dp")
    index = lax.axis_index(AXES)
    units = ff_up.shape[1]
    row_len = block * seq_count
    tokens = rows * block
    seq_bits = [1 << i for i in range(1, seq_count.bit_length() - 1)]
    dp_bits = [seq_count << i for i in range(dp_count.bit_length() - 1)]
    mine = width // seq_count
    padded = -(-mine // 16) * 16
    groups = seq_count if mine == padded and (width // 2) % mine == 0 else 1

    forward, inverse = spectral_tables(block)
    forward_two, inverse_three = jnp.asarray(two_pass(forward)), jnp.asarray(three_pass(inverse))
    forward_three, inverse_two = jnp.asarray(three_pass(forward.T)), jnp.asarray(two_pass(inverse.T))

    before = shifted(hidden_in[:, block - 2 :], 1)
    after = shifted(hidden_in[:, :2], -1)
    normed_one, extended, outer, signal_sent = run_front(
        lengths, hidden_in, before, after, gain_one[None], short_kernel, in_weight, groups
    )
    signal_ch = to_owner(signal_sent, mine, padded)

    signal_sent, filt_first, decay_rate, skip_gain = lax.optimization_barrier(
        (signal_sent, filt_first, decay_rate, skip_gain)
    )
    bands = (filt_first.shape[0] - 1) // 2
    spots = np.arange(row_len)
    turns = (np.arange(1, bands + 1)[:, None] * spots[None, :] % row_len) * (2.0 * math.pi / row_len)
    embedding = jnp.asarray(
        np.concatenate([spots[None, :] / row_len, np.cos(turns), np.sin(turns)], axis=0).astype(
            np.float32
        )
    )
    pre_one = jnp.einsum("ef,el->fl", filt_first, embedding, precision=FULL_PRECISION)
    act_one = jnp.sin(pre_one)
    pre_two = jnp.einsum("fg,fl->gl", filt_second, act_one, precision=FULL_PRECISION)
    act_two = jnp.sin(pre_two)
    my_third = lax.dynamic_slice_in_dim(filt_third, seq_pos * mine, mine, 1)
    my_decay = lax.dynamic_slice_in_dim(decay_rate, seq_pos * mine, mine, 0)
    my_skip = lax.dynamic_slice_in_dim(skip_gain, seq_pos * mine, mine, 0)
    my_skip = jnp.pad(my_skip, (0, padded - mine))[:, None]
    places = jnp.asarray(spots.astype(np.float32))
    envelope = jnp.exp(-my_decay[:, None] * places[None, :]) * row_len ** (-0.5)
    taps = jnp.einsum("gc,gl->cl", my_third, act_two, precision=FULL_PRECISION) * envelope
    taps = taps.reshape(mine, seq_count, block).transpose(1, 0, 2)
    if padded != mine:
        taps = jnp.pad(taps, ((0, 0), (0, padded - mine), (0, 0)))
    pieces = jnp.einsum("kct,tf->kcf", taps, jnp.asarray(forward), precision=FULL_PRECISION)
    sign = jnp.asarray(np.tile(1.0 - 2.0 * (np.arange(block) % 2), 2).astype(np.float32))
    earlier = jnp.concatenate([jnp.zeros_like(pieces[:1]), pieces[:-1]], axis=0)
    spectrum = earlier + sign * pieces
    spec_real, spec_imag = spectrum[..., :block], spectrum[..., block:]
    base = jnp.arange(block) == 0
    spectrum = (
        spec_real,
        jnp.where(base, 0.0, spec_imag),
        jnp.where(base, spec_imag, spec_real),
    )

    conv_ch, _ = run_conv(
        lengths, row_len, signal_ch, my_skip, spectrum, forward_two, inverse_three
    )
    conv = to_block(conv_ch, rows, mine, groups)
    if groups == 1:
        conv = conv[0]

    upstream = out_grad.reshape(tokens, width)
    upstream_got = swap(upstream, 1)
    (
        gain_two_grad, factors_mine, factors_theirs, block_out, last_mine, last_theirs, grad_middle,
        grad_outer, grad_sent,
    ) = run_middle(
        conv, mine, outer, hidden_in, gain_two[None], upstream, out_weight, ff_up, ff_down, groups
    )
    factors_got = swap(factors_theirs, 1)
    grad_ch = to_owner(grad_sent, mine, padded)
    orders = (dp_bits, dp_bits[::-1])
    firsts = (orders[0][0], orders[1][0])
    shape = (1, width // 2, width)
    up_operands = (factors_mine, factors_got)
    down_operands = (factors_mine, factors_got, upstream, upstream_got)
    up_sent, token = run_up_products(firsts, True, up_operands, shape)
    up = Group(orders, seq_bits, up_sent)
    down_sent, token = run_down_products(firsts, True, down_operands, shape, (token,))
    down = Group(orders, seq_bits, down_sent)
    outer_halo = shifted(grad_outer[:, :2], -1)

    back_ch, token = run_conv(
        lengths, row_len, grad_ch, my_skip, spectrum, forward_three, inverse_two, backward=True,
        after=(token,),
    )
    got = to_block(back_ch, rows, mine, groups)
    grad_signal, got = (got, got) if groups > 1 else got
    halo = got[:, 0, padded : padded + 2 * rows, :mine].astype(F32)
    halo = halo.transpose(1, 0, 2).reshape(rows, 2, width)
    last_got, normed_got = swap(last_theirs, 1), swap(normed_one, 1)
    up_kept, token = run_up_products(firsts, False, up_operands, shape, (token,))
    up.halve(up_kept)
    down_kept, token = run_down_products(firsts, False, down_operands, shape, (up.token,))
    down.halve(down_kept)
    up.scatter(None, (down.token,), BRIDGE_A)

    (proj_mine, proj_theirs, kernel_grad, gain_one_grad, input_grad), token = run_last(
        lengths, grad_signal, mine, halo, extended, grad_outer, outer_halo, hidden_in,
        gain_one[None], short_kernel, grad_middle, in_weight, (up.token,) if up.direct else (),
    )
    last_operands = (normed_one, normed_got, proj_mine, swap(proj_theirs, 1), last_mine, last_got)
    if up.direct:
        up.split((token,))
    down.scatter(None, (up.token,), BRIDGE_B)
    last_sent, token = run_last_products(
        firsts, True, last_operands, shape, (down.token,) if up.direct else ()
    )
    last = Group(orders, seq_bits, last_sent)
    last_kept, token = run_last_products(firsts, False, last_operands, shape, (token,))

    grad_taps, token = run_filter_grad(
        lengths, row_len, signal_ch, grad_ch, forward_two, inverse_two, forward_three,
        after=(token,),
    )
    envelope = jnp.pad(envelope, ((0, padded - mine), (0, 0)))
    my_third = jnp.pad(my_third, ((0, 0), (0, padded - mine)))
    net = (act_one, pre_one, act_two, pre_two)
    (my_third_grad, skip_grad, second_grad, first_grad), token = run_filter_back(
        grad_taps, envelope, net, my_third, filt_second, embedding, (token,)
    )
    small = (
        my_third_grad[:, :mine], skip_grad[:1, :mine], kernel_grad, gain_one_grad, gain_two_grad,
        second_grad, first_grad,
    )
    in_shapes = (in_weight.shape, out_weight.shape)
    if up.direct:
        (packed,), token = run_pack(dp_count, *small)
        arrived = lax.all_to_all(packed, "dp", 0, 0, tiled=True)
        up.total((token,))
        down.split((up.token,))
        last.halve(last_kept, (down.token,))
        up.pair((last.token,))
        down.total((up.token,))
        (packed,), token = run_total_all(arrived, (down.token,))
        last.scatter(packed, (token,))
        up.gather((last.token,))
        down.pair((up.token,))
        last.split((down.token,))
        up.join_last((last.token,))
        down.gather((up.token,))
        last.total((down.token,))
        down.join_last((last.token,))
        last.pair((down.token,))
        up.stack((last.token,))
        last.gather((up.token, mark(down.got)))
        up_total = up.place_whole(up_place_kernel, ff_up.shape, (last.token,))
        last.join((up.token,))
        down.stack((last.token,))
        last.place(last_place_kernel, in_shapes, (down.token,))
        down_total = down.place_whole(down_place_kernel, ff_down.shape, (last.token,))
        small, token = run_unpack(
            4, mine, last.small, swap(last.small, 1), filt_third.shape[0],
            filt_first.shape[0], (down.token,),
        )
        in_total, out_total = last.finish(last_place_kernel, in_shapes, (), (token,))
    else:
        last.halve(last_kept)
        last.scatter()
        for group in (up, down):
            group.gather()
            group.join_last()
            group.stack()
        last.gather()
        last.join()
        up_total = up.place_whole(up_place_kernel, ff_up.shape)
        down_total = down.place_whole(down_place_kernel, ff_down.shape)
        in_total, out_total = last.finish(last_place_kernel, in_shapes)
        spread = [
            lax.dynamic_update_slice_in_dim(
                jnp.zeros((part.shape[0], width), F32), part, seq_pos * mine, 1
            )
            for part in small[:2]
        ]
        small = lax.psum((*spread, small[2][:KS], *small[3:]), AXES)
    return (
        block_out, input_grad, small[3][0], in_total, small[2], small[1][0], small[6], small[5],
        small[0], out_total, small[4][0], up_total, down_total,
    )


def solution(mesh):
    tokens = P("dp", "seq", None)
    return jax.shard_map(
        per_device,
        mesh=mesh,
        in_specs=(tokens, P("dp", None)) + (P(),) * 12 + (tokens,),
        out_specs=(tokens, tokens) + (P(),) * 11,
        check_vma=False,
    )
```

```python
from functools import partial
import math

import jax
import jax.numpy as jnp
import numpy as np
from jax import lax
from jax.experimental import pallas as pl
from jax.experimental.pallas import tpu as pltpu
from jax.sharding import PartitionSpec as P

FULL_PRECISION = lax.Precision.HIGHEST
BF16 = jnp.bfloat16
F32 = jnp.float32
AXES = ("dp", "seq")
VMEM_BYTES = 32 * 1024 * 1024
FULL_BYTES = 54 * 1024 * 1024
PLACE_BYTES = 57 * 1024 * 1024
WHOLE_BYTES = 55 * 1024 * 1024
KS = 3


def swap(value, bit):
    count = lax.axis_size(AXES)
    return lax.ppermute(value, AXES, [(i, i ^ bit) for i in range(count)])


def shifted(value, steps):
    count = lax.axis_size("seq")
    first, last = max(0, -steps), min(count, count - steps)
    return lax.ppermute(value, "seq", [(i, i + steps) for i in range(first, last)])


def my_bit(index, bit):
    return (index // bit) % 2


def add(kept, got):
    return (kept.astype(F32) + got.astype(F32)).astype(kept.dtype)


def halve(value, index, bits, axis):
    for bit in bits:
        size = value.shape[axis] // 2
        mine = my_bit(index, bit)
        keep = lax.dynamic_slice_in_dim(value, mine * size, size, axis)
        send = lax.dynamic_slice_in_dim(value, (1 - mine) * size, size, axis)
        value = add(keep, swap(send, bit))
    return value


def double(value, index, bits, axis):
    for bit in reversed(bits):
        other = swap(value, bit)
        low = my_bit(index, bit) == 0
        value = jnp.concatenate(
            [jnp.where(low, value, other), jnp.where(low, other, value)], axis=axis
        )
    return value


def sum_over(value, bits):
    for bit in bits:
        value = value + swap(value, bit)
    return value


def spectral_tables(block):
    points = 2 * block
    spot = np.arange(block)
    freq = np.arange(block)
    angle = (spot[:, None] * freq[None, :] % points) * (2.0 * math.pi / points)
    real, imag = np.cos(angle), -np.sin(angle)
    imag[:, 0] = 1.0 - 2.0 * (spot % 2)
    forward = np.concatenate([real, imag], axis=1)
    late = spot + block
    angle = (freq[:, None] * late[None, :] % points) * (2.0 * math.pi / points)
    weight = np.where(freq == 0, 1.0, 2.0)[:, None] / points
    real, imag = weight * np.cos(angle), -weight * np.sin(angle)
    imag[0, :] = (1.0 - 2.0 * (late % 2)) / points
    inverse = np.concatenate([real, imag], axis=0)
    return forward.astype(np.float32), inverse.astype(np.float32)


def split_table(table):
    high = table.astype(jnp.bfloat16)
    low = (table - high.astype(np.float32)).astype(jnp.bfloat16)
    return np.asarray(high), np.asarray(low)


def two_pass(table):
    high, low = split_table(table)
    return np.concatenate([high, low], axis=0)


def three_pass(table):
    high, low = split_table(table)
    return np.concatenate([high, high, low], axis=0)


def ends_of(lengths_ref, row):
    total, ends = 0, []
    for k in range(lengths_ref.shape[1]):
        total = total + lengths_ref[row, k]
        ends.append(total)
    return ends


def next_end(ends, spot, row_len):
    found = row_len
    for end in reversed(ends):
        found = jnp.where(end > spot, end, found)
    return found


def last_end(ends, spot):
    found = 0
    for end in ends:
        found = jnp.where(end <= spot, end, found)
    return found


def near_mask(ends, spots, step):
    apart = spots < step
    for end in ends:
        apart = apart | ((end <= spots) & (end > spots - step))
    return jnp.where(apart, 0.0, 1.0)


def dot(left, right):
    return jnp.dot(left, right, preferred_element_type=F32)


def dot_nt(left, right):
    return lax.dot_general(left, right, (((1,), (1,)), ((), ())), preferred_element_type=F32)


def head_masks(ends, spot, group, rows, block, row_len):
    lane = lax.broadcasted_iota(jnp.int32, (1, 1, block), 2)
    masks = []
    for g in range(group):
        start = (spot + g) // rows * block
        stop = jnp.where((spot + g) % rows == 0, next_end(ends[0], start, row_len), 0)
        for row in range(1, rows):
            stop = jnp.where(
                (spot + g) % rows == row, next_end(ends[row], start, row_len), stop
            )
        masks.append(jnp.where(lane < stop - start, 1.0, 0.0))
    return jnp.concatenate(masks, axis=0)


def spectra(value_ref, masks, table_ref, head_out, rest_out, group):
    count, channels, block = value_ref.shape

    def step(i, carry):
        spot = pl.ds(i * group, group)
        whole = value_ref[spot].astype(F32)
        first = whole * masks(i * group)
        both = jnp.concatenate([first, whole - first], axis=0).astype(BF16)
        both = both.reshape(2 * group * channels, block)
        found = dot(jnp.concatenate([both, both], axis=1), table_ref[...])
        found = found.reshape(2 * group, channels, 2 * block)
        head_out[spot] = found[:group]
        rest_out[spot] = found[group:]
        return carry

    lax.fori_loop(0, count // group, step, 0)


def back_to_time(head_spec, rest_spec, masks, table_ref, value_ref, skip_ref, group, store):
    count, channels, double_block = head_spec.shape

    def step(i, carry):
        spot = pl.ds(i * group, group)
        both = jnp.concatenate([head_spec[spot], rest_spec[spot]], axis=0)
        both = both.reshape(2 * group * channels, double_block)
        high = both.astype(BF16)
        low = (both - high.astype(F32)).astype(BF16)
        found = dot(jnp.concatenate([high, low, high], axis=1), table_ref[...])
        found = found.reshape(2 * group, channels, double_block // 2)
        rest = found[group:]
        found = rest + masks(i * group) * (found[:group] - rest)
        store(i * group, found + skip_ref[...][None] * value_ref[spot].astype(F32))
        return carry

    lax.fori_loop(0, count // group, step, 0)


def of_row(per_row, row):
    found = per_row[0]
    for k in range(1, len(per_row)):
        found = jnp.where(row == k, per_row[k], found)
    return found


def start_loads(moves, sems):
    loads = [
        pltpu.make_async_copy(source, target, sems.at[i])
        for i, (source, target) in enumerate(moves)
    ]
    for load in loads:
        load.start()
    return loads


def conv_kernel(
    rows, group, row_len, lengths_ref, value_ref, skip_hbm, hr_hbm, hi_hbm, hm_hbm,
    forward_hbm, inverse_hbm, out_ref, skip_ref, hr_ref, hi_ref, hm_ref, forward_ref, inverse_ref,
    sems, head_spec, rest_spec, head_sum, rest_sum,
):
    count, channels, block = value_ref.shape
    loads = start_loads(
        [
            (forward_hbm, forward_ref), (hr_hbm, hr_ref), (hi_hbm, hi_ref), (hm_hbm, hm_ref),
            (inverse_hbm, inverse_ref), (skip_hbm, skip_ref),
        ],
        sems,
    )
    ends = [ends_of(lengths_ref, row) for row in range(rows)]

    def masks(spot):
        return head_masks(ends, spot, group, rows, block, row_len)

    loads[0].wait()
    spectra(value_ref, masks, forward_ref, head_spec, rest_spec, group)
    for load in loads[1:]:
        load.wait()

    def product(real, imag, lag):
        hr, hi, hm = hr_ref[lag], hi_ref[lag], hm_ref[lag]
        return real * hr - imag * hi, real * hi + imag * hm

    def own(j, carry):
        start = j // rows * block
        stop = of_row([next_end(e, start, row_len) for e in ends], j % rows)
        plain = (stop >= start + block).astype(F32)
        head_real, head_imag = product(head_spec[j, :, :block], head_spec[j, :, block:], 0)
        head_sum[j, :, :block] = head_real
        head_sum[j, :, block:] = head_imag
        rest_real, rest_imag = product(rest_spec[j, :, :block], rest_spec[j, :, block:], 0)
        rest_sum[j, :, :block] = rest_real
        rest_sum[j, :, block:] = rest_imag
        rest_spec[j] = rest_spec[j] + plain * head_spec[j]
        return carry

    lax.fori_loop(0, count, own, 0)

    def reach(j, carry):
        spot, row = j // rows, j % rows
        begin = of_row([last_end(e, spot * block) for e in ends], row) // block

        def include(source, sums):
            k = source * rows + row
            real, imag = product(
                rest_spec[k, :, :block], rest_spec[k, :, block:], spot - source
            )
            return sums[0] + real, sums[1] + imag

        start = (head_sum[j, :, :block], head_sum[j, :, block:])
        real, imag = lax.fori_loop(begin, spot, include, start)
        head_sum[j, :, :block] = real
        head_sum[j, :, block:] = imag
        return carry

    lax.fori_loop(rows, count, reach, 0)

    def store(spot, found):
        out_ref[pl.ds(spot, group)] = found.astype(BF16)

    back_to_time(head_sum, rest_sum, masks, inverse_ref, value_ref, skip_ref, group, store)


def conv_back_kernel(
    rows, group, row_len, lengths_ref, value_ref, skip_hbm, hr_hbm, hi_hbm, hm_hbm,
    forward_hbm, inverse_hbm, out_ref, skip_ref, hr_ref, hi_ref, hm_ref, forward_ref, inverse_ref,
    sems, head_spec, rest_spec, head_sum, rest_sum, found_ref,
):
    count, channels, block = value_ref.shape
    loads = start_loads(
        [
            (inverse_hbm, inverse_ref), (hr_hbm, hr_ref), (hi_hbm, hi_ref), (hm_hbm, hm_ref),
            (forward_hbm, forward_ref), (skip_hbm, skip_ref),
        ],
        sems,
    )
    ends = [ends_of(lengths_ref, row) for row in range(rows)]

    def masks(spot):
        return head_masks(ends, spot, group, rows, block, row_len)

    loads[0].wait()
    spectra(value_ref, masks, inverse_ref, head_spec, rest_spec, group)
    for load in loads[1:]:
        load.wait()

    def product(real, imag, lag):
        hr, hi, hm = hr_ref[lag], hi_ref[lag], hm_ref[lag]
        return real * hr + imag * hi, imag * hm - real * hi

    def reach(j, carry):
        spot, row = j // rows, j % rows
        start = spot * block
        plain = of_row([next_end(e, start, row_len) for e in ends], row) >= start + block
        plain = plain.astype(F32)
        until = of_row([next_end(e, start + block - 1, row_len) for e in ends], row)
        until = (until - 1) // block + 1

        def include(source, sums):
            k = source * rows + row
            real, imag = product(
                head_spec[k, :, :block], head_spec[k, :, block:], source - spot
            )
            return sums[0] + real, sums[1] + imag

        empty = jnp.zeros((channels, block), F32)
        real, imag = lax.fori_loop(spot + 1, until, include, (empty, empty))
        head_real, head_imag = product(head_spec[j, :, :block], head_spec[j, :, block:], 0)
        head_sum[j, :, :block] = head_real + plain * real
        head_sum[j, :, block:] = head_imag + plain * imag
        rest_real, rest_imag = product(rest_spec[j, :, :block], rest_spec[j, :, block:], 0)
        rest_sum[j, :, :block] = rest_real + (1.0 - plain) * real
        rest_sum[j, :, block:] = rest_imag + (1.0 - plain) * imag
        return carry

    lax.fori_loop(0, count, reach, 0)

    def store(spot, found):
        found_ref[pl.ds(spot, group)] = found
        out_ref[pl.ds(spot, group), :channels] = found.astype(BF16)

    back_to_time(head_sum, rest_sum, masks, forward_ref, value_ref, skip_ref, group, store)

    lane = lax.broadcasted_iota(jnp.int32, (channels, block), 1)
    per_turn = block // 2
    blocks = count // rows
    for turn in range(-(-count // per_turn)):
        first = turn * per_turn
        last = min(count, first + per_turn)

        def gather(j, picked):
            at = 2 * (j - first)
            moved = pltpu.roll(found_ref[j], at, 1)
            return jnp.where((lane >= at) & (lane < at + 2), moved, picked)

        picked = lax.fori_loop(first, last, gather, jnp.zeros((channels, block), F32))
        if channels < block:
            picked = jnp.concatenate(
                [picked, jnp.zeros((block - channels, block), F32)], axis=0
            )
        flipped = picked.T
        for spot in range(first // rows, last // rows):
            at = 2 * (spot * rows - first)
            tile = jnp.concatenate(
                [flipped[at : at + 2 * rows], jnp.zeros((16 - 2 * rows, block), F32)], axis=0
            )
            if spot > 0:
                out_ref[(spot - 1) * rows, channels:] = tile.astype(BF16)
    out_ref[(blocks - 1) * rows, channels:] = jnp.zeros((16, block), BF16)
    for spot in range(blocks):
        for row in range(1, rows):
            out_ref[spot * rows + row, channels:] = jnp.zeros((16, block), BF16)


def filter_grad_kernel(
    rows, group, row_len, lengths_ref, value_ref, grad_ref, forward_ref,
    inverse_ref, back_ref, out_ref, head_spec, rest_spec, grad_head, grad_rest, total,
):
    count, channels, block = value_ref.shape
    lags = count // rows
    ends = [ends_of(lengths_ref, row) for row in range(rows)]

    def masks(spot):
        return head_masks(ends, spot, group, rows, block, row_len)

    spectra(value_ref, masks, forward_ref, head_spec, rest_spec, group)
    spectra(grad_ref, masks, inverse_ref, grad_head, grad_rest, group)
    lane = lax.broadcasted_iota(jnp.int32, (channels, block), 1)
    base = lane == 0

    def product(grad, spec, k, j):
        gr, gi = grad[k, :, :block], grad[k, :, block:]
        sr, si = spec[j, :, :block], spec[j, :, block:]
        masked = jnp.where(base, 0.0, si)
        swapped = jnp.where(base, si, sr)
        return gr * sr + gi * masked, gi * swapped - gr * masked

    def own(j, sums):
        start = j // rows * block
        stop = of_row([next_end(e, start, row_len) for e in ends], j % rows)
        plain = (stop >= start + block).astype(F32)
        head = product(grad_head, head_spec, j, j)
        rest = product(grad_rest, rest_spec, j, j)
        rest_spec[j] = rest_spec[j] + plain * head_spec[j]
        return sums[0] + head[0] + rest[0], sums[1] + head[1] + rest[1]

    empty = jnp.zeros((channels, block), F32)
    real, imag = lax.fori_loop(0, count, own, (empty, empty))
    total[0, :, :block] = real
    total[0, :, block:] = imag

    def one_lag(lag, carry):
        def include(j, sums):
            spot = j // rows
            begin = of_row([last_end(e, spot * block) for e in ends], j % rows) // block
            near = (begin <= spot - lag).astype(F32)
            real, imag = product(grad_head, rest_spec, j, j - lag * rows)
            return sums[0] + near * real, sums[1] + near * imag

        real, imag = lax.fori_loop(lag * rows, count, include, (empty, empty))
        total[lag, :, :block] = real
        total[lag, :, block:] = imag
        return carry

    lax.fori_loop(1, lags, one_lag, 0)
    wide = lax.broadcasted_iota(jnp.int32, (channels, 2 * block), 1)
    sign = (1 - 2 * (wide % 2)).astype(F32)
    total[lags] = jnp.zeros((channels, 2 * block), F32)

    def one_piece(lag, carry):
        piece = total[lag + 1] + sign * total[lag]
        high = piece.astype(BF16)
        low = (piece - high.astype(F32)).astype(BF16)
        out_ref[lag] = dot(jnp.concatenate([high, low, high], axis=1), back_ref[...])
        return carry

    lax.fori_loop(0, lags, one_piece, 0)


def vmem(count):
    return [pl.BlockSpec(memory_space=pltpu.VMEM)] * count


def smem(count):
    return [pl.BlockSpec(memory_space=pltpu.SMEM)] * count


def hbm(count):
    return [pl.BlockSpec(memory_space=pltpu.HBM)] * count


def anywhere(count):
    return [pl.BlockSpec(memory_space=pl.ANY)] * count


def params(limit=VMEM_BYTES):
    return pltpu.CompilerParams(vmem_limit_bytes=limit)


SHORT = pl.CostEstimate(flops=1, bytes_accessed=1, transcendentals=0)


def takes(micro):
    return pl.CostEstimate(flops=int(micro * 1e9), bytes_accessed=1, transcendentals=0)


BRIDGE_A, BRIDGE_B = takes(2), takes(12)
LINE = takes(8)

TOKEN = (12288, 1024), F32


def launch(
    kernel, operands, outs, in_specs=None, out_specs=None, scratch=(), limit=VMEM_BYTES, after=(),
    aliases=None, estimate=SHORT,
):
    used, made = len(operands), len(outs)

    def call(*refs):
        rest = refs[used + len(after) :]
        kernel(*refs[:used], *rest[:made], *rest[made + 1 :])

    results = pl.pallas_call(
        call,
        name=getattr(kernel, "func", kernel).__name__.replace("<lambda>", "hold"),
        out_shape=tuple(jax.ShapeDtypeStruct(*out) for out in (*outs, TOKEN)),
        in_specs=(vmem(used) if in_specs is None else in_specs) + anywhere(len(after)),
        out_specs=tuple((vmem(made) if out_specs is None else out_specs) + hbm(1)),
        scratch_shapes=list(scratch),
        input_output_aliases=aliases or {},
        compiler_params=params(limit),
        cost_estimate=estimate,
    )(*operands, *after)
    return tuple(results[:-1]), results[-1]


def run_conv(
    lengths, row_len, value, skip, spectrum, forward, inverse, backward=False, after=()
):
    count, channels, block = value.shape
    rows = lengths.shape[0]
    group = 4 if count % 4 == 0 else 1
    spec = pltpu.VMEM((count, channels, 2 * block), F32)
    extra = [pltpu.VMEM((count, channels, block), F32)] if backward else []
    sent = channels + 16 if backward else channels
    (found,), token = launch(
        partial(conv_back_kernel if backward else conv_kernel, rows, group, row_len),
        (lengths, value, skip, *spectrum, forward, inverse),
        [((count, sent, block), BF16)],
        in_specs=smem(1) + vmem(1) + anywhere(6),
        scratch=[
            *[pltpu.VMEM(part.shape, part.dtype) for part in (skip, *spectrum, forward, inverse)],
            pltpu.SemaphoreType.DMA((6,)),
            *[spec] * 4,
            *extra,
        ],
        after=after,
    )
    return found, token


def run_filter_grad(lengths, row_len, value, grad, forward, inverse, back, after=()):
    count, channels, block = value.shape
    rows = lengths.shape[0]
    group = 4 if count % 4 == 0 else 1
    lags = count // rows
    spec = pltpu.VMEM((count, channels, 2 * block), F32)
    (found,), token = launch(
        partial(filter_grad_kernel, rows, group, row_len),
        (lengths, value, grad, forward, inverse, back),
        [((lags, channels, block), F32)],
        in_specs=smem(1) + vmem(5),
        scratch=[spec] * 4 + [pltpu.VMEM((lags + 1, channels, 2 * block), F32)],
        after=after,
    )
    return found, token


def exact(left, right, contract):
    return lax.dot_general(
        left, right, (contract, ((), ())), precision=FULL_PRECISION, preferred_element_type=F32
    )


def filter_back_kernel(
    taps_ref, envelope_ref, act_one_ref, pre_one_ref, act_two_ref, pre_two_ref, third_ref,
    second_ref, embedding_ref, third_grad, skip_grad, second_grad, first_grad,
):
    lags, channels, block = taps_ref.shape
    pick = lax.broadcasted_iota(jnp.int32, (8, block), 1) == 0
    skip_grad[...] = exact(jnp.where(pick, 1.0, 0.0), taps_ref[0], ((1,), (1,)))
    third_grad[...] = jnp.zeros(third_grad.shape, F32)
    second_grad[...] = jnp.zeros(second_grad.shape, F32)
    first_grad[...] = jnp.zeros(first_grad.shape, F32)

    def one_lag(lag, carry):
        here = pl.ds(pl.multiple_of(lag * block, 128), block)
        grad = taps_ref[lag] * envelope_ref[:, here]
        third_grad[...] += exact(act_two_ref[:, here], grad, ((1,), (1,)))
        grad = jnp.cos(pre_two_ref[:, here]) * exact(third_ref[...], grad, ((1,), (0,)))
        second_grad[...] += exact(act_one_ref[:, here], grad, ((1,), (1,)))
        grad = jnp.cos(pre_one_ref[:, here]) * exact(second_ref[...], grad, ((1,), (0,)))
        first_grad[...] += exact(embedding_ref[:, here], grad, ((1,), (1,)))
        return carry

    lax.fori_loop(0, lags, one_lag, 0)


def run_filter_back(taps, envelope, net, third, second, embedding, after):
    hidden, channels = third.shape
    return launch(
        filter_back_kernel,
        (taps, envelope, *net, third, second, embedding),
        [
            ((hidden, channels), F32),
            ((8, channels), F32),
            ((hidden, hidden), F32),
            ((embedding.shape[0], hidden), F32),
        ],
        after=after,
    )


def put_channels(ref, row, chunk, value):
    groups, _, size, _ = ref.shape
    wide = value.shape[0]
    if groups == 1:
        ref[0, row, chunk * wide : (chunk + 1) * wide] = value
    else:
        per = wide // size
        for k in range(per):
            ref[chunk * per + k, row] = value[k * size : (k + 1) * size]


def get_channels(ref, row, chunk, wide, size):
    groups = ref.shape[0]
    if groups == 1:
        return ref[0, row, chunk * wide : (chunk + 1) * wide]
    per = wide // size
    return jnp.concatenate([ref[chunk * per + k, row, :size] for k in range(per)], axis=0)


def moments(value):
    center = value - jnp.mean(value, axis=-1, keepdims=True)
    spread = jnp.mean(center * center, axis=-1, keepdims=True)
    return center, lax.rsqrt(spread + 1e-05)


def norm_back(center, scale, gain, grad):
    unit = center * scale
    inner = grad * gain
    mean_one = jnp.mean(inner, axis=-1, keepdims=True)
    mean_two = jnp.mean(inner * unit, axis=-1, keepdims=True)
    return scale * (inner - mean_one - unit * mean_two), grad * unit


PIECE = 64


def front_kernel(
    lengths_ref, before_ref, after_ref, gain_ref, hidden_hbm, taps_hbm, weight_hbm,
    normed_hbm, extended_hbm, outer_hbm, sent_hbm,
    hidden_ref, taps_ref, weight_ref, normed_ref, extended_ref, outer_ref, sent_ref,
    halo_ref, wide_ref, mixed_ref, sems,
):
    rows, block, width = hidden_ref.shape
    loads = [
        pltpu.make_async_copy(source, target, sems.at[i])
        for i, (source, target) in enumerate(
            [(hidden_hbm, hidden_ref), (weight_hbm, weight_ref), (taps_hbm, taps_ref)]
        )
    ]
    for load in loads:
        load.start()
    gain = gain_ref[...]
    halo = jnp.concatenate(
        [part for row in range(rows) for part in (before_ref[row], after_ref[row])], axis=0
    ).astype(F32)
    center, scale = moments(halo)
    halo = center * scale * gain
    halo_ref[...] = jnp.concatenate(
        [halo, jnp.zeros((halo_ref.shape[0] - 4 * rows, width), F32)], axis=0
    ).astype(BF16)
    first = lax.axis_index("seq") * block
    ends = [ends_of(lengths_ref, row) for row in range(rows)]
    spots = first + lax.broadcasted_iota(jnp.int32, (block, 1), 0)
    near_one = [near_mask(e, spots, 1) for e in ends]
    near_two = [near_mask(e, spots, 2) for e in ends]
    live = [jnp.where(spots < e[-1], 1.0, 0.0) for e in ends]
    loads[0].wait()
    for row in range(rows):
        for start in range(0, block, PIECE):
            center, scale = moments(hidden_ref[row, start : start + PIECE].astype(F32))
            at = row * block + start
            normed_ref[at : at + PIECE] = (center * scale * gain).astype(BF16)
    saves = [
        pltpu.make_async_copy(source, target, sems.at[3 + i])
        for i, (source, target) in enumerate(
            [
                (normed_ref, normed_hbm),
                (sent_ref, sent_hbm),
                (extended_ref, extended_hbm),
                (outer_ref, outer_hbm),
            ]
        )
    ]
    saves[0].start()
    chunk = width // 2
    loads[1].wait()
    loads[2].wait()
    for part in range(3):
        for half in range(2):
            cols = slice(part * width + half * chunk, part * width + (half + 1) * chunk)
            main = dot(normed_ref[...], weight_ref[:, cols])
            edge = dot(halo_ref[...], weight_ref[:, cols])
            taps = taps_ref[:, cols]
            for row in range(rows):
                wide_ref[row, 0:8] = jnp.zeros((8, chunk), F32)
                wide_ref[row, block + 8 :] = jnp.zeros((8, chunk), F32)
                wide_ref[row, 6:8] = edge[4 * row : 4 * row + 2]
                wide_ref[row, 8 : block + 8] = main[row * block : (row + 1) * block]
                wide_ref[row, block + 8 : block + 10] = edge[4 * row + 2 : 4 * row + 4]
                rounded = wide_ref[row].astype(BF16)
                extended_ref[row, :, cols] = rounded
                wide_ref[row] = rounded.astype(F32)
                mixed = (
                    taps[0:1] * wide_ref[row, 8 : block + 8]
                    + taps[1:2] * wide_ref[row, 7 : block + 7] * near_one[row]
                    + taps[2:3] * wide_ref[row, 6 : block + 6] * near_two[row]
                )
                here = slice(half * chunk, (half + 1) * chunk)
                if part == 0:
                    mixed_ref[row, :, here] = mixed
                elif part == 1:
                    signal = mixed_ref[row, :, here] * mixed * live[row]
                    put_channels(sent_ref, row, half, signal.T.astype(BF16))
                else:
                    outer_ref[row, :, here] = mixed
        if part == 1:
            saves[1].start()
    saves[2].start()
    saves[3].start()
    for save in saves:
        save.wait()


def run_front(lengths, hidden, before, after, gain, taps, weight, groups):
    rows, block, width = hidden.shape
    chunk = width // 2
    outs = (
        ((rows * block, width), BF16),
        ((rows, block + 16, 3 * width), BF16),
        ((rows, block, width), F32),
        ((groups, rows, width // groups, block), BF16),
    )
    return pl.pallas_call(
        front_kernel,
        out_shape=tuple(jax.ShapeDtypeStruct(*out) for out in outs),
        in_specs=smem(1) + vmem(3) + hbm(3),
        out_specs=tuple(hbm(4)),
        scratch_shapes=[
            pltpu.VMEM(hidden.shape, BF16),
            pltpu.VMEM(taps.shape, F32),
            pltpu.VMEM(weight.shape, BF16),
            *[pltpu.VMEM(*out) for out in outs],
            pltpu.VMEM((16, width), BF16),
            pltpu.VMEM((rows, block + 16, chunk), F32),
            pltpu.VMEM((rows, block, width), F32),
            pltpu.SemaphoreType.DMA((7,)),
        ],
        compiler_params=params(FULL_BYTES),
        cost_estimate=SHORT,
    )(lengths, before, after, gain, hidden, taps, weight)


def middle_kernel(
    size, conv_ref, gain_ref, outer_hbm, hidden_hbm, upstream_hbm, out_hbm, up_hbm, down_hbm,
    gain_grad_ref, factors_mine_hbm, factors_theirs_hbm, result_hbm, last_mine_hbm, last_theirs_hbm,
    grad_middle_hbm, grad_outer_hbm, sent_hbm,
    outer_ref, hidden_ref, upstream_ref, out_ref, up_ref, down_ref,
    factors_ref, result_ref, last_ref, grad_middle_ref, grad_outer_ref, sent_ref,
    conv_scr, middle_ref, grad_ref, sems,
):
    rows, block, width = hidden_ref.shape
    parts = down_ref.shape[0] // width
    per_core = parts // 2
    units = per_core * width
    chunk = width // 2
    core = lax.axis_index("seq") % 2
    copies = [
        pltpu.make_async_copy(outer_hbm, outer_ref, sems.at[0]),
        pltpu.make_async_copy(out_hbm, out_ref, sems.at[1]),
        pltpu.make_async_copy(hidden_hbm, hidden_ref, sems.at[2]),
        pltpu.make_async_copy(upstream_hbm, upstream_ref, sems.at[3]),
    ]
    for part in range(parts):
        cols = slice(part * width, (part + 1) * width)
        copies.append(
            pltpu.make_async_copy(up_hbm.at[:, cols], up_ref.at[:, cols], sems.at[2 * part + 4])
        )
        copies.append(
            pltpu.make_async_copy(down_hbm.at[cols], down_ref.at[cols], sems.at[2 * part + 5])
        )
    for copy in copies:
        copy.start()
    saves = [
        pltpu.make_async_copy(source, target, sems.at[2 * parts + 4 + i])
        for i, (source, target) in enumerate(
            [
                (result_ref, result_hbm),
                (grad_middle_ref, grad_middle_hbm),
                (last_ref.at[0], last_mine_hbm),
                (last_ref.at[1], last_theirs_hbm),
                (sent_ref, sent_hbm),
                (grad_outer_ref, grad_outer_hbm),
                (factors_ref.at[1], factors_theirs_hbm),
                (factors_ref.at[0], factors_mine_hbm),
            ]
        )
    ]
    for row in range(rows):
        here = slice(row * block, (row + 1) * block)
        for half in range(2):
            cols = slice(half * chunk, (half + 1) * chunk)
            conv_scr[here, cols] = get_channels(conv_ref, row, half, chunk, size).astype(F32).T
    copies[0].wait()
    for row in range(rows):
        here = slice(row * block, (row + 1) * block)
        gated = (outer_ref[row] * conv_scr[here]).astype(BF16)
        last_ref[0, here, :width] = gated
        last_ref[1, here, :width] = gated
    copies[1].wait()
    middle_ref[...] = dot(last_ref[0, :, :width], out_ref[...])
    copies[2].wait()
    gain = gain_ref[...]
    normed = slice(2 * units, 2 * units + width)
    for row in range(rows):
        for start in range(0, block, PIECE):
            here = slice(row * block + start, row * block + start + PIECE)
            middle = middle_ref[here] + hidden_ref[row, start : start + PIECE].astype(F32)
            middle_ref[here] = middle
            center, scale = moments(middle)
            rounded = (center * scale * gain).astype(BF16)
            factors_ref[0, here, normed] = rounded
            factors_ref[1, here, normed] = rounded
    slope = math.sqrt(2.0 / math.pi)
    copies[3].wait()
    for part in range(parts):
        cols = slice(part * width, (part + 1) * width)
        copies[2 * part + 4].wait()
        pre = dot(factors_ref[0, :, normed], up_ref[:, cols])
        copies[2 * part + 5].wait()
        grad_act = dot_nt(upstream_ref[...], down_ref[cols])
        square = pre * pre
        bend = jnp.tanh(slope * pre * (1.0 + 0.044715 * square))
        half_up = 0.5 * (1.0 + bend)
        act = (pre * half_up).astype(BF16)
        turn = half_up + 0.5 * pre * (1.0 - bend * bend) * (
            slope * (1.0 + 3.0 * 0.044715 * square)
        )
        grad_pre = (grad_act * turn).astype(BF16)
        slot = (part // per_core + core) % 2
        at = part % per_core * width
        factors_ref[slot, :, at : at + width] = act
        factors_ref[slot, :, units + at : units + at + width] = grad_pre
        if part == 0:
            grad_ref[...] = dot_nt(grad_pre, up_ref[:, cols])
        else:
            grad_ref[...] += dot_nt(grad_pre, up_ref[:, cols])
        found = dot(act, down_ref[cols])
        for row in range(rows):
            here = slice(row * block, (row + 1) * block)
            if part == 0:
                grad_middle_ref[here] = middle_ref[here] + found[here]
            elif part < parts - 1:
                grad_middle_ref[here] += found[here]
            else:
                result_ref[row] = (grad_middle_ref[here] + found[here]).astype(BF16)
    saves[6].start()
    saves[7].start()
    saves[0].start()
    gain_grad = jnp.zeros((1, width), F32)
    branch_cols = slice(width, width + chunk)
    for at in range(0, rows * block, PIECE):
        here = slice(at, at + PIECE)
        center, scale = moments(middle_ref[here])
        grad, terms = norm_back(center, scale, gain, grad_ref[here])
        gain_grad = gain_grad + jnp.sum(terms, axis=0, keepdims=True)
        grad = upstream_ref[here].astype(F32) + grad
        grad_middle_ref[here] = grad
        branch = grad.astype(BF16)

        last_ref[core, here, branch_cols] = branch[:, :chunk]
        last_ref[1 - core, here, branch_cols] = branch[:, chunk:]

    for save in saves[1:4]:
        save.start()
    gain_grad_ref[...] = gain_grad
    grad_ref[...] = dot_nt(grad_middle_ref[...].astype(BF16), out_ref[...])
    for row in range(rows):
        here = slice(row * block, (row + 1) * block)
        for half in range(2):
            cols = slice(half * chunk, (half + 1) * chunk)
            grad_conv = grad_ref[here, cols] * outer_ref[row, :, cols]
            put_channels(sent_ref, row, half, grad_conv.T.astype(BF16))
    saves[4].start()
    for row in range(rows):
        here = slice(row * block, (row + 1) * block)
        grad_outer_ref[row] = grad_ref[here] * conv_scr[here]
    saves[5].start()
    for save in saves:
        save.wait()


def run_middle(conv, size, outer, hidden, gain, upstream, out_weight, up, down, groups, after):
    rows, block, width = hidden.shape
    tokens = rows * block
    units = up.shape[1]
    parts = units // width
    near = (((1, width), F32),)
    far = (
        ((tokens, units + width), BF16),
        ((tokens, units + width), BF16),
        ((rows, block, width), BF16),
        ((tokens, 3 * width // 2), BF16),
        ((tokens, 3 * width // 2), BF16),
        ((tokens, width), F32),
        ((rows, block, width), F32),
        ((groups, rows, width // groups, block), BF16),
    )
    return pl.pallas_call(
        lambda *refs: middle_kernel(size, *refs[:8], *refs[9:]),
        out_shape=tuple(jax.ShapeDtypeStruct(*out) for out in near + far),
        in_specs=vmem(2) + hbm(6) + anywhere(1),
        out_specs=tuple(vmem(1) + hbm(8)),
        scratch_shapes=[
            pltpu.VMEM(outer.shape, F32),
            pltpu.VMEM(hidden.shape, BF16),
            pltpu.VMEM(upstream.shape, BF16),
            pltpu.VMEM(out_weight.shape, BF16),
            pltpu.VMEM(up.shape, BF16),
            pltpu.VMEM(down.shape, BF16),
            pltpu.VMEM((2, *far[0][0]), BF16),
            pltpu.VMEM(*far[2]),
            pltpu.VMEM((2, *far[3][0]), BF16),
            *[pltpu.VMEM(*out) for out in far[5:]],
            pltpu.VMEM((tokens, width), F32),
            pltpu.VMEM((tokens, width), F32),
            pltpu.VMEM((tokens, width), F32),
            pltpu.SemaphoreType.DMA((2 * parts + 12,)),
        ],
        compiler_params=params(FULL_BYTES),
        cost_estimate=SHORT,
    )(conv, gain, outer, hidden, upstream, out_weight, up, down, after)


def last_kernel(
    size, lengths_ref, signal_ref, halo_ref, outer_halo_ref, gain_ref, taps_ref,
    extended_hbm, outer_hbm, hidden_hbm, grad_middle_hbm, weight_hbm,
    proj_mine, proj_theirs, taps_grad_ref, gain_grad_ref, result_hbm,
    extended_ref, outer_ref, hidden_ref, grad_middle_ref, weight_ref, result_ref,
    wide_ref, mixed_ref, grad_ref, proj_ref, normed_grad, sems,
):
    rows, block, width = hidden_ref.shape
    chunk = width // 2
    loads = [
        pltpu.make_async_copy(source, target, sems.at[i])
        for i, (source, target) in enumerate(
            [
                (extended_hbm, extended_ref),
                (outer_hbm, outer_ref),
                (weight_hbm, weight_ref),
                (hidden_hbm, hidden_ref),
                (grad_middle_hbm, grad_middle_ref),
            ]
        )
    ]
    for load in loads:
        load.start()
    core = lax.axis_index("seq") % 2
    first = lax.axis_index("seq") * block
    longer = block + 8
    spots = first + lax.broadcasted_iota(jnp.int32, (longer, 1), 0)
    taps_grad_ref[...] = jnp.zeros(taps_grad_ref.shape, F32)
    loads[0].wait()
    loads[1].wait()
    for row in range(rows):
        ends = ends_of(lengths_ref, row)
        near_one, near_two = near_mask(ends, spots, 1), near_mask(ends, spots, 2)
        live = jnp.where(spots < ends[-1], 1.0, 0.0)
        for half in range(2):
            cols = slice(half * chunk, (half + 1) * chunk)
            grad_ref[0, :block] = get_channels(signal_ref, row, half, chunk, size).astype(F32).T
            grad_ref[0, block:] = jnp.concatenate(
                [halo_ref[row, :, cols], jnp.zeros((6, chunk), F32)], axis=0
            )
            for part in range(2):
                at = slice(part * width + half * chunk, part * width + (half + 1) * chunk)
                taps = taps_ref[:, at]
                wide_ref[part] = extended_ref[row, :, at].astype(F32)
                mixed_ref[part] = (
                    taps[0:1] * wide_ref[part, 8 : longer + 8]
                    + taps[1:2] * wide_ref[part, 7 : longer + 7] * near_one
                    + taps[2:3] * wide_ref[part, 6 : longer + 6] * near_two
                )
            at = slice(2 * width + half * chunk, 2 * width + (half + 1) * chunk)
            wide_ref[2] = extended_ref[row, :, at].astype(F32)
            signal_grad = grad_ref[0] * live
            grad_ref[0] = signal_grad * mixed_ref[1]
            grad_ref[1] = signal_grad * mixed_ref[0]
            grad_ref[2, :block] = outer_ref[row, :, cols]
            grad_ref[2, block:] = jnp.concatenate(
                [outer_halo_ref[row, :, cols], jnp.zeros((6, chunk), F32)], axis=0
            )
            for part in range(3):
                at = slice(part * width + half * chunk, part * width + (half + 1) * chunk)
                taps = taps_ref[:, at]
                own = grad_ref[part, :block]
                proj = (
                    taps[0:1] * own
                    + taps[1:2] * (grad_ref[part, 1 : block + 1] * near_one[1 : block + 1])
                    + taps[2:3] * (grad_ref[part, 2 : block + 2] * near_two[2 : block + 2])
                )
                proj_ref[row * block : (row + 1) * block, at] = proj.astype(BF16)
                taps_grad_ref[0:1, at] += jnp.sum(
                    own * wide_ref[part, 8 : block + 8], axis=0, keepdims=True
                )
                taps_grad_ref[1:2, at] += jnp.sum(
                    own * wide_ref[part, 7 : block + 7] * near_one[:block], axis=0, keepdims=True
                )
                taps_grad_ref[2:3, at] += jnp.sum(
                    own * wide_ref[part, 6 : block + 6] * near_two[:block], axis=0, keepdims=True
                )
    middle = 3 * width // 2

    @pl.when(core == 0)
    def _():
        proj_mine[...] = proj_ref[:, :middle]
        proj_theirs[...] = proj_ref[:, middle:]

    @pl.when(core != 0)
    def _():
        proj_mine[...] = proj_ref[:, middle:]
        proj_theirs[...] = proj_ref[:, :middle]

    loads[2].wait()
    normed_grad[...] = dot_nt(proj_ref[...], weight_ref[...])
    loads[3].wait()
    loads[4].wait()
    gain = gain_ref[...]
    gain_grad = jnp.zeros((1, width), F32)
    for row in range(rows):
        for start in range(0, block, PIECE):
            here = slice(row * block + start, row * block + start + PIECE)
            center, scale = moments(hidden_ref[row, start : start + PIECE].astype(F32))
            grad, terms = norm_back(center, scale, gain, normed_grad[here])
            gain_grad = gain_grad + jnp.sum(terms, axis=0, keepdims=True)
            result_ref[row, start : start + PIECE] = grad_middle_ref[here] + grad
    gain_grad_ref[...] = gain_grad
    save = pltpu.make_async_copy(result_ref, result_hbm, sems.at[5])
    save.start()
    save.wait()


def run_last(
    lengths, signal, size, halo, extended, outer, outer_halo, hidden, gain, taps, grad_middle,
    weight, after,
):
    rows, block, width = hidden.shape
    tokens = rows * block
    chunk = width // 2
    middle = 3 * width // 2
    return launch(
        partial(last_kernel, size),
        (
            lengths, signal, halo, outer_halo, gain, taps, extended, outer, hidden, grad_middle,
            weight,
        ),
        [
            ((tokens, middle), BF16),
            ((tokens, middle), BF16),
            ((8, 3 * width), F32),
            ((1, width), F32),
            (hidden.shape, F32),
        ],
        in_specs=smem(1) + vmem(5) + hbm(5),
        out_specs=vmem(4) + hbm(1),
        scratch=[
            pltpu.VMEM(extended.shape, BF16),
            pltpu.VMEM(outer.shape, F32),
            pltpu.VMEM(hidden.shape, BF16),
            pltpu.VMEM(grad_middle.shape, F32),
            pltpu.VMEM(weight.shape, BF16),
            pltpu.VMEM(hidden.shape, F32),
            pltpu.VMEM((3, block + 16, chunk), F32),
            pltpu.VMEM((2, block + 8, chunk), F32),
            pltpu.VMEM((3, block + 8, chunk), F32),
            pltpu.VMEM((tokens, 3 * width), BF16),
            pltpu.VMEM((tokens, width), F32),
            pltpu.SemaphoreType.DMA((6,)),
        ],
        limit=FULL_BYTES,
        after=after,
    )


def to_owner(sent, mine, padded):
    count = lax.axis_size("seq")
    groups, rows, size, block = sent.shape
    if groups != count:
        sent = sent.reshape(rows, count, mine, block).transpose(1, 0, 2, 3)
    got = lax.all_to_all(sent, "seq", 0, 0, tiled=True).reshape(count * rows, mine, block)
    if padded != mine:
        got = jnp.pad(got, ((0, 0), (0, padded - mine), (0, 0)))
    return got


def to_block(value, rows, mine, groups):
    count = lax.axis_size("seq")
    size, block = value.shape[1:]
    got = lax.all_to_all(
        value.reshape(count, rows, size, block), "seq", 0, 0, tiled=True
    )
    if groups == count:
        return got
    return got[:, :, :mine].transpose(1, 0, 2, 3).reshape(1, rows, count * mine, block), got


def dot_tn(left, right):
    return lax.dot_general(left, right, (((0,), (0,)), ((), ())), preferred_element_type=F32)


def bit_inside(bit):
    count = lax.axis_size("seq")
    if bit < count:
        return lax.axis_index("seq") // bit % 2
    return lax.axis_index("dp") // (bit // count) % 2


def side(bit, sent):
    mine = bit_inside(bit)
    return 1 - mine if sent else mine


def up_products_kernel(
    bits, sent, mine_hbm, got_hbm, a_ref, b_ref, left_ref, right_ref, sems
):
    _, rows, width = a_ref.shape
    units = 2 * width
    moves = []
    for part in range(2):
        at = pl.multiple_of(2 * units + side(bits[part], sent) * rows, 128)
        cols = slice(units + part * width, units + (part + 1) * width)
        for i, factors in enumerate((mine_hbm, got_hbm)):
            moves.append((factors.at[:, pl.ds(at, rows)], left_ref.at[part, i]))
            moves.append((factors.at[:, cols], right_ref.at[part, i]))
    loads = start_loads(moves, sems)
    for part, out in enumerate((a_ref, b_ref)):
        for load in loads[4 * part : 4 * part + 4]:
            load.wait()
        found = dot_tn(left_ref[part, 0], right_ref[part, 0]) + dot_tn(
            left_ref[part, 1], right_ref[part, 1]
        )
        out[0] = found.astype(BF16)


def down_products_kernel(
    bits, sent, mine_hbm, got_hbm, upstream_hbm, upstream_got_hbm, a_ref, b_ref,
    left_ref, right_ref, sems,
):
    _, rows, width = a_ref.shape
    moves = [(upstream_hbm, right_ref.at[0]), (upstream_got_hbm, right_ref.at[1])]
    for part in range(2):
        at = pl.multiple_of(part * width + side(bits[part], sent) * rows, 128)
        for i, factors in enumerate((mine_hbm, got_hbm)):
            moves.append((factors.at[:, pl.ds(at, rows)], left_ref.at[part, i]))
    loads = start_loads(moves, sems)
    loads[0].wait()
    loads[1].wait()
    for part, out in enumerate((a_ref, b_ref)):
        loads[2 * part + 2].wait()
        loads[2 * part + 3].wait()
        found = dot_tn(left_ref[part, 0], right_ref[0]) + dot_tn(left_ref[part, 1], right_ref[1])
        out[0] = found.astype(BF16)


def last_products_kernel(
    bits, sent, normed_ref, normed_got_ref, proj_ref, proj_got_ref, last_ref, last_got_ref,
    a_ref, b_ref,
):
    rows, width = a_ref.shape[1:]
    half = width // 2
    at = pl.multiple_of(side(bits[0], sent) * rows, 128)
    found = dot_tn(normed_ref[:, pl.ds(at, rows)], proj_ref[:, :width]) + dot_tn(
        normed_got_ref[:, pl.ds(at, rows)], proj_got_ref[:, :width]
    )
    a_ref[0] = found.astype(BF16)
    at = pl.multiple_of(side(bits[1], sent) * rows, 128)
    found = dot_tn(normed_ref[:, pl.ds(at, rows)], proj_ref[:, width:]) + dot_tn(
        normed_got_ref[:, pl.ds(at, rows)], proj_got_ref[:, width:]
    )
    b_ref[0, :, :half] = found.astype(BF16)
    found = dot_tn(last_ref[:, pl.ds(at, rows)], last_ref[:, width:]) + dot_tn(
        last_got_ref[:, pl.ds(at, rows)], last_got_ref[:, width:]
    )
    b_ref[0, :, half:] = found.astype(BF16)


def run_up_products(bits, sent, operands, shape, after=()):
    tokens, (_, rows, width) = operands[0].shape[0], shape
    return launch(
        partial(up_products_kernel, bits, sent),
        operands,
        [(shape, BF16)] * 2,
        in_specs=anywhere(2),
        scratch=[
            pltpu.VMEM((2, 2, tokens, rows), BF16),
            pltpu.VMEM((2, 2, tokens, width), BF16),
            pltpu.SemaphoreType.DMA((8,)),
        ],
        limit=FULL_BYTES,
        after=after,
    )


def run_down_products(bits, sent, operands, shape, after=()):
    tokens, (_, rows, width) = operands[0].shape[0], shape
    return launch(
        partial(down_products_kernel, bits, sent),
        operands,
        [(shape, BF16)] * 2,
        in_specs=anywhere(4),
        scratch=[
            pltpu.VMEM((2, 2, tokens, rows), BF16),
            pltpu.VMEM((2, tokens, width), BF16),
            pltpu.SemaphoreType.DMA((6,)),
        ],
        limit=FULL_BYTES,
        after=after,
    )


def run_last_products(bits, sent, operands, shape, after=()):
    return launch(
        partial(last_products_kernel, bits, sent),
        operands,
        [(shape, BF16)] * 2,
        after=after,
    )


STEP = 96


def steps(rows):
    step = STEP if rows % STEP == 0 else rows
    return [(start, step) for start in range(0, rows, step)]


def halve_kernel(
    bits, kept_a, got_a, kept_b, got_b, sent_a, next_a, sent_b, next_b,
    kept_a_ref, got_a_ref, kept_b_ref, got_b_ref, sems,
):
    moves, work = [], []
    for sent, outs in ((True, (sent_a, sent_b)), (False, (next_a, next_b))):
        for bit, out, kept, got, kept_ref, got_ref in (
            (bits[0], outs[0], kept_a, got_a, kept_a_ref, got_a_ref),
            (bits[1], outs[1], kept_b, got_b, kept_b_ref, got_b_ref),
        ):
            rows = out.shape[1]
            at = pl.ds(pl.multiple_of(side(bit, sent) * rows, 16), rows)
            slot = slice(0, rows) if sent else slice(rows, 2 * rows)
            moves.append((kept.at[:, at], kept_ref.at[:, slot]))
            moves.append((got.at[:, at], got_ref.at[:, slot]))
            work.append((out, kept_ref, got_ref, 0 if sent else rows))
    loads = start_loads(moves, sems)
    for i, (out, kept_ref, got_ref, first) in enumerate(work):
        loads[2 * i].wait()
        loads[2 * i + 1].wait()
        for block in range(out.shape[0]):
            for start, step in steps(out.shape[1]):
                at = slice(first + start, first + start + step)
                total = kept_ref[block, at].astype(F32) + got_ref[block, at].astype(F32)
                out[block, start : start + step] = total.astype(BF16)


def run_halve(bits, parts, after=(), estimate=SHORT):
    def half(array):
        return (array.shape[0], array.shape[1] // 2, array.shape[2]), BF16

    return launch(
        partial(halve_kernel, bits),
        parts,
        [half(parts[0]), half(parts[0]), half(parts[2]), half(parts[2])],
        in_specs=anywhere(4),
        scratch=[
            *[pltpu.VMEM(part.shape, BF16) for part in parts],
            pltpu.SemaphoreType.DMA((8,)),
        ],
        limit=FULL_BYTES,
        after=after,
        estimate=estimate,
    )


SHARED, OWNED = 32, 16
GROUPS = 6
EXTRA = 16


def line_spot():
    return lax.axis_index("seq") // 2


def pieces_of(a_ref, b_ref, count):
    at = 0
    for ref in (a_ref, b_ref):
        blocks, rows, _ = ref.shape
        size = rows // count
        for block in range(blocks):
            yield ref, block, size, at
            at += size


def scatter_kernel(with_small, bit, *refs):
    kept_a, got_a, kept_b, got_b = refs[:4]
    for out, sent in zip(refs[-2:], (True, False)):
        half = out.shape[0] // 2
        for high in range(2):
            place = 2 * high + side(bit, sent)
            for (kept, block, size, at), (got, _, _, _) in zip(
                pieces_of(kept_a, kept_b, 4), pieces_of(got_a, got_b, 4)
            ):
                rows = pl.ds(pl.multiple_of(place * size, 16), size)
                total = kept[block, rows].astype(F32) + got[block, rows].astype(F32)
                out[high * half + at : high * half + at + size] = total.astype(BF16)
            if with_small:
                at = (high + 1) * half - EXTRA
                size = SHARED // 4
                part = refs[4][pl.ds(pl.multiple_of(place * size, 8), size)]
                part = jnp.concatenate(
                    [part, jnp.zeros((EXTRA - size, part.shape[1]), F32)], axis=0
                )
                out[at : at + EXTRA] = part.astype(BF16)


def run_scatter(parts, bit, small=None, after=(), estimate=SHORT):
    share = sum(part.shape[0] * part.shape[1] for part in (parts[0], parts[2])) // 4
    share += 0 if small is None else EXTRA
    return launch(
        partial(scatter_kernel, small is not None, bit),
        parts if small is None else (*parts, small),
        [((2 * share, parts[0].shape[2]), BF16)] * 2,
        after=after,
        estimate=estimate,
    )


def split_kernel(bit, kept, got, sent, following):
    rows = sent.shape[0]
    for out, which in ((sent, side(bit, True)), (following, side(bit, False))):
        at = pl.ds(pl.multiple_of(which * rows, 16), rows)
        out[...] = (kept[at].astype(F32) + got[at].astype(F32)).astype(BF16)


def run_split(bit, kept, got, after=(), estimate=SHORT):
    rows, width = kept.shape
    return launch(
        partial(split_kernel, bit),
        (kept, got),
        [((rows // 2, width), BF16)] * 2,
        after=after,
        estimate=estimate,
    )


def pair_kernel(bit, mine, got, out):
    rows = mine.shape[0]
    out[pl.ds(pl.multiple_of(side(bit, False) * rows, 16), rows)] = mine[...]
    out[pl.ds(pl.multiple_of(side(bit, True) * rows, 16), rows)] = got[...]


def run_pair(bit, mine, got, after=(), estimate=SHORT):
    rows, width = mine.shape
    return launch(
        partial(pair_kernel, bit),
        (mine, got),
        [((2 * rows, width), BF16)],
        after=after,
        estimate=estimate,
    )


def total_kernel(with_small, *refs):
    *parts, out = refs
    if with_small:
        *parts, small = parts
    rows_in = parts[0].shape[0]
    for start, step in steps(rows_in):
        rows = slice(start, start + step)
        total = parts[0][rows].astype(F32)
        for part in parts[1:]:
            total = total + part[rows].astype(F32)
        out[rows] = total.astype(out.dtype)
    if with_small:
        out[rows_in:] = small[SHARED:].astype(out.dtype)


def run_total(parts, small=None, after=(), estimate=SHORT):
    rows, width = parts[0].shape
    return launch(
        partial(total_kernel, small is not None),
        parts if small is None else (*parts, small),
        [((rows if small is None else rows + OWNED, width), parts[0].dtype)],
        after=after,
        estimate=estimate,
    )


def total_all_kernel(parts, out):
    count, rows_in, _ = parts.shape
    for start, step in steps(rows_in):
        rows = slice(start, start + step)
        total = parts[0, rows].astype(F32)
        for place in range(1, count):
            total = total + parts[place, rows].astype(F32)
        out[rows] = total.astype(out.dtype)


def run_total_all(parts, after, kind=F32):
    return launch(total_all_kernel, (parts,), [(parts.shape[1:], kind)], after=after)


def gather_kernel(with_small, bit, mine, got, *outs):
    half = mine.shape[0] // 2
    for pair, sent in ((mine, False), (got, True)):
        for high in range(2):
            place = 2 * high + side(bit, sent)
            for out, block, size, at in pieces_of(outs[0], outs[1], 4):
                rows = pl.ds(pl.multiple_of(place * size, 16), size)
                out[block, rows] = pair[high * half + at : high * half + at + size]
            if with_small:
                at = (high + 1) * half - EXTRA - OWNED
                size = SHARED // 4
                shared = pair[at : at + EXTRA].astype(F32)[:size]
                outs[2][pl.ds(pl.multiple_of(place * size, 8), size)] = shared
                rows = pl.ds(pl.multiple_of(SHARED + place * OWNED, 8), OWNED)
                outs[2][rows] = pair[at + EXTRA : at + EXTRA + OWNED].astype(F32)


def run_gather(bit, mine, got, shapes, with_small, after=(), estimate=SHORT):
    outs = [(shape, BF16) for shape in shapes]
    if with_small:
        outs.append(((SHARED + 4 * OWNED, mine.shape[1]), F32))
    return launch(
        partial(gather_kernel, with_small, bit), (mine, got), outs, after=after, estimate=estimate
    )


def join_kernel(bits, mine_a, got_a, mine_b, got_b, out_a, out_b):
    for bit, mine, got, out in (
        (bits[0], mine_a, got_a, out_a),
        (bits[1], mine_b, got_b, out_b),
    ):
        blocks, rows, _ = mine.shape
        for source, which in ((mine, side(bit, False)), (got, side(bit, True))):
            at = pl.ds(pl.multiple_of(which * rows, 16), rows)
            for block in range(blocks):
                out[block, at] = source[block]


def run_join(bits, parts, after=()):
    def twice(array):
        return (array.shape[0], array.shape[1] * 2, array.shape[2]), BF16

    return launch(
        partial(join_kernel, bits), parts, [twice(parts[0]), twice(parts[2])], after=after
    )


PLACE = 192
SLOTS = 4


def place_all(moves, narrow, wide, sems):
    loads, stores = [], []

    def load(i):
        source, _ = moves[i]
        rows, cols = source.shape
        copy = pltpu.make_async_copy(
            source, narrow.at[i % SLOTS, :rows, :cols], sems.at[i % SLOTS]
        )
        copy.start()
        loads.append(copy)

    for i in range(min(SLOTS, len(moves))):
        load(i)
    for i, (source, target) in enumerate(moves):
        rows, cols = source.shape
        slot = i % SLOTS
        loads[i].wait()
        if i >= SLOTS:
            stores[i - SLOTS].wait()
        wide[slot, :rows, :cols] = narrow[slot, :rows, :cols].astype(F32)
        copy = pltpu.make_async_copy(wide.at[slot, :rows, :cols], target, sems.at[SLOTS + slot])
        copy.start()
        stores.append(copy)
        if i + SLOTS < len(moves):
            load(i + SLOTS)
    for copy in stores[-SLOTS:]:
        copy.wait()


def stack_kernel(bits, mine_a, mine_b, got_a, got_b, out):
    for part, (mine, got) in enumerate(((mine_a, got_a), (mine_b, got_b))):
        rows = mine.shape[1]
        for source, sent in ((mine, False), (got, True)):
            at = pl.ds(pl.multiple_of(side(bits[part], sent) * rows, 16), rows)
            out[part, at] = source[0]


def up_place_kernel(mine, other, out_hbm, narrow, wide, sems):
    core = lax.axis_index("seq") % 2
    moves = []
    for source, owner in ((mine, core), (other, 1 - core)):
        parts, rows, width = source.shape
        for part in range(parts):
            col = pl.multiple_of((2 * owner + part) * width, 128)
            for row in range(0, rows, PLACE):
                target = out_hbm.at[row : row + PLACE, pl.ds(col, width)]
                moves.append((source.at[part, row : row + PLACE], target))
    place_all(moves, narrow, wide, sems)


def down_place_kernel(mine, other, out_hbm, narrow, wide, sems):
    core = lax.axis_index("seq") % 2
    moves = []
    for source, owner in ((mine, core), (other, 1 - core)):
        parts, rows, _ = source.shape
        for part in range(parts):
            for start in range(0, rows, PLACE):
                row = pl.multiple_of((2 * owner + part) * rows + start, 16)
                target = out_hbm.at[pl.ds(row, PLACE)]
                moves.append((source.at[part, start : start + PLACE], target))
    place_all(moves, narrow, wide, sems)


def last_place_kernel(bits, sides, *refs):
    in_hbm, out_hbm, narrow, wide, sems = refs[-5:]
    core = lax.axis_index("seq") % 2
    moves = []
    for i, (sent, owner) in enumerate((s, o) for s in sides for o in (core, 1 - core)):
        source_a, source_b = refs[2 * i : 2 * i + 2]
        _, rows, width = source_a.shape
        half = width // 2
        for start in range(0, rows, PLACE):
            row = pl.multiple_of(side(bits[0], sent) * rows + start, 16)
            col = pl.multiple_of(owner * 3 * half, 128)
            moves.append(
                (
                    source_a.at[0, start : start + PLACE],
                    in_hbm.at[pl.ds(row, PLACE), pl.ds(col, width)],
                )
            )
            row = pl.multiple_of(side(bits[1], sent) * rows + start, 16)
            col = pl.multiple_of(owner * 3 * half + width, 128)
            moves.append(
                (
                    source_b.at[0, start : start + PLACE, :half],
                    in_hbm.at[pl.ds(row, PLACE), pl.ds(col, half)],
                )
            )
            col = pl.multiple_of(owner * half, 128)
            moves.append(
                (
                    source_b.at[0, start : start + PLACE, half:],
                    out_hbm.at[pl.ds(row, PLACE), pl.ds(col, half)],
                )
            )
    place_all(moves, narrow, wide, sems)


def run_place(kernel, bits, sides, sources, outs, shapes, after=()):
    width = sources[0].shape[2]
    return launch(
        partial(kernel, bits, sides),
        (*sources, *outs),
        [(shape, F32) for shape in shapes],
        in_specs=anywhere(len(sources)) + hbm(len(outs)),
        out_specs=hbm(len(shapes)),
        scratch=[
            pltpu.VMEM((SLOTS, PLACE, width), BF16),
            pltpu.VMEM((SLOTS, PLACE, width), F32),
            pltpu.SemaphoreType.DMA((2 * SLOTS,)),
        ],
        limit=PLACE_BYTES,
        after=after,
        aliases={len(sources) + i: i for i in range(len(outs))},
    )


def pack_kernel(
    third_ref, skip_ref, taps_ref, gain_one, gain_two, second_ref, first_ref, copies_ref,
    out_ref, owned_ref, hidden_ref,
):
    hidden, mine = third_ref.shape
    out_ref[...] = jnp.zeros(out_ref.shape, F32)
    width = out_ref.shape[1]
    for tap in range(KS):
        for part in range(3):
            row = 3 * tap + part
            out_ref[row : row + 1] = taps_ref[tap : tap + 1, part * width : (part + 1) * width]
    row = 3 * KS
    out_ref[row : row + 1] = gain_one[...]
    out_ref[row + 1 : row + 2] = gain_two[...]
    row += 2
    owned_ref[...] = jnp.zeros(owned_ref.shape, F32)
    owned_ref[:hidden, :mine] = third_ref[...]
    owned_ref[hidden : hidden + 1, :mine] = skip_ref[...]
    hidden_ref[...] = jnp.zeros(hidden_ref.shape, F32)
    hidden_ref[:hidden, :hidden] = second_ref[...]
    hidden_ref[hidden : hidden + first_ref.shape[0], :hidden] = first_ref[...]
    each, size = hidden_ref.shape[0] // GROUPS, owned_ref.shape[0] // GROUPS
    for group in range(GROUPS):
        lanes = slice(128 * group, 128 * (group + 1))
        out_ref[row : row + each, lanes] = hidden_ref[group * each : (group + 1) * each]
        out_ref[SHARED : SHARED + size, lanes] = owned_ref[group * size : (group + 1) * size]
    for copy in range(copies_ref.shape[0]):
        copies_ref[copy] = out_ref[...]


def small_rows(hidden, embedded):
    return -(-(hidden + 1) // GROUPS) * GROUPS, -(-(hidden + embedded) // GROUPS) * GROUPS


def run_pack(copies, third, skip, taps, gain_one, gain_two, second, first):
    owned, hidden = small_rows(second.shape[0], first.shape[0])
    return launch(
        pack_kernel,
        (third, skip, taps, gain_one, gain_two, second, first),
        [((copies, SHARED + OWNED, gain_one.shape[1]), F32)],
        scratch=[pltpu.VMEM((SHARED + OWNED, gain_one.shape[1]), F32), pltpu.VMEM((owned, 128), F32), pltpu.VMEM((hidden, 128), F32)],
    )


def unpack_kernel(
    count, mine, mine_ref, got_ref, third_ref, skip_ref, taps_ref, gain_one, gain_two, second_ref,
    first_ref, owner_ref, sum_ref, owned_ref, hidden_ref,
):
    hidden, width = third_ref.shape
    core = lax.axis_index("seq") % 2
    for spot in range(count):
        here = slice(SHARED + spot * OWNED, SHARED + (spot + 1) * OWNED)
        owner_ref[2 * spot + core] = mine_ref[here]
        owner_ref[2 * spot + 1 - core] = got_ref[here]
    sum_ref[...] = mine_ref[:SHARED] + got_ref[:SHARED]
    each, size = hidden_ref.shape[0] // GROUPS, owned_ref.shape[0] // GROUPS
    rows = owned_ref.shape[0]
    lane = lax.broadcasted_iota(jnp.int32, (rows, 128), 1)
    wide = [jnp.zeros((rows, 128), F32) for _ in range(width // 128)]
    for owner in range(2 * count):
        for group in range(GROUPS):
            lanes = slice(128 * group, 128 * (group + 1))
            owned_ref[group * size : (group + 1) * size] = owner_ref[owner, :size, lanes]
        at, shift = divmod(owner * mine, 128)
        moved = owned_ref[...]
        if shift:
            moved = pltpu.roll(moved, shift, 1)
        wide[at] = wide[at] + jnp.where(lane >= shift, moved, 0.0)
        if shift + mine > 128:
            wide[at + 1] = wide[at + 1] + jnp.where(lane < shift, moved, 0.0)
    for at, value in enumerate(wide):
        cols = slice(at * 128, (at + 1) * 128)
        third_ref[:, cols] = value[:hidden]
        skip_ref[:, cols] = value[hidden : hidden + 1]
    for tap in range(KS):
        for part in range(3):
            row = 3 * tap + part
            taps_ref[tap : tap + 1, part * width : (part + 1) * width] = sum_ref[row : row + 1]
    row = 3 * KS
    gain_one[...] = sum_ref[row : row + 1]
    gain_two[...] = sum_ref[row + 1 : row + 2]
    row += 2
    for group in range(GROUPS):
        lanes = slice(128 * group, 128 * (group + 1))
        hidden_ref[group * each : (group + 1) * each] = sum_ref[row : row + each, lanes]
    second_ref[...] = hidden_ref[:hidden, :hidden]
    first_ref[...] = hidden_ref[hidden : hidden + first_ref.shape[0], :hidden]


def run_unpack(count, mine, packed, got, hidden, embedded, after):
    width = packed.shape[1]
    owned, both = small_rows(hidden, embedded)
    shapes = (
        (hidden, width), (1, width), (KS, 3 * width), (1, width), (1, width), (hidden, hidden),
        (embedded, hidden),
    )
    return launch(
        partial(unpack_kernel, count, mine),
        (packed, got),
        [(shape, F32) for shape in shapes],
        scratch=[
            pltpu.VMEM((2 * count, OWNED, width), F32),
            pltpu.VMEM((SHARED, width), F32),
            pltpu.VMEM((owned, 128), F32),
            pltpu.VMEM((both, 128), F32),
        ],
        after=after,
    )


def mark(values):
    return launch(
        lambda *refs: None, values, (), in_specs=anywhere(len(values)), limit=FULL_BYTES
    )[1]


def hold(values, after):
    return launch(
        lambda *refs: None,
        values,
        [(value.shape, value.dtype) for value in values],
        in_specs=anywhere(len(values)),
        out_specs=anywhere(len(values)),
        limit=FULL_BYTES,
        after=after,
        aliases={i: i for i in range(len(values))},
    )[0]


class Group:
    def __init__(self, orders, line_bits, sent):
        self.orders, self.line_bits = orders, line_bits
        self.sent = sent
        self.got = self.swap(sent, 0)
        self.aways = [0]
        for bit in line_bits:
            self.aways += [away | bit for away in self.aways]
        self.direct = len(self.aways) == 4

    def bits(self, level):
        return self.orders[0][level], self.orders[1][level]

    def swap(self, pair, level):
        return tuple(swap(value, bit) for value, bit in zip(pair, self.bits(level)))

    def woven(self):
        return self.kept[0], self.got[0], self.kept[1], self.got[1]

    def halve(self, kept, after=(), estimate=SHORT):
        self.kept = kept
        (sent_a, next_a, sent_b, next_b), self.token = run_halve(
            self.bits(1), self.woven(), after, estimate
        )
        self.kept, self.sent = (next_a, next_b), (sent_a, sent_b)
        self.got = self.swap(self.sent, 1)

    def scatter(self, small=None, after=(), estimate=SHORT):
        self.shapes = [part.shape for part in self.kept]
        self.small = small
        if self.direct:
            (sent, self.line_kept), self.token = run_scatter(
                self.woven(), self.line_bits[0], small, after, estimate
            )
            self.line_got = swap(sent, self.line_bits[0])
        else:
            self.shares = tuple(
                halve(add(kept, got), lax.axis_index(AXES), self.line_bits[::-1], 1)
                for kept, got in zip(self.kept, self.got)
            )

    def split(self, after=(), estimate=SHORT):
        (sent, self.line_kept), self.token = run_split(
            self.line_bits[1], self.line_kept, self.line_got, after, estimate
        )
        self.line_got = swap(sent, self.line_bits[1])

    def total(self, after=(), estimate=SHORT):
        (self.share,), self.token = run_total(
            (self.line_kept, self.line_got), self.small, after, estimate
        )
        self.line_got = swap(self.share, self.line_bits[1])

    def pair(self, after=(), estimate=SHORT):
        (self.share,), self.token = run_pair(
            self.line_bits[1], self.share, self.line_got, after, estimate
        )
        self.line_got = swap(self.share, self.line_bits[0])

    def gather(self, after=()):
        if self.direct:
            made, self.token = run_gather(
                self.line_bits[0], self.share, self.line_got, self.shapes,
                self.small is not None, after,
            )
            self.mine = made[:2]
            if self.small is not None:
                self.small = made[2]
        else:
            self.mine = tuple(
                double(share, lax.axis_index(AXES), self.line_bits[::-1], 1)
                for share in self.shares
            )
        self.got = self.swap(self.mine, 1)

    def join(self, after=()):
        self.mine, self.token = run_join(
            self.bits(1), (self.mine[0], self.got[0], self.mine[1], self.got[1]), after
        )
        self.got = self.swap(self.mine, 0)
        self.mine_core = tuple(swap(value, 1) for value in self.mine)
        self.outs = ()

    def join_last(self, after=()):
        self.mine, self.token = run_join(
            self.bits(1), (self.mine[0], self.got[0], self.mine[1], self.got[1]), after
        )
        self.got = self.swap(self.mine, 0)

    def stack(self, after=()):
        _, rows, width = self.mine[0].shape
        (self.whole,), self.token = launch(
            partial(stack_kernel, self.bits(0)),
            (*self.mine, *self.got),
            [((2, 2 * rows, width), BF16)],
            after=after,
        )
        self.other = swap(self.whole, 1)

    def place_whole(self, kernel, shape, after=()):
        width = self.whole.shape[2]
        (out,), self.token = launch(
            kernel,
            (self.whole, self.other),
            [(shape, F32)],
            in_specs=anywhere(2),
            out_specs=hbm(1),
            scratch=[
                pltpu.VMEM((SLOTS, PLACE, width), BF16),
                pltpu.VMEM((SLOTS, PLACE, width), F32),
                pltpu.SemaphoreType.DMA((2 * SLOTS,)),
            ],
            limit=WHOLE_BYTES,
            after=after,
        )
        return out

    def place(self, kernel, shapes, after=()):
        self.outs, self.token = run_place(
            kernel, self.bits(0), (False,), (*self.mine, *self.mine_core), (), shapes, after
        )

    def finish(self, kernel, shapes, after=(), held=()):
        if held:
            self.got = hold(self.got, held)
        got_core = tuple(swap(value, 1) for value in self.got)
        sides, sources = (True,), (*self.got, *got_core)
        if not self.outs:
            sides, sources = (False, True), (*self.mine, *self.mine_core, *sources)
        outs, self.token = run_place(
            kernel, self.bits(0), sides, sources, self.outs, shapes, after
        )
        return outs


def per_device(
    hidden_in, lengths, gain_one, in_weight, short_kernel, skip_gain, decay_rate, filt_first,
    filt_second, filt_third, out_weight, gain_two, ff_up, ff_down, out_grad,
):
    rows, block, width = hidden_in.shape
    seq_count, seq_pos = lax.axis_size("seq"), lax.axis_index("seq")
    dp_count = lax.axis_size("dp")
    index = lax.axis_index(AXES)
    units = ff_up.shape[1]
    row_len = block * seq_count
    tokens = rows * block
    seq_bits = [1 << i for i in range(1, seq_count.bit_length() - 1)]
    dp_bits = [seq_count << i for i in range(dp_count.bit_length() - 1)]
    mine = width // seq_count
    padded = -(-mine // 16) * 16
    groups = seq_count if mine == padded and (width // 2) % mine == 0 else 1

    forward, inverse = spectral_tables(block)
    forward_two, inverse_three = jnp.asarray(two_pass(forward)), jnp.asarray(three_pass(inverse))
    forward_three, inverse_two = jnp.asarray(three_pass(forward.T)), jnp.asarray(two_pass(inverse.T))

    before = shifted(hidden_in[:, block - 2 :], 1)
    after = shifted(hidden_in[:, :2], -1)
    normed_one, extended, outer, signal_sent = run_front(
        lengths, hidden_in, before, after, gain_one[None], short_kernel, in_weight, groups
    )
    signal_ch = to_owner(signal_sent, mine, padded)

    signal_sent, filt_first, decay_rate, skip_gain = lax.optimization_barrier(
        (signal_sent, filt_first, decay_rate, skip_gain)
    )
    bands = (filt_first.shape[0] - 1) // 2
    spots = np.arange(row_len)
    turns = (np.arange(1, bands + 1)[:, None] * spots[None, :] % row_len) * (2.0 * math.pi / row_len)
    embedding = jnp.asarray(
        np.concatenate([spots[None, :] / row_len, np.cos(turns), np.sin(turns)], axis=0).astype(
            np.float32
        )
    )
    pre_one = jnp.einsum("ef,el->fl", filt_first, embedding, precision=FULL_PRECISION)
    act_one = jnp.sin(pre_one)
    pre_two = jnp.einsum("fg,fl->gl", filt_second, act_one, precision=FULL_PRECISION)
    act_two = jnp.sin(pre_two)
    my_third = lax.dynamic_slice_in_dim(filt_third, seq_pos * mine, mine, 1)
    my_decay = lax.dynamic_slice_in_dim(decay_rate, seq_pos * mine, mine, 0)
    my_skip = lax.dynamic_slice_in_dim(skip_gain, seq_pos * mine, mine, 0)
    my_skip = jnp.pad(my_skip, (0, padded - mine))[:, None]
    places = jnp.asarray(spots.astype(np.float32))
    envelope = jnp.exp(-my_decay[:, None] * places[None, :]) * row_len ** (-0.5)
    taps = jnp.einsum("gc,gl->cl", my_third, act_two, precision=FULL_PRECISION) * envelope
    taps = taps.reshape(mine, seq_count, block).transpose(1, 0, 2)
    if padded != mine:
        taps = jnp.pad(taps, ((0, 0), (0, padded - mine), (0, 0)))
    pieces = jnp.einsum("kct,tf->kcf", taps, jnp.asarray(forward), precision=FULL_PRECISION)
    sign = jnp.asarray(np.tile(1.0 - 2.0 * (np.arange(block) % 2), 2).astype(np.float32))
    earlier = jnp.concatenate([jnp.zeros_like(pieces[:1]), pieces[:-1]], axis=0)
    spectrum = earlier + sign * pieces
    spec_real, spec_imag = spectrum[..., :block], spectrum[..., block:]
    base = jnp.arange(block) == 0
    spectrum = (
        spec_real,
        jnp.where(base, 0.0, spec_imag),
        jnp.where(base, spec_imag, spec_real),
    )

    normed_got = swap(normed_one, 1)

    conv_ch, _ = run_conv(
        lengths, row_len, signal_ch, my_skip, spectrum, forward_two, inverse_three
    )
    conv = to_block(conv_ch, rows, mine, groups)
    if groups == 1:
        conv = conv[0]

    upstream = out_grad.reshape(tokens, width)
    upstream_got = swap(upstream, 1)
    (
        gain_two_grad, factors_mine, factors_theirs, block_out, last_mine, last_theirs, grad_middle,
        grad_outer, grad_sent,
    ) = run_middle(
        conv, mine, outer, hidden_in, gain_two[None], upstream, out_weight, ff_up, ff_down, groups,
        normed_got,
    )
    factors_got, last_got = swap(factors_theirs, 1), swap(last_theirs, 1)
    grad_ch = to_owner(grad_sent, mine, padded)
    orders = (dp_bits, dp_bits[::-1])
    firsts = (orders[0][0], orders[1][0])
    shape = (1, width // 2, width)
    up_operands = (factors_mine, factors_got)
    down_operands = (factors_mine, factors_got, upstream, upstream_got)
    up_sent, token = run_up_products(firsts, True, up_operands, shape)
    up = Group(orders, seq_bits, up_sent)
    down_sent, token = run_down_products(
        firsts, True, down_operands, shape, (token, last_got)
    )
    down = Group(orders, seq_bits, down_sent)
    outer_halo = shifted(grad_outer[:, :2], -1)

    back_ch, token = run_conv(
        lengths, row_len, grad_ch, my_skip, spectrum, forward_three, inverse_two, backward=True,
        after=(token,),
    )
    got = to_block(back_ch, rows, mine, groups)
    grad_signal, got = (got, got) if groups > 1 else got
    halo = got[:, 0, padded : padded + 2 * rows, :mine].astype(F32)
    halo = halo.transpose(1, 0, 2).reshape(rows, 2, width)
    up_kept, token = run_up_products(firsts, False, up_operands, shape, (token,))
    up.halve(up_kept)
    down_kept, token = run_down_products(firsts, False, down_operands, shape, (up.token,))
    down.halve(down_kept)
    up.scatter(None, (down.token,), BRIDGE_A)

    (proj_mine, proj_theirs, kernel_grad, gain_one_grad, input_grad), token = run_last(
        lengths, grad_signal, mine, halo, extended, grad_outer, outer_halo, hidden_in,
        gain_one[None], short_kernel, grad_middle, in_weight, (up.token,) if up.direct else (),
    )
    last_operands = (normed_one, normed_got, proj_mine, swap(proj_theirs, 1), last_mine, last_got)
    if up.direct:
        up.split((token,))
    down.scatter(None, (up.token,), BRIDGE_B)
    last_sent, token = run_last_products(
        firsts, True, last_operands, shape, (down.token,) if up.direct else ()
    )
    last = Group(orders, seq_bits, last_sent)
    last_kept, token = run_last_products(firsts, False, last_operands, shape, (token,))

    grad_taps, token = run_filter_grad(
        lengths, row_len, signal_ch, grad_ch, forward_two, inverse_two, forward_three,
        after=(token,),
    )
    envelope = jnp.pad(envelope, ((0, padded - mine), (0, 0)))
    my_third = jnp.pad(my_third, ((0, 0), (0, padded - mine)))
    net = (act_one, pre_one, act_two, pre_two)
    (my_third_grad, skip_grad, second_grad, first_grad), token = run_filter_back(
        grad_taps, envelope, net, my_third, filt_second, embedding, (token,)
    )
    small = (
        my_third_grad[:, :mine], skip_grad[:1, :mine], kernel_grad, gain_one_grad, gain_two_grad,
        second_grad, first_grad,
    )
    in_shapes = (in_weight.shape, out_weight.shape)
    if up.direct:
        (packed,), token = run_pack(dp_count, *small)
        arrived = lax.all_to_all(packed, "dp", 0, 0, tiled=True)
        up.total((token,))
        down.split((up.token,))
        last.halve(last_kept, (down.token,))
        up.pair((last.token,))
        down.total((up.token,))
        (packed,), token = run_total_all(arrived, (down.token,))
        last.scatter(packed, (token,))
        up.gather((last.token,))
        last.split((up.token,))
        down.pair((last.token,))
        up.join_last((down.token,))
        down.gather((up.token,))
        last.total((down.token,))
        down.join_last((last.token,))
        last.pair((down.token,))
        up.stack((last.token,))
        up_total = up.place_whole(up_place_kernel, ff_up.shape, (up.token,))
        last.gather((up.token,))
        last.join((last.token, mark(down.got)))
        down.stack((last.token,))
        last.place(last_place_kernel, in_shapes, (down.token,))
        down_total = down.place_whole(down_place_kernel, ff_down.shape, (last.token,))
        small, token = run_unpack(
            4, mine, last.small, swap(last.small, 1), filt_third.shape[0],
            filt_first.shape[0], (down.token,),
        )
        in_total, out_total = last.finish(last_place_kernel, in_shapes, (), (token,))
    else:
        last.halve(last_kept)
        last.scatter()
        for group in (up, down):
            group.gather()
            group.join_last()
            group.stack()
        last.gather()
        last.join()
        up_total = up.place_whole(up_place_kernel, ff_up.shape)
        down_total = down.place_whole(down_place_kernel, ff_down.shape)
        in_total, out_total = last.finish(last_place_kernel, in_shapes)
        spread = [
            lax.dynamic_update_slice_in_dim(
                jnp.zeros((part.shape[0], width), F32), part, seq_pos * mine, 1
            )
            for part in small[:2]
        ]
        small = lax.psum((*spread, small[2][:KS], *small[3:]), AXES)
    return (
        block_out, input_grad, small[3][0], in_total, small[2], small[1][0], small[6], small[5],
        small[0], out_total, small[4][0], up_total, down_total,
    )


def solution(mesh):
    tokens = P("dp", "seq", None)
    return jax.shard_map(
        per_device,
        mesh=mesh,
        in_specs=(tokens, P("dp", None)) + (P(),) * 12 + (tokens,),
        out_specs=(tokens, tokens) + (P(),) * 11,
        check_vma=False,
    )
```

```python
from functools import partial
import math

import jax
import jax.numpy as jnp
import numpy as np
from jax import lax
from jax.experimental import pallas as pl
from jax.experimental.pallas import tpu as pltpu
from jax.sharding import PartitionSpec as P

FULL_PRECISION = lax.Precision.HIGHEST
BF16 = jnp.bfloat16
F32 = jnp.float32
AXES = ("dp", "seq")
VMEM_BYTES = 32 * 1024 * 1024
FULL_BYTES = 54 * 1024 * 1024
PLACE_BYTES = 57 * 1024 * 1024
WHOLE_BYTES = 55 * 1024 * 1024
KS = 3


def swap(value, bit):
    count = lax.axis_size(AXES)
    return lax.ppermute(value, AXES, [(i, i ^ bit) for i in range(count)])


def shifted(value, steps):
    count = lax.axis_size("seq")
    first, last = max(0, -steps), min(count, count - steps)
    return lax.ppermute(value, "seq", [(i, i + steps) for i in range(first, last)])


def my_bit(index, bit):
    return (index // bit) % 2


def add(kept, got):
    return (kept.astype(F32) + got.astype(F32)).astype(kept.dtype)


def halve(value, index, bits, axis):
    for bit in bits:
        size = value.shape[axis] // 2
        mine = my_bit(index, bit)
        keep = lax.dynamic_slice_in_dim(value, mine * size, size, axis)
        send = lax.dynamic_slice_in_dim(value, (1 - mine) * size, size, axis)
        value = add(keep, swap(send, bit))
    return value


def double(value, index, bits, axis):
    for bit in reversed(bits):
        other = swap(value, bit)
        low = my_bit(index, bit) == 0
        value = jnp.concatenate(
            [jnp.where(low, value, other), jnp.where(low, other, value)], axis=axis
        )
    return value


def sum_over(value, bits):
    for bit in bits:
        value = value + swap(value, bit)
    return value


def spectral_tables(block):
    points = 2 * block
    spot = np.arange(block)
    freq = np.arange(block)
    angle = (spot[:, None] * freq[None, :] % points) * (2.0 * math.pi / points)
    real, imag = np.cos(angle), -np.sin(angle)
    imag[:, 0] = 1.0 - 2.0 * (spot % 2)
    forward = np.concatenate([real, imag], axis=1)
    late = spot + block
    angle = (freq[:, None] * late[None, :] % points) * (2.0 * math.pi / points)
    weight = np.where(freq == 0, 1.0, 2.0)[:, None] / points
    real, imag = weight * np.cos(angle), -weight * np.sin(angle)
    imag[0, :] = (1.0 - 2.0 * (late % 2)) / points
    inverse = np.concatenate([real, imag], axis=0)
    return forward.astype(np.float32), inverse.astype(np.float32)


def split_table(table):
    high = table.astype(jnp.bfloat16)
    low = (table - high.astype(np.float32)).astype(jnp.bfloat16)
    return np.asarray(high), np.asarray(low)


def two_pass(table):
    high, low = split_table(table)
    return np.concatenate([high, low], axis=0)


def three_pass(table):
    high, low = split_table(table)
    return np.concatenate([high, high, low], axis=0)


def ends_of(lengths_ref, row):
    total, ends = 0, []
    for k in range(lengths_ref.shape[1]):
        total = total + lengths_ref[row, k]
        ends.append(total)
    return ends


def next_end(ends, spot, row_len):
    found = row_len
    for end in reversed(ends):
        found = jnp.where(end > spot, end, found)
    return found


def last_end(ends, spot):
    found = 0
    for end in ends:
        found = jnp.where(end <= spot, end, found)
    return found


def near_mask(ends, spots, step):
    apart = spots < step
    for end in ends:
        apart = apart | ((end <= spots) & (end > spots - step))
    return jnp.where(apart, 0.0, 1.0)


def dot(left, right):
    return jnp.dot(left, right, preferred_element_type=F32)


def dot_nt(left, right):
    return lax.dot_general(left, right, (((1,), (1,)), ((), ())), preferred_element_type=F32)


def head_masks(ends, spot, group, rows, block, row_len):
    lane = lax.broadcasted_iota(jnp.int32, (1, 1, block), 2)
    masks = []
    for g in range(group):
        start = (spot + g) // rows * block
        stop = jnp.where((spot + g) % rows == 0, next_end(ends[0], start, row_len), 0)
        for row in range(1, rows):
            stop = jnp.where(
                (spot + g) % rows == row, next_end(ends[row], start, row_len), stop
            )
        masks.append(jnp.where(lane < stop - start, 1.0, 0.0))
    return jnp.concatenate(masks, axis=0)


def spectra(value_ref, masks, table_ref, head_out, rest_out, group):
    count, channels, block = value_ref.shape

    def step(i, carry):
        spot = pl.ds(i * group, group)
        whole = value_ref[spot].astype(F32)
        first = whole * masks(i * group)
        both = jnp.concatenate([first, whole - first], axis=0).astype(BF16)
        both = both.reshape(2 * group * channels, block)
        found = dot(jnp.concatenate([both, both], axis=1), table_ref[...])
        found = found.reshape(2 * group, channels, 2 * block)
        head_out[spot] = found[:group]
        rest_out[spot] = found[group:]
        return carry

    lax.fori_loop(0, count // group, step, 0)


def back_to_time(head_spec, rest_spec, masks, table_ref, value_ref, skip_ref, group, store):
    count, channels, double_block = head_spec.shape

    def step(i, carry):
        spot = pl.ds(i * group, group)
        both = jnp.concatenate([head_spec[spot], rest_spec[spot]], axis=0)
        both = both.reshape(2 * group * channels, double_block)
        high = both.astype(BF16)
        low = (both - high.astype(F32)).astype(BF16)
        found = dot(jnp.concatenate([high, low, high], axis=1), table_ref[...])
        found = found.reshape(2 * group, channels, double_block // 2)
        rest = found[group:]
        found = rest + masks(i * group) * (found[:group] - rest)
        store(i * group, found + skip_ref[...][None] * value_ref[spot].astype(F32))
        return carry

    lax.fori_loop(0, count // group, step, 0)


def of_row(per_row, row):
    found = per_row[0]
    for k in range(1, len(per_row)):
        found = jnp.where(row == k, per_row[k], found)
    return found


def start_loads(moves, sems):
    loads = [
        pltpu.make_async_copy(source, target, sems.at[i])
        for i, (source, target) in enumerate(moves)
    ]
    for load in loads:
        load.start()
    return loads


def conv_kernel(
    rows, group, row_len, lengths_ref, value_ref, skip_ref, hr_ref, hi_ref, hm_ref,
    forward_ref, inverse_ref, out_ref, head_spec, rest_spec, head_sum, rest_sum,
):
    count, channels, block = value_ref.shape
    ends = [ends_of(lengths_ref, row) for row in range(rows)]

    def masks(spot):
        return head_masks(ends, spot, group, rows, block, row_len)

    spectra(value_ref, masks, forward_ref, head_spec, rest_spec, group)

    def product(real, imag, lag):
        hr, hi, hm = hr_ref[lag], hi_ref[lag], hm_ref[lag]
        return real * hr - imag * hi, real * hi + imag * hm

    def own(j, carry):
        start = j // rows * block
        stop = of_row([next_end(e, start, row_len) for e in ends], j % rows)
        plain = (stop >= start + block).astype(F32)
        head_real, head_imag = product(head_spec[j, :, :block], head_spec[j, :, block:], 0)
        head_sum[j, :, :block] = head_real
        head_sum[j, :, block:] = head_imag
        rest_real, rest_imag = product(rest_spec[j, :, :block], rest_spec[j, :, block:], 0)
        rest_sum[j, :, :block] = rest_real
        rest_sum[j, :, block:] = rest_imag
        rest_spec[j] = rest_spec[j] + plain * head_spec[j]
        return carry

    lax.fori_loop(0, count, own, 0)

    def reach(j, carry):
        spot, row = j // rows, j % rows
        begin = of_row([last_end(e, spot * block) for e in ends], row) // block

        def include(source, sums):
            k = source * rows + row
            real, imag = product(
                rest_spec[k, :, :block], rest_spec[k, :, block:], spot - source
            )
            return sums[0] + real, sums[1] + imag

        start = (head_sum[j, :, :block], head_sum[j, :, block:])
        real, imag = lax.fori_loop(begin, spot, include, start)
        head_sum[j, :, :block] = real
        head_sum[j, :, block:] = imag
        return carry

    lax.fori_loop(rows, count, reach, 0)

    def store(spot, found):
        out_ref[pl.ds(spot, group)] = found.astype(BF16)

    back_to_time(head_sum, rest_sum, masks, inverse_ref, value_ref, skip_ref, group, store)


def conv_back_kernel(
    rows, group, row_len, lengths_ref, value_ref, skip_hbm, hr_hbm, hi_hbm, hm_hbm,
    forward_hbm, inverse_hbm, out_ref, skip_ref, hr_ref, hi_ref, hm_ref, forward_ref, inverse_ref,
    sems, head_spec, rest_spec, head_sum, rest_sum, found_ref,
):
    count, channels, block = value_ref.shape
    loads = start_loads(
        [
            (inverse_hbm, inverse_ref), (hr_hbm, hr_ref), (hi_hbm, hi_ref), (hm_hbm, hm_ref),
            (forward_hbm, forward_ref), (skip_hbm, skip_ref),
        ],
        sems,
    )
    ends = [ends_of(lengths_ref, row) for row in range(rows)]

    def masks(spot):
        return head_masks(ends, spot, group, rows, block, row_len)

    loads[0].wait()
    spectra(value_ref, masks, inverse_ref, head_spec, rest_spec, group)
    for load in loads[1:]:
        load.wait()

    def product(real, imag, lag):
        hr, hi, hm = hr_ref[lag], hi_ref[lag], hm_ref[lag]
        return real * hr + imag * hi, imag * hm - real * hi

    def reach(j, carry):
        spot, row = j // rows, j % rows
        start = spot * block
        plain = of_row([next_end(e, start, row_len) for e in ends], row) >= start + block
        plain = plain.astype(F32)
        until = of_row([next_end(e, start + block - 1, row_len) for e in ends], row)
        until = (until - 1) // block + 1

        def include(source, sums):
            k = source * rows + row
            real, imag = product(
                head_spec[k, :, :block], head_spec[k, :, block:], source - spot
            )
            return sums[0] + real, sums[1] + imag

        empty = jnp.zeros((channels, block), F32)
        real, imag = lax.fori_loop(spot + 1, until, include, (empty, empty))
        head_real, head_imag = product(head_spec[j, :, :block], head_spec[j, :, block:], 0)
        head_sum[j, :, :block] = head_real + plain * real
        head_sum[j, :, block:] = head_imag + plain * imag
        rest_real, rest_imag = product(rest_spec[j, :, :block], rest_spec[j, :, block:], 0)
        rest_sum[j, :, :block] = rest_real + (1.0 - plain) * real
        rest_sum[j, :, block:] = rest_imag + (1.0 - plain) * imag
        return carry

    lax.fori_loop(0, count, reach, 0)

    def store(spot, found):
        found_ref[pl.ds(spot, group)] = found
        out_ref[pl.ds(spot, group), :channels] = found.astype(BF16)

    back_to_time(head_sum, rest_sum, masks, forward_ref, value_ref, skip_ref, group, store)

    lane = lax.broadcasted_iota(jnp.int32, (channels, block), 1)
    per_turn = block // 2
    blocks = count // rows
    for turn in range(-(-count // per_turn)):
        first = turn * per_turn
        last = min(count, first + per_turn)

        def gather(j, picked):
            at = 2 * (j - first)
            moved = pltpu.roll(found_ref[j], at, 1)
            return jnp.where((lane >= at) & (lane < at + 2), moved, picked)

        picked = lax.fori_loop(first, last, gather, jnp.zeros((channels, block), F32))
        if channels < block:
            picked = jnp.concatenate(
                [picked, jnp.zeros((block - channels, block), F32)], axis=0
            )
        flipped = picked.T
        for spot in range(first // rows, last // rows):
            at = 2 * (spot * rows - first)
            tile = jnp.concatenate(
                [flipped[at : at + 2 * rows], jnp.zeros((16 - 2 * rows, block), F32)], axis=0
            )
            if spot > 0:
                out_ref[(spot - 1) * rows, channels:] = tile.astype(BF16)
    out_ref[(blocks - 1) * rows, channels:] = jnp.zeros((16, block), BF16)
    for spot in range(blocks):
        for row in range(1, rows):
            out_ref[spot * rows + row, channels:] = jnp.zeros((16, block), BF16)


def filter_grad_kernel(
    rows, group, row_len, lengths_ref, value_ref, grad_ref, forward_ref,
    inverse_ref, back_ref, out_ref, head_spec, rest_spec, grad_head, grad_rest, total,
):
    count, channels, block = value_ref.shape
    lags = count // rows
    ends = [ends_of(lengths_ref, row) for row in range(rows)]

    def masks(spot):
        return head_masks(ends, spot, group, rows, block, row_len)

    spectra(value_ref, masks, forward_ref, head_spec, rest_spec, group)
    spectra(grad_ref, masks, inverse_ref, grad_head, grad_rest, group)
    lane = lax.broadcasted_iota(jnp.int32, (channels, block), 1)
    base = lane == 0

    def product(grad, spec, k, j):
        gr, gi = grad[k, :, :block], grad[k, :, block:]
        sr, si = spec[j, :, :block], spec[j, :, block:]
        masked = jnp.where(base, 0.0, si)
        swapped = jnp.where(base, si, sr)
        return gr * sr + gi * masked, gi * swapped - gr * masked

    def own(j, sums):
        start = j // rows * block
        stop = of_row([next_end(e, start, row_len) for e in ends], j % rows)
        plain = (stop >= start + block).astype(F32)
        head = product(grad_head, head_spec, j, j)
        rest = product(grad_rest, rest_spec, j, j)
        rest_spec[j] = rest_spec[j] + plain * head_spec[j]
        return sums[0] + head[0] + rest[0], sums[1] + head[1] + rest[1]

    empty = jnp.zeros((channels, block), F32)
    real, imag = lax.fori_loop(0, count, own, (empty, empty))
    total[0, :, :block] = real
    total[0, :, block:] = imag

    def one_lag(lag, carry):
        def include(j, sums):
            spot = j // rows
            begin = of_row([last_end(e, spot * block) for e in ends], j % rows) // block
            near = (begin <= spot - lag).astype(F32)
            real, imag = product(grad_head, rest_spec, j, j - lag * rows)
            return sums[0] + near * real, sums[1] + near * imag

        real, imag = lax.fori_loop(lag * rows, count, include, (empty, empty))
        total[lag, :, :block] = real
        total[lag, :, block:] = imag
        return carry

    lax.fori_loop(1, lags, one_lag, 0)
    wide = lax.broadcasted_iota(jnp.int32, (channels, 2 * block), 1)
    sign = (1 - 2 * (wide % 2)).astype(F32)
    total[lags] = jnp.zeros((channels, 2 * block), F32)

    def one_piece(lag, carry):
        piece = total[lag + 1] + sign * total[lag]
        high = piece.astype(BF16)
        low = (piece - high.astype(F32)).astype(BF16)
        out_ref[lag] = dot(jnp.concatenate([high, low, high], axis=1), back_ref[...])
        return carry

    lax.fori_loop(0, lags, one_piece, 0)


def vmem(count):
    return [pl.BlockSpec(memory_space=pltpu.VMEM)] * count


def smem(count):
    return [pl.BlockSpec(memory_space=pltpu.SMEM)] * count


def hbm(count):
    return [pl.BlockSpec(memory_space=pltpu.HBM)] * count


def anywhere(count):
    return [pl.BlockSpec(memory_space=pl.ANY)] * count


def params(limit=VMEM_BYTES):
    return pltpu.CompilerParams(vmem_limit_bytes=limit)


SHORT = pl.CostEstimate(flops=1, bytes_accessed=1, transcendentals=0)


def takes(micro):
    return pl.CostEstimate(flops=int(micro * 1e9), bytes_accessed=1, transcendentals=0)


BRIDGE_A, BRIDGE_B = takes(2), takes(12)
LINE = takes(8)

TOKEN = (12288, 1024), F32


def launch(
    kernel, operands, outs, in_specs=None, out_specs=None, scratch=(), limit=VMEM_BYTES, after=(),
    aliases=None, estimate=SHORT,
):
    used, made = len(operands), len(outs)

    def call(*refs):
        rest = refs[used + len(after) :]
        kernel(*refs[:used], *rest[:made], *rest[made + 1 :])

    results = pl.pallas_call(
        call,
        name=getattr(kernel, "func", kernel).__name__.replace("<lambda>", "hold"),
        out_shape=tuple(jax.ShapeDtypeStruct(*out) for out in (*outs, TOKEN)),
        in_specs=(vmem(used) if in_specs is None else in_specs) + anywhere(len(after)),
        out_specs=tuple((vmem(made) if out_specs is None else out_specs) + hbm(1)),
        scratch_shapes=list(scratch),
        input_output_aliases=aliases or {},
        compiler_params=params(limit),
        cost_estimate=estimate,
    )(*operands, *after)
    return tuple(results[:-1]), results[-1]


def run_conv(
    lengths, row_len, value, skip, spectrum, forward, inverse, backward=False, after=()
):
    count, channels, block = value.shape
    rows = lengths.shape[0]
    group = 4 if count % 4 == 0 else 1
    spec = pltpu.VMEM((count, channels, 2 * block), F32)
    extra = [pltpu.VMEM((count, channels, block), F32)] if backward else []
    sent = channels + 16 if backward else channels
    operands = (lengths, value, skip, *spectrum, forward, inverse)
    if not backward:
        (found,), token = launch(
            partial(conv_kernel, rows, group, row_len),
            operands,
            [((count, sent, block), BF16)],
            in_specs=smem(1) + vmem(7),
            scratch=[spec] * 4,
            after=after,
        )
        return found, token
    (found,), token = launch(
        partial(conv_back_kernel, rows, group, row_len),
        operands,
        [((count, sent, block), BF16)],
        in_specs=smem(1) + vmem(1) + anywhere(6),
        scratch=[
            *[pltpu.VMEM(part.shape, part.dtype) for part in (skip, *spectrum, forward, inverse)],
            pltpu.SemaphoreType.DMA((6,)),
            *[spec] * 4,
            *extra,
        ],
        after=after,
    )
    return found, token


def run_filter_grad(lengths, row_len, value, grad, forward, inverse, back, after=()):
    count, channels, block = value.shape
    rows = lengths.shape[0]
    group = 4 if count % 4 == 0 else 1
    lags = count // rows
    spec = pltpu.VMEM((count, channels, 2 * block), F32)
    (found,), token = launch(
        partial(filter_grad_kernel, rows, group, row_len),
        (lengths, value, grad, forward, inverse, back),
        [((lags, channels, block), F32)],
        in_specs=smem(1) + vmem(5),
        scratch=[spec] * 4 + [pltpu.VMEM((lags + 1, channels, 2 * block), F32)],
        after=after,
    )
    return found, token


def exact(left, right, contract):
    return lax.dot_general(
        left, right, (contract, ((), ())), precision=FULL_PRECISION, preferred_element_type=F32
    )


def filter_back_kernel(
    taps_ref, envelope_ref, act_one_ref, pre_one_ref, act_two_ref, pre_two_ref, third_ref,
    second_ref, embedding_ref, third_grad, skip_grad, second_grad, first_grad,
):
    lags, channels, block = taps_ref.shape
    pick = lax.broadcasted_iota(jnp.int32, (8, block), 1) == 0
    skip_grad[...] = exact(jnp.where(pick, 1.0, 0.0), taps_ref[0], ((1,), (1,)))
    third_grad[...] = jnp.zeros(third_grad.shape, F32)
    second_grad[...] = jnp.zeros(second_grad.shape, F32)
    first_grad[...] = jnp.zeros(first_grad.shape, F32)

    def one_lag(lag, carry):
        here = pl.ds(pl.multiple_of(lag * block, 128), block)
        grad = taps_ref[lag] * envelope_ref[:, here]
        third_grad[...] += exact(act_two_ref[:, here], grad, ((1,), (1,)))
        grad = jnp.cos(pre_two_ref[:, here]) * exact(third_ref[...], grad, ((1,), (0,)))
        second_grad[...] += exact(act_one_ref[:, here], grad, ((1,), (1,)))
        grad = jnp.cos(pre_one_ref[:, here]) * exact(second_ref[...], grad, ((1,), (0,)))
        first_grad[...] += exact(embedding_ref[:, here], grad, ((1,), (1,)))
        return carry

    lax.fori_loop(0, lags, one_lag, 0)


def run_filter_back(taps, envelope, net, third, second, embedding, after):
    hidden, channels = third.shape
    return launch(
        filter_back_kernel,
        (taps, envelope, *net, third, second, embedding),
        [
            ((hidden, channels), F32),
            ((8, channels), F32),
            ((hidden, hidden), F32),
            ((embedding.shape[0], hidden), F32),
        ],
        after=after,
    )


def put_channels(ref, row, chunk, value):
    groups, _, size, _ = ref.shape
    wide = value.shape[0]
    if groups == 1:
        ref[0, row, chunk * wide : (chunk + 1) * wide] = value
    else:
        per = wide // size
        for k in range(per):
            ref[chunk * per + k, row] = value[k * size : (k + 1) * size]


def get_channels(ref, row, chunk, wide, size):
    groups = ref.shape[0]
    if groups == 1:
        return ref[0, row, chunk * wide : (chunk + 1) * wide]
    per = wide // size
    return jnp.concatenate([ref[chunk * per + k, row, :size] for k in range(per)], axis=0)


def moments(value):
    center = value - jnp.mean(value, axis=-1, keepdims=True)
    spread = jnp.mean(center * center, axis=-1, keepdims=True)
    return center, lax.rsqrt(spread + 1e-05)


def norm_back(center, scale, gain, grad):
    unit = center * scale
    inner = grad * gain
    mean_one = jnp.mean(inner, axis=-1, keepdims=True)
    mean_two = jnp.mean(inner * unit, axis=-1, keepdims=True)
    return scale * (inner - mean_one - unit * mean_two), grad * unit


PIECE = 64


def front_kernel(
    lengths_ref, before_ref, after_ref, gain_ref, hidden_hbm, taps_hbm, weight_hbm,
    normed_hbm, extended_hbm, outer_hbm, sent_hbm,
    hidden_ref, taps_ref, weight_ref, normed_ref, extended_ref, outer_ref, sent_ref,
    halo_ref, wide_ref, mixed_ref, sems,
):
    rows, block, width = hidden_ref.shape
    loads = [
        pltpu.make_async_copy(source, target, sems.at[i])
        for i, (source, target) in enumerate(
            [(hidden_hbm, hidden_ref), (weight_hbm, weight_ref), (taps_hbm, taps_ref)]
        )
    ]
    for load in loads:
        load.start()
    gain = gain_ref[...]
    halo = jnp.concatenate(
        [part for row in range(rows) for part in (before_ref[row], after_ref[row])], axis=0
    ).astype(F32)
    center, scale = moments(halo)
    halo = center * scale * gain
    halo_ref[...] = jnp.concatenate(
        [halo, jnp.zeros((halo_ref.shape[0] - 4 * rows, width), F32)], axis=0
    ).astype(BF16)
    first = lax.axis_index("seq") * block
    ends = [ends_of(lengths_ref, row) for row in range(rows)]
    spots = first + lax.broadcasted_iota(jnp.int32, (block, 1), 0)
    near_one = [near_mask(e, spots, 1) for e in ends]
    near_two = [near_mask(e, spots, 2) for e in ends]
    live = [jnp.where(spots < e[-1], 1.0, 0.0) for e in ends]
    loads[0].wait()
    for row in range(rows):
        for start in range(0, block, PIECE):
            center, scale = moments(hidden_ref[row, start : start + PIECE].astype(F32))
            at = row * block + start
            normed_ref[at : at + PIECE] = (center * scale * gain).astype(BF16)
    saves = [
        pltpu.make_async_copy(source, target, sems.at[3 + i])
        for i, (source, target) in enumerate(
            [
                (normed_ref, normed_hbm),
                (sent_ref, sent_hbm),
                (extended_ref, extended_hbm),
                (outer_ref, outer_hbm),
            ]
        )
    ]
    saves[0].start()
    chunk = width // 2
    loads[1].wait()
    loads[2].wait()
    for part in range(3):
        for half in range(2):
            cols = slice(part * width + half * chunk, part * width + (half + 1) * chunk)
            main = dot(normed_ref[...], weight_ref[:, cols])
            edge = dot(halo_ref[...], weight_ref[:, cols])
            taps = taps_ref[:, cols]
            for row in range(rows):
                wide_ref[row, 0:8] = jnp.zeros((8, chunk), F32)
                wide_ref[row, block + 8 :] = jnp.zeros((8, chunk), F32)
                wide_ref[row, 6:8] = edge[4 * row : 4 * row + 2]
                wide_ref[row, 8 : block + 8] = main[row * block : (row + 1) * block]
                wide_ref[row, block + 8 : block + 10] = edge[4 * row + 2 : 4 * row + 4]
                rounded = wide_ref[row].astype(BF16)
                extended_ref[row, :, cols] = rounded
                wide_ref[row] = rounded.astype(F32)
                mixed = (
                    taps[0:1] * wide_ref[row, 8 : block + 8]
                    + taps[1:2] * wide_ref[row, 7 : block + 7] * near_one[row]
                    + taps[2:3] * wide_ref[row, 6 : block + 6] * near_two[row]
                )
                here = slice(half * chunk, (half + 1) * chunk)
                if part == 0:
                    mixed_ref[row, :, here] = mixed
                elif part == 1:
                    signal = mixed_ref[row, :, here] * mixed * live[row]
                    put_channels(sent_ref, row, half, signal.T.astype(BF16))
                else:
                    outer_ref[row, :, here] = mixed
        if part == 1:
            saves[1].start()
    saves[2].start()
    saves[3].start()
    for save in saves:
        save.wait()


def run_front(lengths, hidden, before, after, gain, taps, weight, groups):
    rows, block, width = hidden.shape
    chunk = width // 2
    outs = (
        ((rows * block, width), BF16),
        ((rows, block + 16, 3 * width), BF16),
        ((rows, block, width), F32),
        ((groups, rows, width // groups, block), BF16),
    )
    return pl.pallas_call(
        front_kernel,
        out_shape=tuple(jax.ShapeDtypeStruct(*out) for out in outs),
        in_specs=smem(1) + vmem(3) + hbm(3),
        out_specs=tuple(hbm(4)),
        scratch_shapes=[
            pltpu.VMEM(hidden.shape, BF16),
            pltpu.VMEM(taps.shape, F32),
            pltpu.VMEM(weight.shape, BF16),
            *[pltpu.VMEM(*out) for out in outs],
            pltpu.VMEM((16, width), BF16),
            pltpu.VMEM((rows, block + 16, chunk), F32),
            pltpu.VMEM((rows, block, width), F32),
            pltpu.SemaphoreType.DMA((7,)),
        ],
        compiler_params=params(FULL_BYTES),
        cost_estimate=SHORT,
    )(lengths, before, after, gain, hidden, taps, weight)


def middle_kernel(
    size, conv_ref, gain_ref, outer_hbm, hidden_hbm, upstream_hbm, out_hbm, up_hbm, down_hbm,
    gain_grad_ref, factors_mine_hbm, factors_theirs_hbm, result_hbm, last_mine_hbm, last_theirs_hbm,
    grad_middle_hbm, grad_outer_hbm, sent_hbm,
    outer_ref, hidden_ref, upstream_ref, out_ref, up_ref, down_ref,
    factors_ref, result_ref, last_ref, grad_middle_ref, grad_outer_ref, sent_ref,
    conv_scr, middle_ref, grad_ref, sems,
):
    rows, block, width = hidden_ref.shape
    parts = down_ref.shape[0] // width
    per_core = parts // 2
    units = per_core * width
    chunk = width // 2
    core = lax.axis_index("seq") % 2
    copies = [
        pltpu.make_async_copy(outer_hbm, outer_ref, sems.at[0]),
        pltpu.make_async_copy(out_hbm, out_ref, sems.at[1]),
        pltpu.make_async_copy(hidden_hbm, hidden_ref, sems.at[2]),
        pltpu.make_async_copy(upstream_hbm, upstream_ref, sems.at[3]),
    ]
    for part in range(parts):
        cols = slice(part * width, (part + 1) * width)
        copies.append(
            pltpu.make_async_copy(up_hbm.at[:, cols], up_ref.at[:, cols], sems.at[2 * part + 4])
        )
        copies.append(
            pltpu.make_async_copy(down_hbm.at[cols], down_ref.at[cols], sems.at[2 * part + 5])
        )
    for copy in copies:
        copy.start()
    saves = [
        pltpu.make_async_copy(source, target, sems.at[2 * parts + 4 + i])
        for i, (source, target) in enumerate(
            [
                (result_ref, result_hbm),
                (grad_middle_ref, grad_middle_hbm),
                (last_ref.at[0], last_mine_hbm),
                (last_ref.at[1], last_theirs_hbm),
                (sent_ref, sent_hbm),
                (grad_outer_ref, grad_outer_hbm),
                (factors_ref.at[1], factors_theirs_hbm),
                (factors_ref.at[0], factors_mine_hbm),
            ]
        )
    ]
    for row in range(rows):
        here = slice(row * block, (row + 1) * block)
        for half in range(2):
            cols = slice(half * chunk, (half + 1) * chunk)
            conv_scr[here, cols] = get_channels(conv_ref, row, half, chunk, size).astype(F32).T
    copies[0].wait()
    for row in range(rows):
        here = slice(row * block, (row + 1) * block)
        gated = (outer_ref[row] * conv_scr[here]).astype(BF16)
        last_ref[0, here, :width] = gated
        last_ref[1, here, :width] = gated
    copies[1].wait()
    middle_ref[...] = dot(last_ref[0, :, :width], out_ref[...])
    copies[2].wait()
    gain = gain_ref[...]
    normed = slice(2 * units, 2 * units + width)
    for row in range(rows):
        for start in range(0, block, PIECE):
            here = slice(row * block + start, row * block + start + PIECE)
            middle = middle_ref[here] + hidden_ref[row, start : start + PIECE].astype(F32)
            middle_ref[here] = middle
            center, scale = moments(middle)
            rounded = (center * scale * gain).astype(BF16)
            factors_ref[0, here, normed] = rounded
            factors_ref[1, here, normed] = rounded
    slope = math.sqrt(2.0 / math.pi)
    copies[3].wait()
    for part in range(parts):
        cols = slice(part * width, (part + 1) * width)
        copies[2 * part + 4].wait()
        pre = dot(factors_ref[0, :, normed], up_ref[:, cols])
        copies[2 * part + 5].wait()
        grad_act = dot_nt(upstream_ref[...], down_ref[cols])
        square = pre * pre
        bend = jnp.tanh(slope * pre * (1.0 + 0.044715 * square))
        half_up = 0.5 * (1.0 + bend)
        act = (pre * half_up).astype(BF16)
        turn = half_up + 0.5 * pre * (1.0 - bend * bend) * (
            slope * (1.0 + 3.0 * 0.044715 * square)
        )
        grad_pre = (grad_act * turn).astype(BF16)
        slot = (part // per_core + core) % 2
        at = part % per_core * width
        factors_ref[slot, :, at : at + width] = act
        factors_ref[slot, :, units + at : units + at + width] = grad_pre
        if part == 0:
            grad_ref[...] = dot_nt(grad_pre, up_ref[:, cols])
        else:
            grad_ref[...] += dot_nt(grad_pre, up_ref[:, cols])
        found = dot(act, down_ref[cols])
        for row in range(rows):
            here = slice(row * block, (row + 1) * block)
            if part == 0:
                grad_middle_ref[here] = middle_ref[here] + found[here]
            elif part < parts - 1:
                grad_middle_ref[here] += found[here]
            else:
                result_ref[row] = (grad_middle_ref[here] + found[here]).astype(BF16)
    saves[6].start()
    saves[7].start()
    saves[0].start()
    gain_grad = jnp.zeros((1, width), F32)
    branch_cols = slice(width, width + chunk)
    for at in range(0, rows * block, PIECE):
        here = slice(at, at + PIECE)
        center, scale = moments(middle_ref[here])
        grad, terms = norm_back(center, scale, gain, grad_ref[here])
        gain_grad = gain_grad + jnp.sum(terms, axis=0, keepdims=True)
        grad = upstream_ref[here].astype(F32) + grad
        grad_middle_ref[here] = grad
        branch = grad.astype(BF16)

        last_ref[core, here, branch_cols] = branch[:, :chunk]
        last_ref[1 - core, here, branch_cols] = branch[:, chunk:]

    for save in saves[1:4]:
        save.start()
    gain_grad_ref[...] = gain_grad
    grad_ref[...] = dot_nt(grad_middle_ref[...].astype(BF16), out_ref[...])
    for row in range(rows):
        here = slice(row * block, (row + 1) * block)
        for half in range(2):
            cols = slice(half * chunk, (half + 1) * chunk)
            grad_conv = grad_ref[here, cols] * outer_ref[row, :, cols]
            put_channels(sent_ref, row, half, grad_conv.T.astype(BF16))
    saves[4].start()
    for row in range(rows):
        here = slice(row * block, (row + 1) * block)
        grad_outer_ref[row] = grad_ref[here] * conv_scr[here]
    saves[5].start()
    for save in saves:
        save.wait()


def run_middle(conv, size, outer, hidden, gain, upstream, out_weight, up, down, groups, after):
    rows, block, width = hidden.shape
    tokens = rows * block
    units = up.shape[1]
    parts = units // width
    near = (((1, width), F32),)
    far = (
        ((tokens, units + width), BF16),
        ((tokens, units + width), BF16),
        ((rows, block, width), BF16),
        ((tokens, 3 * width // 2), BF16),
        ((tokens, 3 * width // 2), BF16),
        ((tokens, width), F32),
        ((rows, block, width), F32),
        ((groups, rows, width // groups, block), BF16),
    )
    return pl.pallas_call(
        lambda *refs: middle_kernel(size, *refs[:8], *refs[9:]),
        out_shape=tuple(jax.ShapeDtypeStruct(*out) for out in near + far),
        in_specs=vmem(2) + hbm(6) + anywhere(1),
        out_specs=tuple(vmem(1) + hbm(8)),
        scratch_shapes=[
            pltpu.VMEM(outer.shape, F32),
            pltpu.VMEM(hidden.shape, BF16),
            pltpu.VMEM(upstream.shape, BF16),
            pltpu.VMEM(out_weight.shape, BF16),
            pltpu.VMEM(up.shape, BF16),
            pltpu.VMEM(down.shape, BF16),
            pltpu.VMEM((2, *far[0][0]), BF16),
            pltpu.VMEM(*far[2]),
            pltpu.VMEM((2, *far[3][0]), BF16),
            *[pltpu.VMEM(*out) for out in far[5:]],
            pltpu.VMEM((tokens, width), F32),
            pltpu.VMEM((tokens, width), F32),
            pltpu.VMEM((tokens, width), F32),
            pltpu.SemaphoreType.DMA((2 * parts + 12,)),
        ],
        compiler_params=params(FULL_BYTES),
        cost_estimate=SHORT,
    )(conv, gain, outer, hidden, upstream, out_weight, up, down, after)


def last_kernel(
    size, lengths_ref, signal_ref, halo_ref, outer_halo_ref, gain_ref, taps_ref,
    extended_hbm, outer_hbm, hidden_hbm, grad_middle_hbm, weight_hbm,
    proj_mine, proj_theirs, taps_grad_ref, gain_grad_ref, result_hbm,
    extended_ref, outer_ref, hidden_ref, grad_middle_ref, weight_ref, result_ref,
    wide_ref, mixed_ref, grad_ref, proj_ref, normed_grad, sems,
):
    rows, block, width = hidden_ref.shape
    chunk = width // 2
    loads = [
        pltpu.make_async_copy(source, target, sems.at[i])
        for i, (source, target) in enumerate(
            [
                (extended_hbm, extended_ref),
                (outer_hbm, outer_ref),
                (weight_hbm, weight_ref),
                (hidden_hbm, hidden_ref),
                (grad_middle_hbm, grad_middle_ref),
            ]
        )
    ]
    for load in loads:
        load.start()
    core = lax.axis_index("seq") % 2
    first = lax.axis_index("seq") * block
    longer = block + 8
    spots = first + lax.broadcasted_iota(jnp.int32, (longer, 1), 0)
    taps_grad_ref[...] = jnp.zeros(taps_grad_ref.shape, F32)
    loads[0].wait()
    loads[1].wait()
    for row in range(rows):
        ends = ends_of(lengths_ref, row)
        near_one, near_two = near_mask(ends, spots, 1), near_mask(ends, spots, 2)
        live = jnp.where(spots < ends[-1], 1.0, 0.0)
        for half in range(2):
            cols = slice(half * chunk, (half + 1) * chunk)
            grad_ref[0, :block] = get_channels(signal_ref, row, half, chunk, size).astype(F32).T
            grad_ref[0, block:] = jnp.concatenate(
                [halo_ref[row, :, cols], jnp.zeros((6, chunk), F32)], axis=0
            )
            for part in range(2):
                at = slice(part * width + half * chunk, part * width + (half + 1) * chunk)
                taps = taps_ref[:, at]
                wide_ref[part] = extended_ref[row, :, at].astype(F32)
                mixed_ref[part] = (
                    taps[0:1] * wide_ref[part, 8 : longer + 8]
                    + taps[1:2] * wide_ref[part, 7 : longer + 7] * near_one
                    + taps[2:3] * wide_ref[part, 6 : longer + 6] * near_two
                )
            at = slice(2 * width + half * chunk, 2 * width + (half + 1) * chunk)
            wide_ref[2] = extended_ref[row, :, at].astype(F32)
            signal_grad = grad_ref[0] * live
            grad_ref[0] = signal_grad * mixed_ref[1]
            grad_ref[1] = signal_grad * mixed_ref[0]
            grad_ref[2, :block] = outer_ref[row, :, cols]
            grad_ref[2, block:] = jnp.concatenate(
                [outer_halo_ref[row, :, cols], jnp.zeros((6, chunk), F32)], axis=0
            )
            for part in range(3):
                at = slice(part * width + half * chunk, part * width + (half + 1) * chunk)
                taps = taps_ref[:, at]
                own = grad_ref[part, :block]
                proj = (
                    taps[0:1] * own
                    + taps[1:2] * (grad_ref[part, 1 : block + 1] * near_one[1 : block + 1])
                    + taps[2:3] * (grad_ref[part, 2 : block + 2] * near_two[2 : block + 2])
                )
                proj_ref[row * block : (row + 1) * block, at] = proj.astype(BF16)
                taps_grad_ref[0:1, at] += jnp.sum(
                    own * wide_ref[part, 8 : block + 8], axis=0, keepdims=True
                )
                taps_grad_ref[1:2, at] += jnp.sum(
                    own * wide_ref[part, 7 : block + 7] * near_one[:block], axis=0, keepdims=True
                )
                taps_grad_ref[2:3, at] += jnp.sum(
                    own * wide_ref[part, 6 : block + 6] * near_two[:block], axis=0, keepdims=True
                )
    middle = 3 * width // 2

    @pl.when(core == 0)
    def _():
        proj_mine[...] = proj_ref[:, :middle]
        proj_theirs[...] = proj_ref[:, middle:]

    @pl.when(core != 0)
    def _():
        proj_mine[...] = proj_ref[:, middle:]
        proj_theirs[...] = proj_ref[:, :middle]

    loads[2].wait()
    normed_grad[...] = dot_nt(proj_ref[...], weight_ref[...])
    loads[3].wait()
    loads[4].wait()
    gain = gain_ref[...]
    gain_grad = jnp.zeros((1, width), F32)
    for row in range(rows):
        for start in range(0, block, PIECE):
            here = slice(row * block + start, row * block + start + PIECE)
            center, scale = moments(hidden_ref[row, start : start + PIECE].astype(F32))
            grad, terms = norm_back(center, scale, gain, normed_grad[here])
            gain_grad = gain_grad + jnp.sum(terms, axis=0, keepdims=True)
            result_ref[row, start : start + PIECE] = grad_middle_ref[here] + grad
    gain_grad_ref[...] = gain_grad
    save = pltpu.make_async_copy(result_ref, result_hbm, sems.at[5])
    save.start()
    save.wait()


def run_last(
    lengths, signal, size, halo, extended, outer, outer_halo, hidden, gain, taps, grad_middle,
    weight, after,
):
    rows, block, width = hidden.shape
    tokens = rows * block
    chunk = width // 2
    middle = 3 * width // 2
    return launch(
        partial(last_kernel, size),
        (
            lengths, signal, halo, outer_halo, gain, taps, extended, outer, hidden, grad_middle,
            weight,
        ),
        [
            ((tokens, middle), BF16),
            ((tokens, middle), BF16),
            ((8, 3 * width), F32),
            ((1, width), F32),
            (hidden.shape, F32),
        ],
        in_specs=smem(1) + vmem(5) + hbm(5),
        out_specs=vmem(4) + hbm(1),
        scratch=[
            pltpu.VMEM(extended.shape, BF16),
            pltpu.VMEM(outer.shape, F32),
            pltpu.VMEM(hidden.shape, BF16),
            pltpu.VMEM(grad_middle.shape, F32),
            pltpu.VMEM(weight.shape, BF16),
            pltpu.VMEM(hidden.shape, F32),
            pltpu.VMEM((3, block + 16, chunk), F32),
            pltpu.VMEM((2, block + 8, chunk), F32),
            pltpu.VMEM((3, block + 8, chunk), F32),
            pltpu.VMEM((tokens, 3 * width), BF16),
            pltpu.VMEM((tokens, width), F32),
            pltpu.SemaphoreType.DMA((6,)),
        ],
        limit=FULL_BYTES,
        after=after,
    )


def to_owner(sent, mine, padded):
    count = lax.axis_size("seq")
    groups, rows, size, block = sent.shape
    if groups != count:
        sent = sent.reshape(rows, count, mine, block).transpose(1, 0, 2, 3)
    got = lax.all_to_all(sent, "seq", 0, 0, tiled=True).reshape(count * rows, mine, block)
    if padded != mine:
        got = jnp.pad(got, ((0, 0), (0, padded - mine), (0, 0)))
    return got


def to_block(value, rows, mine, groups):
    count = lax.axis_size("seq")
    size, block = value.shape[1:]
    got = lax.all_to_all(
        value.reshape(count, rows, size, block), "seq", 0, 0, tiled=True
    )
    if groups == count:
        return got
    return got[:, :, :mine].transpose(1, 0, 2, 3).reshape(1, rows, count * mine, block), got


def dot_tn(left, right):
    return lax.dot_general(left, right, (((0,), (0,)), ((), ())), preferred_element_type=F32)


def bit_inside(bit):
    count = lax.axis_size("seq")
    if bit < count:
        return lax.axis_index("seq") // bit % 2
    return lax.axis_index("dp") // (bit // count) % 2


def side(bit, sent):
    mine = bit_inside(bit)
    return 1 - mine if sent else mine


def up_products_kernel(
    bits, sent, mine_hbm, got_hbm, a_ref, b_ref, left_ref, right_ref, sems
):
    _, rows, width = a_ref.shape
    units = 2 * width
    moves = []
    for part in range(2):
        at = pl.multiple_of(2 * units + side(bits[part], sent) * rows, 128)
        cols = slice(units + part * width, units + (part + 1) * width)
        for i, factors in enumerate((mine_hbm, got_hbm)):
            moves.append((factors.at[:, pl.ds(at, rows)], left_ref.at[part, i]))
            moves.append((factors.at[:, cols], right_ref.at[part, i]))
    loads = start_loads(moves, sems)
    for part, out in enumerate((a_ref, b_ref)):
        for load in loads[4 * part : 4 * part + 4]:
            load.wait()
        found = dot_tn(left_ref[part, 0], right_ref[part, 0]) + dot_tn(
            left_ref[part, 1], right_ref[part, 1]
        )
        out[0] = found.astype(BF16)


def down_products_kernel(
    bits, sent, mine_hbm, got_hbm, upstream_hbm, upstream_got_hbm, a_ref, b_ref,
    left_ref, right_ref, sems,
):
    _, rows, width = a_ref.shape
    moves = [(upstream_hbm, right_ref.at[0]), (upstream_got_hbm, right_ref.at[1])]
    for part in range(2):
        at = pl.multiple_of(part * width + side(bits[part], sent) * rows, 128)
        for i, factors in enumerate((mine_hbm, got_hbm)):
            moves.append((factors.at[:, pl.ds(at, rows)], left_ref.at[part, i]))
    loads = start_loads(moves, sems)
    loads[0].wait()
    loads[1].wait()
    for part, out in enumerate((a_ref, b_ref)):
        loads[2 * part + 2].wait()
        loads[2 * part + 3].wait()
        found = dot_tn(left_ref[part, 0], right_ref[0]) + dot_tn(left_ref[part, 1], right_ref[1])
        out[0] = found.astype(BF16)


def last_products_kernel(
    bits, sent, normed_ref, normed_got_ref, proj_ref, proj_got_ref, last_ref, last_got_ref,
    a_ref, b_ref,
):
    rows, width = a_ref.shape[1:]
    half = width // 2
    at = pl.multiple_of(side(bits[0], sent) * rows, 128)
    found = dot_tn(normed_ref[:, pl.ds(at, rows)], proj_ref[:, :width]) + dot_tn(
        normed_got_ref[:, pl.ds(at, rows)], proj_got_ref[:, :width]
    )
    a_ref[0] = found.astype(BF16)
    at = pl.multiple_of(side(bits[1], sent) * rows, 128)
    found = dot_tn(normed_ref[:, pl.ds(at, rows)], proj_ref[:, width:]) + dot_tn(
        normed_got_ref[:, pl.ds(at, rows)], proj_got_ref[:, width:]
    )
    b_ref[0, :, :half] = found.astype(BF16)
    found = dot_tn(last_ref[:, pl.ds(at, rows)], last_ref[:, width:]) + dot_tn(
        last_got_ref[:, pl.ds(at, rows)], last_got_ref[:, width:]
    )
    b_ref[0, :, half:] = found.astype(BF16)


def run_up_products(bits, sent, operands, shape, after=()):
    tokens, (_, rows, width) = operands[0].shape[0], shape
    return launch(
        partial(up_products_kernel, bits, sent),
        operands,
        [(shape, BF16)] * 2,
        in_specs=anywhere(2),
        scratch=[
            pltpu.VMEM((2, 2, tokens, rows), BF16),
            pltpu.VMEM((2, 2, tokens, width), BF16),
            pltpu.SemaphoreType.DMA((8,)),
        ],
        limit=FULL_BYTES,
        after=after,
    )


def run_down_products(bits, sent, operands, shape, after=()):
    tokens, (_, rows, width) = operands[0].shape[0], shape
    return launch(
        partial(down_products_kernel, bits, sent),
        operands,
        [(shape, BF16)] * 2,
        in_specs=anywhere(4),
        scratch=[
            pltpu.VMEM((2, 2, tokens, rows), BF16),
            pltpu.VMEM((2, tokens, width), BF16),
            pltpu.SemaphoreType.DMA((6,)),
        ],
        limit=FULL_BYTES,
        after=after,
    )


def run_last_products(bits, sent, operands, shape, after=()):
    return launch(
        partial(last_products_kernel, bits, sent),
        operands,
        [(shape, BF16)] * 2,
        after=after,
    )


STEP = 96


def steps(rows):
    step = STEP if rows % STEP == 0 else rows
    return [(start, step) for start in range(0, rows, step)]


def halve_kernel(
    bits, kept_a, got_a, kept_b, got_b, sent_a, next_a, sent_b, next_b,
    kept_a_ref, got_a_ref, kept_b_ref, got_b_ref, sems,
):
    moves, work = [], []
    for sent, outs in ((True, (sent_a, sent_b)), (False, (next_a, next_b))):
        for bit, out, kept, got, kept_ref, got_ref in (
            (bits[0], outs[0], kept_a, got_a, kept_a_ref, got_a_ref),
            (bits[1], outs[1], kept_b, got_b, kept_b_ref, got_b_ref),
        ):
            rows = out.shape[1]
            at = pl.ds(pl.multiple_of(side(bit, sent) * rows, 16), rows)
            slot = slice(0, rows) if sent else slice(rows, 2 * rows)
            moves.append((kept.at[:, at], kept_ref.at[:, slot]))
            moves.append((got.at[:, at], got_ref.at[:, slot]))
            work.append((out, kept_ref, got_ref, 0 if sent else rows))
    loads = start_loads(moves, sems)
    for i, (out, kept_ref, got_ref, first) in enumerate(work):
        loads[2 * i].wait()
        loads[2 * i + 1].wait()
        for block in range(out.shape[0]):
            for start, step in steps(out.shape[1]):
                at = slice(first + start, first + start + step)
                total = kept_ref[block, at].astype(F32) + got_ref[block, at].astype(F32)
                out[block, start : start + step] = total.astype(BF16)


def run_halve(bits, parts, after=(), estimate=SHORT):
    def half(array):
        return (array.shape[0], array.shape[1] // 2, array.shape[2]), BF16

    return launch(
        partial(halve_kernel, bits),
        parts,
        [half(parts[0]), half(parts[0]), half(parts[2]), half(parts[2])],
        in_specs=anywhere(4),
        scratch=[
            *[pltpu.VMEM(part.shape, BF16) for part in parts],
            pltpu.SemaphoreType.DMA((8,)),
        ],
        limit=FULL_BYTES,
        after=after,
        estimate=estimate,
    )


SHARED, OWNED = 32, 16
GROUPS = 6
EXTRA = 16


def line_spot():
    return lax.axis_index("seq") // 2


def pieces_of(a_ref, b_ref, count):
    at = 0
    for ref in (a_ref, b_ref):
        blocks, rows, _ = ref.shape
        size = rows // count
        for block in range(blocks):
            yield ref, block, size, at
            at += size


def scatter_kernel(with_small, bit, *refs):
    kept_a, got_a, kept_b, got_b = refs[:4]
    for out, sent in zip(refs[-2:], (True, False)):
        half = out.shape[0] // 2
        for high in range(2):
            place = 2 * high + side(bit, sent)
            for (kept, block, size, at), (got, _, _, _) in zip(
                pieces_of(kept_a, kept_b, 4), pieces_of(got_a, got_b, 4)
            ):
                rows = pl.ds(pl.multiple_of(place * size, 16), size)
                total = kept[block, rows].astype(F32) + got[block, rows].astype(F32)
                out[high * half + at : high * half + at + size] = total.astype(BF16)
            if with_small:
                at = (high + 1) * half - EXTRA
                size = SHARED // 4
                part = refs[4][pl.ds(pl.multiple_of(place * size, 8), size)]
                part = jnp.concatenate(
                    [part, jnp.zeros((EXTRA - size, part.shape[1]), F32)], axis=0
                )
                out[at : at + EXTRA] = part.astype(BF16)


def run_scatter(parts, bit, small=None, after=(), estimate=SHORT):
    share = sum(part.shape[0] * part.shape[1] for part in (parts[0], parts[2])) // 4
    share += 0 if small is None else EXTRA
    return launch(
        partial(scatter_kernel, small is not None, bit),
        parts if small is None else (*parts, small),
        [((2 * share, parts[0].shape[2]), BF16)] * 2,
        after=after,
        estimate=estimate,
    )


def split_kernel(bit, kept, got, sent, following):
    rows = sent.shape[0]
    for out, which in ((sent, side(bit, True)), (following, side(bit, False))):
        at = pl.ds(pl.multiple_of(which * rows, 16), rows)
        out[...] = (kept[at].astype(F32) + got[at].astype(F32)).astype(BF16)


def run_split(bit, kept, got, after=(), estimate=SHORT):
    rows, width = kept.shape
    return launch(
        partial(split_kernel, bit),
        (kept, got),
        [((rows // 2, width), BF16)] * 2,
        after=after,
        estimate=estimate,
    )


def pair_kernel(bit, mine, got, out):
    rows = mine.shape[0]
    out[pl.ds(pl.multiple_of(side(bit, False) * rows, 16), rows)] = mine[...]
    out[pl.ds(pl.multiple_of(side(bit, True) * rows, 16), rows)] = got[...]


def run_pair(bit, mine, got, after=(), estimate=SHORT):
    rows, width = mine.shape
    return launch(
        partial(pair_kernel, bit),
        (mine, got),
        [((2 * rows, width), BF16)],
        after=after,
        estimate=estimate,
    )


def total_kernel(with_small, *refs):
    *parts, out = refs
    if with_small:
        *parts, small = parts
    rows_in = parts[0].shape[0]
    for start, step in steps(rows_in):
        rows = slice(start, start + step)
        total = parts[0][rows].astype(F32)
        for part in parts[1:]:
            total = total + part[rows].astype(F32)
        out[rows] = total.astype(out.dtype)
    if with_small:
        out[rows_in:] = small[SHARED:].astype(out.dtype)


def run_total(parts, small=None, after=(), estimate=SHORT):
    rows, width = parts[0].shape
    return launch(
        partial(total_kernel, small is not None),
        parts if small is None else (*parts, small),
        [((rows if small is None else rows + OWNED, width), parts[0].dtype)],
        after=after,
        estimate=estimate,
    )


def total_all_kernel(parts, out):
    count, rows_in, _ = parts.shape
    for start, step in steps(rows_in):
        rows = slice(start, start + step)
        total = parts[0, rows].astype(F32)
        for place in range(1, count):
            total = total + parts[place, rows].astype(F32)
        out[rows] = total.astype(out.dtype)


def run_total_all(parts, after, kind=F32):
    return launch(total_all_kernel, (parts,), [(parts.shape[1:], kind)], after=after)


def gather_kernel(with_small, bit, mine, got, *outs):
    half = mine.shape[0] // 2
    for pair, sent in ((mine, False), (got, True)):
        for high in range(2):
            place = 2 * high + side(bit, sent)
            for out, block, size, at in pieces_of(outs[0], outs[1], 4):
                rows = pl.ds(pl.multiple_of(place * size, 16), size)
                out[block, rows] = pair[high * half + at : high * half + at + size]
            if with_small:
                at = (high + 1) * half - EXTRA - OWNED
                size = SHARED // 4
                shared = pair[at : at + EXTRA].astype(F32)[:size]
                outs[2][pl.ds(pl.multiple_of(place * size, 8), size)] = shared
                rows = pl.ds(pl.multiple_of(SHARED + place * OWNED, 8), OWNED)
                outs[2][rows] = pair[at + EXTRA : at + EXTRA + OWNED].astype(F32)


def run_gather(bit, mine, got, shapes, with_small, after=(), estimate=SHORT):
    outs = [(shape, BF16) for shape in shapes]
    if with_small:
        outs.append(((SHARED + 4 * OWNED, mine.shape[1]), F32))
    return launch(
        partial(gather_kernel, with_small, bit), (mine, got), outs, after=after, estimate=estimate
    )


def join_kernel(bits, mine_a, got_a, mine_b, got_b, out_a, out_b):
    for bit, mine, got, out in (
        (bits[0], mine_a, got_a, out_a),
        (bits[1], mine_b, got_b, out_b),
    ):
        blocks, rows, _ = mine.shape
        for source, which in ((mine, side(bit, False)), (got, side(bit, True))):
            at = pl.ds(pl.multiple_of(which * rows, 16), rows)
            for block in range(blocks):
                out[block, at] = source[block]


def run_join(bits, parts, after=()):
    def twice(array):
        return (array.shape[0], array.shape[1] * 2, array.shape[2]), BF16

    return launch(
        partial(join_kernel, bits), parts, [twice(parts[0]), twice(parts[2])], after=after
    )


PLACE = 192
SLOTS = 4


def place_all(moves, narrow, wide, sems):
    loads, stores = [], []

    def load(i):
        source, _ = moves[i]
        rows, cols = source.shape
        copy = pltpu.make_async_copy(
            source, narrow.at[i % SLOTS, :rows, :cols], sems.at[i % SLOTS]
        )
        copy.start()
        loads.append(copy)

    for i in range(min(SLOTS, len(moves))):
        load(i)
    for i, (source, target) in enumerate(moves):
        rows, cols = source.shape
        slot = i % SLOTS
        loads[i].wait()
        if i >= SLOTS:
            stores[i - SLOTS].wait()
        wide[slot, :rows, :cols] = narrow[slot, :rows, :cols].astype(F32)
        copy = pltpu.make_async_copy(wide.at[slot, :rows, :cols], target, sems.at[SLOTS + slot])
        copy.start()
        stores.append(copy)
        if i + SLOTS < len(moves):
            load(i + SLOTS)
    for copy in stores[-SLOTS:]:
        copy.wait()


def stack_kernel(bits, mine_a, mine_b, got_a, got_b, out):
    for part, (mine, got) in enumerate(((mine_a, got_a), (mine_b, got_b))):
        rows = mine.shape[1]
        for source, sent in ((mine, False), (got, True)):
            at = pl.ds(pl.multiple_of(side(bits[part], sent) * rows, 16), rows)
            out[part, at] = source[0]


def up_place_kernel(mine, other, out_hbm, narrow, wide, sems):
    core = lax.axis_index("seq") % 2
    moves = []
    for source, owner in ((mine, core), (other, 1 - core)):
        parts, rows, width = source.shape
        for part in range(parts):
            col = pl.multiple_of((2 * owner + part) * width, 128)
            for row in range(0, rows, PLACE):
                target = out_hbm.at[row : row + PLACE, pl.ds(col, width)]
                moves.append((source.at[part, row : row + PLACE], target))
    place_all(moves, narrow, wide, sems)


def down_place_kernel(mine, other, out_hbm, narrow, wide, sems):
    core = lax.axis_index("seq") % 2
    moves = []
    for source, owner in ((mine, core), (other, 1 - core)):
        parts, rows, _ = source.shape
        for part in range(parts):
            for start in range(0, rows, PLACE):
                row = pl.multiple_of((2 * owner + part) * rows + start, 16)
                target = out_hbm.at[pl.ds(row, PLACE)]
                moves.append((source.at[part, start : start + PLACE], target))
    place_all(moves, narrow, wide, sems)


def last_place_kernel(bits, sides, *refs):
    in_hbm, out_hbm, narrow, wide, sems = refs[-5:]
    core = lax.axis_index("seq") % 2
    moves = []
    for i, (sent, owner) in enumerate((s, o) for s in sides for o in (core, 1 - core)):
        source_a, source_b = refs[2 * i : 2 * i + 2]
        _, rows, width = source_a.shape
        half = width // 2
        for start in range(0, rows, PLACE):
            row = pl.multiple_of(side(bits[0], sent) * rows + start, 16)
            col = pl.multiple_of(owner * 3 * half, 128)
            moves.append(
                (
                    source_a.at[0, start : start + PLACE],
                    in_hbm.at[pl.ds(row, PLACE), pl.ds(col, width)],
                )
            )
            row = pl.multiple_of(side(bits[1], sent) * rows + start, 16)
            col = pl.multiple_of(owner * 3 * half + width, 128)
            moves.append(
                (
                    source_b.at[0, start : start + PLACE, :half],
                    in_hbm.at[pl.ds(row, PLACE), pl.ds(col, half)],
                )
            )
            col = pl.multiple_of(owner * half, 128)
            moves.append(
                (
                    source_b.at[0, start : start + PLACE, half:],
                    out_hbm.at[pl.ds(row, PLACE), pl.ds(col, half)],
                )
            )
    place_all(moves, narrow, wide, sems)


def run_place(kernel, bits, sides, sources, outs, shapes, after=()):
    width = sources[0].shape[2]
    return launch(
        partial(kernel, bits, sides),
        (*sources, *outs),
        [(shape, F32) for shape in shapes],
        in_specs=anywhere(len(sources)) + hbm(len(outs)),
        out_specs=hbm(len(shapes)),
        scratch=[
            pltpu.VMEM((SLOTS, PLACE, width), BF16),
            pltpu.VMEM((SLOTS, PLACE, width), F32),
            pltpu.SemaphoreType.DMA((2 * SLOTS,)),
        ],
        limit=PLACE_BYTES,
        after=after,
        aliases={len(sources) + i: i for i in range(len(outs))},
    )


def pack_kernel(
    third_ref, skip_ref, taps_ref, gain_one, gain_two, second_ref, first_ref, copies_ref,
    out_ref, owned_ref, hidden_ref,
):
    hidden, mine = third_ref.shape
    out_ref[...] = jnp.zeros(out_ref.shape, F32)
    width = out_ref.shape[1]
    for tap in range(KS):
        for part in range(3):
            row = 3 * tap + part
            out_ref[row : row + 1] = taps_ref[tap : tap + 1, part * width : (part + 1) * width]
    row = 3 * KS
    out_ref[row : row + 1] = gain_one[...]
    out_ref[row + 1 : row + 2] = gain_two[...]
    row += 2
    owned_ref[...] = jnp.zeros(owned_ref.shape, F32)
    owned_ref[:hidden, :mine] = third_ref[...]
    owned_ref[hidden : hidden + 1, :mine] = skip_ref[...]
    hidden_ref[...] = jnp.zeros(hidden_ref.shape, F32)
    hidden_ref[:hidden, :hidden] = second_ref[...]
    hidden_ref[hidden : hidden + first_ref.shape[0], :hidden] = first_ref[...]
    each, size = hidden_ref.shape[0] // GROUPS, owned_ref.shape[0] // GROUPS
    for group in range(GROUPS):
        lanes = slice(128 * group, 128 * (group + 1))
        out_ref[row : row + each, lanes] = hidden_ref[group * each : (group + 1) * each]
        out_ref[SHARED : SHARED + size, lanes] = owned_ref[group * size : (group + 1) * size]
    for copy in range(copies_ref.shape[0]):
        copies_ref[copy] = out_ref[...]


def small_rows(hidden, embedded):
    return -(-(hidden + 1) // GROUPS) * GROUPS, -(-(hidden + embedded) // GROUPS) * GROUPS


def run_pack(copies, third, skip, taps, gain_one, gain_two, second, first):
    owned, hidden = small_rows(second.shape[0], first.shape[0])
    return launch(
        pack_kernel,
        (third, skip, taps, gain_one, gain_two, second, first),
        [((copies, SHARED + OWNED, gain_one.shape[1]), F32)],
        scratch=[pltpu.VMEM((SHARED + OWNED, gain_one.shape[1]), F32), pltpu.VMEM((owned, 128), F32), pltpu.VMEM((hidden, 128), F32)],
    )


def unpack_kernel(
    count, mine, mine_ref, got_ref, third_ref, skip_ref, taps_ref, gain_one, gain_two, second_ref,
    first_ref, owner_ref, sum_ref, owned_ref, hidden_ref,
):
    hidden, width = third_ref.shape
    core = lax.axis_index("seq") % 2
    for spot in range(count):
        here = slice(SHARED + spot * OWNED, SHARED + (spot + 1) * OWNED)
        owner_ref[2 * spot + core] = mine_ref[here]
        owner_ref[2 * spot + 1 - core] = got_ref[here]
    sum_ref[...] = mine_ref[:SHARED] + got_ref[:SHARED]
    each, size = hidden_ref.shape[0] // GROUPS, owned_ref.shape[0] // GROUPS
    rows = owned_ref.shape[0]
    lane = lax.broadcasted_iota(jnp.int32, (rows, 128), 1)
    wide = [jnp.zeros((rows, 128), F32) for _ in range(width // 128)]
    for owner in range(2 * count):
        for group in range(GROUPS):
            lanes = slice(128 * group, 128 * (group + 1))
            owned_ref[group * size : (group + 1) * size] = owner_ref[owner, :size, lanes]
        at, shift = divmod(owner * mine, 128)
        moved = owned_ref[...]
        if shift:
            moved = pltpu.roll(moved, shift, 1)
        wide[at] = wide[at] + jnp.where(lane >= shift, moved, 0.0)
        if shift + mine > 128:
            wide[at + 1] = wide[at + 1] + jnp.where(lane < shift, moved, 0.0)
    for at, value in enumerate(wide):
        cols = slice(at * 128, (at + 1) * 128)
        third_ref[:, cols] = value[:hidden]
        skip_ref[:, cols] = value[hidden : hidden + 1]
    for tap in range(KS):
        for part in range(3):
            row = 3 * tap + part
            taps_ref[tap : tap + 1, part * width : (part + 1) * width] = sum_ref[row : row + 1]
    row = 3 * KS
    gain_one[...] = sum_ref[row : row + 1]
    gain_two[...] = sum_ref[row + 1 : row + 2]
    row += 2
    for group in range(GROUPS):
        lanes = slice(128 * group, 128 * (group + 1))
        hidden_ref[group * each : (group + 1) * each] = sum_ref[row : row + each, lanes]
    second_ref[...] = hidden_ref[:hidden, :hidden]
    first_ref[...] = hidden_ref[hidden : hidden + first_ref.shape[0], :hidden]


def run_unpack(count, mine, packed, got, hidden, embedded, after):
    width = packed.shape[1]
    owned, both = small_rows(hidden, embedded)
    shapes = (
        (hidden, width), (1, width), (KS, 3 * width), (1, width), (1, width), (hidden, hidden),
        (embedded, hidden),
    )
    return launch(
        partial(unpack_kernel, count, mine),
        (packed, got),
        [(shape, F32) for shape in shapes],
        scratch=[
            pltpu.VMEM((2 * count, OWNED, width), F32),
            pltpu.VMEM((SHARED, width), F32),
            pltpu.VMEM((owned, 128), F32),
            pltpu.VMEM((both, 128), F32),
        ],
        after=after,
    )


def mark(values):
    return launch(
        lambda *refs: None, values, (), in_specs=anywhere(len(values)), limit=FULL_BYTES
    )[1]


def hold(values, after):
    return launch(
        lambda *refs: None,
        values,
        [(value.shape, value.dtype) for value in values],
        in_specs=anywhere(len(values)),
        out_specs=anywhere(len(values)),
        limit=FULL_BYTES,
        after=after,
        aliases={i: i for i in range(len(values))},
    )[0]


class Group:
    def __init__(self, orders, line_bits, sent):
        self.orders, self.line_bits = orders, line_bits
        self.sent = sent
        self.got = self.swap(sent, 0)
        self.aways = [0]
        for bit in line_bits:
            self.aways += [away | bit for away in self.aways]
        self.direct = len(self.aways) == 4

    def bits(self, level):
        return self.orders[0][level], self.orders[1][level]

    def swap(self, pair, level):
        return tuple(swap(value, bit) for value, bit in zip(pair, self.bits(level)))

    def woven(self):
        return self.kept[0], self.got[0], self.kept[1], self.got[1]

    def halve(self, kept, after=(), estimate=SHORT):
        self.kept = kept
        (sent_a, next_a, sent_b, next_b), self.token = run_halve(
            self.bits(1), self.woven(), after, estimate
        )
        self.kept, self.sent = (next_a, next_b), (sent_a, sent_b)
        self.got = self.swap(self.sent, 1)

    def scatter(self, small=None, after=(), estimate=SHORT):
        self.shapes = [part.shape for part in self.kept]
        self.small = small
        if self.direct:
            (sent, self.line_kept), self.token = run_scatter(
                self.woven(), self.line_bits[0], small, after, estimate
            )
            self.line_got = swap(sent, self.line_bits[0])
        else:
            self.shares = tuple(
                halve(add(kept, got), lax.axis_index(AXES), self.line_bits[::-1], 1)
                for kept, got in zip(self.kept, self.got)
            )

    def split(self, after=(), estimate=SHORT):
        (sent, self.line_kept), self.token = run_split(
            self.line_bits[1], self.line_kept, self.line_got, after, estimate
        )
        self.line_got = swap(sent, self.line_bits[1])

    def total(self, after=(), estimate=SHORT):
        (self.share,), self.token = run_total(
            (self.line_kept, self.line_got), self.small, after, estimate
        )
        self.line_got = swap(self.share, self.line_bits[1])

    def pair(self, after=(), estimate=SHORT):
        (self.share,), self.token = run_pair(
            self.line_bits[1], self.share, self.line_got, after, estimate
        )
        self.line_got = swap(self.share, self.line_bits[0])

    def gather(self, after=()):
        if self.direct:
            made, self.token = run_gather(
                self.line_bits[0], self.share, self.line_got, self.shapes,
                self.small is not None, after,
            )
            self.mine = made[:2]
            if self.small is not None:
                self.small = made[2]
        else:
            self.mine = tuple(
                double(share, lax.axis_index(AXES), self.line_bits[::-1], 1)
                for share in self.shares
            )
        self.got = self.swap(self.mine, 1)

    def join(self, after=()):
        self.mine, self.token = run_join(
            self.bits(1), (self.mine[0], self.got[0], self.mine[1], self.got[1]), after
        )
        self.got = self.swap(self.mine, 0)
        self.mine_core = tuple(swap(value, 1) for value in self.mine)
        self.outs = ()

    def join_last(self, after=()):
        self.mine, self.token = run_join(
            self.bits(1), (self.mine[0], self.got[0], self.mine[1], self.got[1]), after
        )
        self.got = self.swap(self.mine, 0)

    def stack(self, after=()):
        _, rows, width = self.mine[0].shape
        (self.whole,), self.token = launch(
            partial(stack_kernel, self.bits(0)),
            (*self.mine, *self.got),
            [((2, 2 * rows, width), BF16)],
            after=after,
        )
        self.other = swap(self.whole, 1)

    def place_whole(self, kernel, shape, after=()):
        width = self.whole.shape[2]
        (out,), self.token = launch(
            kernel,
            (self.whole, self.other),
            [(shape, F32)],
            in_specs=anywhere(2),
            out_specs=hbm(1),
            scratch=[
                pltpu.VMEM((SLOTS, PLACE, width), BF16),
                pltpu.VMEM((SLOTS, PLACE, width), F32),
                pltpu.SemaphoreType.DMA((2 * SLOTS,)),
            ],
            limit=WHOLE_BYTES,
            after=after,
        )
        return out

    def place(self, kernel, shapes, after=()):
        self.outs, self.token = run_place(
            kernel, self.bits(0), (False,), (*self.mine, *self.mine_core), (), shapes, after
        )

    def finish(self, kernel, shapes, after=(), held=()):
        if held:
            self.got = hold(self.got, held)
        got_core = tuple(swap(value, 1) for value in self.got)
        sides, sources = (True,), (*self.got, *got_core)
        if not self.outs:
            sides, sources = (False, True), (*self.mine, *self.mine_core, *sources)
        outs, self.token = run_place(
            kernel, self.bits(0), sides, sources, self.outs, shapes, after
        )
        return outs


def per_device(
    hidden_in, lengths, gain_one, in_weight, short_kernel, skip_gain, decay_rate, filt_first,
    filt_second, filt_third, out_weight, gain_two, ff_up, ff_down, out_grad,
):
    rows, block, width = hidden_in.shape
    seq_count, seq_pos = lax.axis_size("seq"), lax.axis_index("seq")
    dp_count = lax.axis_size("dp")
    index = lax.axis_index(AXES)
    units = ff_up.shape[1]
    row_len = block * seq_count
    tokens = rows * block
    seq_bits = [1 << i for i in range(1, seq_count.bit_length() - 1)]
    dp_bits = [seq_count << i for i in range(dp_count.bit_length() - 1)]
    mine = width // seq_count
    padded = -(-mine // 16) * 16
    groups = seq_count if mine == padded and (width // 2) % mine == 0 else 1

    forward, inverse = spectral_tables(block)
    forward_two, inverse_three = jnp.asarray(two_pass(forward)), jnp.asarray(three_pass(inverse))
    forward_three, inverse_two = jnp.asarray(three_pass(forward.T)), jnp.asarray(two_pass(inverse.T))

    before = shifted(hidden_in[:, block - 2 :], 1)
    after = shifted(hidden_in[:, :2], -1)
    normed_one, extended, outer, signal_sent = run_front(
        lengths, hidden_in, before, after, gain_one[None], short_kernel, in_weight, groups
    )
    signal_ch = to_owner(signal_sent, mine, padded)

    signal_sent, filt_first, decay_rate, skip_gain = lax.optimization_barrier(
        (signal_sent, filt_first, decay_rate, skip_gain)
    )
    bands = (filt_first.shape[0] - 1) // 2
    spots = np.arange(row_len)
    turns = (np.arange(1, bands + 1)[:, None] * spots[None, :] % row_len) * (2.0 * math.pi / row_len)
    embedding = jnp.asarray(
        np.concatenate([spots[None, :] / row_len, np.cos(turns), np.sin(turns)], axis=0).astype(
            np.float32
        )
    )
    pre_one = jnp.einsum("ef,el->fl", filt_first, embedding, precision=FULL_PRECISION)
    act_one = jnp.sin(pre_one)
    pre_two = jnp.einsum("fg,fl->gl", filt_second, act_one, precision=FULL_PRECISION)
    act_two = jnp.sin(pre_two)
    my_third = lax.dynamic_slice_in_dim(filt_third, seq_pos * mine, mine, 1)
    my_decay = lax.dynamic_slice_in_dim(decay_rate, seq_pos * mine, mine, 0)
    my_skip = lax.dynamic_slice_in_dim(skip_gain, seq_pos * mine, mine, 0)
    my_skip = jnp.pad(my_skip, (0, padded - mine))[:, None]
    places = jnp.asarray(spots.astype(np.float32))
    envelope = jnp.exp(-my_decay[:, None] * places[None, :]) * row_len ** (-0.5)
    taps = jnp.einsum("gc,gl->cl", my_third, act_two, precision=FULL_PRECISION) * envelope
    taps = taps.reshape(mine, seq_count, block).transpose(1, 0, 2)
    if padded != mine:
        taps = jnp.pad(taps, ((0, 0), (0, padded - mine), (0, 0)))
    pieces = jnp.einsum("kct,tf->kcf", taps, jnp.asarray(forward), precision=FULL_PRECISION)
    sign = jnp.asarray(np.tile(1.0 - 2.0 * (np.arange(block) % 2), 2).astype(np.float32))
    earlier = jnp.concatenate([jnp.zeros_like(pieces[:1]), pieces[:-1]], axis=0)
    spectrum = earlier + sign * pieces
    spec_real, spec_imag = spectrum[..., :block], spectrum[..., block:]
    base = jnp.arange(block) == 0
    spectrum = (
        spec_real,
        jnp.where(base, 0.0, spec_imag),
        jnp.where(base, spec_imag, spec_real),
    )

    normed_got = swap(normed_one, 1)

    conv_ch, _ = run_conv(
        lengths, row_len, signal_ch, my_skip, spectrum, forward_two, inverse_three
    )
    conv = to_block(conv_ch, rows, mine, groups)
    if groups == 1:
        conv = conv[0]

    upstream = out_grad.reshape(tokens, width)
    upstream_got = swap(upstream, 1)
    (
        gain_two_grad, factors_mine, factors_theirs, block_out, last_mine, last_theirs, grad_middle,
        grad_outer, grad_sent,
    ) = run_middle(
        conv, mine, outer, hidden_in, gain_two[None], upstream, out_weight, ff_up, ff_down, groups,
        normed_got,
    )
    factors_got, last_got = swap(factors_theirs, 1), swap(last_theirs, 1)
    grad_ch = to_owner(grad_sent, mine, padded)
    orders = (dp_bits, dp_bits[::-1])
    firsts = (orders[0][0], orders[1][0])
    shape = (1, width // 2, width)
    up_operands = (factors_mine, factors_got)
    down_operands = (factors_mine, factors_got, upstream, upstream_got)
    up_sent, token = run_up_products(firsts, True, up_operands, shape)
    up = Group(orders, seq_bits, up_sent)
    down_sent, token = run_down_products(
        firsts, True, down_operands, shape, (token, last_got)
    )
    down = Group(orders, seq_bits, down_sent)
    outer_halo = shifted(grad_outer[:, :2], -1)

    back_ch, token = run_conv(
        lengths, row_len, grad_ch, my_skip, spectrum, forward_three, inverse_two, backward=True,
        after=(token,),
    )
    got = to_block(back_ch, rows, mine, groups)
    grad_signal, got = (got, got) if groups > 1 else got
    halo = got[:, 0, padded : padded + 2 * rows, :mine].astype(F32)
    halo = halo.transpose(1, 0, 2).reshape(rows, 2, width)
    up_kept, token = run_up_products(firsts, False, up_operands, shape, (token,))
    up.halve(up_kept)
    down_kept, token = run_down_products(firsts, False, down_operands, shape, (up.token,))
    down.halve(down_kept)
    up.scatter(None, (down.token,), BRIDGE_A)

    (proj_mine, proj_theirs, kernel_grad, gain_one_grad, input_grad), token = run_last(
        lengths, grad_signal, mine, halo, extended, grad_outer, outer_halo, hidden_in,
        gain_one[None], short_kernel, grad_middle, in_weight, (up.token,) if up.direct else (),
    )
    last_operands = (normed_one, normed_got, proj_mine, swap(proj_theirs, 1), last_mine, last_got)
    if up.direct:
        up.split((token,))
    down.scatter(None, (up.token,), BRIDGE_B)
    last_sent, token = run_last_products(
        firsts, True, last_operands, shape, (down.token,) if up.direct else ()
    )
    last = Group(orders, seq_bits, last_sent)
    last_kept, token = run_last_products(firsts, False, last_operands, shape, (token,))

    grad_taps, token = run_filter_grad(
        lengths, row_len, signal_ch, grad_ch, forward_two, inverse_two, forward_three,
        after=(token,),
    )
    envelope = jnp.pad(envelope, ((0, padded - mine), (0, 0)))
    my_third = jnp.pad(my_third, ((0, 0), (0, padded - mine)))
    net = (act_one, pre_one, act_two, pre_two)
    (my_third_grad, skip_grad, second_grad, first_grad), token = run_filter_back(
        grad_taps, envelope, net, my_third, filt_second, embedding, (token,)
    )
    small = (
        my_third_grad[:, :mine], skip_grad[:1, :mine], kernel_grad, gain_one_grad, gain_two_grad,
        second_grad, first_grad,
    )
    in_shapes = (in_weight.shape, out_weight.shape)
    if up.direct:
        (packed,), token = run_pack(dp_count, *small)
        arrived = lax.all_to_all(packed, "dp", 0, 0, tiled=True)
        up.total((token,))
        down.split((up.token,))
        last.halve(last_kept, (down.token,))
        up.pair((last.token,))
        down.total((up.token,))
        (packed,), token = run_total_all(arrived, (down.token,))
        last.scatter(packed, (token,))
        up.gather((last.token,))
        last.split((up.token,))
        down.pair((last.token,))
        up.join_last((down.token,))
        down.gather((up.token,))
        last.total((down.token,))
        down.join_last((last.token,))
        last.pair((down.token,))
        up.stack((last.token,))
        up_total = up.place_whole(up_place_kernel, ff_up.shape, (up.token,))
        last.gather((up.token,))
        last.join((last.token, mark(down.got)))
        down.stack((last.token,))
        last.place(last_place_kernel, in_shapes, (down.token,))
        down_total = down.place_whole(down_place_kernel, ff_down.shape, (last.token,))
        small, token = run_unpack(
            4, mine, last.small, swap(last.small, 1), filt_third.shape[0],
            filt_first.shape[0], (down.token,),
        )
        in_total, out_total = last.finish(last_place_kernel, in_shapes, (), (token,))
    else:
        last.halve(last_kept)
        last.scatter()
        for group in (up, down):
            group.gather()
            group.join_last()
            group.stack()
        last.gather()
        last.join()
        up_total = up.place_whole(up_place_kernel, ff_up.shape)
        down_total = down.place_whole(down_place_kernel, ff_down.shape)
        in_total, out_total = last.finish(last_place_kernel, in_shapes)
        spread = [
            lax.dynamic_update_slice_in_dim(
                jnp.zeros((part.shape[0], width), F32), part, seq_pos * mine, 1
            )
            for part in small[:2]
        ]
        small = lax.psum((*spread, small[2][:KS], *small[3:]), AXES)
    return (
        block_out, input_grad, small[3][0], in_total, small[2], small[1][0], small[6], small[5],
        small[0], out_total, small[4][0], up_total, down_total,
    )


def solution(mesh):
    tokens = P("dp", "seq", None)
    return jax.shard_map(
        per_device,
        mesh=mesh,
        in_specs=(tokens, P("dp", None)) + (P(),) * 12 + (tokens,),
        out_specs=(tokens, tokens) + (P(),) * 11,
        check_vma=False,
    )
```

```python
from functools import partial
import math

import jax
import jax.numpy as jnp
import numpy as np
from jax import lax
from jax.experimental import pallas as pl
from jax.experimental.pallas import tpu as pltpu
from jax.sharding import PartitionSpec as P

FULL_PRECISION = lax.Precision.HIGHEST
BF16 = jnp.bfloat16
F32 = jnp.float32
AXES = ("dp", "seq")
VMEM_BYTES = 32 * 1024 * 1024
FULL_BYTES = 54 * 1024 * 1024
PLACE_BYTES = 57 * 1024 * 1024
WHOLE_BYTES = 55 * 1024 * 1024
KS = 3


def swap(value, bit):
    count = lax.axis_size(AXES)
    return lax.ppermute(value, AXES, [(i, i ^ bit) for i in range(count)])


def shifted(value, steps):
    count = lax.axis_size("seq")
    first, last = max(0, -steps), min(count, count - steps)
    return lax.ppermute(value, "seq", [(i, i + steps) for i in range(first, last)])


def my_bit(index, bit):
    return (index // bit) % 2


def add(kept, got):
    return (kept.astype(F32) + got.astype(F32)).astype(kept.dtype)


def halve(value, index, bits, axis):
    for bit in bits:
        size = value.shape[axis] // 2
        mine = my_bit(index, bit)
        keep = lax.dynamic_slice_in_dim(value, mine * size, size, axis)
        send = lax.dynamic_slice_in_dim(value, (1 - mine) * size, size, axis)
        value = add(keep, swap(send, bit))
    return value


def double(value, index, bits, axis):
    for bit in reversed(bits):
        other = swap(value, bit)
        low = my_bit(index, bit) == 0
        value = jnp.concatenate(
            [jnp.where(low, value, other), jnp.where(low, other, value)], axis=axis
        )
    return value


def sum_over(value, bits):
    for bit in bits:
        value = value + swap(value, bit)
    return value


def spectral_tables(block):
    points = 2 * block
    spot = np.arange(block)
    freq = np.arange(block)
    angle = (spot[:, None] * freq[None, :] % points) * (2.0 * math.pi / points)
    real, imag = np.cos(angle), -np.sin(angle)
    imag[:, 0] = 1.0 - 2.0 * (spot % 2)
    forward = np.concatenate([real, imag], axis=1)
    late = spot + block
    angle = (freq[:, None] * late[None, :] % points) * (2.0 * math.pi / points)
    weight = np.where(freq == 0, 1.0, 2.0)[:, None] / points
    real, imag = weight * np.cos(angle), -weight * np.sin(angle)
    imag[0, :] = (1.0 - 2.0 * (late % 2)) / points
    inverse = np.concatenate([real, imag], axis=0)
    return forward.astype(np.float32), inverse.astype(np.float32)


def split_table(table):
    high = table.astype(jnp.bfloat16)
    low = (table - high.astype(np.float32)).astype(jnp.bfloat16)
    return np.asarray(high), np.asarray(low)


def two_pass(table):
    high, low = split_table(table)
    return np.concatenate([high, low], axis=0)


def three_pass(table):
    high, low = split_table(table)
    return np.concatenate([high, high, low], axis=0)


def ends_of(lengths_ref, row):
    total, ends = 0, []
    for k in range(lengths_ref.shape[1]):
        total = total + lengths_ref[row, k]
        ends.append(total)
    return ends


def next_end(ends, spot, row_len):
    found = row_len
    for end in reversed(ends):
        found = jnp.where(end > spot, end, found)
    return found


def last_end(ends, spot):
    found = 0
    for end in ends:
        found = jnp.where(end <= spot, end, found)
    return found


def near_mask(ends, spots, step):
    apart = spots < step
    for end in ends:
        apart = apart | ((end <= spots) & (end > spots - step))
    return jnp.where(apart, 0.0, 1.0)


def dot(left, right):
    return jnp.dot(left, right, preferred_element_type=F32)


def dot_nt(left, right):
    return lax.dot_general(left, right, (((1,), (1,)), ((), ())), preferred_element_type=F32)


def head_masks(ends, spot, group, rows, block, row_len):
    lane = lax.broadcasted_iota(jnp.int32, (1, 1, block), 2)
    masks = []
    for g in range(group):
        start = (spot + g) // rows * block
        stop = jnp.where((spot + g) % rows == 0, next_end(ends[0], start, row_len), 0)
        for row in range(1, rows):
            stop = jnp.where(
                (spot + g) % rows == row, next_end(ends[row], start, row_len), stop
            )
        masks.append(jnp.where(lane < stop - start, 1.0, 0.0))
    return jnp.concatenate(masks, axis=0)


def spectra(value_ref, masks, table_ref, head_out, rest_out, group):
    count, channels, block = value_ref.shape

    def step(i, carry):
        spot = pl.ds(i * group, group)
        whole = value_ref[spot].astype(F32)
        first = whole * masks(i * group)
        both = jnp.concatenate([first, whole - first], axis=0).astype(BF16)
        both = both.reshape(2 * group * channels, block)
        found = dot(jnp.concatenate([both, both], axis=1), table_ref[...])
        found = found.reshape(2 * group, channels, 2 * block)
        head_out[spot] = found[:group]
        rest_out[spot] = found[group:]
        return carry

    lax.fori_loop(0, count // group, step, 0)


def back_to_time(head_spec, rest_spec, masks, table_ref, value_ref, skip_ref, group, store):
    count, channels, double_block = head_spec.shape

    def step(i, carry):
        spot = pl.ds(i * group, group)
        both = jnp.concatenate([head_spec[spot], rest_spec[spot]], axis=0)
        both = both.reshape(2 * group * channels, double_block)
        high = both.astype(BF16)
        low = (both - high.astype(F32)).astype(BF16)
        found = dot(jnp.concatenate([high, low, high], axis=1), table_ref[...])
        found = found.reshape(2 * group, channels, double_block // 2)
        rest = found[group:]
        found = rest + masks(i * group) * (found[:group] - rest)
        store(i * group, found + skip_ref[...][None] * value_ref[spot].astype(F32))
        return carry

    lax.fori_loop(0, count // group, step, 0)


def of_row(per_row, row):
    found = per_row[0]
    for k in range(1, len(per_row)):
        found = jnp.where(row == k, per_row[k], found)
    return found


def start_loads(moves, sems):
    loads = [
        pltpu.make_async_copy(source, target, sems.at[i])
        for i, (source, target) in enumerate(moves)
    ]
    for load in loads:
        load.start()
    return loads


def conv_kernel(
    rows, group, row_len, lengths_ref, value_ref, skip_ref, hr_ref, hi_ref, hm_ref,
    forward_ref, inverse_ref, out_ref, head_spec, rest_spec, head_sum, rest_sum,
):
    count, channels, block = value_ref.shape
    ends = [ends_of(lengths_ref, row) for row in range(rows)]

    def masks(spot):
        return head_masks(ends, spot, group, rows, block, row_len)

    spectra(value_ref, masks, forward_ref, head_spec, rest_spec, group)

    def product(real, imag, lag):
        hr, hi, hm = hr_ref[lag], hi_ref[lag], hm_ref[lag]
        return real * hr - imag * hi, real * hi + imag * hm

    def own(j, carry):
        start = j // rows * block
        stop = of_row([next_end(e, start, row_len) for e in ends], j % rows)
        plain = (stop >= start + block).astype(F32)
        head_real, head_imag = product(head_spec[j, :, :block], head_spec[j, :, block:], 0)
        head_sum[j, :, :block] = head_real
        head_sum[j, :, block:] = head_imag
        rest_real, rest_imag = product(rest_spec[j, :, :block], rest_spec[j, :, block:], 0)
        rest_sum[j, :, :block] = rest_real
        rest_sum[j, :, block:] = rest_imag
        rest_spec[j] = rest_spec[j] + plain * head_spec[j]
        return carry

    lax.fori_loop(0, count, own, 0)

    def reach(j, carry):
        spot, row = j // rows, j % rows
        begin = of_row([last_end(e, spot * block) for e in ends], row) // block

        def include(source, sums):
            k = source * rows + row
            real, imag = product(
                rest_spec[k, :, :block], rest_spec[k, :, block:], spot - source
            )
            return sums[0] + real, sums[1] + imag

        start = (head_sum[j, :, :block], head_sum[j, :, block:])
        real, imag = lax.fori_loop(begin, spot, include, start)
        head_sum[j, :, :block] = real
        head_sum[j, :, block:] = imag
        return carry

    lax.fori_loop(rows, count, reach, 0)

    def store(spot, found):
        out_ref[pl.ds(spot, group)] = found.astype(BF16)

    back_to_time(head_sum, rest_sum, masks, inverse_ref, value_ref, skip_ref, group, store)


def conv_back_kernel(
    rows, group, row_len, lengths_ref, value_ref, skip_hbm, hr_hbm, hi_hbm, hm_hbm,
    forward_hbm, inverse_hbm, out_ref, skip_ref, hr_ref, hi_ref, hm_ref, forward_ref, inverse_ref,
    sems, head_spec, rest_spec, head_sum, rest_sum, found_ref,
):
    count, channels, block = value_ref.shape
    loads = start_loads(
        [
            (inverse_hbm, inverse_ref), (hr_hbm, hr_ref), (hi_hbm, hi_ref), (hm_hbm, hm_ref),
            (forward_hbm, forward_ref), (skip_hbm, skip_ref),
        ],
        sems,
    )
    ends = [ends_of(lengths_ref, row) for row in range(rows)]

    def masks(spot):
        return head_masks(ends, spot, group, rows, block, row_len)

    loads[0].wait()
    spectra(value_ref, masks, inverse_ref, head_spec, rest_spec, group)
    for load in loads[1:]:
        load.wait()

    def product(real, imag, lag):
        hr, hi, hm = hr_ref[lag], hi_ref[lag], hm_ref[lag]
        return real * hr + imag * hi, imag * hm - real * hi

    def reach(j, carry):
        spot, row = j // rows, j % rows
        start = spot * block
        plain = of_row([next_end(e, start, row_len) for e in ends], row) >= start + block
        plain = plain.astype(F32)
        until = of_row([next_end(e, start + block - 1, row_len) for e in ends], row)
        until = (until - 1) // block + 1

        def include(source, sums):
            k = source * rows + row
            real, imag = product(
                head_spec[k, :, :block], head_spec[k, :, block:], source - spot
            )
            return sums[0] + real, sums[1] + imag

        empty = jnp.zeros((channels, block), F32)
        real, imag = lax.fori_loop(spot + 1, until, include, (empty, empty))
        head_real, head_imag = product(head_spec[j, :, :block], head_spec[j, :, block:], 0)
        head_sum[j, :, :block] = head_real + plain * real
        head_sum[j, :, block:] = head_imag + plain * imag
        rest_real, rest_imag = product(rest_spec[j, :, :block], rest_spec[j, :, block:], 0)
        rest_sum[j, :, :block] = rest_real + (1.0 - plain) * real
        rest_sum[j, :, block:] = rest_imag + (1.0 - plain) * imag
        return carry

    lax.fori_loop(0, count, reach, 0)

    def store(spot, found):
        found_ref[pl.ds(spot, group)] = found
        out_ref[pl.ds(spot, group), :channels] = found.astype(BF16)

    back_to_time(head_sum, rest_sum, masks, forward_ref, value_ref, skip_ref, group, store)

    lane = lax.broadcasted_iota(jnp.int32, (channels, block), 1)
    per_turn = block // 2
    blocks = count // rows
    for turn in range(-(-count // per_turn)):
        first = turn * per_turn
        last = min(count, first + per_turn)

        def gather(j, picked):
            at = 2 * (j - first)
            moved = pltpu.roll(found_ref[j], at, 1)
            return jnp.where((lane >= at) & (lane < at + 2), moved, picked)

        picked = lax.fori_loop(first, last, gather, jnp.zeros((channels, block), F32))
        if channels < block:
            picked = jnp.concatenate(
                [picked, jnp.zeros((block - channels, block), F32)], axis=0
            )
        flipped = picked.T
        for spot in range(first // rows, last // rows):
            at = 2 * (spot * rows - first)
            tile = jnp.concatenate(
                [flipped[at : at + 2 * rows], jnp.zeros((16 - 2 * rows, block), F32)], axis=0
            )
            if spot > 0:
                out_ref[(spot - 1) * rows, channels:] = tile.astype(BF16)
    out_ref[(blocks - 1) * rows, channels:] = jnp.zeros((16, block), BF16)
    for spot in range(blocks):
        for row in range(1, rows):
            out_ref[spot * rows + row, channels:] = jnp.zeros((16, block), BF16)


def filter_grad_kernel(
    rows, group, row_len, lengths_ref, value_ref, grad_ref, forward_ref,
    inverse_ref, back_ref, out_ref, head_spec, rest_spec, grad_head, grad_rest, total,
):
    count, channels, block = value_ref.shape
    lags = count // rows
    ends = [ends_of(lengths_ref, row) for row in range(rows)]

    def masks(spot):
        return head_masks(ends, spot, group, rows, block, row_len)

    spectra(value_ref, masks, forward_ref, head_spec, rest_spec, group)
    spectra(grad_ref, masks, inverse_ref, grad_head, grad_rest, group)
    lane = lax.broadcasted_iota(jnp.int32, (channels, block), 1)
    base = lane == 0

    def product(grad, spec, k, j):
        gr, gi = grad[k, :, :block], grad[k, :, block:]
        sr, si = spec[j, :, :block], spec[j, :, block:]
        masked = jnp.where(base, 0.0, si)
        swapped = jnp.where(base, si, sr)
        return gr * sr + gi * masked, gi * swapped - gr * masked

    def own(j, sums):
        start = j // rows * block
        stop = of_row([next_end(e, start, row_len) for e in ends], j % rows)
        plain = (stop >= start + block).astype(F32)
        head = product(grad_head, head_spec, j, j)
        rest = product(grad_rest, rest_spec, j, j)
        rest_spec[j] = rest_spec[j] + plain * head_spec[j]
        return sums[0] + head[0] + rest[0], sums[1] + head[1] + rest[1]

    empty = jnp.zeros((channels, block), F32)
    real, imag = lax.fori_loop(0, count, own, (empty, empty))
    total[0, :, :block] = real
    total[0, :, block:] = imag

    def one_lag(lag, carry):
        def include(j, sums):
            spot = j // rows
            begin = of_row([last_end(e, spot * block) for e in ends], j % rows) // block
            near = (begin <= spot - lag).astype(F32)
            real, imag = product(grad_head, rest_spec, j, j - lag * rows)
            return sums[0] + near * real, sums[1] + near * imag

        real, imag = lax.fori_loop(lag * rows, count, include, (empty, empty))
        total[lag, :, :block] = real
        total[lag, :, block:] = imag
        return carry

    lax.fori_loop(1, lags, one_lag, 0)
    wide = lax.broadcasted_iota(jnp.int32, (channels, 2 * block), 1)
    sign = (1 - 2 * (wide % 2)).astype(F32)
    total[lags] = jnp.zeros((channels, 2 * block), F32)

    def one_piece(lag, carry):
        piece = total[lag + 1] + sign * total[lag]
        high = piece.astype(BF16)
        low = (piece - high.astype(F32)).astype(BF16)
        out_ref[lag] = dot(jnp.concatenate([high, low, high], axis=1), back_ref[...])
        return carry

    lax.fori_loop(0, lags, one_piece, 0)


def vmem(count):
    return [pl.BlockSpec(memory_space=pltpu.VMEM)] * count


def smem(count):
    return [pl.BlockSpec(memory_space=pltpu.SMEM)] * count


def hbm(count):
    return [pl.BlockSpec(memory_space=pltpu.HBM)] * count


def anywhere(count):
    return [pl.BlockSpec(memory_space=pl.ANY)] * count


def params(limit=VMEM_BYTES):
    return pltpu.CompilerParams(vmem_limit_bytes=limit)


SHORT = pl.CostEstimate(flops=1, bytes_accessed=1, transcendentals=0)


def takes(micro):
    return pl.CostEstimate(flops=int(micro * 1e9), bytes_accessed=1, transcendentals=0)


BRIDGE_A, BRIDGE_B = takes(2), takes(12)
LINE = takes(8)

TOKEN = (12288, 1024), F32


def launch(
    kernel, operands, outs, in_specs=None, out_specs=None, scratch=(), limit=VMEM_BYTES, after=(),
    aliases=None, estimate=SHORT,
):
    used, made = len(operands), len(outs)

    def call(*refs):
        rest = refs[used + len(after) :]
        kernel(*refs[:used], *rest[:made], *rest[made + 1 :])

    results = pl.pallas_call(
        call,
        name=getattr(kernel, "func", kernel).__name__.replace("<lambda>", "hold"),
        out_shape=tuple(jax.ShapeDtypeStruct(*out) for out in (*outs, TOKEN)),
        in_specs=(vmem(used) if in_specs is None else in_specs) + anywhere(len(after)),
        out_specs=tuple((vmem(made) if out_specs is None else out_specs) + hbm(1)),
        scratch_shapes=list(scratch),
        input_output_aliases=aliases or {},
        compiler_params=params(limit),
        cost_estimate=estimate,
    )(*operands, *after)
    return tuple(results[:-1]), results[-1]


def run_conv(
    lengths, row_len, value, skip, spectrum, forward, inverse, backward=False, after=()
):
    count, channels, block = value.shape
    rows = lengths.shape[0]
    group = 4 if count % 4 == 0 else 1
    spec = pltpu.VMEM((count, channels, 2 * block), F32)
    extra = [pltpu.VMEM((count, channels, block), F32)] if backward else []
    sent = channels + 16 if backward else channels
    operands = (lengths, value, skip, *spectrum, forward, inverse)
    if not backward:
        (found,), token = launch(
            partial(conv_kernel, rows, group, row_len),
            operands,
            [((count, sent, block), BF16)],
            in_specs=smem(1) + vmem(7),
            scratch=[spec] * 4,
            after=after,
        )
        return found, token
    (found,), token = launch(
        partial(conv_back_kernel, rows, group, row_len),
        operands,
        [((count, sent, block), BF16)],
        in_specs=smem(1) + vmem(1) + anywhere(6),
        scratch=[
            *[pltpu.VMEM(part.shape, part.dtype) for part in (skip, *spectrum, forward, inverse)],
            pltpu.SemaphoreType.DMA((6,)),
            *[spec] * 4,
            *extra,
        ],
        after=after,
    )
    return found, token


def run_filter_grad(lengths, row_len, value, grad, forward, inverse, back, after=()):
    count, channels, block = value.shape
    rows = lengths.shape[0]
    group = 4 if count % 4 == 0 else 1
    lags = count // rows
    spec = pltpu.VMEM((count, channels, 2 * block), F32)
    (found,), token = launch(
        partial(filter_grad_kernel, rows, group, row_len),
        (lengths, value, grad, forward, inverse, back),
        [((lags, channels, block), F32)],
        in_specs=smem(1) + vmem(5),
        scratch=[spec] * 4 + [pltpu.VMEM((lags + 1, channels, 2 * block), F32)],
        after=after,
    )
    return found, token


def exact(left, right, contract):
    return lax.dot_general(
        left, right, (contract, ((), ())), precision=FULL_PRECISION, preferred_element_type=F32
    )


def filter_back_kernel(
    taps_ref, envelope_ref, act_one_ref, pre_one_ref, act_two_ref, pre_two_ref, third_ref,
    second_ref, embedding_ref, third_grad, skip_grad, second_grad, first_grad,
):
    lags, channels, block = taps_ref.shape
    pick = lax.broadcasted_iota(jnp.int32, (8, block), 1) == 0
    skip_grad[...] = exact(jnp.where(pick, 1.0, 0.0), taps_ref[0], ((1,), (1,)))
    third_grad[...] = jnp.zeros(third_grad.shape, F32)
    second_grad[...] = jnp.zeros(second_grad.shape, F32)
    first_grad[...] = jnp.zeros(first_grad.shape, F32)

    def one_lag(lag, carry):
        here = pl.ds(pl.multiple_of(lag * block, 128), block)
        grad = taps_ref[lag] * envelope_ref[:, here]
        third_grad[...] += exact(act_two_ref[:, here], grad, ((1,), (1,)))
        grad = jnp.cos(pre_two_ref[:, here]) * exact(third_ref[...], grad, ((1,), (0,)))
        second_grad[...] += exact(act_one_ref[:, here], grad, ((1,), (1,)))
        grad = jnp.cos(pre_one_ref[:, here]) * exact(second_ref[...], grad, ((1,), (0,)))
        first_grad[...] += exact(embedding_ref[:, here], grad, ((1,), (1,)))
        return carry

    lax.fori_loop(0, lags, one_lag, 0)


def run_filter_back(taps, envelope, net, third, second, embedding, after):
    hidden, channels = third.shape
    return launch(
        filter_back_kernel,
        (taps, envelope, *net, third, second, embedding),
        [
            ((hidden, channels), F32),
            ((8, channels), F32),
            ((hidden, hidden), F32),
            ((embedding.shape[0], hidden), F32),
        ],
        after=after,
    )


def put_channels(ref, row, chunk, value):
    groups, _, size, _ = ref.shape
    wide = value.shape[0]
    if groups == 1:
        ref[0, row, chunk * wide : (chunk + 1) * wide] = value
    else:
        per = wide // size
        for k in range(per):
            ref[chunk * per + k, row] = value[k * size : (k + 1) * size]


def get_channels(ref, row, chunk, wide, size):
    groups = ref.shape[0]
    if groups == 1:
        return ref[0, row, chunk * wide : (chunk + 1) * wide]
    per = wide // size
    return jnp.concatenate([ref[chunk * per + k, row, :size] for k in range(per)], axis=0)


def moments(value):
    center = value - jnp.mean(value, axis=-1, keepdims=True)
    spread = jnp.mean(center * center, axis=-1, keepdims=True)
    return center, lax.rsqrt(spread + 1e-05)


def norm_back(center, scale, gain, grad):
    unit = center * scale
    inner = grad * gain
    mean_one = jnp.mean(inner, axis=-1, keepdims=True)
    mean_two = jnp.mean(inner * unit, axis=-1, keepdims=True)
    return scale * (inner - mean_one - unit * mean_two), grad * unit


PIECE = 64


def front_kernel(
    lengths_ref, before_ref, after_ref, gain_ref, hidden_hbm, taps_hbm, weight_hbm,
    normed_hbm, extended_hbm, outer_hbm, sent_hbm,
    hidden_ref, taps_ref, weight_ref, normed_ref, extended_ref, outer_ref, sent_ref,
    halo_ref, wide_ref, mixed_ref, sems,
):
    rows, block, width = hidden_ref.shape
    loads = [
        pltpu.make_async_copy(source, target, sems.at[i])
        for i, (source, target) in enumerate(
            [(hidden_hbm, hidden_ref), (weight_hbm, weight_ref), (taps_hbm, taps_ref)]
        )
    ]
    for load in loads:
        load.start()
    gain = gain_ref[...]
    halo = jnp.concatenate(
        [part for row in range(rows) for part in (before_ref[row], after_ref[row])], axis=0
    ).astype(F32)
    center, scale = moments(halo)
    halo = center * scale * gain
    halo_ref[...] = jnp.concatenate(
        [halo, jnp.zeros((halo_ref.shape[0] - 4 * rows, width), F32)], axis=0
    ).astype(BF16)
    first = lax.axis_index("seq") * block
    ends = [ends_of(lengths_ref, row) for row in range(rows)]
    spots = first + lax.broadcasted_iota(jnp.int32, (block, 1), 0)
    near_one = [near_mask(e, spots, 1) for e in ends]
    near_two = [near_mask(e, spots, 2) for e in ends]
    live = [jnp.where(spots < e[-1], 1.0, 0.0) for e in ends]
    loads[0].wait()
    for row in range(rows):
        for start in range(0, block, PIECE):
            center, scale = moments(hidden_ref[row, start : start + PIECE].astype(F32))
            at = row * block + start
            normed_ref[at : at + PIECE] = (center * scale * gain).astype(BF16)
    saves = [
        pltpu.make_async_copy(source, target, sems.at[3 + i])
        for i, (source, target) in enumerate(
            [
                (normed_ref, normed_hbm),
                (sent_ref, sent_hbm),
                (extended_ref, extended_hbm),
                (outer_ref, outer_hbm),
            ]
        )
    ]
    saves[0].start()
    chunk = width // 2
    loads[1].wait()
    loads[2].wait()
    for part in range(3):
        for half in range(2):
            cols = slice(part * width + half * chunk, part * width + (half + 1) * chunk)
            main = dot(normed_ref[...], weight_ref[:, cols])
            edge = dot(halo_ref[...], weight_ref[:, cols])
            taps = taps_ref[:, cols]
            for row in range(rows):
                wide_ref[row, 0:8] = jnp.zeros((8, chunk), F32)
                wide_ref[row, block + 8 :] = jnp.zeros((8, chunk), F32)
                wide_ref[row, 6:8] = edge[4 * row : 4 * row + 2]
                wide_ref[row, 8 : block + 8] = main[row * block : (row + 1) * block]
                wide_ref[row, block + 8 : block + 10] = edge[4 * row + 2 : 4 * row + 4]
                rounded = wide_ref[row].astype(BF16)
                extended_ref[row, :, cols] = rounded
                wide_ref[row] = rounded.astype(F32)
                mixed = (
                    taps[0:1] * wide_ref[row, 8 : block + 8]
                    + taps[1:2] * wide_ref[row, 7 : block + 7] * near_one[row]
                    + taps[2:3] * wide_ref[row, 6 : block + 6] * near_two[row]
                )
                here = slice(half * chunk, (half + 1) * chunk)
                if part == 0:
                    mixed_ref[row, :, here] = mixed
                elif part == 1:
                    signal = mixed_ref[row, :, here] * mixed * live[row]
                    put_channels(sent_ref, row, half, signal.T.astype(BF16))
                else:
                    outer_ref[row, :, here] = mixed
        if part == 1:
            saves[1].start()
    saves[2].start()
    saves[3].start()
    for save in saves:
        save.wait()


def run_front(lengths, hidden, before, after, gain, taps, weight, groups):
    rows, block, width = hidden.shape
    chunk = width // 2
    outs = (
        ((rows * block, width), BF16),
        ((rows, block + 16, 3 * width), BF16),
        ((rows, block, width), F32),
        ((groups, rows, width // groups, block), BF16),
    )
    return pl.pallas_call(
        front_kernel,
        out_shape=tuple(jax.ShapeDtypeStruct(*out) for out in outs),
        in_specs=smem(1) + vmem(3) + hbm(3),
        out_specs=tuple(hbm(4)),
        scratch_shapes=[
            pltpu.VMEM(hidden.shape, BF16),
            pltpu.VMEM(taps.shape, F32),
            pltpu.VMEM(weight.shape, BF16),
            *[pltpu.VMEM(*out) for out in outs],
            pltpu.VMEM((16, width), BF16),
            pltpu.VMEM((rows, block + 16, chunk), F32),
            pltpu.VMEM((rows, block, width), F32),
            pltpu.SemaphoreType.DMA((7,)),
        ],
        compiler_params=params(FULL_BYTES),
        cost_estimate=SHORT,
    )(lengths, before, after, gain, hidden, taps, weight)


def middle_kernel(
    size, conv_ref, gain_ref, outer_hbm, hidden_hbm, upstream_hbm, out_hbm, up_hbm, down_hbm,
    gain_grad_ref, factors_mine_hbm, factors_theirs_hbm, result_hbm, last_mine_hbm, last_theirs_hbm,
    grad_middle_hbm, grad_outer_hbm, sent_hbm,
    outer_ref, hidden_ref, upstream_ref, out_ref, up_ref, down_ref,
    factors_ref, result_ref, last_ref, grad_middle_ref, grad_outer_ref, sent_ref,
    conv_scr, middle_ref, grad_ref, sems,
):
    rows, block, width = hidden_ref.shape
    parts = down_ref.shape[0] // width
    per_core = parts // 2
    units = per_core * width
    chunk = width // 2
    core = lax.axis_index("seq") % 2
    copies = [
        pltpu.make_async_copy(outer_hbm, outer_ref, sems.at[0]),
        pltpu.make_async_copy(out_hbm, out_ref, sems.at[1]),
        pltpu.make_async_copy(hidden_hbm, hidden_ref, sems.at[2]),
        pltpu.make_async_copy(upstream_hbm, upstream_ref, sems.at[3]),
    ]
    for part in range(parts):
        cols = slice(part * width, (part + 1) * width)
        copies.append(
            pltpu.make_async_copy(up_hbm.at[:, cols], up_ref.at[:, cols], sems.at[2 * part + 4])
        )
        copies.append(
            pltpu.make_async_copy(down_hbm.at[cols], down_ref.at[cols], sems.at[2 * part + 5])
        )
    for copy in copies:
        copy.start()
    saves = [
        pltpu.make_async_copy(source, target, sems.at[2 * parts + 4 + i])
        for i, (source, target) in enumerate(
            [
                (result_ref, result_hbm),
                (grad_middle_ref, grad_middle_hbm),
                (last_ref.at[0], last_mine_hbm),
                (last_ref.at[1], last_theirs_hbm),
                (sent_ref, sent_hbm),
                (grad_outer_ref, grad_outer_hbm),
                (factors_ref.at[1], factors_theirs_hbm),
                (factors_ref.at[0], factors_mine_hbm),
            ]
        )
    ]
    for row in range(rows):
        here = slice(row * block, (row + 1) * block)
        for half in range(2):
            cols = slice(half * chunk, (half + 1) * chunk)
            conv_scr[here, cols] = get_channels(conv_ref, row, half, chunk, size).astype(F32).T
    copies[0].wait()
    for row in range(rows):
        here = slice(row * block, (row + 1) * block)
        gated = (outer_ref[row] * conv_scr[here]).astype(BF16)
        last_ref[0, here, :width] = gated
        last_ref[1, here, :width] = gated
    copies[1].wait()
    middle_ref[...] = dot(last_ref[0, :, :width], out_ref[...])
    copies[2].wait()
    gain = gain_ref[...]
    normed = slice(2 * units, 2 * units + width)
    for row in range(rows):
        for start in range(0, block, PIECE):
            here = slice(row * block + start, row * block + start + PIECE)
            middle = middle_ref[here] + hidden_ref[row, start : start + PIECE].astype(F32)
            middle_ref[here] = middle
            center, scale = moments(middle)
            rounded = (center * scale * gain).astype(BF16)
            factors_ref[0, here, normed] = rounded
            factors_ref[1, here, normed] = rounded
    slope = math.sqrt(2.0 / math.pi)
    copies[3].wait()
    for part in range(parts):
        cols = slice(part * width, (part + 1) * width)
        copies[2 * part + 4].wait()
        pre = dot(factors_ref[0, :, normed], up_ref[:, cols])
        copies[2 * part + 5].wait()
        grad_act = dot_nt(upstream_ref[...], down_ref[cols])
        square = pre * pre
        bend = jnp.tanh(slope * pre * (1.0 + 0.044715 * square))
        half_up = 0.5 * (1.0 + bend)
        act = (pre * half_up).astype(BF16)
        turn = half_up + 0.5 * pre * (1.0 - bend * bend) * (
            slope * (1.0 + 3.0 * 0.044715 * square)
        )
        grad_pre = (grad_act * turn).astype(BF16)
        slot = (part // per_core + core) % 2
        at = part % per_core * width
        factors_ref[slot, :, at : at + width] = act
        factors_ref[slot, :, units + at : units + at + width] = grad_pre
        if part == 0:
            grad_ref[...] = dot_nt(grad_pre, up_ref[:, cols])
        else:
            grad_ref[...] += dot_nt(grad_pre, up_ref[:, cols])
        found = dot(act, down_ref[cols])
        for row in range(rows):
            here = slice(row * block, (row + 1) * block)
            if part == 0:
                grad_middle_ref[here] = middle_ref[here] + found[here]
            elif part < parts - 1:
                grad_middle_ref[here] += found[here]
            else:
                result_ref[row] = (grad_middle_ref[here] + found[here]).astype(BF16)
    saves[6].start()
    saves[7].start()
    saves[0].start()
    gain_grad = jnp.zeros((1, width), F32)
    branch_cols = slice(width, width + chunk)
    for at in range(0, rows * block, PIECE):
        here = slice(at, at + PIECE)
        center, scale = moments(middle_ref[here])
        grad, terms = norm_back(center, scale, gain, grad_ref[here])
        gain_grad = gain_grad + jnp.sum(terms, axis=0, keepdims=True)
        grad = upstream_ref[here].astype(F32) + grad
        grad_middle_ref[here] = grad
        branch = grad.astype(BF16)

        last_ref[core, here, branch_cols] = branch[:, :chunk]
        last_ref[1 - core, here, branch_cols] = branch[:, chunk:]

    for save in saves[1:4]:
        save.start()
    gain_grad_ref[...] = gain_grad
    grad_ref[...] = dot_nt(grad_middle_ref[...].astype(BF16), out_ref[...])
    for row in range(rows):
        here = slice(row * block, (row + 1) * block)
        for half in range(2):
            cols = slice(half * chunk, (half + 1) * chunk)
            grad_conv = grad_ref[here, cols] * outer_ref[row, :, cols]
            put_channels(sent_ref, row, half, grad_conv.T.astype(BF16))
    saves[4].start()
    for row in range(rows):
        here = slice(row * block, (row + 1) * block)
        grad_outer_ref[row] = grad_ref[here] * conv_scr[here]
    saves[5].start()
    for save in saves:
        save.wait()


def run_middle(conv, size, outer, hidden, gain, upstream, out_weight, up, down, groups, after):
    rows, block, width = hidden.shape
    tokens = rows * block
    units = up.shape[1]
    parts = units // width
    near = (((1, width), F32),)
    far = (
        ((tokens, units + width), BF16),
        ((tokens, units + width), BF16),
        ((rows, block, width), BF16),
        ((tokens, 3 * width // 2), BF16),
        ((tokens, 3 * width // 2), BF16),
        ((tokens, width), F32),
        ((rows, block, width), F32),
        ((groups, rows, width // groups, block), BF16),
    )
    return pl.pallas_call(
        lambda *refs: middle_kernel(size, *refs[:8], *refs[9:]),
        out_shape=tuple(jax.ShapeDtypeStruct(*out) for out in near + far),
        in_specs=vmem(2) + hbm(6) + anywhere(1),
        out_specs=tuple(vmem(1) + hbm(8)),
        scratch_shapes=[
            pltpu.VMEM(outer.shape, F32),
            pltpu.VMEM(hidden.shape, BF16),
            pltpu.VMEM(upstream.shape, BF16),
            pltpu.VMEM(out_weight.shape, BF16),
            pltpu.VMEM(up.shape, BF16),
            pltpu.VMEM(down.shape, BF16),
            pltpu.VMEM((2, *far[0][0]), BF16),
            pltpu.VMEM(*far[2]),
            pltpu.VMEM((2, *far[3][0]), BF16),
            *[pltpu.VMEM(*out) for out in far[5:]],
            pltpu.VMEM((tokens, width), F32),
            pltpu.VMEM((tokens, width), F32),
            pltpu.VMEM((tokens, width), F32),
            pltpu.SemaphoreType.DMA((2 * parts + 12,)),
        ],
        compiler_params=params(FULL_BYTES),
        cost_estimate=SHORT,
    )(conv, gain, outer, hidden, upstream, out_weight, up, down, after)


def last_kernel(
    size, lengths_ref, signal_ref, halo_ref, outer_halo_ref, gain_ref, taps_ref,
    extended_hbm, outer_hbm, hidden_hbm, grad_middle_hbm, weight_hbm,
    proj_mine, proj_theirs, taps_grad_ref, gain_grad_ref, result_hbm,
    extended_ref, outer_ref, hidden_ref, grad_middle_ref, weight_ref, result_ref,
    wide_ref, mixed_ref, grad_ref, proj_ref, normed_grad, sems,
):
    rows, block, width = hidden_ref.shape
    chunk = width // 2
    loads = [
        pltpu.make_async_copy(source, target, sems.at[i])
        for i, (source, target) in enumerate(
            [
                (extended_hbm, extended_ref),
                (outer_hbm, outer_ref),
                (weight_hbm, weight_ref),
                (hidden_hbm, hidden_ref),
                (grad_middle_hbm, grad_middle_ref),
            ]
        )
    ]
    for load in loads:
        load.start()
    core = lax.axis_index("seq") % 2
    first = lax.axis_index("seq") * block
    longer = block + 8
    spots = first + lax.broadcasted_iota(jnp.int32, (longer, 1), 0)
    taps_grad_ref[...] = jnp.zeros(taps_grad_ref.shape, F32)
    loads[0].wait()
    loads[1].wait()
    for row in range(rows):
        ends = ends_of(lengths_ref, row)
        near_one, near_two = near_mask(ends, spots, 1), near_mask(ends, spots, 2)
        live = jnp.where(spots < ends[-1], 1.0, 0.0)
        for half in range(2):
            cols = slice(half * chunk, (half + 1) * chunk)
            grad_ref[0, :block] = get_channels(signal_ref, row, half, chunk, size).astype(F32).T
            grad_ref[0, block:] = jnp.concatenate(
                [halo_ref[row, :, cols], jnp.zeros((6, chunk), F32)], axis=0
            )
            for part in range(2):
                at = slice(part * width + half * chunk, part * width + (half + 1) * chunk)
                taps = taps_ref[:, at]
                wide_ref[part] = extended_ref[row, :, at].astype(F32)
                mixed_ref[part] = (
                    taps[0:1] * wide_ref[part, 8 : longer + 8]
                    + taps[1:2] * wide_ref[part, 7 : longer + 7] * near_one
                    + taps[2:3] * wide_ref[part, 6 : longer + 6] * near_two
                )
            at = slice(2 * width + half * chunk, 2 * width + (half + 1) * chunk)
            wide_ref[2] = extended_ref[row, :, at].astype(F32)
            signal_grad = grad_ref[0] * live
            grad_ref[0] = signal_grad * mixed_ref[1]
            grad_ref[1] = signal_grad * mixed_ref[0]
            grad_ref[2, :block] = outer_ref[row, :, cols]
            grad_ref[2, block:] = jnp.concatenate(
                [outer_halo_ref[row, :, cols], jnp.zeros((6, chunk), F32)], axis=0
            )
            for part in range(3):
                at = slice(part * width + half * chunk, part * width + (half + 1) * chunk)
                taps = taps_ref[:, at]
                own = grad_ref[part, :block]
                proj = (
                    taps[0:1] * own
                    + taps[1:2] * (grad_ref[part, 1 : block + 1] * near_one[1 : block + 1])
                    + taps[2:3] * (grad_ref[part, 2 : block + 2] * near_two[2 : block + 2])
                )
                proj_ref[row * block : (row + 1) * block, at] = proj.astype(BF16)
                taps_grad_ref[0:1, at] += jnp.sum(
                    own * wide_ref[part, 8 : block + 8], axis=0, keepdims=True
                )
                taps_grad_ref[1:2, at] += jnp.sum(
                    own * wide_ref[part, 7 : block + 7] * near_one[:block], axis=0, keepdims=True
                )
                taps_grad_ref[2:3, at] += jnp.sum(
                    own * wide_ref[part, 6 : block + 6] * near_two[:block], axis=0, keepdims=True
                )
    middle = 3 * width // 2

    @pl.when(core == 0)
    def _():
        proj_mine[...] = proj_ref[:, :middle]
        proj_theirs[...] = proj_ref[:, middle:]

    @pl.when(core != 0)
    def _():
        proj_mine[...] = proj_ref[:, middle:]
        proj_theirs[...] = proj_ref[:, :middle]

    loads[2].wait()
    normed_grad[...] = dot_nt(proj_ref[...], weight_ref[...])
    loads[3].wait()
    loads[4].wait()
    gain = gain_ref[...]
    gain_grad = jnp.zeros((1, width), F32)
    for row in range(rows):
        for start in range(0, block, PIECE):
            here = slice(row * block + start, row * block + start + PIECE)
            center, scale = moments(hidden_ref[row, start : start + PIECE].astype(F32))
            grad, terms = norm_back(center, scale, gain, normed_grad[here])
            gain_grad = gain_grad + jnp.sum(terms, axis=0, keepdims=True)
            result_ref[row, start : start + PIECE] = grad_middle_ref[here] + grad
    gain_grad_ref[...] = gain_grad
    save = pltpu.make_async_copy(result_ref, result_hbm, sems.at[5])
    save.start()
    save.wait()


def run_last(
    lengths, signal, size, halo, extended, outer, outer_halo, hidden, gain, taps, grad_middle,
    weight, after,
):
    rows, block, width = hidden.shape
    tokens = rows * block
    chunk = width // 2
    middle = 3 * width // 2
    return launch(
        partial(last_kernel, size),
        (
            lengths, signal, halo, outer_halo, gain, taps, extended, outer, hidden, grad_middle,
            weight,
        ),
        [
            ((tokens, middle), BF16),
            ((tokens, middle), BF16),
            ((8, 3 * width), F32),
            ((1, width), F32),
            (hidden.shape, F32),
        ],
        in_specs=smem(1) + vmem(5) + hbm(5),
        out_specs=vmem(4) + hbm(1),
        scratch=[
            pltpu.VMEM(extended.shape, BF16),
            pltpu.VMEM(outer.shape, F32),
            pltpu.VMEM(hidden.shape, BF16),
            pltpu.VMEM(grad_middle.shape, F32),
            pltpu.VMEM(weight.shape, BF16),
            pltpu.VMEM(hidden.shape, F32),
            pltpu.VMEM((3, block + 16, chunk), F32),
            pltpu.VMEM((2, block + 8, chunk), F32),
            pltpu.VMEM((3, block + 8, chunk), F32),
            pltpu.VMEM((tokens, 3 * width), BF16),
            pltpu.VMEM((tokens, width), F32),
            pltpu.SemaphoreType.DMA((6,)),
        ],
        limit=FULL_BYTES,
        after=after,
    )


def to_owner(sent, mine, padded):
    count = lax.axis_size("seq")
    groups, rows, size, block = sent.shape
    if groups != count:
        sent = sent.reshape(rows, count, mine, block).transpose(1, 0, 2, 3)
    got = lax.all_to_all(sent, "seq", 0, 0, tiled=True).reshape(count * rows, mine, block)
    if padded != mine:
        got = jnp.pad(got, ((0, 0), (0, padded - mine), (0, 0)))
    return got


def to_block(value, rows, mine, groups):
    count = lax.axis_size("seq")
    size, block = value.shape[1:]
    got = lax.all_to_all(
        value.reshape(count, rows, size, block), "seq", 0, 0, tiled=True
    )
    if groups == count:
        return got
    return got[:, :, :mine].transpose(1, 0, 2, 3).reshape(1, rows, count * mine, block), got


def dot_tn(left, right):
    return lax.dot_general(left, right, (((0,), (0,)), ((), ())), preferred_element_type=F32)


def bit_inside(bit):
    count = lax.axis_size("seq")
    if bit < count:
        return lax.axis_index("seq") // bit % 2
    return lax.axis_index("dp") // (bit // count) % 2


def side(bit, sent):
    mine = bit_inside(bit)
    return 1 - mine if sent else mine


def up_products_kernel(
    bits, sent, mine_hbm, got_hbm, a_ref, b_ref, left_ref, right_ref, sems
):
    _, rows, width = a_ref.shape
    units = 2 * width
    moves = []
    for part in range(2):
        at = pl.multiple_of(2 * units + side(bits[part], sent) * rows, 128)
        cols = slice(units + part * width, units + (part + 1) * width)
        for i, factors in enumerate((mine_hbm, got_hbm)):
            moves.append((factors.at[:, pl.ds(at, rows)], left_ref.at[part, i]))
            moves.append((factors.at[:, cols], right_ref.at[part, i]))
    loads = start_loads(moves, sems)
    for part, out in enumerate((a_ref, b_ref)):
        for load in loads[4 * part : 4 * part + 4]:
            load.wait()
        found = dot_tn(left_ref[part, 0], right_ref[part, 0]) + dot_tn(
            left_ref[part, 1], right_ref[part, 1]
        )
        out[0] = found.astype(BF16)


def down_products_kernel(
    bits, sent, mine_hbm, got_hbm, upstream_hbm, upstream_got_hbm, a_ref, b_ref,
    left_ref, right_ref, sems,
):
    _, rows, width = a_ref.shape
    moves = [(upstream_hbm, right_ref.at[0]), (upstream_got_hbm, right_ref.at[1])]
    for part in range(2):
        at = pl.multiple_of(part * width + side(bits[part], sent) * rows, 128)
        for i, factors in enumerate((mine_hbm, got_hbm)):
            moves.append((factors.at[:, pl.ds(at, rows)], left_ref.at[part, i]))
    loads = start_loads(moves, sems)
    loads[0].wait()
    loads[1].wait()
    for part, out in enumerate((a_ref, b_ref)):
        loads[2 * part + 2].wait()
        loads[2 * part + 3].wait()
        found = dot_tn(left_ref[part, 0], right_ref[0]) + dot_tn(left_ref[part, 1], right_ref[1])
        out[0] = found.astype(BF16)


def last_products_kernel(
    bits, sent, normed_ref, normed_got_ref, proj_ref, proj_got_ref, last_ref, last_got_ref,
    a_ref, b_ref,
):
    rows, width = a_ref.shape[1:]
    half = width // 2
    at = pl.multiple_of(side(bits[0], sent) * rows, 128)
    found = dot_tn(normed_ref[:, pl.ds(at, rows)], proj_ref[:, :width]) + dot_tn(
        normed_got_ref[:, pl.ds(at, rows)], proj_got_ref[:, :width]
    )
    a_ref[0] = found.astype(BF16)
    at = pl.multiple_of(side(bits[1], sent) * rows, 128)
    found = dot_tn(normed_ref[:, pl.ds(at, rows)], proj_ref[:, width:]) + dot_tn(
        normed_got_ref[:, pl.ds(at, rows)], proj_got_ref[:, width:]
    )
    b_ref[0, :, :half] = found.astype(BF16)
    found = dot_tn(last_ref[:, pl.ds(at, rows)], last_ref[:, width:]) + dot_tn(
        last_got_ref[:, pl.ds(at, rows)], last_got_ref[:, width:]
    )
    b_ref[0, :, half:] = found.astype(BF16)


def run_up_products(bits, sent, operands, shape, after=()):
    tokens, (_, rows, width) = operands[0].shape[0], shape
    return launch(
        partial(up_products_kernel, bits, sent),
        operands,
        [(shape, BF16)] * 2,
        in_specs=anywhere(2),
        scratch=[
            pltpu.VMEM((2, 2, tokens, rows), BF16),
            pltpu.VMEM((2, 2, tokens, width), BF16),
            pltpu.SemaphoreType.DMA((8,)),
        ],
        limit=FULL_BYTES,
        after=after,
    )


def run_down_products(bits, sent, operands, shape, after=()):
    tokens, (_, rows, width) = operands[0].shape[0], shape
    return launch(
        partial(down_products_kernel, bits, sent),
        operands,
        [(shape, BF16)] * 2,
        in_specs=anywhere(4),
        scratch=[
            pltpu.VMEM((2, 2, tokens, rows), BF16),
            pltpu.VMEM((2, tokens, width), BF16),
            pltpu.SemaphoreType.DMA((6,)),
        ],
        limit=FULL_BYTES,
        after=after,
    )


def run_last_products(bits, sent, operands, shape, after=()):
    return launch(
        partial(last_products_kernel, bits, sent),
        operands,
        [(shape, BF16)] * 2,
        after=after,
    )


STEP = 96


def steps(rows):
    step = STEP if rows % STEP == 0 else rows
    return [(start, step) for start in range(0, rows, step)]


def halve_kernel(
    bits, kept_a, got_a, kept_b, got_b, sent_a, next_a, sent_b, next_b,
    kept_a_ref, got_a_ref, kept_b_ref, got_b_ref, sems,
):
    moves, work = [], []
    for sent, outs in ((True, (sent_a, sent_b)), (False, (next_a, next_b))):
        for bit, out, kept, got, kept_ref, got_ref in (
            (bits[0], outs[0], kept_a, got_a, kept_a_ref, got_a_ref),
            (bits[1], outs[1], kept_b, got_b, kept_b_ref, got_b_ref),
        ):
            rows = out.shape[1]
            at = pl.ds(pl.multiple_of(side(bit, sent) * rows, 16), rows)
            slot = slice(0, rows) if sent else slice(rows, 2 * rows)
            moves.append((kept.at[:, at], kept_ref.at[:, slot]))
            moves.append((got.at[:, at], got_ref.at[:, slot]))
            work.append((out, kept_ref, got_ref, 0 if sent else rows))
    loads = start_loads(moves, sems)
    for i, (out, kept_ref, got_ref, first) in enumerate(work):
        loads[2 * i].wait()
        loads[2 * i + 1].wait()
        for block in range(out.shape[0]):
            for start, step in steps(out.shape[1]):
                at = slice(first + start, first + start + step)
                total = kept_ref[block, at].astype(F32) + got_ref[block, at].astype(F32)
                out[block, start : start + step] = total.astype(BF16)


def run_halve(bits, parts, after=(), estimate=SHORT):
    def half(array):
        return (array.shape[0], array.shape[1] // 2, array.shape[2]), BF16

    return launch(
        partial(halve_kernel, bits),
        parts,
        [half(parts[0]), half(parts[0]), half(parts[2]), half(parts[2])],
        in_specs=anywhere(4),
        scratch=[
            *[pltpu.VMEM(part.shape, BF16) for part in parts],
            pltpu.SemaphoreType.DMA((8,)),
        ],
        limit=FULL_BYTES,
        after=after,
        estimate=estimate,
    )


SHARED, OWNED = 32, 16
GROUPS = 6
EXTRA = 16


def line_spot():
    return lax.axis_index("seq") // 2


def pieces_of(a_ref, b_ref, count):
    at = 0
    for ref in (a_ref, b_ref):
        blocks, rows, _ = ref.shape
        size = rows // count
        for block in range(blocks):
            yield ref, block, size, at
            at += size


def scatter_kernel(with_small, bit, *refs):
    kept_a, got_a, kept_b, got_b = refs[:4]
    for out, sent in zip(refs[-2:], (True, False)):
        half = out.shape[0] // 2
        for high in range(2):
            place = 2 * high + side(bit, sent)
            for (kept, block, size, at), (got, _, _, _) in zip(
                pieces_of(kept_a, kept_b, 4), pieces_of(got_a, got_b, 4)
            ):
                rows = pl.ds(pl.multiple_of(place * size, 16), size)
                total = kept[block, rows].astype(F32) + got[block, rows].astype(F32)
                out[high * half + at : high * half + at + size] = total.astype(BF16)
            if with_small:
                at = (high + 1) * half - EXTRA
                size = SHARED // 4
                part = refs[4][pl.ds(pl.multiple_of(place * size, 8), size)]
                part = jnp.concatenate(
                    [part, jnp.zeros((EXTRA - size, part.shape[1]), F32)], axis=0
                )
                out[at : at + EXTRA] = part.astype(BF16)


def run_scatter(parts, bit, small=None, after=(), estimate=SHORT):
    share = sum(part.shape[0] * part.shape[1] for part in (parts[0], parts[2])) // 4
    share += 0 if small is None else EXTRA
    return launch(
        partial(scatter_kernel, small is not None, bit),
        parts if small is None else (*parts, small),
        [((2 * share, parts[0].shape[2]), BF16)] * 2,
        after=after,
        estimate=estimate,
    )


def split_kernel(bit, kept, got, sent, following):
    rows = sent.shape[0]
    for out, which in ((sent, side(bit, True)), (following, side(bit, False))):
        at = pl.ds(pl.multiple_of(which * rows, 16), rows)
        out[...] = (kept[at].astype(F32) + got[at].astype(F32)).astype(BF16)


def run_split(bit, kept, got, after=(), estimate=SHORT):
    rows, width = kept.shape
    return launch(
        partial(split_kernel, bit),
        (kept, got),
        [((rows // 2, width), BF16)] * 2,
        after=after,
        estimate=estimate,
    )


def pair_kernel(bit, mine, got, out):
    rows = mine.shape[0]
    out[pl.ds(pl.multiple_of(side(bit, False) * rows, 16), rows)] = mine[...]
    out[pl.ds(pl.multiple_of(side(bit, True) * rows, 16), rows)] = got[...]


def run_pair(bit, mine, got, after=(), estimate=SHORT):
    rows, width = mine.shape
    return launch(
        partial(pair_kernel, bit),
        (mine, got),
        [((2 * rows, width), BF16)],
        after=after,
        estimate=estimate,
    )


def total_kernel(with_small, *refs):
    *parts, out = refs
    if with_small:
        *parts, small = parts
    rows_in = parts[0].shape[0]
    for start, step in steps(rows_in):
        rows = slice(start, start + step)
        total = parts[0][rows].astype(F32)
        for part in parts[1:]:
            total = total + part[rows].astype(F32)
        out[rows] = total.astype(out.dtype)
    if with_small:
        out[rows_in:] = small[SHARED:].astype(out.dtype)


def run_total(parts, small=None, after=(), estimate=SHORT):
    rows, width = parts[0].shape
    return launch(
        partial(total_kernel, small is not None),
        parts if small is None else (*parts, small),
        [((rows if small is None else rows + OWNED, width), parts[0].dtype)],
        after=after,
        estimate=estimate,
    )


def total_all_kernel(parts, out):
    count, rows_in, _ = parts.shape
    for start, step in steps(rows_in):
        rows = slice(start, start + step)
        total = parts[0, rows].astype(F32)
        for place in range(1, count):
            total = total + parts[place, rows].astype(F32)
        out[rows] = total.astype(out.dtype)


def run_total_all(parts, after, kind=F32):
    return launch(total_all_kernel, (parts,), [(parts.shape[1:], kind)], after=after)


def gather_kernel(with_small, bit, mine, got, *outs):
    half = mine.shape[0] // 2
    for pair, sent in ((mine, False), (got, True)):
        for high in range(2):
            place = 2 * high + side(bit, sent)
            for out, block, size, at in pieces_of(outs[0], outs[1], 4):
                rows = pl.ds(pl.multiple_of(place * size, 16), size)
                out[block, rows] = pair[high * half + at : high * half + at + size]
            if with_small:
                at = (high + 1) * half - EXTRA - OWNED
                size = SHARED // 4
                shared = pair[at : at + EXTRA].astype(F32)[:size]
                outs[2][pl.ds(pl.multiple_of(place * size, 8), size)] = shared
                rows = pl.ds(pl.multiple_of(SHARED + place * OWNED, 8), OWNED)
                outs[2][rows] = pair[at + EXTRA : at + EXTRA + OWNED].astype(F32)


def run_gather(bit, mine, got, shapes, with_small, after=(), estimate=SHORT):
    outs = [(shape, BF16) for shape in shapes]
    if with_small:
        outs.append(((SHARED + 4 * OWNED, mine.shape[1]), F32))
    return launch(
        partial(gather_kernel, with_small, bit), (mine, got), outs, after=after, estimate=estimate
    )


def join_kernel(bits, mine_a, got_a, mine_b, got_b, out_a, out_b):
    for bit, mine, got, out in (
        (bits[0], mine_a, got_a, out_a),
        (bits[1], mine_b, got_b, out_b),
    ):
        blocks, rows, _ = mine.shape
        for source, which in ((mine, side(bit, False)), (got, side(bit, True))):
            at = pl.ds(pl.multiple_of(which * rows, 16), rows)
            for block in range(blocks):
                out[block, at] = source[block]


def run_join(bits, parts, after=()):
    def twice(array):
        return (array.shape[0], array.shape[1] * 2, array.shape[2]), BF16

    return launch(
        partial(join_kernel, bits), parts, [twice(parts[0]), twice(parts[2])], after=after
    )


PLACE = 192
SLOTS = 8


def place_all(moves, narrow, wide, sems):
    loads, stores = [], []

    def load(i):
        source, _ = moves[i]
        rows, cols = source.shape
        copy = pltpu.make_async_copy(
            source, narrow.at[i % SLOTS, :rows, :cols], sems.at[i % SLOTS]
        )
        copy.start()
        loads.append(copy)

    for i in range(min(SLOTS, len(moves))):
        load(i)
    for i, (source, target) in enumerate(moves):
        rows, cols = source.shape
        slot = i % SLOTS
        loads[i].wait()
        if i >= SLOTS:
            stores[i - SLOTS].wait()
        wide[slot, :rows, :cols] = narrow[slot, :rows, :cols].astype(F32)
        copy = pltpu.make_async_copy(wide.at[slot, :rows, :cols], target, sems.at[SLOTS + slot])
        copy.start()
        stores.append(copy)
        if i + SLOTS < len(moves):
            load(i + SLOTS)
    for copy in stores[-SLOTS:]:
        copy.wait()


def stack_kernel(bits, mine_a, mine_b, got_a, got_b, out):
    for part, (mine, got) in enumerate(((mine_a, got_a), (mine_b, got_b))):
        rows = mine.shape[1]
        for source, sent in ((mine, False), (got, True)):
            at = pl.ds(pl.multiple_of(side(bits[part], sent) * rows, 16), rows)
            out[part, at] = source[0]


def up_place_kernel(mine, other, out_hbm, narrow, wide, sems):
    core = lax.axis_index("seq") % 2
    moves = []
    for source, owner in ((mine, core), (other, 1 - core)):
        parts, rows, width = source.shape
        for part in range(parts):
            col = pl.multiple_of((2 * owner + part) * width, 128)
            for row in range(0, rows, PLACE):
                target = out_hbm.at[row : row + PLACE, pl.ds(col, width)]
                moves.append((source.at[part, row : row + PLACE], target))
    place_all(moves, narrow, wide, sems)


def down_place_kernel(mine, other, out_hbm, narrow, wide, sems):
    core = lax.axis_index("seq") % 2
    moves = []
    for source, owner in ((mine, core), (other, 1 - core)):
        parts, rows, _ = source.shape
        for part in range(parts):
            for start in range(0, rows, PLACE):
                row = pl.multiple_of((2 * owner + part) * rows + start, 16)
                target = out_hbm.at[pl.ds(row, PLACE)]
                moves.append((source.at[part, start : start + PLACE], target))
    place_all(moves, narrow, wide, sems)


def last_place_kernel(bits, sides, *refs):
    in_hbm, out_hbm, narrow, wide, sems = refs[-5:]
    core = lax.axis_index("seq") % 2
    moves = []
    for i, (sent, owner) in enumerate((s, o) for s in sides for o in (core, 1 - core)):
        source_a, source_b = refs[2 * i : 2 * i + 2]
        _, rows, width = source_a.shape
        half = width // 2
        for start in range(0, rows, PLACE):
            row = pl.multiple_of(side(bits[0], sent) * rows + start, 16)
            col = pl.multiple_of(owner * 3 * half, 128)
            moves.append(
                (
                    source_a.at[0, start : start + PLACE],
                    in_hbm.at[pl.ds(row, PLACE), pl.ds(col, width)],
                )
            )
            row = pl.multiple_of(side(bits[1], sent) * rows + start, 16)
            col = pl.multiple_of(owner * 3 * half + width, 128)
            moves.append(
                (
                    source_b.at[0, start : start + PLACE, :half],
                    in_hbm.at[pl.ds(row, PLACE), pl.ds(col, half)],
                )
            )
            col = pl.multiple_of(owner * half, 128)
            moves.append(
                (
                    source_b.at[0, start : start + PLACE, half:],
                    out_hbm.at[pl.ds(row, PLACE), pl.ds(col, half)],
                )
            )
    place_all(moves, narrow, wide, sems)


def run_place(kernel, bits, sides, sources, outs, shapes, after=()):
    width = sources[0].shape[2]
    return launch(
        partial(kernel, bits, sides),
        (*sources, *outs),
        [(shape, F32) for shape in shapes],
        in_specs=anywhere(len(sources)) + hbm(len(outs)),
        out_specs=hbm(len(shapes)),
        scratch=[
            pltpu.VMEM((SLOTS, PLACE, width), BF16),
            pltpu.VMEM((SLOTS, PLACE, width), F32),
            pltpu.SemaphoreType.DMA((2 * SLOTS,)),
        ],
        limit=PLACE_BYTES,
        after=after,
        aliases={len(sources) + i: i for i in range(len(outs))},
    )


def pack_kernel(
    third_ref, skip_ref, taps_ref, gain_one, gain_two, second_ref, first_ref, copies_ref,
    out_ref, owned_ref, hidden_ref,
):
    hidden, mine = third_ref.shape
    out_ref[...] = jnp.zeros(out_ref.shape, F32)
    width = out_ref.shape[1]
    for tap in range(KS):
        for part in range(3):
            row = 3 * tap + part
            out_ref[row : row + 1] = taps_ref[tap : tap + 1, part * width : (part + 1) * width]
    row = 3 * KS
    out_ref[row : row + 1] = gain_one[...]
    out_ref[row + 1 : row + 2] = gain_two[...]
    row += 2
    owned_ref[...] = jnp.zeros(owned_ref.shape, F32)
    owned_ref[:hidden, :mine] = third_ref[...]
    owned_ref[hidden : hidden + 1, :mine] = skip_ref[...]
    hidden_ref[...] = jnp.zeros(hidden_ref.shape, F32)
    hidden_ref[:hidden, :hidden] = second_ref[...]
    hidden_ref[hidden : hidden + first_ref.shape[0], :hidden] = first_ref[...]
    each, size = hidden_ref.shape[0] // GROUPS, owned_ref.shape[0] // GROUPS
    for group in range(GROUPS):
        lanes = slice(128 * group, 128 * (group + 1))
        out_ref[row : row + each, lanes] = hidden_ref[group * each : (group + 1) * each]
        out_ref[SHARED : SHARED + size, lanes] = owned_ref[group * size : (group + 1) * size]
    for copy in range(copies_ref.shape[0]):
        copies_ref[copy] = out_ref[...]


def small_rows(hidden, embedded):
    return -(-(hidden + 1) // GROUPS) * GROUPS, -(-(hidden + embedded) // GROUPS) * GROUPS


def run_pack(copies, third, skip, taps, gain_one, gain_two, second, first):
    owned, hidden = small_rows(second.shape[0], first.shape[0])
    return launch(
        pack_kernel,
        (third, skip, taps, gain_one, gain_two, second, first),
        [((copies, SHARED + OWNED, gain_one.shape[1]), F32)],
        scratch=[pltpu.VMEM((SHARED + OWNED, gain_one.shape[1]), F32), pltpu.VMEM((owned, 128), F32), pltpu.VMEM((hidden, 128), F32)],
    )


def unpack_kernel(
    count, mine, mine_ref, got_ref, third_ref, skip_ref, taps_ref, gain_one, gain_two, second_ref,
    first_ref, owner_ref, sum_ref, owned_ref, hidden_ref,
):
    hidden, width = third_ref.shape
    core = lax.axis_index("seq") % 2
    for spot in range(count):
        here = slice(SHARED + spot * OWNED, SHARED + (spot + 1) * OWNED)
        owner_ref[2 * spot + core] = mine_ref[here]
        owner_ref[2 * spot + 1 - core] = got_ref[here]
    sum_ref[...] = mine_ref[:SHARED] + got_ref[:SHARED]
    each, size = hidden_ref.shape[0] // GROUPS, owned_ref.shape[0] // GROUPS
    rows = owned_ref.shape[0]
    lane = lax.broadcasted_iota(jnp.int32, (rows, 128), 1)
    wide = [jnp.zeros((rows, 128), F32) for _ in range(width // 128)]
    for owner in range(2 * count):
        for group in range(GROUPS):
            lanes = slice(128 * group, 128 * (group + 1))
            owned_ref[group * size : (group + 1) * size] = owner_ref[owner, :size, lanes]
        at, shift = divmod(owner * mine, 128)
        moved = owned_ref[...]
        if shift:
            moved = pltpu.roll(moved, shift, 1)
        wide[at] = wide[at] + jnp.where(lane >= shift, moved, 0.0)
        if shift + mine > 128:
            wide[at + 1] = wide[at + 1] + jnp.where(lane < shift, moved, 0.0)
    for at, value in enumerate(wide):
        cols = slice(at * 128, (at + 1) * 128)
        third_ref[:, cols] = value[:hidden]
        skip_ref[:, cols] = value[hidden : hidden + 1]
    for tap in range(KS):
        for part in range(3):
            row = 3 * tap + part
            taps_ref[tap : tap + 1, part * width : (part + 1) * width] = sum_ref[row : row + 1]
    row = 3 * KS
    gain_one[...] = sum_ref[row : row + 1]
    gain_two[...] = sum_ref[row + 1 : row + 2]
    row += 2
    for group in range(GROUPS):
        lanes = slice(128 * group, 128 * (group + 1))
        hidden_ref[group * each : (group + 1) * each] = sum_ref[row : row + each, lanes]
    second_ref[...] = hidden_ref[:hidden, :hidden]
    first_ref[...] = hidden_ref[hidden : hidden + first_ref.shape[0], :hidden]


def run_unpack(count, mine, packed, got, hidden, embedded, after):
    width = packed.shape[1]
    owned, both = small_rows(hidden, embedded)
    shapes = (
        (hidden, width), (1, width), (KS, 3 * width), (1, width), (1, width), (hidden, hidden),
        (embedded, hidden),
    )
    return launch(
        partial(unpack_kernel, count, mine),
        (packed, got),
        [(shape, F32) for shape in shapes],
        scratch=[
            pltpu.VMEM((2 * count, OWNED, width), F32),
            pltpu.VMEM((SHARED, width), F32),
            pltpu.VMEM((owned, 128), F32),
            pltpu.VMEM((both, 128), F32),
        ],
        after=after,
    )


def mark(values):
    return launch(
        lambda *refs: None, values, (), in_specs=anywhere(len(values)), limit=FULL_BYTES
    )[1]


def hold(values, after):
    return launch(
        lambda *refs: None,
        values,
        [(value.shape, value.dtype) for value in values],
        in_specs=anywhere(len(values)),
        out_specs=anywhere(len(values)),
        limit=FULL_BYTES,
        after=after,
        aliases={i: i for i in range(len(values))},
    )[0]


class Group:
    def __init__(self, orders, line_bits, sent):
        self.orders, self.line_bits = orders, line_bits
        self.sent = sent
        self.got = self.swap(sent, 0)
        self.aways = [0]
        for bit in line_bits:
            self.aways += [away | bit for away in self.aways]
        self.direct = len(self.aways) == 4

    def bits(self, level):
        return self.orders[0][level], self.orders[1][level]

    def swap(self, pair, level):
        return tuple(swap(value, bit) for value, bit in zip(pair, self.bits(level)))

    def woven(self):
        return self.kept[0], self.got[0], self.kept[1], self.got[1]

    def halve(self, kept, after=(), estimate=SHORT):
        self.kept = kept
        (sent_a, next_a, sent_b, next_b), self.token = run_halve(
            self.bits(1), self.woven(), after, estimate
        )
        self.kept, self.sent = (next_a, next_b), (sent_a, sent_b)
        self.got = self.swap(self.sent, 1)

    def scatter(self, small=None, after=(), estimate=SHORT):
        self.shapes = [part.shape for part in self.kept]
        self.small = small
        if self.direct:
            (sent, self.line_kept), self.token = run_scatter(
                self.woven(), self.line_bits[0], small, after, estimate
            )
            self.line_got = swap(sent, self.line_bits[0])
        else:
            self.shares = tuple(
                halve(add(kept, got), lax.axis_index(AXES), self.line_bits[::-1], 1)
                for kept, got in zip(self.kept, self.got)
            )

    def split(self, after=(), estimate=SHORT):
        (sent, self.line_kept), self.token = run_split(
            self.line_bits[1], self.line_kept, self.line_got, after, estimate
        )
        self.line_got = swap(sent, self.line_bits[1])

    def total(self, after=(), estimate=SHORT):
        (self.share,), self.token = run_total(
            (self.line_kept, self.line_got), self.small, after, estimate
        )
        self.line_got = swap(self.share, self.line_bits[1])

    def pair(self, after=(), estimate=SHORT):
        (self.share,), self.token = run_pair(
            self.line_bits[1], self.share, self.line_got, after, estimate
        )
        self.line_got = swap(self.share, self.line_bits[0])

    def gather(self, after=()):
        if self.direct:
            made, self.token = run_gather(
                self.line_bits[0], self.share, self.line_got, self.shapes,
                self.small is not None, after,
            )
            self.mine = made[:2]
            if self.small is not None:
                self.small = made[2]
        else:
            self.mine = tuple(
                double(share, lax.axis_index(AXES), self.line_bits[::-1], 1)
                for share in self.shares
            )
        self.got = self.swap(self.mine, 1)

    def join(self, after=()):
        self.mine, self.token = run_join(
            self.bits(1), (self.mine[0], self.got[0], self.mine[1], self.got[1]), after
        )
        self.got = self.swap(self.mine, 0)
        self.mine_core = tuple(swap(value, 1) for value in self.mine)
        self.outs = ()

    def join_last(self, after=()):
        self.mine, self.token = run_join(
            self.bits(1), (self.mine[0], self.got[0], self.mine[1], self.got[1]), after
        )
        self.got = self.swap(self.mine, 0)

    def stack(self, after=()):
        _, rows, width = self.mine[0].shape
        (self.whole,), self.token = launch(
            partial(stack_kernel, self.bits(0)),
            (*self.mine, *self.got),
            [((2, 2 * rows, width), BF16)],
            after=after,
        )
        self.other = swap(self.whole, 1)

    def place_whole(self, kernel, shape, after=()):
        width = self.whole.shape[2]
        (out,), self.token = launch(
            kernel,
            (self.whole, self.other),
            [(shape, F32)],
            in_specs=anywhere(2),
            out_specs=hbm(1),
            scratch=[
                pltpu.VMEM((SLOTS, PLACE, width), BF16),
                pltpu.VMEM((SLOTS, PLACE, width), F32),
                pltpu.SemaphoreType.DMA((2 * SLOTS,)),
            ],
            limit=WHOLE_BYTES,
            after=after,
        )
        return out

    def place(self, kernel, shapes, after=()):
        self.outs, self.token = run_place(
            kernel, self.bits(0), (False,), (*self.mine, *self.mine_core), (), shapes, after
        )

    def finish(self, kernel, shapes, after=(), held=()):
        if held:
            self.got = hold(self.got, held)
        got_core = tuple(swap(value, 1) for value in self.got)
        sides, sources = (True,), (*self.got, *got_core)
        if not self.outs:
            sides, sources = (False, True), (*self.mine, *self.mine_core, *sources)
        outs, self.token = run_place(
            kernel, self.bits(0), sides, sources, self.outs, shapes, after
        )
        return outs


def per_device(
    hidden_in, lengths, gain_one, in_weight, short_kernel, skip_gain, decay_rate, filt_first,
    filt_second, filt_third, out_weight, gain_two, ff_up, ff_down, out_grad,
):
    rows, block, width = hidden_in.shape
    seq_count, seq_pos = lax.axis_size("seq"), lax.axis_index("seq")
    dp_count = lax.axis_size("dp")
    index = lax.axis_index(AXES)
    units = ff_up.shape[1]
    row_len = block * seq_count
    tokens = rows * block
    seq_bits = [1 << i for i in range(1, seq_count.bit_length() - 1)]
    dp_bits = [seq_count << i for i in range(dp_count.bit_length() - 1)]
    mine = width // seq_count
    padded = -(-mine // 16) * 16
    groups = seq_count if mine == padded and (width // 2) % mine == 0 else 1

    forward, inverse = spectral_tables(block)
    forward_two, inverse_three = jnp.asarray(two_pass(forward)), jnp.asarray(three_pass(inverse))
    forward_three, inverse_two = jnp.asarray(three_pass(forward.T)), jnp.asarray(two_pass(inverse.T))

    before = shifted(hidden_in[:, block - 2 :], 1)
    after = shifted(hidden_in[:, :2], -1)
    normed_one, extended, outer, signal_sent = run_front(
        lengths, hidden_in, before, after, gain_one[None], short_kernel, in_weight, groups
    )
    signal_ch = to_owner(signal_sent, mine, padded)

    signal_sent, filt_first, decay_rate, skip_gain = lax.optimization_barrier(
        (signal_sent, filt_first, decay_rate, skip_gain)
    )
    bands = (filt_first.shape[0] - 1) // 2
    spots = np.arange(row_len)
    turns = (np.arange(1, bands + 1)[:, None] * spots[None, :] % row_len) * (2.0 * math.pi / row_len)
    embedding = jnp.asarray(
        np.concatenate([spots[None, :] / row_len, np.cos(turns), np.sin(turns)], axis=0).astype(
            np.float32
        )
    )
    pre_one = jnp.einsum("ef,el->fl", filt_first, embedding, precision=FULL_PRECISION)
    act_one = jnp.sin(pre_one)
    pre_two = jnp.einsum("fg,fl->gl", filt_second, act_one, precision=FULL_PRECISION)
    act_two = jnp.sin(pre_two)
    my_third = lax.dynamic_slice_in_dim(filt_third, seq_pos * mine, mine, 1)
    my_decay = lax.dynamic_slice_in_dim(decay_rate, seq_pos * mine, mine, 0)
    my_skip = lax.dynamic_slice_in_dim(skip_gain, seq_pos * mine, mine, 0)
    my_skip = jnp.pad(my_skip, (0, padded - mine))[:, None]
    places = jnp.asarray(spots.astype(np.float32))
    envelope = jnp.exp(-my_decay[:, None] * places[None, :]) * row_len ** (-0.5)
    taps = jnp.einsum("gc,gl->cl", my_third, act_two, precision=FULL_PRECISION) * envelope
    taps = taps.reshape(mine, seq_count, block).transpose(1, 0, 2)
    if padded != mine:
        taps = jnp.pad(taps, ((0, 0), (0, padded - mine), (0, 0)))
    pieces = jnp.einsum("kct,tf->kcf", taps, jnp.asarray(forward), precision=FULL_PRECISION)
    sign = jnp.asarray(np.tile(1.0 - 2.0 * (np.arange(block) % 2), 2).astype(np.float32))
    earlier = jnp.concatenate([jnp.zeros_like(pieces[:1]), pieces[:-1]], axis=0)
    spectrum = earlier + sign * pieces
    spec_real, spec_imag = spectrum[..., :block], spectrum[..., block:]
    base = jnp.arange(block) == 0
    spectrum = (
        spec_real,
        jnp.where(base, 0.0, spec_imag),
        jnp.where(base, spec_imag, spec_real),
    )

    normed_got = swap(normed_one, 1)

    conv_ch, _ = run_conv(
        lengths, row_len, signal_ch, my_skip, spectrum, forward_two, inverse_three
    )
    conv = to_block(conv_ch, rows, mine, groups)
    if groups == 1:
        conv = conv[0]

    upstream = out_grad.reshape(tokens, width)
    upstream_got = swap(upstream, 1)
    (
        gain_two_grad, factors_mine, factors_theirs, block_out, last_mine, last_theirs, grad_middle,
        grad_outer, grad_sent,
    ) = run_middle(
        conv, mine, outer, hidden_in, gain_two[None], upstream, out_weight, ff_up, ff_down, groups,
        normed_got,
    )
    factors_got, last_got = swap(factors_theirs, 1), swap(last_theirs, 1)
    grad_ch = to_owner(grad_sent, mine, padded)
    orders = (dp_bits, dp_bits[::-1])
    firsts = (orders[0][0], orders[1][0])
    shape = (1, width // 2, width)
    up_operands = (factors_mine, factors_got)
    down_operands = (factors_mine, factors_got, upstream, upstream_got)
    up_sent, token = run_up_products(firsts, True, up_operands, shape)
    up = Group(orders, seq_bits, up_sent)
    down_sent, token = run_down_products(
        firsts, True, down_operands, shape, (token, last_got)
    )
    down = Group(orders, seq_bits, down_sent)
    outer_halo = shifted(grad_outer[:, :2], -1)

    back_ch, token = run_conv(
        lengths, row_len, grad_ch, my_skip, spectrum, forward_three, inverse_two, backward=True,
        after=(token,),
    )
    got = to_block(back_ch, rows, mine, groups)
    grad_signal, got = (got, got) if groups > 1 else got
    halo = got[:, 0, padded : padded + 2 * rows, :mine].astype(F32)
    halo = halo.transpose(1, 0, 2).reshape(rows, 2, width)
    up_kept, token = run_up_products(firsts, False, up_operands, shape, (token,))
    up.halve(up_kept)
    down_kept, token = run_down_products(firsts, False, down_operands, shape, (up.token,))
    down.halve(down_kept)
    up.scatter(None, (down.token,), BRIDGE_A)

    (proj_mine, proj_theirs, kernel_grad, gain_one_grad, input_grad), token = run_last(
        lengths, grad_signal, mine, halo, extended, grad_outer, outer_halo, hidden_in,
        gain_one[None], short_kernel, grad_middle, in_weight, (up.token,) if up.direct else (),
    )
    last_operands = (normed_one, normed_got, proj_mine, swap(proj_theirs, 1), last_mine, last_got)
    if up.direct:
        up.split((token,))
    down.scatter(None, (up.token,), BRIDGE_B)
    last_sent, token = run_last_products(
        firsts, True, last_operands, shape, (down.token,) if up.direct else ()
    )
    last = Group(orders, seq_bits, last_sent)
    last_kept, token = run_last_products(firsts, False, last_operands, shape, (token,))

    grad_taps, token = run_filter_grad(
        lengths, row_len, signal_ch, grad_ch, forward_two, inverse_two, forward_three,
        after=(token,),
    )
    envelope = jnp.pad(envelope, ((0, padded - mine), (0, 0)))
    my_third = jnp.pad(my_third, ((0, 0), (0, padded - mine)))
    net = (act_one, pre_one, act_two, pre_two)
    (my_third_grad, skip_grad, second_grad, first_grad), token = run_filter_back(
        grad_taps, envelope, net, my_third, filt_second, embedding, (token,)
    )
    small = (
        my_third_grad[:, :mine], skip_grad[:1, :mine], kernel_grad, gain_one_grad, gain_two_grad,
        second_grad, first_grad,
    )
    in_shapes = (in_weight.shape, out_weight.shape)
    if up.direct:
        (packed,), token = run_pack(dp_count, *small)
        arrived = lax.all_to_all(packed, "dp", 0, 0, tiled=True)
        up.total((token,))
        down.split((up.token,))
        last.halve(last_kept, (down.token,))
        up.pair((last.token,))
        down.total((up.token,))
        (packed,), token = run_total_all(arrived, (down.token,))
        last.scatter(packed, (token,))
        up.gather((last.token,))
        last.split((up.token,))
        down.pair((last.token,))
        up.join_last((down.token,))
        down.gather((up.token,))
        last.total((down.token,))
        down.join_last((last.token,))
        last.pair((down.token,))
        up.stack((last.token,))
        up_total = up.place_whole(up_place_kernel, ff_up.shape, (up.token,))
        last.gather((up.token,))
        last.join((last.token, mark(down.got)))
        down.stack((last.token,))
        last.place(last_place_kernel, in_shapes, (down.token,))
        down_total = down.place_whole(down_place_kernel, ff_down.shape, (last.token,))
        small, token = run_unpack(
            4, mine, last.small, swap(last.small, 1), filt_third.shape[0],
            filt_first.shape[0], (down.token,),
        )
        in_total, out_total = last.finish(last_place_kernel, in_shapes, (), (token,))
    else:
        last.halve(last_kept)
        last.scatter()
        for group in (up, down):
            group.gather()
            group.join_last()
            group.stack()
        last.gather()
        last.join()
        up_total = up.place_whole(up_place_kernel, ff_up.shape)
        down_total = down.place_whole(down_place_kernel, ff_down.shape)
        in_total, out_total = last.finish(last_place_kernel, in_shapes)
        spread = [
            lax.dynamic_update_slice_in_dim(
                jnp.zeros((part.shape[0], width), F32), part, seq_pos * mine, 1
            )
            for part in small[:2]
        ]
        small = lax.psum((*spread, small[2][:KS], *small[3:]), AXES)
    return (
        block_out, input_grad, small[3][0], in_total, small[2], small[1][0], small[6], small[5],
        small[0], out_total, small[4][0], up_total, down_total,
    )


def solution(mesh):
    tokens = P("dp", "seq", None)
    return jax.shard_map(
        per_device,
        mesh=mesh,
        in_specs=(tokens, P("dp", None)) + (P(),) * 12 + (tokens,),
        out_specs=(tokens, tokens) + (P(),) * 11,
        check_vma=False,
    )
```
